32 devices in a mesh: seq: 8 (over z, x), rep: 4 (over y, core).
Axes of the slice: x: 2, y: 2, z: 4, core: 2. Of those that a mesh axis runs over, the one named last changes fastest.
Arguments:
- tokens: bfloat16 [4096, 1024], P(('seq', 'rep')), may hold values from -40 to 40
- cotangent: bfloat16 [4096, 1024], P(('seq', 'rep')), may hold values from -6 to 6
- lengths: int32 [2], replicated, may hold values from 256 to 2048, as said below
- in_weight: bfloat16 [1, 1024, 3, 1024], P(None, 'seq', None, 'rep'), may hold values from -0.1875 to 0.1875
- in_bias: float32 [1, 3, 1024], replicated, may hold values from -2 to 2
- short_taps: float32 [1, 3, 3, 1024], replicated, may hold values from -1 to 1
- short_bias: float32 [1, 3, 1024], replicated, may hold values from -1.5 to 1.5
- feat_weight: float32 [1, 33, 64], replicated, may hold values from -1 to 1
- feat_bias: float32 [1, 64], replicated, may hold values from -4 to 4
- inner_weight: float32 [1, 64, 64], replicated, may hold values from -0.75 to 0.75
- inner_bias: float32 [1, 64], replicated, may hold values from -3 to 3
- deep_weight: float32 [1, 64, 64], replicated, may hold values from -0.75 to 0.75
- deep_bias: float32 [1, 64], replicated, may hold values from -3 to 3
- sine_freq: float32 [1, 64], replicated, may hold values from 0.5 to 1.5
- kernel_weight: float32 [1, 64, 1024], replicated, may hold values from -0.078125 to 0.078125
- skip_gain: float32 [1, 1024], replicated, may hold values from -4 to 4
- out_weight: bfloat16 [1, 1024, 1024], P(None, 'seq', 'rep'), may hold values from -0.1875 to 0.1875
- out_bias: float32 [1, 1024], replicated, may hold values from -1.5 to 1.5
- norm1_gain: float32 [1, 1024], replicated, may hold values from 0.5 to 1.5
- norm1_shift: float32 [1, 1024], replicated, may hold values from -1.5 to 1.5
- norm2_gain: float32 [1, 1024], replicated, may hold values from 0.5 to 1.5
- norm2_shift: float32 [1, 1024], replicated, may hold values from -1.5 to 1.5
- up_weight: bfloat16 [1, 1024, 4096], P(None, 'seq', 'rep'), may hold values from -0.1875 to 0.1875
- up_bias: float32 [1, 4096], replicated, may hold values from -2 to 2
- down_weight: bfloat16 [1, 1024, 4096], P(None, 'seq', 'rep'), may hold values from -0.125 to 0.125
- down_bias: float32 [1, 1024], replicated, may hold values from -1.5 to 1.5
Outputs:
- layer_out: bfloat16 [4096, 1024], P(('seq', 'rep'))
- grad_tokens: float32 [4096, 1024], P(('seq', 'rep'))
- grad_in_weight: float32 [1, 1024, 3, 1024], P(None, 'seq', None, 'rep')
- grad_in_bias: float32 [1, 3, 1024], replicated
- grad_short_taps: float32 [1, 3, 3, 1024], replicated
- grad_short_bias: float32 [1, 3, 1024], replicated
- grad_feat_weight: float32 [1, 33, 64], replicated
- grad_feat_bias: float32 [1, 64], replicated
- grad_inner_weight: float32 [1, 64, 64], replicated
- grad_inner_bias: float32 [1, 64], replicated
- grad_deep_weight: float32 [1, 64, 64], replicated
- grad_deep_bias: float32 [1, 64], replicated
- grad_sine_freq: float32 [1, 64], replicated
- grad_kernel_weight: float32 [1, 64, 1024], replicated
- grad_skip_gain: float32 [1, 1024], replicated
- grad_out_weight: float32 [1, 1024, 1024], P(None, 'seq', 'rep')
- grad_out_bias: float32 [1, 1024], replicated
- grad_norm1_gain: float32 [1, 1024], replicated
- grad_norm1_shift: float32 [1, 1024], replicated
- grad_norm2_gain: float32 [1, 1024], replicated
- grad_norm2_shift: float32 [1, 1024], replicated
- grad_up_weight: float32 [1, 1024, 4096], P(None, 'seq', 'rep')
- grad_up_bias: float32 [1, 4096], replicated
- grad_down_weight: float32 [1, 1024, 4096], P(None, 'seq', 'rep')
- grad_down_bias: float32 [1, 1024], replicated
The draws below stay inside these ranges and needn't reach their ends.
Inputs may be any that keep to these rules, and one draw needn't show every extreme that they name: lengths[0] is 2048; lengths[1] lies between 256 and 512.
All inputs are finite; a program needn't handle non-finite values.
Results may differ from the reference program's by a relative error of at most 0.017.
Values may be sent and summed in bfloat16 or wider, within the bound.
No kernel may reach another device: no remote copies, remote signals or barrier semaphores. Data moves between devices by JAX's collectives and lax.ppermute only.
A program may use at most 192 MiB of HBM per device.

```python
import math
import jax
import jax.numpy as jnp
from jax import lax

D = 1024
FF = 4096
FILT = 64
FEAT = 33
LAYERS = 1
TOKENS = 4096
LEN = 2048


def draw_tokens(key, part):
    key_base, key_rows = jax.random.split(key, 2)
    values = jax.random.normal(key_base, (TOKENS, D), jnp.float32)
    row_scale = jnp.exp(jax.random.uniform(key_rows, (TOKENS, 1), jnp.float32, -0.7, 0.7))
    values = values * row_scale
    return jnp.clip(values, -40.0, 40.0).astype(jnp.bfloat16)


def draw_lengths(key, part):
    short_len = jax.random.randint(key, (1,), LEN // 8, LEN // 4 + 1, dtype=jnp.int32)
    return jnp.concatenate([jnp.full((1,), LEN, dtype=jnp.int32), short_len])


def shard_levels(own_key, shape, cuts, smallest, high):
    factor_of = 1.0
    for dim, shards_of in cuts:
        steps = jax.random.uniform(jax.random.fold_in(jax.random.fold_in(own_key, 6), dim), (shards_of,), jnp.float32, smallest / len(cuts), high / len(cuts))
        factor_of = factor_of * jnp.repeat(jnp.exp(steps), shape[dim] // shards_of).reshape((-1,) + (1,) * (len(shape) - 1 - dim))
    return factor_of


def bell_draw(rng, shape, spread, bound, cuts=(), kind=jnp.bfloat16):
    level = shard_levels(rng, shape, cuts, -0.22, 0.18) if cuts else 1.0
    values = jax.random.normal(rng, shape, jnp.float32) * spread * level
    return jnp.minimum(jnp.maximum(values, -bound), bound).astype(kind)


def setup_inputs(seed: int = 0) -> dict:
    key_list = jax.random.split(jax.random.key(seed), 27)
    tokens = draw_tokens(jax.random.fold_in(key_list[26], 71), 0)
    cotangent = bell_draw(key_list[1], (TOKENS, D), 1.0, 6.0, ((0, 32),))
    lengths = draw_lengths(jax.random.fold_in(key_list[26], 71), 0)
    in_weight = bell_draw(key_list[3], (LAYERS, D, 3, D), D ** -0.5, 0.1875, ((1, 8), (3, 4)))
    in_bias = bell_draw(key_list[4], (LAYERS, 3, D), 0.3, 2.0, (), jnp.float32)
    short_taps = jnp.clip(jax.random.uniform(key_list[5], (LAYERS, 3, 3, D), jnp.float32, -1.0, 1.0), -1.0, 1.0)
    short_bias = bell_draw(key_list[6], (LAYERS, 3, D), 0.2, 1.5, (), jnp.float32)
    feat_weight = bell_draw(key_list[7], (LAYERS, FEAT, FILT), FEAT ** -0.5, 1.0, (), jnp.float32)
    feat_bias = bell_draw(key_list[8], (LAYERS, FILT), 1.0, 4.0, (), jnp.float32)
    inner_weight = bell_draw(key_list[9], (LAYERS, FILT, FILT), FILT ** -0.5, 0.75, (), jnp.float32)
    inner_bias = bell_draw(key_list[10], (LAYERS, FILT), 0.5, 3.0, (), jnp.float32)
    deep_weight = bell_draw(key_list[11], (LAYERS, FILT, FILT), FILT ** -0.5, 0.75, (), jnp.float32)
    deep_bias = bell_draw(key_list[12], (LAYERS, FILT), 0.5, 3.0, (), jnp.float32)
    sine_freq = jnp.clip(jax.random.uniform(key_list[13], (LAYERS, FILT), jnp.float32, 0.5, 1.5), 0.5, 1.5)
    kernel_weight = bell_draw(key_list[14], (LAYERS, FILT, D), (3 * LEN) ** -0.5, 0.078125, (), jnp.float32)
    skip_gain = bell_draw(key_list[15], (LAYERS, D), 1.0, 4.0, (), jnp.float32)
    out_weight = bell_draw(key_list[16], (LAYERS, D, D), D ** -0.5, 0.1875, ((1, 8), (2, 4)))
    out_bias = bell_draw(key_list[17], (LAYERS, D), 0.2, 1.5, (), jnp.float32)
    norm1_gain = jnp.clip(1.0 + 0.1 * jax.random.normal(key_list[18], (LAYERS, D), jnp.float32), 0.5, 1.5)
    norm1_shift = bell_draw(key_list[19], (LAYERS, D), 0.2, 1.5, (), jnp.float32)
    norm2_gain = jnp.clip(1.0 + 0.1 * jax.random.normal(key_list[20], (LAYERS, D), jnp.float32), 0.5, 1.5)
    norm2_shift = bell_draw(key_list[21], (LAYERS, D), 0.2, 1.5, (), jnp.float32)
    up_weight = bell_draw(key_list[22], (LAYERS, D, FF), D ** -0.5, 0.1875, ((1, 8), (2, 4)))
    up_bias = bell_draw(key_list[23], (LAYERS, FF), 0.3, 2.0, (), jnp.float32)
    down_weight = bell_draw(key_list[24], (LAYERS, D, FF), (FF // 2) ** -0.5, 0.125, ((1, 8), (2, 4)))
    down_bias = bell_draw(key_list[25], (LAYERS, D), 0.2, 1.5, (), jnp.float32)
    return {"tokens": tokens, "cotangent": cotangent, "lengths": lengths, "in_weight": in_weight, "in_bias": in_bias, "short_taps": short_taps, "short_bias": short_bias, "feat_weight": feat_weight, "feat_bias": feat_bias, "inner_weight": inner_weight, "inner_bias": inner_bias, "deep_weight": deep_weight, "deep_bias": deep_bias, "sine_freq": sine_freq, "kernel_weight": kernel_weight, "skip_gain": skip_gain, "out_weight": out_weight, "out_bias": out_bias, "norm1_gain": norm1_gain, "norm1_shift": norm1_shift, "norm2_gain": norm2_gain, "norm2_shift": norm2_shift, "up_weight": up_weight, "up_bias": up_bias, "down_weight": down_weight, "down_bias": down_bias}


@jax.custom_vjp
def low(v):
    return lax.optimization_barrier(v.astype(jnp.bfloat16)).astype(jnp.float32)

@jax.custom_vjp
def low_back(v):
    return v

def low_keep(v):
    return (low(v), None)

def low_pass(kept, grad):
    return (grad,)

def back_keep(v):
    return (v, None)

def back_low(kept, grad):
    return (low(grad),)
low.defvjp(low_keep, low_pass)
low_back.defvjp(back_keep, back_low)
EPS = 1e-05
HIGH = lax.Precision.HIGHEST

def matmul(left, right):
    return jnp.dot(left, right, precision=HIGH, preferred_element_type=jnp.float32)

def layer_norm(rows, gain, shift):
    row_mean = lax.optimization_barrier(jnp.mean(rows, axis=-1, keepdims=True))
    centred = rows - row_mean
    variance = lax.optimization_barrier(jnp.mean(centred * centred, axis=-1, keepdims=True))
    return centred * lax.rsqrt(variance + EPS) * gain + shift

def features(length, feat_count):
    ramp_unit = jnp.linspace(0.0, 1.0, length, dtype=jnp.float32)
    angles = jnp.arange(length, dtype=jnp.float32)[:, None] * (2.0 * math.pi / length)
    band_freqs = jnp.linspace(0.0001, (feat_count - 1) // 2 - 1.0, (feat_count - 1) // 2, dtype=jnp.float32)[None, :]
    phase_grid = band_freqs * angles
    grid_out = jnp.concatenate([ramp_unit[:, None], jnp.cos(phase_grid), -jnp.sin(phase_grid)], axis=1)
    return (grid_out, ramp_unit)

def kernel_table(feature_grid, ramp_unit, feat_weight, feat_bias, inner_weight, inner_bias, deep_weight, deep_bias, sine_freq, kernel_weight):
    hidden = jnp.sin(sine_freq * (matmul(feature_grid, feat_weight) + feat_bias))
    hidden = jnp.sin(sine_freq * (matmul(hidden, inner_weight) + inner_bias))
    hidden = jnp.sin(sine_freq * (matmul(hidden, deep_weight) + deep_bias))
    deltas = jnp.abs(jnp.linspace(math.log(0.01) / 0.3, math.log(0.01) / 1.5, D, dtype=jnp.float32))
    return matmul(hidden, kernel_weight) * jnp.exp(-ramp_unit[:, None] * deltas[None, :])

def long_conv(signal, kernel):
    size_fft = 2 * LEN
    spectrum = jnp.fft.rfft(signal, n=size_fft, axis=1) * jnp.fft.rfft(kernel, n=size_fft, axis=0)[None]
    return jnp.fft.irfft(spectrum, n=size_fft, axis=1)[:, :LEN]

def block(residual, params, row_mask, feature_grid, ramp_unit):
    in_weight, in_bias, short_taps, short_bias, feat_weight, feat_bias, inner_weight, inner_bias, deep_weight, deep_bias, sine_freq, kernel_weight, skip_gain, out_weight, out_bias, norm1_gain, norm1_shift, norm2_gain, norm2_shift, up_weight, up_bias, down_weight, down_bias = params
    normed_one = low(layer_norm(residual, norm1_gain, norm1_shift))
    projected = matmul(normed_one, in_weight.reshape(D, 3 * D)).reshape(-1, 3, D) + in_bias
    projected = low(low_back(projected))
    items = projected.reshape(2, LEN, 3, D)
    padded = jnp.pad(items, ((0, 0), (2, 0), (0, 0), (0, 0)))
    shorted = short_taps[0] * padded[:, :LEN] + short_taps[1] * padded[:, 1:LEN + 1] + short_taps[2] * items + short_bias
    gated_in = shorted[:, :, 2] * shorted[:, :, 1] * row_mask.reshape(2, LEN, 1)
    kernel = kernel_table(feature_grid, ramp_unit, feat_weight, feat_bias, inner_weight, inner_bias, deep_weight, deep_bias, sine_freq, kernel_weight)
    mixed_sum = long_conv(gated_in, kernel) + skip_gain * gated_in
    mixed_rows = low(low_back((shorted[:, :, 0] * mixed_sum).reshape(-1, D)))
    middle = residual + low_back(matmul(mixed_rows, out_weight.T) + out_bias)
    normed_two = low(layer_norm(middle, norm2_gain, norm2_shift))
    pre_act = low_back(matmul(normed_two, up_weight) + up_bias)
    activated = low(jax.nn.gelu(pre_act, approximate=False))
    return middle + low_back(matmul(activated, down_weight.T) + down_bias)

def reference(tokens, cotangent, lengths, in_weight, in_bias, short_taps, short_bias, feat_weight, feat_bias, inner_weight, inner_bias, deep_weight, deep_bias, sine_freq, kernel_weight, skip_gain, out_weight, out_bias, norm1_gain, norm1_shift, norm2_gain, norm2_shift, up_weight, up_bias, down_weight, down_bias):
    token_ids = jnp.arange(TOKENS, dtype=jnp.int32)
    limits = jnp.where(token_ids // LEN == 0, lengths[0], lengths[1])
    row_mask = (token_ids % LEN < limits).astype(jnp.float32)
    feature_grid, ramp_unit = features(LEN, FEAT)
    weights = (in_weight, in_bias, short_taps, short_bias, feat_weight, feat_bias, inner_weight, inner_bias, deep_weight, deep_bias, sine_freq, kernel_weight, skip_gain, out_weight, out_bias, norm1_gain, norm1_shift, norm2_gain, norm2_shift, up_weight, up_bias, down_weight, down_bias)
    params = tuple((stacked.astype(jnp.float32) for stacked in weights))

    def forward(start_rows, layer_params):
        residual = start_rows
        for layer_idx in range(LAYERS):
            residual = block(residual, tuple((stacked[layer_idx] for stacked in layer_params)), row_mask, feature_grid, ramp_unit)
        return residual
    layer_out, pullback = jax.vjp(forward, tokens.astype(jnp.float32), params)
    grad_tokens, grad_list = pullback(cotangent.astype(jnp.float32) * row_mask[:, None])
    return (layer_out.astype(jnp.bfloat16), grad_tokens, grad_list[0], grad_list[1], grad_list[2], grad_list[3], grad_list[4], grad_list[5], grad_list[6], grad_list[7], grad_list[8], grad_list[9], grad_list[10], grad_list[11], grad_list[12], grad_list[13], grad_list[14], grad_list[15], grad_list[16], grad_list[17], grad_list[18], grad_list[19], grad_list[20], grad_list[21], grad_list[22])
```

```python
from functools import partial
import math

import jax
import jax.numpy as jnp
import numpy as np
from jax import lax
from jax.experimental import pallas as pl
from jax.experimental.pallas import tpu as pltpu
from jax.sharding import PartitionSpec as P

EPS = 1e-05
HIGH = lax.Precision.HIGHEST
F32 = jnp.float32
B16 = jnp.bfloat16
LANE = 128
HALO = 16
VMEM_BYTES = 48 * 2**20


def swap(values, axis_name, bit):
    size = lax.axis_size(axis_name)
    return lax.ppermute(values, axis_name, [(i, i ^ bit) for i in range(size)])


def gather_rel(rows):
    far = swap(rows, "rep", 2)
    near = swap(rows, "rep", 1)
    diag = swap(far, "rep", 1)
    return jnp.concatenate([rows, near, far, diag], axis=0)


def scatter_rel(part):
    rows = part.shape[0] // 4
    blocks = part.reshape(4, rows, part.shape[1])
    far_in = swap(blocks[3].astype(B16), "rep", 1)
    far_sum = (blocks[2] + far_in.astype(F32)).astype(B16)
    near_in = swap(blocks[1].astype(B16), "rep", 1)
    far_out = swap(far_sum, "rep", 2)
    return blocks[0] + near_in.astype(F32) + far_out.astype(F32)


def ring_order(count):
    if count == 8:
        return [0, 2, 4, 6, 7, 5, 3, 1]
    return list(range(count))


def ring_gather(shard):
    count = lax.axis_size("seq")
    if count != 8:
        return lax.all_gather(shard, "seq", axis=0)
    order = ring_order(count)
    ahead = [(order[i], order[(i + 1) % count]) for i in range(count)]
    back = [(b, a) for a, b in ahead]
    me = lax.axis_index("seq")
    place = jnp.asarray(np.argsort(order), jnp.int32)[me]
    owners = jnp.asarray(order, jnp.int32)
    full = jnp.zeros((count,) + shard.shape, shard.dtype)

    def put(full, piece, step, lo=0):
        owner = owners[(place + step + count) % count]
        start = (owner, lo) + (0,) * (shard.ndim - 1)
        return lax.dynamic_update_slice(full, piece[None], start)

    full = put(full, shard, 0)
    left = right = shard
    for step in range(1, count // 2):
        left = lax.ppermute(left, "seq", ahead)
        right = lax.ppermute(right, "seq", back)
        full = put(full, left, -step)
        full = put(full, right, step)
    half = shard.shape[0] // 2
    left = lax.ppermute(left[:half], "seq", ahead)
    right = lax.ppermute(right[half:], "seq", back)
    full = put(full, left, -(count // 2))
    full = put(full, right, count // 2, half)
    return full


def shift_seq(values, step):
    count = lax.axis_size("seq")
    return lax.ppermute(values, "seq", [(i, (i + step) % count) for i in range(count)])


def unmix(values, axis, index):
    size, bit = values.shape[axis], 1
    while bit < size:
        cut = values.shape[:axis] + (size // (2 * bit), 2, bit) + values.shape[axis + 1 :]
        split = values.reshape(cut)
        values = jnp.where((index // bit) % 2 == 1, jnp.flip(split, axis + 1), split).reshape(values.shape)
        bit *= 2
    return values


def sync_small(total, group, own):
    n_seq, n_rep = lax.axis_size("seq"), lax.axis_size("rep")
    group_list, own_list = [group], [own]
    for axis_name, size in (("seq", n_seq), ("rep", n_rep)):
        bit = 1
        while bit < size:
            parts = [total] + group_list + own_list
            sizes = np.cumsum([0] + [p.shape[0] for p in parts])
            came = swap(jnp.concatenate(parts, axis=0), axis_name, bit)
            came = [came[a:b] for a, b in zip(sizes[:-1], sizes[1:])]
            total = total + came[0]
            count = len(group_list)
            if axis_name == "seq":
                group_list = [group_list[0] + came[1]]
            else:
                group_list = group_list + came[1 : 1 + count]
            own_list = own_list + came[1 + count :]
            bit *= 2
    groups = unmix(jnp.stack(group_list), 0, lax.axis_index("rep"))
    owns = jnp.stack(own_list).reshape((n_rep, n_seq) + own.shape)
    owns = unmix(unmix(owns, 0, lax.axis_index("rep")), 1, lax.axis_index("seq"))
    return total, groups, owns


def layer_norm(rows, gain, shift):
    row_mean = jnp.mean(rows, axis=-1, keepdims=True)
    centred = rows - row_mean
    variance = jnp.mean(centred * centred, axis=-1, keepdims=True)
    inverse = lax.rsqrt(variance + EPS)
    normed = centred * inverse
    return (normed * gain + shift, normed, inverse)


def norm_back(grad_rows, normed, inverse, gain):
    scaled = grad_rows * gain
    mean_one = jnp.mean(scaled, axis=-1, keepdims=True)
    mean_two = jnp.mean(scaled * normed, axis=-1, keepdims=True)
    grad_in = inverse * (scaled - mean_one - normed * mean_two)
    return (grad_in, jnp.sum(grad_rows * normed, axis=0), jnp.sum(grad_rows, axis=0))


def features(length, feat_count):
    ramp_unit = jnp.linspace(0.0, 1.0, length, dtype=F32)
    angles = jnp.arange(length, dtype=F32)[:, None] * (2.0 * math.pi / length)
    band_freqs = jnp.linspace(
        0.0001, (feat_count - 1) // 2 - 1.0, (feat_count - 1) // 2, dtype=F32
    )[None, :]
    phase_grid = band_freqs * angles
    grid_out = jnp.concatenate(
        [ramp_unit[:, None], jnp.cos(phase_grid), -jnp.sin(phase_grid)], axis=1
    )
    return (grid_out, ramp_unit)


def filter_columns(
    feature_grid,
    ramp_unit,
    start_chan,
    chan_count,
    model_width,
    feat_weight,
    feat_bias,
    inner_weight,
    inner_bias,
    deep_weight,
    deep_bias,
    sine_freq,
    columns,
):
    freq = sine_freq[:, None]

    def layer(weight, bias, below):
        grown = lax.dot_general(weight, below, (((0,), (0,)), ((), ())), precision=HIGH)
        return jnp.sin(freq * (grown + bias[:, None]))

    hidden = layer(feat_weight, feat_bias, feature_grid.T)
    hidden = layer(inner_weight, inner_bias, hidden)
    hidden = layer(deep_weight, deep_bias, hidden)
    deltas = jnp.abs(
        jnp.linspace(math.log(0.01) / 0.3, math.log(0.01) / 1.5, model_width, dtype=F32)
    )
    local_rates = lax.dynamic_slice_in_dim(deltas, start_chan, chan_count)
    return lax.dot_general(
        columns, hidden, (((0,), (0,)), ((), ())), precision=HIGH
    ) * jnp.exp(-ramp_unit[None, :] * local_rates[:, None])


def transform_tables(blocks, length):
    time = np.arange(blocks * length).reshape(blocks, 1, length)
    cls = np.arange(blocks).reshape(1, blocks, 1)
    period = 4 * blocks * length
    turn = (time * (2 * cls + 1)) % period * (2.0 * np.pi / period)
    twist = np.stack([np.cos(turn), -np.sin(turn)], axis=2).astype(np.float32)
    step = np.arange(length)
    turn = (step[:, None] * step[None, :]) % length * (2.0 * np.pi / length)
    cos, sin = np.cos(turn), np.sin(turn)
    table = np.block([[cos, -sin], [sin, cos]]).astype(np.float32)
    return twist, table


def spectrum_of(signal, twist, table):
    turned = jnp.einsum("bqzl,brl->qrzl", twist[: signal.shape[0]], signal, precision=HIGH)
    flat = turned.reshape(turned.shape[:2] + (-1,))
    return jnp.einsum("qrk,kf->qrf", flat, table, precision=HIGH)


def signal_of(spectrum, twist, table):
    blocks, length = twist.shape[0], twist.shape[3]
    turned = jnp.einsum("qrf,kf->qrk", spectrum, table, precision=HIGH)
    turned = turned.reshape(turned.shape[:2] + (2, length))
    return jnp.einsum("bqzl,qrzl->brl", twist, turned, precision=HIGH) * (1.0 / (blocks * length))


def times(left, right, conj_right):
    half = left.shape[-1] // 2
    lr, li = left[..., :half], left[..., half:]
    rr, ri = right[..., :half], right[..., half:]
    if conj_right:
        return jnp.concatenate([lr * rr + li * ri, li * rr - lr * ri], axis=-1)
    return jnp.concatenate([lr * rr - li * ri, lr * ri + li * rr], axis=-1)


def dot_split(values, hi, lo, dims):
    top = values.astype(B16)
    rest = (values - top.astype(F32)).astype(B16)
    dot = partial(lax.dot_general, dimension_numbers=(dims, ((), ())), preferred_element_type=F32)
    return dot(top, hi) + dot(rest, hi) + dot(top, lo)


def turn_rows(blocks_in, twist_ref, z_ref, base, classes):
    rows, length = blocks_in[0].shape
    for q in range(classes):
        for z in range(2):
            acc = None
            for b, block in enumerate(blocks_in):
                term = block * twist_ref[b, q, z : z + 1]
                acc = term if acc is None else acc + term
            z_ref[base + q * rows : base + (q + 1) * rows, z * length : (z + 1) * length] = acc


def back_rows(w, base, rows, block, twist_ref, classes):
    length = w.shape[1] // 2
    acc = None
    for q in range(classes):
        lo, hi = base + q * rows, base + (q + 1) * rows
        for z in range(2):
            term = w[lo:hi, z * length : (z + 1) * length] * twist_ref[block, q, z : z + 1]
            acc = term if acc is None else acc + term
    return acc * (1.0 / (classes * length))


def conv_forward_kernel(short_blocks, x_ref, kern_ref, twist_ref, hi_ref, lo_ref, skip_ref, out_ref, spec_ref, z_ref):
    blocks = twist_ref.shape[0]
    rows = x_ref.shape[1]
    span = blocks * rows
    first = [x_ref[b].astype(F32) for b in range(blocks)]
    second = [x_ref[blocks + b].astype(F32) for b in range(short_blocks)]
    turn_rows(first, twist_ref, z_ref, 0, blocks)
    turn_rows(second, twist_ref, z_ref, span, blocks)
    spec = dot_split(z_ref[...], hi_ref[...], lo_ref[...], ((1,), (0,)))
    spec_ref[...] = spec
    kern = kern_ref[...]
    prod = jnp.concatenate([times(spec[:span], kern, False), times(spec[span:], kern, False)], axis=0)
    w = dot_split(prod, hi_ref[...], lo_ref[...], ((1,), (1,)))
    skip = skip_ref[...]
    for b in range(blocks):
        out_ref[b] = (back_rows(w, 0, rows, b, twist_ref, blocks) + skip * first[b]).astype(B16)
        acc = back_rows(w, span, rows, b, twist_ref, blocks)
        if b < short_blocks:
            acc = acc + skip * second[b]
        out_ref[blocks + b] = acc.astype(B16)


def conv_backward_kernel(
    short_blocks, g_ref, spec_ref, kern_ref, twist_ref, hi_ref, lo_ref, skip_ref, out_ref, grad_kern_ref, z_ref, p_ref
):
    blocks = twist_ref.shape[0]
    rows = g_ref.shape[1]
    span = blocks * rows
    first = [g_ref[b].astype(F32) for b in range(blocks)]
    second = [g_ref[blocks + b].astype(F32) for b in range(short_blocks)]
    turn_rows(first, twist_ref, z_ref, 0, blocks)
    turn_rows(second, twist_ref, z_ref, span, blocks)
    grad = dot_split(z_ref[...], hi_ref[...], lo_ref[...], ((1,), (0,)))
    kern = kern_ref[...]
    p_ref[0:span] = times(grad[:span], kern, True)
    p_ref[span : 2 * span] = times(grad[span:], kern, True)
    p_ref[2 * span :] = times(grad[:span], spec_ref[0:span], True) + times(
        grad[span:], spec_ref[span:], True
    )
    w = dot_split(p_ref[...], hi_ref[...], lo_ref[...], ((1,), (1,)))
    skip = skip_ref[...]
    for b in range(blocks):
        out_ref[b] = (back_rows(w, 0, rows, b, twist_ref, blocks) + skip * first[b]).astype(B16)
        if b < short_blocks:
            acc = back_rows(w, span, rows, b, twist_ref, blocks) + skip * second[b]
            out_ref[blocks + b] = acc.astype(B16)
        else:
            out_ref[blocks + b] = jnp.zeros(out_ref.shape[1:], B16)
        grad_kern_ref[b] = back_rows(w, 2 * span, rows, b, twist_ref, blocks)


def conv_forward(received, kern_spec, twist, table, skip_local):
    blocks, rows, length = received.shape[0] // 2, received.shape[1], received.shape[2]
    short_blocks = -(-blocks // 4)
    skip = skip_local[:, None]
    if blocks != 4:
        x = received.astype(F32)
        spec = jnp.concatenate(
            [
                spectrum_of(x[:blocks], twist, table),
                spectrum_of(x[blocks : blocks + short_blocks], twist, table),
            ],
            axis=0,
        )
        kern = jnp.concatenate([kern_spec, kern_spec], axis=0)
        prod = times(spec, kern, False)
        out = jnp.concatenate(
            [signal_of(prod[:blocks], twist, table), signal_of(prod[blocks:], twist, table)], axis=0
        )
        return ((out + skip * x).astype(B16), spec)
    hi = jnp.asarray(table).astype(B16)
    lo = (jnp.asarray(table) - hi.astype(F32)).astype(B16)
    height = 2 * blocks * rows
    out, spec = pl.pallas_call(
        partial(conv_forward_kernel, short_blocks),
        out_shape=(
            jax.ShapeDtypeStruct(received.shape, B16),
            jax.ShapeDtypeStruct((height, 2 * length), F32),
        ),
        scratch_shapes=[pltpu.VMEM((height, 2 * length), F32)],
        compiler_params=pltpu.CompilerParams(vmem_limit_bytes=VMEM_BYTES),
        name="conv_forward",
    )(received, kern_spec.reshape(blocks * rows, 2 * length), twist, hi, lo, skip)
    return out, spec


def conv_backward(grads, spec, kern_spec, twist, table, skip_local):
    blocks, rows, length = grads.shape[0] // 2, grads.shape[1], grads.shape[2]
    short_blocks = -(-blocks // 4)
    skip = skip_local[:, None]
    if blocks != 4:
        g = grads.astype(F32)
        first = spectrum_of(g[:blocks], twist, table)
        second = spectrum_of(g[blocks : blocks + short_blocks], twist, table)
        one = signal_of(times(first, kern_spec, True), twist, table)
        two = signal_of(times(second, kern_spec, True), twist, table)
        cross = times(first, spec[:blocks], True) + times(second, spec[blocks:], True)
        out = jnp.concatenate([one, two], axis=0) + skip * g
        return (out.astype(B16), signal_of(cross, twist, table))
    hi = jnp.asarray(table).astype(B16)
    lo = (jnp.asarray(table) - hi.astype(F32)).astype(B16)
    span = blocks * rows
    out, grad_kern = pl.pallas_call(
        partial(conv_backward_kernel, short_blocks),
        out_shape=(
            jax.ShapeDtypeStruct(grads.shape, B16),
            jax.ShapeDtypeStruct((blocks, rows, length), F32),
        ),
        scratch_shapes=[
            pltpu.VMEM((2 * span, 2 * length), F32),
            pltpu.VMEM((3 * span, 2 * length), F32),
        ],
        compiler_params=pltpu.CompilerParams(vmem_limit_bytes=VMEM_BYTES),
        name="conv_backward",
    )(grads, spec, kern_spec.reshape(span, 2 * length), twist, hi, lo, skip)
    return out, grad_kern


def in_order(ref, rep, lead=()):
    count = ref.shape[-1] // LANE
    return [
        ref[lead + (slice(None), pl.ds(pl.multiple_of((rep ^ j) * LANE, LANE), LANE))]
        for j in range(count)
    ]


def put_rel(ref, rep, values, lead=()):
    for j in range(ref.shape[-1] // LANE):
        ref[lead + (slice(None), pl.ds(pl.multiple_of((rep ^ j) * LANE, LANE), LANE))] = values[
            :, j * LANE : (j + 1) * LANE
        ]


def extended(proj_ref, halo_ref, exists, rep, p):
    blocks = [halo_ref[p, :, :LANE]] + in_order(proj_ref, rep, (p,)) + [halo_ref[p, :, LANE:]]
    return jnp.concatenate(blocks, axis=1).astype(F32) * exists


def short_of(ext, col_ref, p):
    return (
        col_ref[:, p : p + 1] * pltpu.roll(ext, 2, 1)
        + col_ref[:, 3 + p : 4 + p] * pltpu.roll(ext, 1, 1)
        + col_ref[:, 6 + p : 7 + p] * ext
        + col_ref[:, 9 + p : 10 + p]
    )


def gate_kernel(rep_ref, proj_ref, halo_ref, col_ref, mask_ref, out_ref):
    rep = rep_ref[0]
    mask, exists = mask_ref[0:1], mask_ref[1:2]
    gate_in = short_of(extended(proj_ref, halo_ref, exists, rep, 1), col_ref, 1)
    values = short_of(extended(proj_ref, halo_ref, exists, rep, 2), col_ref, 2)
    gated = values * gate_in * mask
    out_ref[...] = gated[:, LANE:-LANE].astype(B16)


def output_kernel(rep_ref, proj_ref, halo_ref, col_ref, mask_ref, mixed_ref, out_ref):
    rep = rep_ref[0]
    gate_out = short_of(extended(proj_ref, halo_ref, mask_ref[1:2], rep, 0), col_ref, 0)
    put_rel(out_ref, rep, (gate_out[:, LANE:-LANE] * mixed_ref[...].astype(F32)).astype(B16))


def grad_mix_kernel(rep_ref, proj_ref, halo_ref, col_ref, mask_ref, mixed_ref, gy_ref, out_ref, first_ref):
    rep = rep_ref[0]
    gate_out = short_of(extended(proj_ref, halo_ref, mask_ref[1:2], rep, 0), col_ref, 0)
    gy = jnp.concatenate(in_order(gy_ref, rep), axis=1).astype(F32)
    out_ref[...] = (gy * gate_out[:, LANE:-LANE]).astype(B16)
    first_ref[...] = gy[:, :LANE] * mixed_ref[:, :LANE].astype(F32)


def grad_proj_kernel(
    rep_ref, proj_ref, halo_ref, col_ref, mask_ref, mixed_ref, gy_ref, ggated_ref, gnext_ref, onext_ref, out_ref, sum_ref
):
    rep = rep_ref[0]
    mask, exists = mask_ref[0:1], mask_ref[1:2]
    size = mask_ref.shape[1]
    mid = slice(LANE, size - LANE)
    gy = jnp.concatenate(in_order(gy_ref, rep), axis=1).astype(F32)
    zero = jnp.zeros((gy.shape[0], LANE), F32)
    next_on = exists[:, size - LANE :]
    ext = [extended(proj_ref, halo_ref, exists, rep, p) for p in range(3)]
    short = [short_of(ext[p], col_ref, p) for p in range(3)]
    ggated = jnp.concatenate(
        [zero, ggated_ref[...].astype(F32), gnext_ref[...].astype(F32) * next_on], axis=1
    )
    ggated = ggated * mask
    gout = gy * mixed_ref[...].astype(F32)
    gshort = [
        jnp.concatenate([zero, gout, onext_ref[...] * next_on], axis=1),
        ggated * short[2],
        ggated * short[1],
    ]
    gated = short[2][:, mid] * short[1][:, mid] * mask[:, mid]
    sums = [jnp.sum(gy * short[0][:, mid] * gated, axis=1, keepdims=True)]
    for p in range(3):
        mine = gshort[p][:, mid]
        sums.append(jnp.sum(mine, axis=1, keepdims=True))
        sums.append(jnp.sum(mine * ext[p][:, mid], axis=1, keepdims=True))
        sums.append(jnp.sum(mine * pltpu.roll(ext[p], 1, 1)[:, mid], axis=1, keepdims=True))
        sums.append(jnp.sum(mine * pltpu.roll(ext[p], 2, 1)[:, mid], axis=1, keepdims=True))
        gproj = (
            col_ref[:, 6 + p : 7 + p] * gshort[p]
            + col_ref[:, 3 + p : 4 + p] * pltpu.roll(gshort[p], size - 1, 1)
            + col_ref[:, p : p + 1] * pltpu.roll(gshort[p], size - 2, 1)
        )[:, mid].astype(B16)
        sums.append(jnp.sum(gproj.astype(F32), axis=1, keepdims=True))
        put_rel(out_ref, rep, gproj, (p,))
    sum_ref[...] = jnp.concatenate(sums, axis=1)


def token_call(kernel, name, arrays, outs):
    step = 64

    def spec(shape, cut):
        if not cut:
            return pl.BlockSpec(shape, lambda i: (0,) * len(shape))
        if len(shape) == 3:
            return pl.BlockSpec((shape[0], step, shape[2]), lambda i: (0, i, 0))
        return pl.BlockSpec((step, shape[1]), lambda i: (i, 0))

    width = outs[0].shape[-2]
    return pl.pallas_call(
        kernel,
        grid=(width // step,),
        in_specs=[pl.BlockSpec(memory_space=pltpu.SMEM)] + [spec(a.shape, cut) for a, cut in arrays[1:]],
        out_specs=[spec(o.shape, True) for o in outs],
        out_shape=outs,
        compiler_params=pltpu.CompilerParams(vmem_limit_bytes=VMEM_BYTES),
        name=name,
    )(*[a for a, _ in arrays])


def rows128(values):
    flat = values.reshape(-1)
    return jnp.pad(flat, (0, -flat.shape[0] % 1024)).reshape(-1, 128)


def per_device(
    tokens,
    cotangent,
    lengths,
    in_weight,
    in_bias,
    short_taps,
    short_bias,
    feat_weight,
    feat_bias,
    inner_weight,
    inner_bias,
    deep_weight,
    deep_bias,
    sine_freq,
    kernel_weight,
    skip_gain,
    out_weight,
    out_bias,
    norm1_gain,
    norm1_shift,
    norm2_gain,
    norm2_shift,
    up_weight,
    up_bias,
    down_weight,
    down_bias,
):
    n_seq, n_rep = lax.axis_size("seq"), lax.axis_size("rep")
    seq, rep = lax.axis_index("seq"), lax.axis_index("rep")
    tok_rows, model = tokens.shape
    group = tok_rows * n_rep
    blocks = n_seq // 2
    seq_len = blocks * group
    chan = model // (n_seq * n_rep)
    width = model // n_rep
    hidden = up_weight.shape[2]
    block_start = rep * width
    chan_start = block_start + seq * chan
    rep_scalar = jnp.reshape(rep, (1,)).astype(jnp.int32)

    item_len = jnp.where(seq // blocks == 0, lengths[0], lengths[1])
    at = (seq % blocks) * group
    row_mask = (at + rep * tok_rows + jnp.arange(tok_rows, dtype=jnp.int32) < item_len).astype(F32)[:, None]
    position = at - LANE + jnp.arange(group + 2 * LANE, dtype=jnp.int32)
    mask_ext = jnp.stack([position < item_len, (position >= 0) & (position < seq_len)]).astype(F32)
    mask_ext = jnp.pad(mask_ext, ((0, 6), (0, 0)))

    full_in = ring_gather(in_weight[0]).reshape(model, 3, width)
    full_out = lax.all_gather(out_weight[0], "seq", axis=0, tiled=True)
    full_up = lax.all_gather(up_weight[0], "seq", axis=0, tiled=True)
    full_down = lax.all_gather(down_weight[0], "seq", axis=0, tiled=True)

    residual = tokens.astype(F32)
    normed_one, unit_one, scale_one = layer_norm(residual, norm1_gain[0], norm1_shift[0])
    normed_one = normed_one.astype(B16)
    rows_one = gather_rel(normed_one)
    rel = rows_one.reshape(n_rep, tok_rows, model)
    last_rows = lax.dynamic_index_in_dim(rel, rep ^ (n_rep - 1), 0, False)[-HALO:]
    first_rows = lax.dynamic_index_in_dim(rel, rep, 0, False)[:HALO]
    before = shift_seq(last_rows, 1)
    after = shift_seq(first_rows, -1)
    gap = jnp.zeros((LANE - HALO, model), B16)
    halo_rows = jnp.concatenate([gap, before, after, gap], axis=0)
    proj_bias = lax.dynamic_slice_in_dim(in_bias[0], block_start, width, 1)[:, :, None]

    def project(rows):
        return (
            jnp.einsum("td,dpc->pct", rows, full_in, preferred_element_type=F32) + proj_bias
        ).astype(B16)

    proj = project(rows_one)
    halo = project(halo_rows)

    tap_cols = lax.dynamic_slice_in_dim(short_taps[0], block_start, width, 2).reshape(9, width)
    bias_cols = lax.dynamic_slice_in_dim(short_bias[0], block_start, width, 1)
    cols = jnp.pad(jnp.concatenate([tap_cols, bias_cols], axis=0), ((0, 4), (0, 0))).T
    common = [(rep_scalar, True), (proj, True), (halo, True), (cols, True), (mask_ext, False)]
    flat_shape = jax.ShapeDtypeStruct((width, group), B16)
    (gated,) = token_call(gate_kernel, "gate", common, [flat_shape])
    received = lax.all_to_all(gated.reshape(n_seq, chan, group), "seq", 0, 0, tiled=True)

    skip_local = lax.dynamic_slice_in_dim(skip_gain[0], chan_start, chan, 0)
    columns = lax.dynamic_slice_in_dim(kernel_weight[0], chan_start, chan, 1)
    feature_grid, ramp_unit = features(seq_len, feat_weight.shape[1])
    twist, table = transform_tables(blocks, group)
    kernel, kernel_pull = jax.vjp(
        partial(filter_columns, feature_grid, ramp_unit, chan_start, chan, model),
        feat_weight[0],
        feat_bias[0],
        inner_weight[0],
        inner_bias[0],
        deep_weight[0],
        deep_bias[0],
        sine_freq[0],
        columns,
    )
    kern_blocks = kernel.reshape(chan, blocks, group).transpose(1, 0, 2)
    kern_spec = spectrum_of(kern_blocks, twist, table)
    mixed_chan, kept_spec = conv_forward(received, kern_spec, twist, table, skip_local)
    mixed = lax.all_to_all(mixed_chan, "seq", 0, 0, tiled=True).reshape(width, group)
    (y_cols,) = token_call(output_kernel, "output", common + [(mixed, True)], [flat_shape])

    middle_part = jnp.einsum("ct,oc->to", y_cols, full_out, preferred_element_type=F32)
    middle = residual + (scatter_rel(middle_part) + out_bias[0])
    normed_two, unit_two, scale_two = layer_norm(middle, norm2_gain[0], norm2_shift[0])
    rows_two = gather_rel(normed_two.astype(B16))

    grad_top = cotangent.astype(F32) * row_mask
    grad_mlp = grad_top.astype(B16)
    mlp_rows = gather_rel(grad_mlp)
    grad_act = jnp.dot(mlp_rows, full_down, preferred_element_type=F32)
    up_block = lax.dynamic_slice_in_dim(up_bias[0], rep * hidden, hidden, 0)
    pre_act = jnp.dot(rows_two, full_up, preferred_element_type=F32) + up_block
    phi = 0.5 * (1.0 + lax.erf(pre_act * math.sqrt(0.5)))
    act_rows = (pre_act * phi).astype(B16)
    slope = phi + pre_act * (jnp.exp(-0.5 * pre_act * pre_act) * (1.0 / math.sqrt(2.0 * math.pi)))
    grad_pre = (grad_act * slope).astype(B16)
    grad_two = scatter_rel(jnp.einsum("tf,df->td", grad_pre, full_up, preferred_element_type=F32))
    mlp_part = jnp.einsum("tf,of->to", act_rows, full_down, preferred_element_type=F32)
    layer_out = (middle + (scatter_rel(mlp_part) + down_bias[0])).astype(B16)
    term_down = jnp.einsum("to,tf->of", mlp_rows, act_rows, preferred_element_type=F32)
    term_up = jnp.einsum("td,tf->df", rows_two, grad_pre, preferred_element_type=F32)
    grad_down_bias = jnp.sum(grad_mlp.astype(F32), axis=0)
    grad_up_block = jnp.sum(grad_pre.astype(F32), axis=0)

    def to_owner(term):
        return lax.psum_scatter(term.astype(B16), "seq", scatter_dimension=0, tiled=True).astype(F32)

    grad_up = to_owner(term_up)
    grad_down = to_owner(term_down)

    grad_unit_two, grad_gain_two, grad_shift_two = norm_back(
        grad_two, unit_two, scale_two, norm2_gain[0]
    )
    grad_middle = grad_top + grad_unit_two
    grad_mix = grad_middle.astype(B16)
    grad_out_bias = jnp.sum(grad_mix.astype(F32), axis=0)
    mix_rows = gather_rel(grad_mix)
    gy_cols = jnp.einsum("to,oc->ct", mix_rows, full_out, preferred_element_type=F32).astype(B16)
    term_out = jnp.einsum("to,ct->oc", mix_rows, y_cols, preferred_element_type=F32)
    grad_out = to_owner(term_out)

    grad_mixed, gate_first = token_call(
        grad_mix_kernel,
        "grad_mix",
        common + [(mixed, True), (gy_cols, True)],
        [flat_shape, jax.ShapeDtypeStruct((width, LANE), F32)],
    )
    gate_next = shift_seq(gate_first, -1)
    grads_chan = lax.all_to_all(grad_mixed.reshape(n_seq, chan, group), "seq", 0, 0, tiled=True)
    ggated_chan, grad_kernel = conv_backward(grads_chan, kept_spec, kern_spec, twist, table, skip_local)
    ggated = lax.all_to_all(ggated_chan, "seq", 0, 0, tiled=True).reshape(width, group)
    ggated_next = shift_seq(ggated[:, :LANE], -1)
    kernel_grads = kernel_pull(grad_kernel.transpose(1, 0, 2).reshape(chan, seq_len))
    grad_proj, col_sums = token_call(
        grad_proj_kernel,
        "grad_proj",
        common
        + [(mixed, True), (gy_cols, True), (ggated, True), (ggated_next, True), (gate_next, True)],
        [jax.ShapeDtypeStruct((3, width, group), B16), jax.ShapeDtypeStruct((width, 16), F32)],
    )

    one_part = jnp.einsum("pct,dpc->td", grad_proj, full_in, preferred_element_type=F32)
    grad_one = scatter_rel(one_part)
    term_in = jnp.einsum("td,pct->dpc", rows_one, grad_proj, preferred_element_type=F32)
    grad_in = to_owner(term_in)
    grad_unit_one, grad_gain_one, grad_shift_one = norm_back(
        grad_one, unit_one, scale_one, norm1_gain[0]
    )
    grad_tokens = grad_middle + grad_unit_one

    totals = [
        *kernel_grads[:7],
        grad_gain_one,
        grad_shift_one,
        grad_gain_two,
        grad_shift_two,
        grad_out_bias,
        grad_down_bias,
    ]
    packed = [rows128(t) for t in totals]
    group_part = jnp.concatenate([rows128(col_sums.T), rows128(grad_up_block)], axis=0)
    total, groups, owns = sync_small(jnp.concatenate(packed, axis=0), group_part, rows128(kernel_grads[7]))
    outs = []
    start = 0
    for t, p in zip(totals, packed):
        outs.append(total[start : start + p.shape[0]].reshape(-1)[: t.size].reshape((1,) + t.shape))
        start += p.shape[0]
    flat = groups.reshape(n_rep, -1)
    sums = flat[:, : 16 * width].reshape(n_rep, 16, width).transpose(1, 0, 2).reshape(16, model)
    grad_up_bias = flat[:, 16 * width : 16 * width + hidden].reshape(1, -1)
    filt = columns.shape[0]
    grad_kernel_weight = (
        owns.reshape(n_rep, n_seq, -1)[:, :, : filt * chan]
        .reshape(n_rep, n_seq, filt, chan)
        .transpose(2, 0, 1, 3)
        .reshape(1, filt, model)
    )
    pick = lambda offset: jnp.stack([sums[1 + 5 * p + offset] for p in range(3)])
    grad_skip = sums[0][None]
    grad_short_bias = pick(0)[None]
    grad_short_taps = jnp.stack([pick(3), pick(2), pick(1)])[None]
    grad_in_bias = pick(4)[None]
    return (
        layer_out,
        grad_tokens,
        grad_in[None],
        grad_in_bias,
        grad_short_taps,
        grad_short_bias,
        outs[0],
        outs[1],
        outs[2],
        outs[3],
        outs[4],
        outs[5],
        outs[6],
        grad_kernel_weight,
        grad_skip,
        grad_out[None],
        outs[11],
        outs[7],
        outs[8],
        outs[9],
        outs[10],
        grad_up[None],
        grad_up_bias,
        grad_down[None],
        outs[12],
    )


def solution(mesh):
    rows = P(("seq", "rep"), None)
    cut = P(None, "seq", "rep")
    wide = P(None, "seq", None, "rep")
    whole = P()
    ins = [rows, rows, whole, wide] + [whole] * 12 + [cut] + [whole] * 5 + [cut, whole, cut, whole]
    outs = [rows, rows, wide] + [whole] * 12 + [cut] + [whole] * 5 + [cut, whole, cut, whole]
    return jax.shard_map(
        per_device, mesh=mesh, in_specs=tuple(ins), out_specs=tuple(outs), check_vma=False
    )
```

```python
from functools import partial
import math

import jax
import jax.numpy as jnp
import numpy as np
from jax import lax
from jax.experimental import pallas as pl
from jax.experimental.pallas import tpu as pltpu
from jax.sharding import PartitionSpec as P

EPS = 1e-05
HIGH = lax.Precision.HIGHEST
F32 = jnp.float32
B16 = jnp.bfloat16
LANE = 128
HALO = 16
VMEM_BYTES = 48 * 2**20


def swap(values, axis_name, bit):
    size = lax.axis_size(axis_name)
    return lax.ppermute(values, axis_name, [(i, i ^ bit) for i in range(size)])


def gather_rel(rows):
    far = swap(rows, "rep", 2)
    near = swap(rows, "rep", 1)
    diag = swap(far, "rep", 1)
    return jnp.concatenate([rows, near, far, diag], axis=0)


def scatter_rel(part):
    rows = part.shape[0] // 4
    blocks = part.reshape(4, rows, part.shape[1])
    far_in = swap(blocks[3].astype(B16), "rep", 1)
    far_sum = (blocks[2] + far_in.astype(F32)).astype(B16)
    near_in = swap(blocks[1].astype(B16), "rep", 1)
    far_out = swap(far_sum, "rep", 2)
    return blocks[0] + near_in.astype(F32) + far_out.astype(F32)


def ring_order(count):
    if count == 8:
        return [0, 2, 4, 6, 7, 5, 3, 1]
    return list(range(count))


def ring_maps(count):
    order = ring_order(count)
    ahead = [(order[i], order[(i + 1) % count]) for i in range(count)]
    return order, ahead, [(b, a) for a, b in ahead]


def ring_gather(shard):
    count = lax.axis_size("seq")
    if count != 8:
        return lax.all_gather(shard, "seq", axis=0)
    order, ahead, back = ring_maps(count)
    place = jnp.asarray(np.argsort(order), jnp.int32)[lax.axis_index("seq")]
    owners = jnp.asarray(order, jnp.int32)
    full = jnp.zeros((count,) + shard.shape, shard.dtype)

    def put(full, piece, step, lo=0):
        owner = owners[(place + step + count) % count]
        start = (owner, lo) + (0,) * (shard.ndim - 1)
        return lax.dynamic_update_slice(full, piece[None], start)

    full = put(full, shard, 0)
    left = right = shard
    for step in range(1, count // 2):
        left = lax.ppermute(left, "seq", ahead)
        right = lax.ppermute(right, "seq", back)
        full = put(full, left, -step)
        full = put(full, right, step)
    half = shard.shape[0] // 2
    left = lax.ppermute(left[:half], "seq", ahead)
    right = lax.ppermute(right[half:], "seq", back)
    full = put(full, left, -(count // 2))
    full = put(full, right, count // 2, half)
    return full


def ring_scatter(term):
    count = lax.axis_size("seq")
    if count != 8:
        return lax.psum_scatter(term, "seq", scatter_dimension=0, tiled=True).astype(F32)
    order, ahead, back = ring_maps(count)
    place = jnp.asarray(np.argsort(order), jnp.int32)[lax.axis_index("seq")]
    owners = jnp.asarray(order, jnp.int32)
    rows = term.shape[0] // count
    half = rows // 2

    def mine(step, lo):
        owner = owners[(place + step + 2 * count) % count]
        return lax.dynamic_slice_in_dim(term, owner * rows + lo, half, 0)

    left, right = mine(-1, 0), mine(1, half)
    for step in range(2, count + 1):
        left = lax.ppermute(left, "seq", ahead).astype(F32) + mine(-step, 0).astype(F32)
        right = lax.ppermute(right, "seq", back).astype(F32) + mine(step, half).astype(F32)
        if step < count:
            left, right = left.astype(B16), right.astype(B16)
    return jnp.concatenate([left, right], axis=0)


def halve_scatter(term):
    count = lax.axis_size("seq")
    bits = count.bit_length() - 1
    seq = lax.axis_index("seq")
    rows = term.shape[0] // count
    half = rows // 2
    split = term.reshape((2,) * bits + (2, half, term.shape[1]))
    results = []
    for part, order in enumerate(([0] + list(range(bits - 1, 0, -1)), list(range(bits - 1, -1, -1)))):
        value = lax.index_in_dim(split, part, bits, keepdims=False)
        left = list(range(bits - 1, -1, -1))
        for bit in order:
            at = left.index(bit)
            on = (seq >> bit) & 1
            keep = lax.dynamic_index_in_dim(value, on, at, keepdims=False)
            give = lax.dynamic_index_in_dim(value, 1 - on, at, keepdims=False)
            value = keep.astype(F32) + swap(give, "seq", 1 << bit).astype(F32)
            left.remove(bit)
            if left:
                value = value.astype(B16)
        results.append(value)
    return jnp.concatenate(results, axis=0)


def spread_gather(shard):
    count = lax.axis_size("seq")
    copies = jnp.broadcast_to(shard[None], (count,) + shard.shape)
    full = lax.all_to_all(copies, "seq", 0, 0, tiled=True)
    return full.reshape((count * shard.shape[0],) + shard.shape[1:])


def shift_seq(values, step):
    count = lax.axis_size("seq")
    return lax.ppermute(values, "seq", [(i, (i + step) % count) for i in range(count)])


def unmix(values, axis, index):
    size, bit = values.shape[axis], 1
    while bit < size:
        cut = values.shape[:axis] + (size // (2 * bit), 2, bit) + values.shape[axis + 1 :]
        split = values.reshape(cut)
        values = jnp.where((index // bit) % 2 == 1, jnp.flip(split, axis + 1), split).reshape(values.shape)
        bit *= 2
    return values


def sync_small(total, group, own):
    n_seq, n_rep = lax.axis_size("seq"), lax.axis_size("rep")
    group_list, own_list = [group], [own]
    for axis_name, size in (("seq", n_seq), ("rep", n_rep)):
        bit = 1
        while bit < size:
            parts = [total] + group_list + own_list
            sizes = np.cumsum([0] + [p.shape[0] for p in parts])
            came = swap(jnp.concatenate(parts, axis=0), axis_name, bit)
            came = [came[a:b] for a, b in zip(sizes[:-1], sizes[1:])]
            total = total + came[0]
            count = len(group_list)
            if axis_name == "seq":
                group_list = [group_list[0] + came[1]]
            else:
                group_list = group_list + came[1 : 1 + count]
            own_list = own_list + came[1 + count :]
            bit *= 2
    groups = unmix(jnp.stack(group_list), 0, lax.axis_index("rep"))
    owns = jnp.stack(own_list).reshape((n_rep, n_seq) + own.shape)
    owns = unmix(unmix(owns, 0, lax.axis_index("rep")), 1, lax.axis_index("seq"))
    return total, groups, owns


def layer_norm(rows, gain, shift):
    row_mean = jnp.mean(rows, axis=-1, keepdims=True)
    centred = rows - row_mean
    variance = jnp.mean(centred * centred, axis=-1, keepdims=True)
    inverse = lax.rsqrt(variance + EPS)
    normed = centred * inverse
    return (normed * gain + shift, normed, inverse)


def norm_back(grad_rows, normed, inverse, gain):
    scaled = grad_rows * gain
    mean_one = jnp.mean(scaled, axis=-1, keepdims=True)
    mean_two = jnp.mean(scaled * normed, axis=-1, keepdims=True)
    grad_in = inverse * (scaled - mean_one - normed * mean_two)
    return (grad_in, jnp.sum(grad_rows * normed, axis=0), jnp.sum(grad_rows, axis=0))


def features(length, feat_count):
    ramp_unit = jnp.linspace(0.0, 1.0, length, dtype=F32)
    angles = jnp.arange(length, dtype=F32)[:, None] * (2.0 * math.pi / length)
    band_freqs = jnp.linspace(
        0.0001, (feat_count - 1) // 2 - 1.0, (feat_count - 1) // 2, dtype=F32
    )[None, :]
    phase_grid = band_freqs * angles
    grid_out = jnp.concatenate(
        [ramp_unit[:, None], jnp.cos(phase_grid), -jnp.sin(phase_grid)], axis=1
    )
    return (grid_out, ramp_unit)


def filter_columns(
    feature_grid,
    ramp_unit,
    start_chan,
    chan_count,
    model_width,
    feat_weight,
    feat_bias,
    inner_weight,
    inner_bias,
    deep_weight,
    deep_bias,
    sine_freq,
    columns,
):
    freq = sine_freq[:, None]

    def layer(weight, bias, below):
        grown = lax.dot_general(weight, below, (((0,), (0,)), ((), ())), precision=HIGH)
        return jnp.sin(freq * (grown + bias[:, None]))

    hidden = layer(feat_weight, feat_bias, feature_grid.T)
    hidden = layer(inner_weight, inner_bias, hidden)
    hidden = layer(deep_weight, deep_bias, hidden)
    deltas = jnp.abs(
        jnp.linspace(math.log(0.01) / 0.3, math.log(0.01) / 1.5, model_width, dtype=F32)
    )
    local_rates = lax.dynamic_slice_in_dim(deltas, start_chan, chan_count)
    return lax.dot_general(
        columns, hidden, (((0,), (0,)), ((), ())), precision=HIGH
    ) * jnp.exp(-ramp_unit[None, :] * local_rates[:, None])


def sin_cos(x):
    turns = jnp.floor(x * (1.0 / math.pi) + 0.5)
    r = x - turns * 3.140625
    r = r - turns * 9.67502593994140625e-4
    r = r - turns * 1.509957990978376432e-7
    sign = 1.0 - 2.0 * (turns - 2.0 * jnp.floor(turns * 0.5))
    q = r * r
    sin = r + r * q * (
        -1.6666666666e-1
        + q * (8.3333333e-3 + q * (-1.98412698e-4 + q * (2.7557319e-6 + q * -2.505210838e-8)))
    )
    cos = 1.0 + q * (
        -0.5
        + q * (4.16666666e-2 + q * (-1.3888888e-3 + q * (2.48015873e-5 + q * (-2.75573192e-7 + q * 2.0876757e-9))))
    )
    return sin * sign, cos * sign


def dot_high(left, right, dims):
    return lax.dot_general(left, right, (dims, ((), ())), precision=HIGH, preferred_element_type=F32)


def filter_forward_kernel(
    grid_ref, ramp_ref, rate_ref, w1_ref, w2_ref, w3_ref, small_ref, columns_ref, twist_ref, hi_ref, lo_ref,
    spec_ref, sin_ref, cos_ref, z_ref
):
    blocks, length = twist_ref.shape[0], twist_ref.shape[3]
    freq = small_ref[:, 3:4]
    below = grid_ref[...]
    for i, w_ref in enumerate((w1_ref, w2_ref, w3_ref)):
        grown = dot_high(w_ref[...].T, below, ((1,), (0,)))
        sin, cos = sin_cos(freq * (grown + small_ref[:, i : i + 1]))
        sin_ref[i] = sin
        cos_ref[i] = cos
        below = sin
    kern = dot_high(columns_ref[...].T, below, ((1,), (0,))) * jnp.exp(-rate_ref[...] * ramp_ref[...])
    cut = [kern[:, b * length : (b + 1) * length] for b in range(blocks)]
    turn_rows(cut, twist_ref, z_ref, 0, blocks)
    spec_ref[...] = dot_split(z_ref[...], hi_ref[...], lo_ref[...], ((1,), (0,)))


def filter_backward_kernel(
    gk_ref, grid_ref, ramp_ref, rate_ref, w1_ref, w2_ref, w3_ref, small_ref, columns_ref, sin_ref, cos_ref,
    gc_ref, g1_ref, g2_ref, g3_ref, gsmall_ref
):
    freq = small_ref[:, 3:4]
    gk = jnp.concatenate([gk_ref[b] for b in range(gk_ref.shape[0])], axis=1)
    gk = gk * jnp.exp(-rate_ref[...] * ramp_ref[...])
    last = ((1,), (1,))
    gc_ref[...] = dot_high(sin_ref[2], gk, last)
    grad = dot_high(columns_ref[...], gk, ((1,), (0,)))
    gfreq = jnp.zeros(freq.shape, F32)
    gbias = [None] * 3
    for i, w_ref, g_ref in ((2, w3_ref, g3_ref), (1, w2_ref, g2_ref), (0, w1_ref, g1_ref)):
        turn = grad * cos_ref[i]
        below = sin_ref[i - 1] if i else grid_ref[...]
        raw = dot_high(turn, below, last)
        total = jnp.sum(turn, axis=1, keepdims=True)
        g_ref[...] = raw * freq
        gbias[i] = total * freq
        gfreq = gfreq + jnp.sum(raw * w_ref[...].T, axis=1, keepdims=True) + total * small_ref[:, i : i + 1]
        if i:
            grad = dot_high(w_ref[...], turn * freq, ((1,), (0,)))
    gsmall_ref[...] = jnp.concatenate(gbias + [gfreq], axis=1)


def feature_table(length, feat_count):
    ramp = np.linspace(0.0, 1.0, length, dtype=np.float32)
    angles = np.arange(length, dtype=np.float32)[:, None] * np.float32(2.0 * math.pi / length)
    half = (feat_count - 1) // 2
    bands = np.linspace(0.0001, half - 1.0, half, dtype=np.float32)[None, :]
    phase = (bands * angles).astype(np.float64)
    table = np.concatenate([ramp[:, None], np.cos(phase), -np.sin(phase)], axis=1)
    return np.ascontiguousarray(table.T).astype(np.float32), ramp[None, :]


def decay_rates(model):
    return np.abs(
        np.linspace(math.log(0.01) / 0.3, math.log(0.01) / 1.5, model, dtype=np.float32)
    )[:, None]


def transform_tables(blocks, length):
    time = np.arange(blocks * length).reshape(blocks, 1, length)
    cls = np.arange(blocks).reshape(1, blocks, 1)
    period = 4 * blocks * length
    turn = (time * (2 * cls + 1)) % period * (2.0 * np.pi / period)
    twist = np.stack([np.cos(turn), -np.sin(turn)], axis=2).astype(np.float32)
    step = np.arange(length)
    turn = (step[:, None] * step[None, :]) % length * (2.0 * np.pi / length)
    cos, sin = np.cos(turn), np.sin(turn)
    table = np.block([[cos, -sin], [sin, cos]]).astype(np.float32)
    return twist, table


def split_table(table):
    hi = table.astype(B16)
    return jnp.asarray(hi), jnp.asarray((table - hi.astype(np.float32)).astype(B16))


def spectrum_of(signal, twist, table):
    turned = jnp.einsum("bqzl,brl->qrzl", twist[: signal.shape[0]], signal, precision=HIGH)
    flat = turned.reshape(turned.shape[:2] + (-1,))
    return jnp.einsum("qrk,kf->qrf", flat, table, precision=HIGH)


def signal_of(spectrum, twist, table):
    blocks, length = twist.shape[0], twist.shape[3]
    turned = jnp.einsum("qrf,kf->qrk", spectrum, table, precision=HIGH)
    turned = turned.reshape(turned.shape[:2] + (2, length))
    return jnp.einsum("bqzl,qrzl->brl", twist, turned, precision=HIGH) * (1.0 / (blocks * length))


def times(left, right, conj_right):
    half = left.shape[-1] // 2
    lr, li = left[..., :half], left[..., half:]
    rr, ri = right[..., :half], right[..., half:]
    if conj_right:
        return jnp.concatenate([lr * rr + li * ri, li * rr - lr * ri], axis=-1)
    return jnp.concatenate([lr * rr - li * ri, lr * ri + li * rr], axis=-1)


def dot_split(values, hi, lo, dims):
    top = values.astype(B16)
    rest = (values - top.astype(F32)).astype(B16)
    dot = partial(lax.dot_general, dimension_numbers=(dims, ((), ())), preferred_element_type=F32)
    return dot(top, hi) + dot(rest, hi) + dot(top, lo)


def turn_rows(blocks_in, twist_ref, z_ref, base, classes):
    rows, length = blocks_in[0].shape
    for q in range(classes):
        for z in range(2):
            acc = None
            for b, block in enumerate(blocks_in):
                term = block * twist_ref[b, q, z : z + 1]
                acc = term if acc is None else acc + term
            z_ref[base + q * rows : base + (q + 1) * rows, z * length : (z + 1) * length] = acc


def back_rows(w, base, rows, block, twist_ref, classes):
    length = w.shape[1] // 2
    acc = None
    for q in range(classes):
        lo, hi = base + q * rows, base + (q + 1) * rows
        for z in range(2):
            term = w[lo:hi, z * length : (z + 1) * length] * twist_ref[block, q, z : z + 1]
            acc = term if acc is None else acc + term
    return acc * (1.0 / (classes * length))


def conv_forward_kernel(short_blocks, x_ref, kern_ref, twist_ref, hi_ref, lo_ref, skip_ref, out_ref, spec_ref, z_ref):
    blocks = twist_ref.shape[0]
    rows = x_ref.shape[1]
    span = blocks * rows
    first = [x_ref[b].astype(F32) for b in range(blocks)]
    second = [x_ref[blocks + b].astype(F32) for b in range(short_blocks)]
    turn_rows(first, twist_ref, z_ref, 0, blocks)
    turn_rows(second, twist_ref, z_ref, span, blocks)
    spec = dot_split(z_ref[...], hi_ref[...], lo_ref[...], ((1,), (0,)))
    spec_ref[...] = spec
    kern = kern_ref[...]
    prod = jnp.concatenate([times(spec[:span], kern, False), times(spec[span:], kern, False)], axis=0)
    w = dot_split(prod, hi_ref[...], lo_ref[...], ((1,), (1,)))
    skip = skip_ref[...]
    for b in range(blocks):
        out_ref[b] = (back_rows(w, 0, rows, b, twist_ref, blocks) + skip * first[b]).astype(B16)
        acc = back_rows(w, span, rows, b, twist_ref, blocks)
        if b < short_blocks:
            acc = acc + skip * second[b]
        out_ref[blocks + b] = acc.astype(B16)


def conv_backward_kernel(
    short_blocks, g_ref, spec_ref, kern_ref, twist_ref, hi_ref, lo_ref, skip_ref, out_ref, grad_kern_ref, z_ref, p_ref
):
    blocks = twist_ref.shape[0]
    rows = g_ref.shape[1]
    span = blocks * rows
    first = [g_ref[b].astype(F32) for b in range(blocks)]
    second = [g_ref[blocks + b].astype(F32) for b in range(short_blocks)]
    turn_rows(first, twist_ref, z_ref, 0, blocks)
    turn_rows(second, twist_ref, z_ref, span, blocks)
    grad = dot_split(z_ref[...], hi_ref[...], lo_ref[...], ((1,), (0,)))
    kern = kern_ref[...]
    p_ref[0:span] = times(grad[:span], kern, True)
    p_ref[span : 2 * span] = times(grad[span:], kern, True)
    p_ref[2 * span :] = times(grad[:span], spec_ref[0:span], True) + times(
        grad[span:], spec_ref[span:], True
    )
    w = dot_split(p_ref[...], hi_ref[...], lo_ref[...], ((1,), (1,)))
    skip = skip_ref[...]
    for b in range(blocks):
        out_ref[b] = (back_rows(w, 0, rows, b, twist_ref, blocks) + skip * first[b]).astype(B16)
        if b < short_blocks:
            acc = back_rows(w, span, rows, b, twist_ref, blocks) + skip * second[b]
            out_ref[blocks + b] = acc.astype(B16)
        else:
            out_ref[blocks + b] = jnp.zeros(out_ref.shape[1:], B16)
        grad_kern_ref[b] = back_rows(w, 2 * span, rows, b, twist_ref, blocks)


def conv_forward(received, kern_spec, twist, table, skip_local):
    blocks, rows, length = received.shape[0] // 2, received.shape[1], received.shape[2]
    short_blocks = -(-blocks // 4)
    skip = skip_local[:, None]
    if blocks != 4:
        x = received.astype(F32)
        spec = jnp.concatenate(
            [
                spectrum_of(x[:blocks], twist, table),
                spectrum_of(x[blocks : blocks + short_blocks], twist, table),
            ],
            axis=0,
        )
        kern = jnp.concatenate([kern_spec, kern_spec], axis=0)
        prod = times(spec, kern, False)
        out = jnp.concatenate(
            [signal_of(prod[:blocks], twist, table), signal_of(prod[blocks:], twist, table)], axis=0
        )
        return ((out + skip * x).astype(B16), spec)
    hi, lo = split_table(table)
    height = 2 * blocks * rows
    out, spec = pl.pallas_call(
        partial(conv_forward_kernel, short_blocks),
        out_shape=(
            jax.ShapeDtypeStruct(received.shape, B16),
            jax.ShapeDtypeStruct((height, 2 * length), F32),
        ),
        scratch_shapes=[pltpu.VMEM((height, 2 * length), F32)],
        compiler_params=pltpu.CompilerParams(vmem_limit_bytes=VMEM_BYTES),
        name="conv_forward",
    )(received, kern_spec.reshape(blocks * rows, 2 * length), twist, hi, lo, skip)
    return out, spec


def conv_backward(grads, spec, kern_spec, twist, table, skip_local):
    blocks, rows, length = grads.shape[0] // 2, grads.shape[1], grads.shape[2]
    short_blocks = -(-blocks // 4)
    skip = skip_local[:, None]
    if blocks != 4:
        g = grads.astype(F32)
        first = spectrum_of(g[:blocks], twist, table)
        second = spectrum_of(g[blocks : blocks + short_blocks], twist, table)
        one = signal_of(times(first, kern_spec, True), twist, table)
        two = signal_of(times(second, kern_spec, True), twist, table)
        cross = times(first, spec[:blocks], True) + times(second, spec[blocks:], True)
        out = jnp.concatenate([one, two], axis=0) + skip * g
        return (out.astype(B16), signal_of(cross, twist, table))
    hi, lo = split_table(table)
    span = blocks * rows
    out, grad_kern = pl.pallas_call(
        partial(conv_backward_kernel, short_blocks),
        out_shape=(
            jax.ShapeDtypeStruct(grads.shape, B16),
            jax.ShapeDtypeStruct((blocks, rows, length), F32),
        ),
        scratch_shapes=[
            pltpu.VMEM((2 * span, 2 * length), F32),
            pltpu.VMEM((3 * span, 2 * length), F32),
        ],
        compiler_params=pltpu.CompilerParams(vmem_limit_bytes=VMEM_BYTES),
        name="conv_backward",
    )(grads, spec, kern_spec.reshape(span, 2 * length), twist, hi, lo, skip)
    return out, grad_kern


def in_order(ref, rep, lead=()):
    count = ref.shape[-1] // LANE
    return [
        ref[lead + (slice(None), pl.ds(pl.multiple_of((rep ^ j) * LANE, LANE), LANE))]
        for j in range(count)
    ]


def put_rel(ref, rep, values, lead=()):
    for j in range(ref.shape[-1] // LANE):
        ref[lead + (slice(None), pl.ds(pl.multiple_of((rep ^ j) * LANE, LANE), LANE))] = values[
            :, j * LANE : (j + 1) * LANE
        ]


def extended(proj_ref, halo_ref, exists, rep, p):
    blocks = [halo_ref[p, :, :LANE]] + in_order(proj_ref, rep, (p,)) + [halo_ref[p, :, LANE:]]
    return jnp.concatenate(blocks, axis=1).astype(F32) * exists


def short_of(ext, col_ref, p):
    return (
        col_ref[:, p : p + 1] * pltpu.roll(ext, 2, 1)
        + col_ref[:, 3 + p : 4 + p] * pltpu.roll(ext, 1, 1)
        + col_ref[:, 6 + p : 7 + p] * ext
        + col_ref[:, 9 + p : 10 + p]
    )


def gate_kernel(rep_ref, proj_ref, halo_ref, col_ref, mask_ref, out_ref):
    rep = rep_ref[0]
    mask, exists = mask_ref[0:1], mask_ref[1:2]
    gate_in = short_of(extended(proj_ref, halo_ref, exists, rep, 1), col_ref, 1)
    values = short_of(extended(proj_ref, halo_ref, exists, rep, 2), col_ref, 2)
    gated = values * gate_in * mask
    out_ref[...] = gated[:, LANE:-LANE].astype(B16)


def output_kernel(rep_ref, proj_ref, halo_ref, col_ref, mask_ref, mixed_ref, out_ref):
    rep = rep_ref[0]
    gate_out = short_of(extended(proj_ref, halo_ref, mask_ref[1:2], rep, 0), col_ref, 0)
    put_rel(out_ref, rep, (gate_out[:, LANE:-LANE] * mixed_ref[...].astype(F32)).astype(B16))


def grad_mix_kernel(rep_ref, proj_ref, halo_ref, col_ref, mask_ref, mixed_ref, gy_ref, out_ref, first_ref):
    rep = rep_ref[0]
    gate_out = short_of(extended(proj_ref, halo_ref, mask_ref[1:2], rep, 0), col_ref, 0)
    gy = jnp.concatenate(in_order(gy_ref, rep), axis=1).astype(F32)
    out_ref[...] = (gy * gate_out[:, LANE:-LANE]).astype(B16)
    first_ref[...] = gy[:, :LANE] * mixed_ref[:, :LANE].astype(F32)


def grad_proj_kernel(
    rep_ref, proj_ref, halo_ref, col_ref, mask_ref, mixed_ref, gy_ref, ggated_ref, gnext_ref, onext_ref, out_ref, sum_ref
):
    rep = rep_ref[0]
    mask, exists = mask_ref[0:1], mask_ref[1:2]
    size = mask_ref.shape[1]
    mid = slice(LANE, size - LANE)
    gy = jnp.concatenate(in_order(gy_ref, rep), axis=1).astype(F32)
    zero = jnp.zeros((gy.shape[0], LANE), F32)
    next_on = exists[:, size - LANE :]
    ext = [extended(proj_ref, halo_ref, exists, rep, p) for p in range(3)]
    short = [short_of(ext[p], col_ref, p) for p in range(3)]
    ggated = jnp.concatenate(
        [zero, ggated_ref[...].astype(F32), gnext_ref[...].astype(F32) * next_on], axis=1
    )
    ggated = ggated * mask
    gout = gy * mixed_ref[...].astype(F32)
    gshort = [
        jnp.concatenate([zero, gout, onext_ref[...] * next_on], axis=1),
        ggated * short[2],
        ggated * short[1],
    ]
    gated = short[2][:, mid] * short[1][:, mid] * mask[:, mid]
    sums = [jnp.sum(gy * short[0][:, mid] * gated, axis=1, keepdims=True)]
    for p in range(3):
        mine = gshort[p][:, mid]
        sums.append(jnp.sum(mine, axis=1, keepdims=True))
        sums.append(jnp.sum(mine * ext[p][:, mid], axis=1, keepdims=True))
        sums.append(jnp.sum(mine * pltpu.roll(ext[p], 1, 1)[:, mid], axis=1, keepdims=True))
        sums.append(jnp.sum(mine * pltpu.roll(ext[p], 2, 1)[:, mid], axis=1, keepdims=True))
        gproj = (
            col_ref[:, 6 + p : 7 + p] * gshort[p]
            + col_ref[:, 3 + p : 4 + p] * pltpu.roll(gshort[p], size - 1, 1)
            + col_ref[:, p : p + 1] * pltpu.roll(gshort[p], size - 2, 1)
        )[:, mid].astype(B16)
        sums.append(jnp.sum(gproj.astype(F32), axis=1, keepdims=True))
        put_rel(out_ref, rep, gproj, (p,))
    sum_ref[...] = jnp.concatenate(sums, axis=1)


def token_call(kernel, name, arrays, outs):
    step = 64

    def spec(shape, cut):
        if not cut:
            return pl.BlockSpec(shape, lambda i: (0,) * len(shape))
        if len(shape) == 3:
            return pl.BlockSpec((shape[0], step, shape[2]), lambda i: (0, i, 0))
        return pl.BlockSpec((step, shape[1]), lambda i: (i, 0))

    width = outs[0].shape[-2]
    return pl.pallas_call(
        kernel,
        grid=(width // step,),
        in_specs=[pl.BlockSpec(memory_space=pltpu.SMEM)] + [spec(a.shape, cut) for a, cut in arrays[1:]],
        out_specs=[spec(o.shape, True) for o in outs],
        out_shape=outs,
        compiler_params=pltpu.CompilerParams(vmem_limit_bytes=VMEM_BYTES),
        name=name,
    )(*[a for a, _ in arrays])


def rows128(values):
    flat = values.reshape(-1)
    return jnp.pad(flat, (0, -flat.shape[0] % 1024)).reshape(-1, 128)


def per_device(
    tokens,
    cotangent,
    lengths,
    in_weight,
    in_bias,
    short_taps,
    short_bias,
    feat_weight,
    feat_bias,
    inner_weight,
    inner_bias,
    deep_weight,
    deep_bias,
    sine_freq,
    kernel_weight,
    skip_gain,
    out_weight,
    out_bias,
    norm1_gain,
    norm1_shift,
    norm2_gain,
    norm2_shift,
    up_weight,
    up_bias,
    down_weight,
    down_bias,
):
    n_seq, n_rep = lax.axis_size("seq"), lax.axis_size("rep")
    seq, rep = lax.axis_index("seq"), lax.axis_index("rep")
    tok_rows, model = tokens.shape
    group = tok_rows * n_rep
    blocks = n_seq // 2
    seq_len = blocks * group
    chan = model // (n_seq * n_rep)
    width = model // n_rep
    hidden = up_weight.shape[2]
    block_start = rep * width
    chan_start = block_start + seq * chan
    rep_scalar = jnp.reshape(rep, (1,)).astype(jnp.int32)

    item_len = jnp.where(seq // blocks == 0, lengths[0], lengths[1])
    at = (seq % blocks) * group
    row_mask = (at + rep * tok_rows + jnp.arange(tok_rows, dtype=jnp.int32) < item_len).astype(F32)[:, None]
    position = at - LANE + jnp.arange(group + 2 * LANE, dtype=jnp.int32)
    mask_ext = jnp.stack([position < item_len, (position >= 0) & (position < seq_len)]).astype(F32)
    mask_ext = jnp.pad(mask_ext, ((0, 6), (0, 0)))

    full_in = ring_gather(in_weight[0]).reshape(model, 3, width)
    full_out = spread_gather(out_weight[0])
    full_up = lax.all_gather(up_weight[0], "seq", axis=0, tiled=True)
    full_down = lax.all_gather(down_weight[0], "seq", axis=0, tiled=True)

    residual = tokens.astype(F32)
    normed_one, unit_one, scale_one = layer_norm(residual, norm1_gain[0], norm1_shift[0])
    normed_one = normed_one.astype(B16)
    rows_one = gather_rel(normed_one)
    rel = rows_one.reshape(n_rep, tok_rows, model)
    last_rows = lax.dynamic_index_in_dim(rel, rep ^ (n_rep - 1), 0, False)[-HALO:]
    first_rows = lax.dynamic_index_in_dim(rel, rep, 0, False)[:HALO]
    before = shift_seq(last_rows, 1)
    after = shift_seq(first_rows, -1)
    gap = jnp.zeros((LANE - HALO, model), B16)
    halo_rows = jnp.concatenate([gap, before, after, gap], axis=0)
    proj_bias = lax.dynamic_slice_in_dim(in_bias[0], block_start, width, 1)[:, :, None]

    def project(rows):
        return (
            jnp.einsum("td,dpc->pct", rows, full_in, preferred_element_type=F32) + proj_bias
        ).astype(B16)

    proj = project(rows_one)
    halo = project(halo_rows)

    tap_cols = lax.dynamic_slice_in_dim(short_taps[0], block_start, width, 2).reshape(9, width)
    bias_cols = lax.dynamic_slice_in_dim(short_bias[0], block_start, width, 1)
    cols = jnp.pad(jnp.concatenate([tap_cols, bias_cols], axis=0), ((0, 4), (0, 0))).T
    common = [(rep_scalar, True), (proj, True), (halo, True), (cols, True), (mask_ext, False)]
    flat_shape = jax.ShapeDtypeStruct((width, group), B16)
    (gated,) = token_call(gate_kernel, "gate", common, [flat_shape])
    received = lax.all_to_all(gated.reshape(n_seq, chan, group), "seq", 0, 0, tiled=True)

    skip_local = lax.dynamic_slice_in_dim(skip_gain[0], chan_start, chan, 0)
    columns = lax.dynamic_slice_in_dim(kernel_weight[0], chan_start, chan, 1)
    twist, table = transform_tables(blocks, group)
    nets = (feat_weight[0], inner_weight[0], deep_weight[0])
    if blocks == 4:
        grid, ramp = feature_table(seq_len, feat_weight.shape[1])
        rates = lax.dynamic_slice_in_dim(jnp.asarray(decay_rates(model)), chan_start, chan, 0)
        smalls = jnp.concatenate([feat_bias, inner_bias, deep_bias, sine_freq], axis=0).T
        filt = smalls.shape[0]
        hi, lo = split_table(table)
        kern_spec, sines, cosines = pl.pallas_call(
            filter_forward_kernel,
            out_shape=(
                jax.ShapeDtypeStruct((blocks * chan, 2 * group), F32),
                jax.ShapeDtypeStruct((3, filt, seq_len), F32),
                jax.ShapeDtypeStruct((3, filt, seq_len), F32),
            ),
            scratch_shapes=[pltpu.VMEM((blocks * chan, 2 * group), F32)],
            compiler_params=pltpu.CompilerParams(vmem_limit_bytes=VMEM_BYTES),
            cost_estimate=pl.CostEstimate(flops=10**6, bytes_accessed=10**6, transcendentals=0),
            name="filter_forward",
        )(grid, ramp, rates, *nets, smalls, columns, twist, hi, lo)
        kern_spec = kern_spec.reshape(blocks, chan, 2 * group)

        def kernel_pull(grad_kernel):
            shapes = [columns.shape] + [w.shape[::-1] for w in nets] + [smalls.shape]
            gcols, g1, g2, g3, gsmalls = pl.pallas_call(
                filter_backward_kernel,
                out_shape=tuple(jax.ShapeDtypeStruct(shape, F32) for shape in shapes),
                compiler_params=pltpu.CompilerParams(vmem_limit_bytes=VMEM_BYTES),
                cost_estimate=pl.CostEstimate(flops=10**6, bytes_accessed=10**6, transcendentals=0),
                name="filter_backward",
            )(grad_kernel, grid, ramp, rates, *nets, smalls, columns, sines, cosines)
            gs = gsmalls.T
            return (g1.T, gs[0], g2.T, gs[1], g3.T, gs[2], gs[3], gcols)

    else:
        feature_grid, ramp_unit = features(seq_len, feat_weight.shape[1])
        kernel, pull = jax.vjp(
            partial(filter_columns, feature_grid, ramp_unit, chan_start, chan, model),
            feat_weight[0],
            feat_bias[0],
            inner_weight[0],
            inner_bias[0],
            deep_weight[0],
            deep_bias[0],
            sine_freq[0],
            columns,
        )
        kern_spec = spectrum_of(kernel.reshape(chan, blocks, group).transpose(1, 0, 2), twist, table)

        def kernel_pull(grad_kernel):
            return pull(grad_kernel.transpose(1, 0, 2).reshape(chan, seq_len))

    mixed_chan, kept_spec = conv_forward(received, kern_spec, twist, table, skip_local)
    mixed = lax.all_to_all(mixed_chan, "seq", 0, 0, tiled=True).reshape(width, group)
    (y_cols,) = token_call(output_kernel, "output", common + [(mixed, True)], [flat_shape])

    middle_part = jnp.einsum("ct,oc->to", y_cols, full_out, preferred_element_type=F32)
    middle = residual + (scatter_rel(middle_part) + out_bias[0])
    normed_two, unit_two, scale_two = layer_norm(middle, norm2_gain[0], norm2_shift[0])
    rows_two = gather_rel(normed_two.astype(B16))

    grad_top = cotangent.astype(F32) * row_mask
    grad_mlp = grad_top.astype(B16)
    mlp_rows = gather_rel(grad_mlp)
    grad_act = jnp.dot(mlp_rows, full_down, preferred_element_type=F32)
    up_block = lax.dynamic_slice_in_dim(up_bias[0], rep * hidden, hidden, 0)
    pre_act = jnp.dot(rows_two, full_up, preferred_element_type=F32) + up_block
    phi = 0.5 * (1.0 + lax.erf(pre_act * math.sqrt(0.5)))
    act_rows = (pre_act * phi).astype(B16)
    slope = phi + pre_act * (jnp.exp(-0.5 * pre_act * pre_act) * (1.0 / math.sqrt(2.0 * math.pi)))
    grad_pre = (grad_act * slope).astype(B16)
    grad_two = scatter_rel(jnp.einsum("tf,df->td", grad_pre, full_up, preferred_element_type=F32))
    mlp_part = jnp.einsum("tf,of->to", act_rows, full_down, preferred_element_type=F32)
    layer_out = (middle + (scatter_rel(mlp_part) + down_bias[0])).astype(B16)
    term_down = jnp.einsum("to,tf->of", mlp_rows, act_rows, preferred_element_type=F32)
    term_up = jnp.einsum("td,tf->df", rows_two, grad_pre, preferred_element_type=F32)
    grad_two, term_down = lax.optimization_barrier((grad_two, term_down.astype(B16)))
    grad_down_bias = jnp.sum(grad_mlp.astype(F32), axis=0)
    grad_up_block = jnp.sum(grad_pre.astype(F32), axis=0)

    grad_down = lax.psum_scatter(
        term_down, "seq", scatter_dimension=0, tiled=True
    ).astype(F32)
    grad_up = ring_scatter(term_up.astype(B16))

    grad_unit_two, grad_gain_two, grad_shift_two = norm_back(
        grad_two, unit_two, scale_two, norm2_gain[0]
    )
    grad_middle = grad_top + grad_unit_two
    grad_mix = grad_middle.astype(B16)
    grad_out_bias = jnp.sum(grad_mix.astype(F32), axis=0)
    mix_rows = gather_rel(grad_mix)
    gy_cols = jnp.einsum("to,oc->ct", mix_rows, full_out, preferred_element_type=F32).astype(B16)
    term_out = jnp.einsum("to,ct->oc", mix_rows, y_cols, preferred_element_type=F32)
    grad_out = halve_scatter(term_out.astype(B16))

    grad_mixed, gate_first = token_call(
        grad_mix_kernel,
        "grad_mix",
        common + [(mixed, True), (gy_cols, True)],
        [flat_shape, jax.ShapeDtypeStruct((width, LANE), F32)],
    )
    gate_next = shift_seq(gate_first, -1)
    grads_chan = lax.all_to_all(grad_mixed.reshape(n_seq, chan, group), "seq", 0, 0, tiled=True)
    ggated_chan, grad_kernel = conv_backward(grads_chan, kept_spec, kern_spec, twist, table, skip_local)
    ggated = lax.all_to_all(ggated_chan, "seq", 0, 0, tiled=True).reshape(width, group)
    ggated_next = shift_seq(ggated[:, :LANE], -1)
    kernel_grads = kernel_pull(grad_kernel)
    grad_proj, col_sums = token_call(
        grad_proj_kernel,
        "grad_proj",
        common
        + [(mixed, True), (gy_cols, True), (ggated, True), (ggated_next, True), (gate_next, True)],
        [jax.ShapeDtypeStruct((3, width, group), B16), jax.ShapeDtypeStruct((width, 16), F32)],
    )

    one_part = jnp.einsum("pct,dpc->td", grad_proj, full_in, preferred_element_type=F32)
    grad_one = scatter_rel(one_part)
    term_in = jnp.einsum("td,pct->dpc", rows_one, grad_proj, preferred_element_type=F32)
    grad_in = halve_scatter(term_in.reshape(model, 3 * width).astype(B16))
    grad_in = grad_in.reshape(-1, 3, width)
    grad_unit_one, grad_gain_one, grad_shift_one = norm_back(
        grad_one, unit_one, scale_one, norm1_gain[0]
    )
    grad_tokens = grad_middle + grad_unit_one

    totals = [
        *kernel_grads[:7],
        grad_gain_one,
        grad_shift_one,
        grad_gain_two,
        grad_shift_two,
        grad_out_bias,
        grad_down_bias,
    ]
    packed = [rows128(t) for t in totals]
    group_part = jnp.concatenate([rows128(col_sums.T), rows128(grad_up_block)], axis=0)
    total, groups, owns = sync_small(jnp.concatenate(packed, axis=0), group_part, rows128(kernel_grads[7]))
    outs = []
    start = 0
    for t, p in zip(totals, packed):
        outs.append(total[start : start + p.shape[0]].reshape(-1)[: t.size].reshape((1,) + t.shape))
        start += p.shape[0]
    flat = groups.reshape(n_rep, -1)
    sums = flat[:, : 16 * width].reshape(n_rep, 16, width).transpose(1, 0, 2).reshape(16, model)
    grad_up_bias = flat[:, 16 * width : 16 * width + hidden].reshape(1, -1)
    filt = columns.shape[0]
    grad_kernel_weight = (
        owns.reshape(n_rep, n_seq, -1)[:, :, : filt * chan]
        .reshape(n_rep, n_seq, filt, chan)
        .transpose(2, 0, 1, 3)
        .reshape(1, filt, model)
    )
    pick = lambda offset: jnp.stack([sums[1 + 5 * p + offset] for p in range(3)])
    grad_skip = sums[0][None]
    grad_short_bias = pick(0)[None]
    grad_short_taps = jnp.stack([pick(3), pick(2), pick(1)])[None]
    grad_in_bias = pick(4)[None]
    return (
        layer_out,
        grad_tokens,
        grad_in[None],
        grad_in_bias,
        grad_short_taps,
        grad_short_bias,
        outs[0],
        outs[1],
        outs[2],
        outs[3],
        outs[4],
        outs[5],
        outs[6],
        grad_kernel_weight,
        grad_skip,
        grad_out[None],
        outs[11],
        outs[7],
        outs[8],
        outs[9],
        outs[10],
        grad_up[None],
        grad_up_bias,
        grad_down[None],
        outs[12],
    )


def solution(mesh):
    rows = P(("seq", "rep"), None)
    cut = P(None, "seq", "rep")
    wide = P(None, "seq", None, "rep")
    whole = P()
    ins = [rows, rows, whole, wide] + [whole] * 12 + [cut] + [whole] * 5 + [cut, whole, cut, whole]
    outs = [rows, rows, wide] + [whole] * 12 + [cut] + [whole] * 5 + [cut, whole, cut, whole]
    return jax.shard_map(
        per_device, mesh=mesh, in_specs=tuple(ins), out_specs=tuple(outs), check_vma=False
    )
```

```python
from functools import partial
import math

import jax
import jax.numpy as jnp
import numpy as np
from jax import lax
from jax.experimental import pallas as pl
from jax.experimental.pallas import tpu as pltpu
from jax.sharding import PartitionSpec as P

EPS = 1e-05
HIGH = lax.Precision.HIGHEST
F32 = jnp.float32
B16 = jnp.bfloat16
LANE = 128
HALO = 16
VMEM_BYTES = 48 * 2**20


def swap(values, axis_name, bit):
    size = lax.axis_size(axis_name)
    return lax.ppermute(values, axis_name, [(i, i ^ bit) for i in range(size)])


def gather_rel(rows):
    far = swap(rows, "rep", 2)
    near = swap(rows, "rep", 1)
    diag = swap(far, "rep", 1)
    return jnp.concatenate([rows, near, far, diag], axis=0)


def scatter_rel(part):
    rows = part.shape[0] // 4
    blocks = part.reshape(4, rows, part.shape[1])
    far_in = swap(blocks[3].astype(B16), "rep", 1)
    far_sum = (blocks[2] + far_in.astype(F32)).astype(B16)
    near_in = swap(blocks[1].astype(B16), "rep", 1)
    far_out = swap(far_sum, "rep", 2)
    return blocks[0] + near_in.astype(F32) + far_out.astype(F32)


def ring_order(count):
    if count == 8:
        return [0, 2, 4, 6, 7, 5, 3, 1]
    return list(range(count))


def ring_maps(count):
    order = ring_order(count)
    ahead = [(order[i], order[(i + 1) % count]) for i in range(count)]
    return order, ahead, [(b, a) for a, b in ahead]


def ring_gather(shard):
    count = lax.axis_size("seq")
    if count != 8:
        return lax.all_gather(shard, "seq", axis=0)
    order, ahead, back = ring_maps(count)
    place = jnp.asarray(np.argsort(order), jnp.int32)[lax.axis_index("seq")]
    owners = jnp.asarray(order, jnp.int32)
    full = jnp.zeros((count,) + shard.shape, shard.dtype)

    def put(full, piece, step, lo=0):
        owner = owners[(place + step + count) % count]
        start = (owner, lo) + (0,) * (shard.ndim - 1)
        return lax.dynamic_update_slice(full, piece[None], start)

    full = put(full, shard, 0)
    left = right = shard
    for step in range(1, count // 2):
        left = lax.ppermute(left, "seq", ahead)
        right = lax.ppermute(right, "seq", back)
        full = put(full, left, -step)
        full = put(full, right, step)
    half = shard.shape[0] // 2
    left = lax.ppermute(left[:half], "seq", ahead)
    right = lax.ppermute(right[half:], "seq", back)
    full = put(full, left, -(count // 2))
    full = put(full, right, count // 2, half)
    return full


def ring_scatter(term):
    count = lax.axis_size("seq")
    if count != 8:
        return lax.psum_scatter(term, "seq", scatter_dimension=0, tiled=True).astype(F32)
    order, ahead, back = ring_maps(count)
    place = jnp.asarray(np.argsort(order), jnp.int32)[lax.axis_index("seq")]
    owners = jnp.asarray(order, jnp.int32)
    rows = term.shape[0] // count
    half = rows // 2

    def mine(step, lo):
        owner = owners[(place + step + 2 * count) % count]
        return lax.dynamic_slice_in_dim(term, owner * rows + lo, half, 0)

    left, right = mine(-1, 0), mine(1, half)
    for step in range(2, count + 1):
        left = lax.ppermute(left, "seq", ahead).astype(F32) + mine(-step, 0).astype(F32)
        right = lax.ppermute(right, "seq", back).astype(F32) + mine(step, half).astype(F32)
        if step < count:
            left, right = left.astype(B16), right.astype(B16)
    return jnp.concatenate([left, right], axis=0)


def halve_scatter(term):
    count = lax.axis_size("seq")
    bits = count.bit_length() - 1
    seq = lax.axis_index("seq")
    rows = term.shape[0] // count
    half = rows // 2
    split = term.reshape((2,) * bits + (2, half, term.shape[1]))
    results = []
    for part, order in enumerate(([0] + list(range(bits - 1, 0, -1)), list(range(bits - 1, -1, -1)))):
        value = lax.index_in_dim(split, part, bits, keepdims=False)
        left = list(range(bits - 1, -1, -1))
        for bit in order:
            at = left.index(bit)
            on = (seq >> bit) & 1
            keep = lax.dynamic_index_in_dim(value, on, at, keepdims=False)
            give = lax.dynamic_index_in_dim(value, 1 - on, at, keepdims=False)
            value = keep.astype(F32) + swap(give, "seq", 1 << bit).astype(F32)
            left.remove(bit)
            if left:
                value = value.astype(B16)
        results.append(value)
    return jnp.concatenate(results, axis=0)


def spread_gather(shard):
    count = lax.axis_size("seq")
    copies = jnp.broadcast_to(shard[None], (count,) + shard.shape)
    full = lax.all_to_all(copies, "seq", 0, 0, tiled=True)
    return full.reshape((count * shard.shape[0],) + shard.shape[1:])


def shift_seq(values, step):
    count = lax.axis_size("seq")
    return lax.ppermute(values, "seq", [(i, (i + step) % count) for i in range(count)])


def unmix(values, axis, index):
    size, bit = values.shape[axis], 1
    while bit < size:
        cut = values.shape[:axis] + (size // (2 * bit), 2, bit) + values.shape[axis + 1 :]
        split = values.reshape(cut)
        values = jnp.where((index // bit) % 2 == 1, jnp.flip(split, axis + 1), split).reshape(values.shape)
        bit *= 2
    return values


def sync_small(total, group, own):
    n_seq, n_rep = lax.axis_size("seq"), lax.axis_size("rep")
    group_list, own_list = [group], [own]
    for axis_name, size in (("seq", n_seq), ("rep", n_rep)):
        bit = 1
        while bit < size:
            parts = [total] + group_list + own_list
            sizes = np.cumsum([0] + [p.shape[0] for p in parts])
            came = swap(jnp.concatenate(parts, axis=0), axis_name, bit)
            came = [came[a:b] for a, b in zip(sizes[:-1], sizes[1:])]
            total = total + came[0]
            count = len(group_list)
            if axis_name == "seq":
                group_list = [group_list[0] + came[1]]
            else:
                group_list = group_list + came[1 : 1 + count]
            own_list = own_list + came[1 + count :]
            bit *= 2
    groups = unmix(jnp.stack(group_list), 0, lax.axis_index("rep"))
    owns = jnp.stack(own_list).reshape((n_rep, n_seq) + own.shape)
    owns = unmix(unmix(owns, 0, lax.axis_index("rep")), 1, lax.axis_index("seq"))
    return total, groups, owns


def layer_norm(rows, gain, shift):
    row_mean = jnp.mean(rows, axis=-1, keepdims=True)
    centred = rows - row_mean
    variance = jnp.mean(centred * centred, axis=-1, keepdims=True)
    inverse = lax.rsqrt(variance + EPS)
    normed = centred * inverse
    return (normed * gain + shift, normed, inverse)


def norm_back(grad_rows, normed, inverse, gain):
    scaled = grad_rows * gain
    mean_one = jnp.mean(scaled, axis=-1, keepdims=True)
    mean_two = jnp.mean(scaled * normed, axis=-1, keepdims=True)
    grad_in = inverse * (scaled - mean_one - normed * mean_two)
    return (grad_in, jnp.sum(grad_rows * normed, axis=0), jnp.sum(grad_rows, axis=0))


def features(length, feat_count):
    ramp_unit = jnp.linspace(0.0, 1.0, length, dtype=F32)
    angles = jnp.arange(length, dtype=F32)[:, None] * (2.0 * math.pi / length)
    band_freqs = jnp.linspace(
        0.0001, (feat_count - 1) // 2 - 1.0, (feat_count - 1) // 2, dtype=F32
    )[None, :]
    phase_grid = band_freqs * angles
    grid_out = jnp.concatenate(
        [ramp_unit[:, None], jnp.cos(phase_grid), -jnp.sin(phase_grid)], axis=1
    )
    return (grid_out, ramp_unit)


def filter_columns(
    feature_grid,
    ramp_unit,
    start_chan,
    chan_count,
    model_width,
    feat_weight,
    feat_bias,
    inner_weight,
    inner_bias,
    deep_weight,
    deep_bias,
    sine_freq,
    columns,
):
    freq = sine_freq[:, None]

    def layer(weight, bias, below):
        grown = lax.dot_general(weight, below, (((0,), (0,)), ((), ())), precision=HIGH)
        return jnp.sin(freq * (grown + bias[:, None]))

    hidden = layer(feat_weight, feat_bias, feature_grid.T)
    hidden = layer(inner_weight, inner_bias, hidden)
    hidden = layer(deep_weight, deep_bias, hidden)
    deltas = jnp.abs(
        jnp.linspace(math.log(0.01) / 0.3, math.log(0.01) / 1.5, model_width, dtype=F32)
    )
    local_rates = lax.dynamic_slice_in_dim(deltas, start_chan, chan_count)
    return lax.dot_general(
        columns, hidden, (((0,), (0,)), ((), ())), precision=HIGH
    ) * jnp.exp(-ramp_unit[None, :] * local_rates[:, None])


def sin_cos(x):
    turns = jnp.floor(x * (1.0 / math.pi) + 0.5)
    r = x - turns * 3.140625
    r = r - turns * 9.67502593994140625e-4
    r = r - turns * 1.509957990978376432e-7
    sign = 1.0 - 2.0 * (turns - 2.0 * jnp.floor(turns * 0.5))
    q = r * r
    sin = r + r * q * (
        -1.6666666666e-1
        + q * (8.3333333e-3 + q * (-1.98412698e-4 + q * (2.7557319e-6 + q * -2.505210838e-8)))
    )
    cos = 1.0 + q * (
        -0.5
        + q * (4.16666666e-2 + q * (-1.3888888e-3 + q * (2.48015873e-5 + q * (-2.75573192e-7 + q * 2.0876757e-9))))
    )
    return sin * sign, cos * sign


def dot_high(left, right, dims):
    return lax.dot_general(left, right, (dims, ((), ())), precision=HIGH, preferred_element_type=F32)


def filter_forward_kernel(
    grid_ref, ramp_ref, rate_ref, w1_ref, w2_ref, w3_ref, small_ref, columns_ref, twist_ref, hi_ref, lo_ref,
    spec_ref, sin_ref, cos_ref, z_ref
):
    blocks, length = twist_ref.shape[0], twist_ref.shape[3]
    freq = small_ref[:, 3:4]
    below = grid_ref[...]
    for i, w_ref in enumerate((w1_ref, w2_ref, w3_ref)):
        grown = dot_high(w_ref[...].T, below, ((1,), (0,)))
        sin, cos = sin_cos(freq * (grown + small_ref[:, i : i + 1]))
        sin_ref[i] = sin
        cos_ref[i] = cos
        below = sin
    kern = dot_high(columns_ref[...].T, below, ((1,), (0,))) * jnp.exp(-rate_ref[...] * ramp_ref[...])
    cut = [kern[:, b * length : (b + 1) * length] for b in range(blocks)]
    turn_rows(cut, twist_ref, z_ref, 0, blocks)
    spec_ref[...] = dot_split(z_ref[...], hi_ref[...], lo_ref[...], ((1,), (0,)))


def filter_backward_kernel(
    gk_ref, grid_ref, ramp_ref, rate_ref, w1_ref, w2_ref, w3_ref, small_ref, columns_ref, sin_ref, cos_ref,
    gc_ref, g1_ref, g2_ref, g3_ref, gsmall_ref
):
    freq = small_ref[:, 3:4]
    gk = jnp.concatenate([gk_ref[b] for b in range(gk_ref.shape[0])], axis=1)
    gk = gk * jnp.exp(-rate_ref[...] * ramp_ref[...])
    last = ((1,), (1,))
    gc_ref[...] = dot_high(sin_ref[2], gk, last)
    grad = dot_high(columns_ref[...], gk, ((1,), (0,)))
    gfreq = jnp.zeros(freq.shape, F32)
    gbias = [None] * 3
    for i, w_ref, g_ref in ((2, w3_ref, g3_ref), (1, w2_ref, g2_ref), (0, w1_ref, g1_ref)):
        turn = grad * cos_ref[i]
        below = sin_ref[i - 1] if i else grid_ref[...]
        raw = dot_high(turn, below, last)
        total = jnp.sum(turn, axis=1, keepdims=True)
        g_ref[...] = raw * freq
        gbias[i] = total * freq
        gfreq = gfreq + jnp.sum(raw * w_ref[...].T, axis=1, keepdims=True) + total * small_ref[:, i : i + 1]
        if i:
            grad = dot_high(w_ref[...], turn * freq, ((1,), (0,)))
    gsmall_ref[...] = jnp.concatenate(gbias + [gfreq], axis=1)


def feature_table(length, feat_count):
    ramp = np.linspace(0.0, 1.0, length, dtype=np.float32)
    angles = np.arange(length, dtype=np.float32)[:, None] * np.float32(2.0 * math.pi / length)
    half = (feat_count - 1) // 2
    bands = np.linspace(0.0001, half - 1.0, half, dtype=np.float32)[None, :]
    phase = (bands * angles).astype(np.float64)
    table = np.concatenate([ramp[:, None], np.cos(phase), -np.sin(phase)], axis=1)
    return np.ascontiguousarray(table.T).astype(np.float32), ramp[None, :]


def decay_rates(model):
    return np.abs(
        np.linspace(math.log(0.01) / 0.3, math.log(0.01) / 1.5, model, dtype=np.float32)
    )[:, None]


def transform_tables(blocks, length):
    time = np.arange(blocks * length).reshape(blocks, 1, length)
    cls = np.arange(blocks).reshape(1, blocks, 1)
    period = 4 * blocks * length
    turn = (time * (2 * cls + 1)) % period * (2.0 * np.pi / period)
    twist = np.stack([np.cos(turn), -np.sin(turn)], axis=2).astype(np.float32)
    step = np.arange(length)
    turn = (step[:, None] * step[None, :]) % length * (2.0 * np.pi / length)
    cos, sin = np.cos(turn), np.sin(turn)
    table = np.block([[cos, -sin], [sin, cos]]).astype(np.float32)
    return twist, table


def split_table(table):
    hi = table.astype(B16)
    return jnp.asarray(hi), jnp.asarray((table - hi.astype(np.float32)).astype(B16))


def spectrum_of(signal, twist, table):
    turned = jnp.einsum("bqzl,brl->qrzl", twist[: signal.shape[0]], signal, precision=HIGH)
    flat = turned.reshape(turned.shape[:2] + (-1,))
    return jnp.einsum("qrk,kf->qrf", flat, table, precision=HIGH)


def signal_of(spectrum, twist, table):
    blocks, length = twist.shape[0], twist.shape[3]
    turned = jnp.einsum("qrf,kf->qrk", spectrum, table, precision=HIGH)
    turned = turned.reshape(turned.shape[:2] + (2, length))
    return jnp.einsum("bqzl,qrzl->brl", twist, turned, precision=HIGH) * (1.0 / (blocks * length))


def times(left, right, conj_right):
    half = left.shape[-1] // 2
    lr, li = left[..., :half], left[..., half:]
    rr, ri = right[..., :half], right[..., half:]
    if conj_right:
        return jnp.concatenate([lr * rr + li * ri, li * rr - lr * ri], axis=-1)
    return jnp.concatenate([lr * rr - li * ri, lr * ri + li * rr], axis=-1)


def dot_split(values, hi, lo, dims):
    top = values.astype(B16)
    rest = (values - top.astype(F32)).astype(B16)
    dot = partial(lax.dot_general, dimension_numbers=(dims, ((), ())), preferred_element_type=F32)
    return dot(top, hi) + dot(rest, hi) + dot(top, lo)


def turn_rows(blocks_in, twist_ref, z_ref, base, classes):
    rows, length = blocks_in[0].shape
    for q in range(classes):
        for z in range(2):
            acc = None
            for b, block in enumerate(blocks_in):
                term = block * twist_ref[b, q, z : z + 1]
                acc = term if acc is None else acc + term
            z_ref[base + q * rows : base + (q + 1) * rows, z * length : (z + 1) * length] = acc


def back_rows(w, base, rows, block, twist_ref, classes):
    length = w.shape[1] // 2
    acc = None
    for q in range(classes):
        lo, hi = base + q * rows, base + (q + 1) * rows
        for z in range(2):
            term = w[lo:hi, z * length : (z + 1) * length] * twist_ref[block, q, z : z + 1]
            acc = term if acc is None else acc + term
    return acc * (1.0 / (classes * length))


def conv_forward_kernel(short_blocks, x_ref, kern_ref, twist_ref, hi_ref, lo_ref, skip_ref, out_ref, spec_ref, z_ref):
    blocks = twist_ref.shape[0]
    rows = x_ref.shape[1]
    span = blocks * rows
    first = [x_ref[b].astype(F32) for b in range(blocks)]
    second = [x_ref[blocks + b].astype(F32) for b in range(short_blocks)]
    turn_rows(first, twist_ref, z_ref, 0, blocks)
    turn_rows(second, twist_ref, z_ref, span, blocks)
    spec = dot_split(z_ref[...], hi_ref[...], lo_ref[...], ((1,), (0,)))
    spec_ref[...] = spec
    kern = kern_ref[...]
    prod = jnp.concatenate([times(spec[:span], kern, False), times(spec[span:], kern, False)], axis=0)
    w = dot_split(prod, hi_ref[...], lo_ref[...], ((1,), (1,)))
    skip = skip_ref[...]
    for b in range(blocks):
        out_ref[b] = (back_rows(w, 0, rows, b, twist_ref, blocks) + skip * first[b]).astype(B16)
        acc = back_rows(w, span, rows, b, twist_ref, blocks)
        if b < short_blocks:
            acc = acc + skip * second[b]
        out_ref[blocks + b] = acc.astype(B16)


def conv_backward_kernel(
    short_blocks, g_ref, spec_ref, kern_ref, twist_ref, hi_ref, lo_ref, skip_ref, out_ref, grad_kern_ref, z_ref, p_ref
):
    blocks = twist_ref.shape[0]
    rows = g_ref.shape[1]
    span = blocks * rows
    first = [g_ref[b].astype(F32) for b in range(blocks)]
    second = [g_ref[blocks + b].astype(F32) for b in range(short_blocks)]
    turn_rows(first, twist_ref, z_ref, 0, blocks)
    turn_rows(second, twist_ref, z_ref, span, blocks)
    grad = dot_split(z_ref[...], hi_ref[...], lo_ref[...], ((1,), (0,)))
    kern = kern_ref[...]
    p_ref[0:span] = times(grad[:span], kern, True)
    p_ref[span : 2 * span] = times(grad[span:], kern, True)
    p_ref[2 * span :] = times(grad[:span], spec_ref[0:span], True) + times(
        grad[span:], spec_ref[span:], True
    )
    w = dot_split(p_ref[...], hi_ref[...], lo_ref[...], ((1,), (1,)))
    skip = skip_ref[...]
    for b in range(blocks):
        out_ref[b] = (back_rows(w, 0, rows, b, twist_ref, blocks) + skip * first[b]).astype(B16)
        if b < short_blocks:
            acc = back_rows(w, span, rows, b, twist_ref, blocks) + skip * second[b]
            out_ref[blocks + b] = acc.astype(B16)
        else:
            out_ref[blocks + b] = jnp.zeros(out_ref.shape[1:], B16)
        grad_kern_ref[b] = back_rows(w, 2 * span, rows, b, twist_ref, blocks)


def conv_forward(received, kern_spec, twist, table, skip_local):
    blocks, rows, length = received.shape[0] // 2, received.shape[1], received.shape[2]
    short_blocks = -(-blocks // 4)
    skip = skip_local[:, None]
    if blocks != 4:
        x = received.astype(F32)
        spec = jnp.concatenate(
            [
                spectrum_of(x[:blocks], twist, table),
                spectrum_of(x[blocks : blocks + short_blocks], twist, table),
            ],
            axis=0,
        )
        kern = jnp.concatenate([kern_spec, kern_spec], axis=0)
        prod = times(spec, kern, False)
        out = jnp.concatenate(
            [signal_of(prod[:blocks], twist, table), signal_of(prod[blocks:], twist, table)], axis=0
        )
        return ((out + skip * x).astype(B16), spec)
    hi, lo = split_table(table)
    height = 2 * blocks * rows
    out, spec = pl.pallas_call(
        partial(conv_forward_kernel, short_blocks),
        out_shape=(
            jax.ShapeDtypeStruct(received.shape, B16),
            jax.ShapeDtypeStruct((height, 2 * length), F32),
        ),
        scratch_shapes=[pltpu.VMEM((height, 2 * length), F32)],
        compiler_params=pltpu.CompilerParams(vmem_limit_bytes=VMEM_BYTES),
        name="conv_forward",
    )(received, kern_spec.reshape(blocks * rows, 2 * length), twist, hi, lo, skip)
    return out, spec


def conv_backward(grads, spec, kern_spec, twist, table, skip_local):
    blocks, rows, length = grads.shape[0] // 2, grads.shape[1], grads.shape[2]
    short_blocks = -(-blocks // 4)
    skip = skip_local[:, None]
    if blocks != 4:
        g = grads.astype(F32)
        first = spectrum_of(g[:blocks], twist, table)
        second = spectrum_of(g[blocks : blocks + short_blocks], twist, table)
        one = signal_of(times(first, kern_spec, True), twist, table)
        two = signal_of(times(second, kern_spec, True), twist, table)
        cross = times(first, spec[:blocks], True) + times(second, spec[blocks:], True)
        out = jnp.concatenate([one, two], axis=0) + skip * g
        return (out.astype(B16), signal_of(cross, twist, table))
    hi, lo = split_table(table)
    span = blocks * rows
    out, grad_kern = pl.pallas_call(
        partial(conv_backward_kernel, short_blocks),
        out_shape=(
            jax.ShapeDtypeStruct(grads.shape, B16),
            jax.ShapeDtypeStruct((blocks, rows, length), F32),
        ),
        scratch_shapes=[
            pltpu.VMEM((2 * span, 2 * length), F32),
            pltpu.VMEM((3 * span, 2 * length), F32),
        ],
        compiler_params=pltpu.CompilerParams(vmem_limit_bytes=VMEM_BYTES),
        name="conv_backward",
    )(grads, spec, kern_spec.reshape(span, 2 * length), twist, hi, lo, skip)
    return out, grad_kern


def in_order(ref, rep, lead=()):
    count = ref.shape[-1] // LANE
    return [
        ref[lead + (slice(None), pl.ds(pl.multiple_of((rep ^ j) * LANE, LANE), LANE))]
        for j in range(count)
    ]


def put_rel(ref, rep, values, lead=()):
    for j in range(ref.shape[-1] // LANE):
        ref[lead + (slice(None), pl.ds(pl.multiple_of((rep ^ j) * LANE, LANE), LANE))] = values[
            :, j * LANE : (j + 1) * LANE
        ]


def extended(proj_ref, halo_ref, exists, rep, p):
    blocks = [halo_ref[p, :, :LANE]] + in_order(proj_ref, rep, (p,)) + [halo_ref[p, :, LANE:]]
    return jnp.concatenate(blocks, axis=1).astype(F32) * exists


def short_of(ext, col_ref, p):
    return (
        col_ref[:, p : p + 1] * pltpu.roll(ext, 2, 1)
        + col_ref[:, 3 + p : 4 + p] * pltpu.roll(ext, 1, 1)
        + col_ref[:, 6 + p : 7 + p] * ext
        + col_ref[:, 9 + p : 10 + p]
    )


def gate_kernel(rep_ref, proj_ref, halo_ref, col_ref, mask_ref, out_ref):
    rep = rep_ref[0]
    mask, exists = mask_ref[0:1], mask_ref[1:2]
    gate_in = short_of(extended(proj_ref, halo_ref, exists, rep, 1), col_ref, 1)
    values = short_of(extended(proj_ref, halo_ref, exists, rep, 2), col_ref, 2)
    gated = values * gate_in * mask
    out_ref[...] = gated[:, LANE:-LANE].astype(B16)


def output_kernel(rep_ref, proj_ref, halo_ref, col_ref, mask_ref, mixed_ref, out_ref):
    rep = rep_ref[0]
    gate_out = short_of(extended(proj_ref, halo_ref, mask_ref[1:2], rep, 0), col_ref, 0)
    put_rel(out_ref, rep, (gate_out[:, LANE:-LANE] * mixed_ref[...].astype(F32)).astype(B16))


def grad_mix_kernel(rep_ref, proj_ref, halo_ref, col_ref, mask_ref, mixed_ref, gy_ref, out_ref, first_ref):
    rep = rep_ref[0]
    gate_out = short_of(extended(proj_ref, halo_ref, mask_ref[1:2], rep, 0), col_ref, 0)
    gy = jnp.concatenate(in_order(gy_ref, rep), axis=1).astype(F32)
    out_ref[...] = (gy * gate_out[:, LANE:-LANE]).astype(B16)
    first_ref[...] = gy[:, :LANE] * mixed_ref[:, :LANE].astype(F32)


def grad_proj_kernel(
    rep_ref, proj_ref, halo_ref, col_ref, mask_ref, mixed_ref, gy_ref, ggated_ref, gnext_ref, onext_ref, out_ref, sum_ref
):
    rep = rep_ref[0]
    mask, exists = mask_ref[0:1], mask_ref[1:2]
    size = mask_ref.shape[1]
    mid = slice(LANE, size - LANE)
    gy = jnp.concatenate(in_order(gy_ref, rep), axis=1).astype(F32)
    zero = jnp.zeros((gy.shape[0], LANE), F32)
    next_on = exists[:, size - LANE :]
    ext = [extended(proj_ref, halo_ref, exists, rep, p) for p in range(3)]
    short = [short_of(ext[p], col_ref, p) for p in range(3)]
    ggated = jnp.concatenate(
        [zero, ggated_ref[...].astype(F32), gnext_ref[...].astype(F32) * next_on], axis=1
    )
    ggated = ggated * mask
    gout = gy * mixed_ref[...].astype(F32)
    gshort = [
        jnp.concatenate([zero, gout, onext_ref[...] * next_on], axis=1),
        ggated * short[2],
        ggated * short[1],
    ]
    gated = short[2][:, mid] * short[1][:, mid] * mask[:, mid]
    sums = [jnp.sum(gy * short[0][:, mid] * gated, axis=1, keepdims=True)]
    for p in range(3):
        mine = gshort[p][:, mid]
        sums.append(jnp.sum(mine, axis=1, keepdims=True))
        sums.append(jnp.sum(mine * ext[p][:, mid], axis=1, keepdims=True))
        sums.append(jnp.sum(mine * pltpu.roll(ext[p], 1, 1)[:, mid], axis=1, keepdims=True))
        sums.append(jnp.sum(mine * pltpu.roll(ext[p], 2, 1)[:, mid], axis=1, keepdims=True))
        gproj = (
            col_ref[:, 6 + p : 7 + p] * gshort[p]
            + col_ref[:, 3 + p : 4 + p] * pltpu.roll(gshort[p], size - 1, 1)
            + col_ref[:, p : p + 1] * pltpu.roll(gshort[p], size - 2, 1)
        )[:, mid].astype(B16)
        sums.append(jnp.sum(gproj.astype(F32), axis=1, keepdims=True))
        put_rel(out_ref, rep, gproj, (p,))
    sum_ref[...] = jnp.concatenate(sums, axis=1)


def token_call(kernel, name, arrays, outs):
    step = 64

    def spec(shape, cut):
        if not cut:
            return pl.BlockSpec(shape, lambda i: (0,) * len(shape))
        if len(shape) == 3:
            return pl.BlockSpec((shape[0], step, shape[2]), lambda i: (0, i, 0))
        return pl.BlockSpec((step, shape[1]), lambda i: (i, 0))

    width = outs[0].shape[-2]
    return pl.pallas_call(
        kernel,
        grid=(width // step,),
        in_specs=[pl.BlockSpec(memory_space=pltpu.SMEM)] + [spec(a.shape, cut) for a, cut in arrays[1:]],
        out_specs=[spec(o.shape, True) for o in outs],
        out_shape=outs,
        compiler_params=pltpu.CompilerParams(vmem_limit_bytes=VMEM_BYTES),
        name=name,
    )(*[a for a, _ in arrays])


def rows128(values):
    flat = values.reshape(-1)
    return jnp.pad(flat, (0, -flat.shape[0] % 1024)).reshape(-1, 128)


def per_device(
    tokens,
    cotangent,
    lengths,
    in_weight,
    in_bias,
    short_taps,
    short_bias,
    feat_weight,
    feat_bias,
    inner_weight,
    inner_bias,
    deep_weight,
    deep_bias,
    sine_freq,
    kernel_weight,
    skip_gain,
    out_weight,
    out_bias,
    norm1_gain,
    norm1_shift,
    norm2_gain,
    norm2_shift,
    up_weight,
    up_bias,
    down_weight,
    down_bias,
):
    n_seq, n_rep = lax.axis_size("seq"), lax.axis_size("rep")
    seq, rep = lax.axis_index("seq"), lax.axis_index("rep")
    tok_rows, model = tokens.shape
    group = tok_rows * n_rep
    blocks = n_seq // 2
    seq_len = blocks * group
    chan = model // (n_seq * n_rep)
    width = model // n_rep
    hidden = up_weight.shape[2]
    block_start = rep * width
    chan_start = block_start + seq * chan
    rep_scalar = jnp.reshape(rep, (1,)).astype(jnp.int32)

    item_len = jnp.where(seq // blocks == 0, lengths[0], lengths[1])
    at = (seq % blocks) * group
    row_mask = (at + rep * tok_rows + jnp.arange(tok_rows, dtype=jnp.int32) < item_len).astype(F32)[:, None]
    position = at - LANE + jnp.arange(group + 2 * LANE, dtype=jnp.int32)
    mask_ext = jnp.stack([position < item_len, (position >= 0) & (position < seq_len)]).astype(F32)
    mask_ext = jnp.pad(mask_ext, ((0, 6), (0, 0)))

    full_in = ring_gather(in_weight[0]).reshape(model, 3, width)
    full_out = spread_gather(out_weight[0])
    full_up = lax.all_gather(up_weight[0], "seq", axis=0, tiled=True)
    full_down = lax.all_gather(down_weight[0], "seq", axis=0, tiled=True)

    residual = tokens.astype(F32)
    normed_one, unit_one, scale_one = layer_norm(residual, norm1_gain[0], norm1_shift[0])
    normed_one = normed_one.astype(B16)
    rows_one = gather_rel(normed_one)
    rel = rows_one.reshape(n_rep, tok_rows, model)
    last_rows = lax.dynamic_index_in_dim(rel, rep ^ (n_rep - 1), 0, False)[-HALO:]
    first_rows = lax.dynamic_index_in_dim(rel, rep, 0, False)[:HALO]
    before = shift_seq(last_rows, 1)
    after = shift_seq(first_rows, -1)
    gap = jnp.zeros((LANE - HALO, model), B16)
    halo_rows = jnp.concatenate([gap, before, after, gap], axis=0)
    proj_bias = lax.dynamic_slice_in_dim(in_bias[0], block_start, width, 1)[:, :, None]

    def project(rows):
        return (
            jnp.einsum("td,dpc->pct", rows, full_in, preferred_element_type=F32) + proj_bias
        ).astype(B16)

    proj = project(rows_one)
    halo = project(halo_rows)

    tap_cols = lax.dynamic_slice_in_dim(short_taps[0], block_start, width, 2).reshape(9, width)
    bias_cols = lax.dynamic_slice_in_dim(short_bias[0], block_start, width, 1)
    cols = jnp.pad(jnp.concatenate([tap_cols, bias_cols], axis=0), ((0, 4), (0, 0))).T
    common = [(rep_scalar, True), (proj, True), (halo, True), (cols, True), (mask_ext, False)]
    flat_shape = jax.ShapeDtypeStruct((width, group), B16)
    (gated,) = token_call(gate_kernel, "gate", common, [flat_shape])
    received = lax.all_to_all(gated.reshape(n_seq, chan, group), "seq", 0, 0, tiled=True)

    skip_local = lax.dynamic_slice_in_dim(skip_gain[0], chan_start, chan, 0)
    columns = lax.dynamic_slice_in_dim(kernel_weight[0], chan_start, chan, 1)
    twist, table = transform_tables(blocks, group)
    nets = (feat_weight[0], inner_weight[0], deep_weight[0])
    if blocks == 4:
        grid, ramp = feature_table(seq_len, feat_weight.shape[1])
        rates = lax.dynamic_slice_in_dim(jnp.asarray(decay_rates(model)), chan_start, chan, 0)
        smalls = jnp.concatenate([feat_bias, inner_bias, deep_bias, sine_freq], axis=0).T
        filt = smalls.shape[0]
        hi, lo = split_table(table)
        kern_spec, sines, cosines = pl.pallas_call(
            filter_forward_kernel,
            out_shape=(
                jax.ShapeDtypeStruct((blocks * chan, 2 * group), F32),
                jax.ShapeDtypeStruct((3, filt, seq_len), F32),
                jax.ShapeDtypeStruct((3, filt, seq_len), F32),
            ),
            scratch_shapes=[pltpu.VMEM((blocks * chan, 2 * group), F32)],
            compiler_params=pltpu.CompilerParams(vmem_limit_bytes=VMEM_BYTES),
            cost_estimate=pl.CostEstimate(flops=10**6, bytes_accessed=10**6, transcendentals=0),
            name="filter_forward",
        )(grid, ramp, rates, *nets, smalls, columns, twist, hi, lo)
        kern_spec = kern_spec.reshape(blocks, chan, 2 * group)

        def kernel_pull(grad_kernel):
            shapes = [columns.shape] + [w.shape[::-1] for w in nets] + [smalls.shape]
            gcols, g1, g2, g3, gsmalls = pl.pallas_call(
                filter_backward_kernel,
                out_shape=tuple(jax.ShapeDtypeStruct(shape, F32) for shape in shapes),
                compiler_params=pltpu.CompilerParams(vmem_limit_bytes=VMEM_BYTES),
                cost_estimate=pl.CostEstimate(flops=10**6, bytes_accessed=10**6, transcendentals=0),
                name="filter_backward",
            )(grad_kernel, grid, ramp, rates, *nets, smalls, columns, sines, cosines)
            gs = gsmalls.T
            return (g1.T, gs[0], g2.T, gs[1], g3.T, gs[2], gs[3], gcols)

    else:
        feature_grid, ramp_unit = features(seq_len, feat_weight.shape[1])
        kernel, pull = jax.vjp(
            partial(filter_columns, feature_grid, ramp_unit, chan_start, chan, model),
            feat_weight[0],
            feat_bias[0],
            inner_weight[0],
            inner_bias[0],
            deep_weight[0],
            deep_bias[0],
            sine_freq[0],
            columns,
        )
        kern_spec = spectrum_of(kernel.reshape(chan, blocks, group).transpose(1, 0, 2), twist, table)

        def kernel_pull(grad_kernel):
            return pull(grad_kernel.transpose(1, 0, 2).reshape(chan, seq_len))

    mixed_chan, kept_spec = conv_forward(received, kern_spec, twist, table, skip_local)
    mixed = lax.all_to_all(mixed_chan, "seq", 0, 0, tiled=True).reshape(width, group)
    (y_cols,) = token_call(output_kernel, "output", common + [(mixed, True)], [flat_shape])

    middle_part = jnp.einsum("ct,oc->to", y_cols, full_out, preferred_element_type=F32)
    middle = residual + (scatter_rel(middle_part) + out_bias[0])
    normed_two, unit_two, scale_two = layer_norm(middle, norm2_gain[0], norm2_shift[0])
    rows_two = gather_rel(normed_two.astype(B16))

    grad_top = cotangent.astype(F32) * row_mask
    grad_mlp = grad_top.astype(B16)
    mlp_rows = gather_rel(grad_mlp)
    grad_act = jnp.dot(mlp_rows, full_down, preferred_element_type=F32)
    up_block = lax.dynamic_slice_in_dim(up_bias[0], rep * hidden, hidden, 0)
    pre_act = jnp.dot(rows_two, full_up, preferred_element_type=F32) + up_block
    phi = 0.5 * (1.0 + lax.erf(pre_act * math.sqrt(0.5)))
    act_rows = (pre_act * phi).astype(B16)
    slope = phi + pre_act * (jnp.exp(-0.5 * pre_act * pre_act) * (1.0 / math.sqrt(2.0 * math.pi)))
    grad_pre = (grad_act * slope).astype(B16)
    grad_two = scatter_rel(jnp.einsum("tf,df->td", grad_pre, full_up, preferred_element_type=F32))
    mlp_part = jnp.einsum("tf,of->to", act_rows, full_down, preferred_element_type=F32)
    layer_out = (middle + (scatter_rel(mlp_part) + down_bias[0])).astype(B16)
    term_down = jnp.einsum("to,tf->of", mlp_rows, act_rows, preferred_element_type=F32)
    term_up = jnp.einsum("td,tf->df", rows_two, grad_pre, preferred_element_type=F32)
    grad_two, term_down = lax.optimization_barrier((grad_two, term_down.astype(B16)))
    grad_down_bias = jnp.sum(grad_mlp.astype(F32), axis=0)
    grad_up_block = jnp.sum(grad_pre.astype(F32), axis=0)

    grad_down = lax.psum_scatter(
        term_down, "seq", scatter_dimension=0, tiled=True
    ).astype(F32)
    grad_up = ring_scatter(term_up.astype(B16))

    grad_unit_two, grad_gain_two, grad_shift_two = norm_back(
        grad_two, unit_two, scale_two, norm2_gain[0]
    )
    grad_middle = grad_top + grad_unit_two
    grad_mix = grad_middle.astype(B16)
    grad_out_bias = jnp.sum(grad_mix.astype(F32), axis=0)
    mix_rows = gather_rel(grad_mix)
    gy_cols = jnp.einsum("to,oc->ct", mix_rows, full_out, preferred_element_type=F32).astype(B16)
    term_out = jnp.einsum("to,ct->oc", mix_rows, y_cols, preferred_element_type=F32)
    grad_out = halve_scatter(term_out.astype(B16))

    grad_mixed, gate_first = token_call(
        grad_mix_kernel,
        "grad_mix",
        common + [(mixed, True), (gy_cols, True)],
        [flat_shape, jax.ShapeDtypeStruct((width, LANE), F32)],
    )
    gate_next = shift_seq(gate_first, -1)
    grads_chan = lax.all_to_all(grad_mixed.reshape(n_seq, chan, group), "seq", 0, 0, tiled=True)
    ggated_chan, grad_kernel = conv_backward(grads_chan, kept_spec, kern_spec, twist, table, skip_local)
    ggated = lax.all_to_all(ggated_chan, "seq", 0, 0, tiled=True).reshape(width, group)
    ggated_next = shift_seq(ggated[:, :LANE], -1)
    kernel_grads = kernel_pull(grad_kernel)
    grad_proj, col_sums = token_call(
        grad_proj_kernel,
        "grad_proj",
        common
        + [(mixed, True), (gy_cols, True), (ggated, True), (ggated_next, True), (gate_next, True)],
        [jax.ShapeDtypeStruct((3, width, group), B16), jax.ShapeDtypeStruct((width, 16), F32)],
    )

    one_part = jnp.einsum("pct,dpc->td", grad_proj, full_in, preferred_element_type=F32)
    grad_one = scatter_rel(one_part)
    term_in = jnp.einsum("td,pct->dpc", rows_one, grad_proj, preferred_element_type=F32)
    grad_in = halve_scatter(term_in.reshape(model, 3 * width).astype(B16))
    grad_in = grad_in.reshape(-1, 3, width)
    grad_unit_one, grad_gain_one, grad_shift_one = norm_back(
        grad_one, unit_one, scale_one, norm1_gain[0]
    )
    grad_tokens = grad_middle + grad_unit_one

    totals = [
        *kernel_grads[:7],
        grad_gain_one,
        grad_shift_one,
        grad_gain_two,
        grad_shift_two,
        grad_out_bias,
        grad_down_bias,
    ]
    packed = [rows128(t) for t in totals]
    group_part = jnp.concatenate([rows128(col_sums.T), rows128(grad_up_block)], axis=0)
    total, groups, owns = sync_small(jnp.concatenate(packed, axis=0), group_part, rows128(kernel_grads[7]))
    outs = []
    start = 0
    for t, p in zip(totals, packed):
        outs.append(total[start : start + p.shape[0]].reshape(-1)[: t.size].reshape((1,) + t.shape))
        start += p.shape[0]
    flat = groups.reshape(n_rep, -1)
    sums = flat[:, : 16 * width].reshape(n_rep, 16, width).transpose(1, 0, 2).reshape(16, model)
    grad_up_bias = flat[:, 16 * width : 16 * width + hidden].reshape(1, -1)
    filt = columns.shape[0]
    grad_kernel_weight = (
        owns.reshape(n_rep, n_seq, -1)[:, :, : filt * chan]
        .reshape(n_rep, n_seq, filt, chan)
        .transpose(2, 0, 1, 3)
        .reshape(1, filt, model)
    )
    pick = lambda offset: jnp.stack([sums[1 + 5 * p + offset] for p in range(3)])
    grad_skip = sums[0][None]
    grad_short_bias = pick(0)[None]
    grad_short_taps = jnp.stack([pick(3), pick(2), pick(1)])[None]
    grad_in_bias = pick(4)[None]
    return (
        layer_out,
        grad_tokens,
        grad_in[None],
        grad_in_bias,
        grad_short_taps,
        grad_short_bias,
        outs[0],
        outs[1],
        outs[2],
        outs[3],
        outs[4],
        outs[5],
        outs[6],
        grad_kernel_weight,
        grad_skip,
        grad_out[None],
        outs[11],
        outs[7],
        outs[8],
        outs[9],
        outs[10],
        grad_up[None],
        grad_up_bias,
        grad_down[None],
        outs[12],
    )


NN = ((1,), (0,))
NT = ((1,), (1,))
TN = ((0,), (0,))
PART = 64
REP, SEQ, AT, ITEM, OLDER, YOUNGER, OWNER, LEFT, RIGHT = 0, 1, 2, 3, 4, 5, 8, 16, 25
RING = [0, 2, 4, 6, 7, 5, 3, 1]
AHEAD = [(RING[i], RING[(i + 1) % 8]) for i in range(8)]
BACK = [(b, a) for a, b in AHEAD]


def meta_table(group):
    rows = []
    for seq in range(8):
        p = RING.index(seq)
        for rep in range(4):
            row = [rep, seq, (seq % 4) * group, seq // 4, int(seq % 4 != 0), int(seq % 4 != 3), 0, 0]
            row += [RING[(p + k) % 8] for k in (0, -1, 1, -2, 2, -3, 3, 4)]
            row += [RING[(p - k) % 8] for k in range(9)]
            row += [RING[(p + k) % 8] for k in range(9)]
            rows.append(row)
    return np.asarray(rows, np.int32)


def call(kernel, name, args, outs, scratch=(), limit=24):
    def space(a):
        small = a.dtype == jnp.int32
        return pl.BlockSpec(memory_space=pltpu.SMEM if small else pltpu.VMEM)

    return pl.pallas_call(
        kernel,
        out_shape=outs,
        in_specs=[space(a) for a in args],
        out_specs=[pl.BlockSpec(memory_space=pltpu.VMEM) for _ in outs],
        scratch_shapes=list(scratch),
        compiler_params=pltpu.CompilerParams(vmem_limit_bytes=limit * 2**20),
        cost_estimate=pl.CostEstimate(flops=10**6, bytes_accessed=10**5, transcendentals=0),
        name=name,
    )(*args)


def shape(dims, kind):
    return jax.ShapeDtypeStruct(tuple(dims), kind)


def dot(left, right, dims):
    return lax.dot_general(left, right, (dims, ((), ())), preferred_element_type=F32)


def place(index):
    return pl.ds(pl.multiple_of(index * LANE, LANE), LANE)


def normed_of(rows):
    centred = rows - jnp.mean(rows, axis=1, keepdims=True)
    inverse = lax.rsqrt(jnp.mean(centred * centred, axis=1, keepdims=True) + EPS)
    return centred * inverse, inverse


def item_length(meta_ref, len_ref):
    return jnp.where(meta_ref[ITEM] == 0, len_ref[0], len_ref[1])


def lane_masks(meta_ref, len_ref, size):
    lane = lax.broadcasted_iota(jnp.int32, (1, size), 1)
    real = (meta_ref[AT] - LANE + lane < item_length(meta_ref, len_ref)).astype(F32)
    older, younger = meta_ref[OLDER].astype(F32), meta_ref[YOUNGER].astype(F32)
    exists = jnp.where(lane < LANE, older, jnp.where(lane >= size - LANE, younger, 1.0))
    return real, exists


def pack_io_kernel(in_ref, out_w_ref, out_ref):
    width = out_w_ref.shape[2]
    for p in range(3):
        out_ref[:, p * width : (p + 1) * width] = in_ref[0, :, p, :]
    out_ref[:, 3 * width :] = out_w_ref[0]


def pack_ud_kernel(up_ref, down_ref, out_ref):
    out_ref[0] = up_ref[0]
    out_ref[1] = down_ref[0]


def halves_kernel(left_ref, right_ref, a_ref, b_ref):
    half = a_ref.shape[0]
    a_ref[...] = left_ref[:half]
    b_ref[...] = right_ref[half:]


def assemble_kernel(meta_ref, p0, p1, p2, p3, p4, p5, p6, a_ref, b_ref, out_ref):
    for k, ref in enumerate((p0, p1, p2, p3, p4, p5, p6)):
        out_ref[meta_ref[OWNER + k]] = ref[...]
    half = a_ref.shape[0]
    out_ref[meta_ref[OWNER + 7], :half] = a_ref[...]
    out_ref[meta_ref[OWNER + 7], half:] = b_ref[...]


def norm_first_kernel(x_ref, gain_ref, shift_ref, out_ref):
    unit, _ = normed_of(x_ref[...].astype(F32))
    out_ref[...] = (unit * gain_ref[...] + shift_ref[...]).astype(B16)


def own_mask(meta_ref, len_ref, rows):
    row = lax.broadcasted_iota(jnp.int32, (rows, 1), 0)
    return (meta_ref[AT] + meta_ref[REP] * rows + row < item_length(meta_ref, len_ref)).astype(F32)


def top_kernel(meta_ref, len_ref, top_ref, out_ref):
    mask = own_mask(meta_ref, len_ref, top_ref.shape[0])
    out_ref[...] = (top_ref[...].astype(F32) * mask).astype(B16)


def setup_kernel(
    meta_ref, taps_ref, short_bias_ref, in_bias_ref, up_bias_ref, skip_ref, rate_ref, kern_w_ref, fb_ref, ib_ref, db_ref, sf_ref,
    cols_ref, up_ref, chan_ref, columns_ref, small_col_ref, small_row_ref
):
    width = cols_ref.shape[0]
    chan = chan_ref.shape[0]
    rep, seq = meta_ref[REP], meta_ref[SEQ]
    lanes = pl.ds(pl.multiple_of(rep * width, width), width)
    rows = [taps_ref[0, j, :, lanes] for j in range(3)] + [short_bias_ref[0, :, lanes], in_bias_ref[0, :, lanes]]
    stack = jnp.concatenate(rows + [jnp.zeros((LANE - 15, width), F32)], axis=0)
    cols_ref[...] = stack.T[:, :16]
    up_ref[...] = up_bias_ref[:, pl.ds(pl.multiple_of(rep * up_ref.shape[1], LANE), up_ref.shape[1])]
    turn = width - seq * chan
    stack = jnp.concatenate([skip_ref[:, lanes], rate_ref[:, lanes], jnp.zeros((LANE - 2, width), F32)], axis=0)
    chan_ref[...] = pltpu.roll(stack, turn, 1)[:, :LANE].T[:chan, :2]
    columns_ref[...] = pltpu.roll(kern_w_ref[0, :, lanes], turn, 1)[:, :chan]
    filt = small_row_ref.shape[1]
    small = jnp.concatenate([fb_ref[...], ib_ref[...], db_ref[...], sf_ref[...]], axis=0)
    small_row_ref[...] = small
    wide = jnp.concatenate([small, jnp.zeros((4, LANE - filt), F32)], axis=1)
    wide = jnp.concatenate([wide, jnp.zeros((LANE - 4, LANE), F32)], axis=0)
    small_col_ref[...] = wide.T[:filt, :4]


def edges_kernel(meta_ref, x0, x1, x2, x3, last_ref, first_ref):
    rep = meta_ref[REP]
    refs = (x0, x1, x2, x3)

    def chosen(index, lo):
        value = refs[0][lo : lo + HALO]
        for i in range(1, 4):
            value = jnp.where(index == i, refs[i][lo : lo + HALO].astype(F32), value.astype(F32))
        return value.astype(B16)

    last_ref[...] = chosen(rep ^ 3, x0.shape[0] - HALO)
    first_ref[...] = chosen(rep, 0)


def ext_of(proj_ref, halo_ref, exists, p, rows):
    return (
        jnp.concatenate(
            [halo_ref[p, rows, :LANE], proj_ref[p, rows, :], halo_ref[p, rows, LANE:]], axis=1
        ).astype(F32)
        * exists
    )


def short_from(ext, cols, p):
    return (
        cols[:, p : p + 1] * pltpu.roll(ext, 2, 1)
        + cols[:, 3 + p : 4 + p] * pltpu.roll(ext, 1, 1)
        + cols[:, 6 + p : 7 + p] * ext
        + cols[:, 9 + p : 10 + p]
    )


def project_kernel(
    meta_ref, len_ref, x0, x1, x2, x3, before_ref, after_ref, io_ref, cols_ref, proj_ref, halo_ref, gated_ref
):
    rep = meta_ref[REP]
    width, group = gated_ref.shape
    weight = io_ref[:, : 3 * width]
    for i, x_ref in enumerate((x0, x1, x2, x3)):
        cut = dot(x_ref[...], weight, NN).T
        for p in range(3):
            proj_ref[p, :, place(rep ^ i)] = (
                cut[p * width : (p + 1) * width] + cols_ref[:, 12 + p : 13 + p]
            ).astype(B16)
    edge = dot(jnp.concatenate([before_ref[...], after_ref[...]], axis=0), weight, NN)
    gap = jnp.zeros((LANE - HALO, 3 * width), F32)
    edge = jnp.concatenate([gap, edge, gap], axis=0).T
    for p in range(3):
        halo_ref[p] = (edge[p * width : (p + 1) * width] + cols_ref[:, 12 + p : 13 + p]).astype(B16)
    mask, exists = lane_masks(meta_ref, len_ref, group + 2 * LANE)
    for lo in range(0, width, PART):
        rows = slice(lo, lo + PART)
        cols = cols_ref[rows, :]
        gate_in = short_from(ext_of(proj_ref, halo_ref, exists, 1, rows), cols, 1)
        values = short_from(ext_of(proj_ref, halo_ref, exists, 2, rows), cols, 2)
        gated_ref[rows, :] = (values * gate_in * mask)[:, LANE:-LANE].astype(B16)


def out_project_kernel(
    meta_ref, len_ref, proj_ref, halo_ref, cols_ref, mixed_ref, io_ref, y_ref, give3_ref, give1_ref, keep2_ref, keep0_ref
):
    rep = meta_ref[REP]
    width, group = mixed_ref.shape
    _, exists = lane_masks(meta_ref, len_ref, group + 2 * LANE)
    for lo in range(0, width, LANE):
        rows = slice(lo, lo + LANE)
        gate_out = short_from(ext_of(proj_ref, halo_ref, exists, 0, rows), cols_ref[rows, :], 0)
        y = gate_out[:, LANE:-LANE] * mixed_ref[rows, :].astype(F32)
        for j in range(4):
            y_ref[rep ^ j, :, rows] = y[:, j * LANE : (j + 1) * LANE].T.astype(B16)
    outs = (keep0_ref, give1_ref, keep2_ref, give3_ref)
    left = y_ref[...].reshape(-1, width)
    rows = y_ref.shape[1]
    for lo in range(0, io_ref.shape[0], 256):
        part = dot(left, io_ref[lo : lo + 256, 3 * width :], NT)
        for i, ref in enumerate(outs):
            ref[:, lo : lo + 256] = part[i * rows : (i + 1) * rows].astype(ref.dtype)


def norm_second_kernel(x_ref, keep_ref, near_ref, far_ref, bias_ref, gain_ref, shift_ref, middle_ref, out_ref):
    middle = x_ref[...].astype(F32) + (
        keep_ref[...] + near_ref[...].astype(F32) + far_ref[...].astype(F32) + bias_ref[...]
    )
    middle_ref[...] = middle
    unit, _ = normed_of(middle)
    out_ref[...] = (unit * gain_ref[...] + shift_ref[...]).astype(B16)


def mlp_kernel(x0, x1, x2, x3, g0, g1, g2, g3, ud_ref, bias_ref, act_ref, gpre_ref, sum_ref):
    step = 256
    rows, model = x0.shape
    pieces = ((x0, g0), (x1, g1), (x2, g2), (x3, g3))
    for lo in range(0, act_ref.shape[1], step):
        cut = slice(lo, lo + step)
        up = ud_ref[:, 0, :, cut].reshape(model, step)
        down = ud_ref[:, 1, :, cut].reshape(model, step)
        total = None
        for i, (x_ref, g_ref) in enumerate(pieces):
            at = slice(i * rows, (i + 1) * rows)
            pre = dot(x_ref[...], up, NN) + bias_ref[:, cut]
            gact = dot(g_ref[...], down, NN)
            phi = 0.5 * (1.0 + lax.erf(pre * math.sqrt(0.5)))
            slope = phi + pre * (jnp.exp(-0.5 * pre * pre) * (1.0 / math.sqrt(2.0 * math.pi)))
            act_ref[at, cut] = (pre * phi).astype(B16)
            gpre = (gact * slope).astype(B16)
            gpre_ref[at, cut] = gpre
            part = jnp.sum(gpre.astype(F32), axis=0, keepdims=True)
            total = part if total is None else total + part
        sum_ref[:, cut] = total


def rows_kernel(which, left_ref, ud_ref, give3_ref, give1_ref, keep2_ref, keep0_ref):
    rows, model = give3_ref.shape
    owned = ud_ref.shape[2]
    outs = (keep0_ref, give1_ref, keep2_ref, give3_ref)
    for k in range(0, ud_ref.shape[0], 2):
        weight = ud_ref[k : k + 2, which].reshape(2 * owned, -1)
        part = dot(left_ref[...], weight, NT)
        for i, ref in enumerate(outs):
            ref[:, k * owned : (k + 2) * owned] = part[i * rows : (i + 1) * rows].astype(ref.dtype)


def mlp_grad_kernel(meta_ref, x0, x1, x2, x3, g0, g1, g2, g3, act_ref, gpre_ref, out_ref, left_ref, right_ref):
    owners, _, owned, wide = out_ref.shape
    for which, refs, right in ((0, (x0, x1, x2, x3), gpre_ref), (1, (g0, g1, g2, g3), act_ref)):
        for k in range(0, owners, 2):
            left = jnp.concatenate([r[:, k * owned : (k + 2) * owned] for r in refs], axis=0)
            part = dot(left, right[...], TN).astype(B16)
            out_ref[k, which] = part[:owned]
            out_ref[k + 1, which] = part[owned:]
    left_ref[...] = out_ref[meta_ref[LEFT + 1], 0]
    right_ref[...] = out_ref[meta_ref[RIGHT + 1], 1]


def ring_add_kernel(step, meta_ref, term_ref, left_in, right_in, left_ref, right_ref):
    mine = term_ref[meta_ref[LEFT + step], 0].astype(F32)
    left_ref[...] = (left_in[...].astype(F32) + mine).astype(left_ref.dtype)
    mine = term_ref[meta_ref[RIGHT + step], 1].astype(F32)
    right_ref[...] = (right_in[...].astype(F32) + mine).astype(right_ref.dtype)


def norm_second_back_kernel(
    meta_ref, len_ref, keep_ref, near_ref, far_ref, middle_ref, top_ref, gain_ref, out_ref, gx_ref, sum_ref
):
    grad = keep_ref[...] + near_ref[...].astype(F32) + far_ref[...].astype(F32)
    unit, inverse = normed_of(middle_ref[...])
    scaled = grad * gain_ref[...]
    one = jnp.mean(scaled, axis=1, keepdims=True)
    two = jnp.mean(scaled * unit, axis=1, keepdims=True)
    top = top_ref[...].astype(F32) * own_mask(meta_ref, len_ref, top_ref.shape[0])
    out = top + inverse * (scaled - one - unit * two)
    out_ref[...] = out
    gx = out.astype(B16)
    gx_ref[...] = gx
    rows = [grad * unit, grad, gx.astype(F32), top]
    sums = [jnp.sum(r, axis=0, keepdims=True) for r in rows]
    sum_ref[...] = jnp.concatenate(sums + [jnp.zeros((4, sums[0].shape[1]), F32)], axis=0)


def grad_gate_kernel(
    meta_ref, len_ref, x0, x1, x2, x3, io_ref, proj_ref, halo_ref, cols_ref, mixed_ref, gy_ref, gmix_ref, first_ref
):
    rep = meta_ref[REP]
    width, group = mixed_ref.shape
    _, exists = lane_masks(meta_ref, len_ref, group + 2 * LANE)
    weight = io_ref[:, 3 * width :]
    for i, x_ref in enumerate((x0, x1, x2, x3)):
        gy_ref[:, place(rep ^ i)] = dot(x_ref[...], weight, NN).T.astype(B16)
    for lo in range(0, width, PART):
        rows = slice(lo, lo + PART)
        gate_out = short_from(ext_of(proj_ref, halo_ref, exists, 0, rows), cols_ref[rows, :], 0)
        gy = gy_ref[rows, :].astype(F32)
        gmix_ref[rows, :] = (gy * gate_out[:, LANE:-LANE]).astype(B16)
        first_ref[rows, :] = gy[:, :LANE] * mixed_ref[rows, :LANE].astype(F32)


def conv_back_kernel(
    g_ref, spec_ref, kern_ref, twist_ref, hi_ref, lo_ref, chan_ref, out_ref, grad_kern_ref, z_ref, p_ref
):
    blocks, rows, length = twist_ref.shape[0], g_ref.shape[1], g_ref.shape[2]
    short_blocks = blocks // 4
    span = blocks * rows
    first = [g_ref[b].astype(F32) for b in range(blocks)]
    second = [g_ref[blocks + b].astype(F32) for b in range(short_blocks)]
    turn_rows(first, twist_ref, z_ref, 0, blocks)
    turn_rows(second, twist_ref, z_ref, span, blocks)
    grad = dot_split(z_ref[...], hi_ref[...], lo_ref[...], ((1,), (0,)))
    kern = kern_ref[...]
    p_ref[0:span] = times(grad[:span], kern, True)
    p_ref[span : 2 * span] = times(grad[span:], kern, True)
    p_ref[2 * span :] = times(grad[:span], spec_ref[0:span], True) + times(grad[span:], spec_ref[span:], True)
    w = dot_split(p_ref[...], hi_ref[...], lo_ref[...], ((1,), (1,)))
    skip = chan_ref[:, 0:1]
    zero = jnp.zeros((rows, LANE), B16)
    for b in range(blocks):
        acc = (back_rows(w, 0, rows, b, twist_ref, blocks) + skip * first[b]).astype(B16)
        out_ref[b, :, :length] = acc
        if b:
            out_ref[b - 1, :, length:] = acc[:, :LANE]
        if b < short_blocks:
            acc = (back_rows(w, span, rows, b, twist_ref, blocks) + skip * second[b]).astype(B16)
        else:
            acc = jnp.zeros((rows, length), B16)
        out_ref[blocks + b, :, :length] = acc
        if b:
            out_ref[blocks + b - 1, :, length:] = acc[:, :LANE]
        grad_kern_ref[b] = back_rows(w, 2 * span, rows, b, twist_ref, blocks)
    out_ref[blocks - 1, :, length:] = zero
    out_ref[2 * blocks - 1, :, length:] = zero


def conv_ahead_kernel(x_ref, kern_ref, twist_ref, hi_ref, lo_ref, chan_ref, out_ref, spec_ref, z_ref):
    conv_forward_kernel(
        twist_ref.shape[0] // 4, x_ref, kern_ref, twist_ref, hi_ref, lo_ref, chan_ref.at[:, 0:1], out_ref, spec_ref, z_ref
    )


def filter_ahead_kernel(
    grid_ref, ramp_ref, chan_ref, w1_ref, w2_ref, w3_ref, small_ref, columns_ref, twist_ref, hi_ref, lo_ref,
    spec_ref, sin_ref, cos_ref, z_ref
):
    filter_forward_kernel(
        grid_ref, ramp_ref, chan_ref.at[:, 1:2], w1_ref.at[0], w2_ref.at[0], w3_ref.at[0], small_ref, columns_ref,
        twist_ref, hi_ref, lo_ref, spec_ref, sin_ref, cos_ref, z_ref
    )


def filter_back_kernel(
    meta_ref, gk_ref, grid_ref, ramp_ref, chan_ref, w1_ref, w2_ref, w3_ref, col_ref, row_ref, columns_ref, sin_ref, cos_ref,
    side_ref, wide_ref
):
    freq, freq_row = col_ref[:, 3:4], row_ref[3:4, :]
    filt = freq.shape[0]
    gk = jnp.concatenate([gk_ref[b] for b in range(gk_ref.shape[0])], axis=1)
    gk = gk * jnp.exp(-chan_ref[:, 1:2] * ramp_ref[...])
    gcols = dot_high(sin_ref[2], gk, NT)
    chan, width = gcols.shape[1], wide_ref.shape[1]
    row = lax.broadcasted_iota(jnp.int32, (chan, width), 0)
    lane = lax.broadcasted_iota(jnp.int32, (chan, width), 1)
    pick = (lane == row + meta_ref[SEQ] * chan).astype(F32)
    wide_ref[...] = dot_high(gcols, pick, NN)
    grad = dot_high(columns_ref[...], gk, NN)
    ones = jnp.ones((8, gk.shape[1]), F32)
    gfreq = jnp.zeros((1, filt), F32)
    grads, biases = [None] * 3, [None] * 3
    for i, w_ref in ((2, w3_ref), (1, w2_ref), (0, w1_ref)):
        turn = grad * cos_ref[i]
        below = sin_ref[i - 1] if i else grid_ref[...]
        raw = dot_high(below, turn, NT)
        total = dot_high(ones, turn, NT)[0:1]
        grads[i] = raw * freq_row
        biases[i] = total * freq_row
        gfreq = gfreq + jnp.sum(raw * w_ref[0], axis=0, keepdims=True) + total * row_ref[i : i + 1, :]
        if i:
            grad = dot_high(w_ref[0], turn * freq, NN)
    gap = jnp.zeros((filt - grads[0].shape[0], filt), F32)
    small = jnp.concatenate(biases + [gfreq, jnp.zeros((filt - 4, filt), F32)], axis=0)
    side_ref[...] = jnp.concatenate(
        [grads[1], grads[2], jnp.concatenate([grads[0], gap], axis=0), small], axis=1
    )


def grad_short_kernel(
    meta_ref, len_ref, proj_ref, halo_ref, cols_ref, mixed_ref, gy_ref, ggated_ref, onext_ref, io_ref,
    x0, x1, x2, x3, gain_ref, shift_ref,
    tok_ref, sum_ref, norm_ref, give3_ref, give1_ref, keep2_ref, keep0_ref
):
    rep = meta_ref[REP]
    width, group = mixed_ref.shape
    size = group + 2 * LANE
    mask, exists = lane_masks(meta_ref, len_ref, size)
    mid = slice(LANE, size - LANE)
    next_on = exists[:, size - LANE :]
    ones = jnp.ones((LANE, group), F32)
    del ones
    columns = []
    for lo in range(0, width, PART):
        rows = slice(lo, lo + PART)
        cols = cols_ref[rows, :]
        gy = gy_ref[rows, :].astype(F32)
        zero = jnp.zeros((PART, LANE), F32)
        ext = [ext_of(proj_ref, halo_ref, exists, p, rows) for p in range(3)]
        short = [short_from(ext[p], cols, p) for p in range(3)]
        ggated = jnp.concatenate([zero, ggated_ref[rows, :].astype(F32)], axis=1) * (mask * exists)
        gout = gy * mixed_ref[rows, :].astype(F32)
        gshort = [
            jnp.concatenate([zero, gout, onext_ref[rows, :] * next_on], axis=1),
            ggated * short[2],
            ggated * short[1],
        ]
        gated = short[2][:, mid] * short[1][:, mid] * mask[:, mid]

        def summed(value):
            parts = [value[:, k : k + LANE] for k in range(0, group, LANE)]
            total = parts[0]
            for part in parts[1:]:
                total = total + part
            return jnp.sum(total, axis=1, keepdims=True)

        sums = [summed(gy * short[0][:, mid] * gated)]
        for p in range(3):
            mine = gshort[p][:, mid]
            sums.append(summed(mine))
            sums.append(summed(mine * ext[p][:, mid]))
            sums.append(summed(mine * pltpu.roll(ext[p], 1, 1)[:, mid]))
            sums.append(summed(mine * pltpu.roll(ext[p], 2, 1)[:, mid]))
            gproj = (
                cols[:, 6 + p : 7 + p] * gshort[p]
                + cols[:, 3 + p : 4 + p] * pltpu.roll(gshort[p], size - 1, 1)
                + cols[:, p : p + 1] * pltpu.roll(gshort[p], size - 2, 1)
            )[:, mid].astype(B16).astype(F32)
            sums.append(summed(gproj))
            at = slice(p * width + lo, p * width + lo + PART)
            for j in range(4):
                tok_ref[rep ^ j, :, at] = gproj[:, j * LANE : (j + 1) * LANE].T.astype(B16)
        columns.append(jnp.concatenate(sums + [jnp.zeros((PART, LANE - 16), F32)], axis=1))
    sum_ref[...] = jnp.concatenate(columns, axis=0).T[:16]
    outs = (keep0_ref, give1_ref, keep2_ref, give3_ref)
    left = tok_ref[...].reshape(-1, 3 * width)
    tall = tok_ref.shape[1]
    for lo in range(0, io_ref.shape[0], 256):
        cut = slice(lo, lo + 256)
        part = dot(left, io_ref[cut, : 3 * width], NT)
        plain = jnp.sum(part, axis=0, keepdims=True)
        cross = None
        for i, (ref, x_ref) in enumerate(zip(outs, (x0, x1, x2, x3))):
            mine = part[i * tall : (i + 1) * tall]
            ref[:, cut] = mine.astype(ref.dtype)
            two = jnp.sum(mine * x_ref[:, cut].astype(F32), axis=0, keepdims=True)
            cross = two if cross is None else cross + two
        norm_ref[0:1, cut] = (cross - shift_ref[:, cut] * plain) / gain_ref[:, cut]
        norm_ref[1:2, cut] = plain


def give_first(meta_ref, term_ref, a_ref, b_ref):
    half = a_ref.shape[2]
    seq = meta_ref[SEQ]
    s0, s1 = seq & 1, (seq >> 1) & 1
    for i in range(2):
        for j in range(2):
            a_ref[i, j] = term_ref[i, j, 1 - s0, :half]
            b_ref[i, j] = term_ref[i, 1 - s1, j, half:]


def weight_grad_kernel(meta_ref, x0, x1, x2, x3, right_ref, out_ref, a_ref, b_ref):
    owned, wide = out_ref.shape[3], out_ref.shape[4]
    right = right_ref[...].reshape(-1, wide)
    for k in range(0, 8, 2):
        left = jnp.concatenate([r[:, k * owned : (k + 2) * owned] for r in (x0, x1, x2, x3)], axis=0)
        part = dot(left, right, TN).astype(B16)
        out_ref[k // 4, (k // 2) % 2, 0] = part[:owned]
        out_ref[k // 4, (k // 2) % 2, 1] = part[owned:]
    give_first(meta_ref, out_ref, a_ref, b_ref)


def halve_one_kernel(meta_ref, term_ref, a_in, b_in, keep_a, keep_b, give_a, give_b):
    half = a_in.shape[2]
    seq = meta_ref[SEQ]
    s0, s1 = seq & 1, (seq >> 1) & 1
    for i in range(2):
        keep_a[i] = term_ref[i, s1, s0, :half].astype(F32) + a_in[i, s1].astype(F32)
        give_a[i] = (term_ref[i, 1 - s1, s0, :half].astype(F32) + a_in[i, 1 - s1].astype(F32)).astype(B16)
        keep_b[i] = term_ref[i, s1, s0, half:].astype(F32) + b_in[i, s0].astype(F32)
        give_b[i] = (term_ref[i, s1, 1 - s0, half:].astype(F32) + b_in[i, 1 - s0].astype(F32)).astype(B16)


def halve_two_kernel(meta_ref, keep_a_in, keep_b_in, a_in, b_in, keep_a, keep_b, give_a, give_b):
    s2 = meta_ref[SEQ] >> 2
    keep_a[...] = keep_a_in[s2] + a_in[s2].astype(F32)
    give_a[...] = (keep_a_in[1 - s2] + a_in[1 - s2].astype(F32)).astype(B16)
    keep_b[...] = keep_b_in[s2] + b_in[s2].astype(F32)
    give_b[...] = (keep_b_in[1 - s2] + b_in[1 - s2].astype(F32)).astype(B16)


def halve_last_kernel(keep_a, keep_b, a_in, b_in, out_ref):
    half = keep_a.shape[0]
    if len(out_ref.shape) == 3:
        out_ref[0, :half] = keep_a[...] + a_in[...].astype(F32)
        out_ref[0, half:] = keep_b[...] + b_in[...].astype(F32)
        return
    width = out_ref.shape[3]
    for p in range(3):
        cut = slice(p * width, (p + 1) * width)
        out_ref[0, :half, p, :] = keep_a[:, cut] + a_in[:, cut].astype(F32)
        out_ref[0, half:, p, :] = keep_b[:, cut] + b_in[:, cut].astype(F32)


def norm_first_back_kernel(keep_ref, near_ref, far_ref, x_ref, middle_ref, gain_ref, out_ref):
    grad = keep_ref[...] + near_ref[...].astype(F32) + far_ref[...].astype(F32)
    unit, inverse = normed_of(x_ref[...].astype(F32))
    scaled = grad * gain_ref[...]
    one = jnp.mean(scaled, axis=1, keepdims=True)
    two = jnp.mean(scaled * unit, axis=1, keepdims=True)
    out_ref[...] = middle_ref[...] + inverse * (scaled - one - unit * two)


def layer_out_kernel(keep_ref, near_ref, far_ref, middle_ref, bias_ref, out_ref):
    part = keep_ref[...] + near_ref[...].astype(F32) + far_ref[...].astype(F32)
    out_ref[...] = (middle_ref[...] + (part + bias_ref[...])).astype(B16)


def add_far_kernel(keep_ref, came_ref, out_ref):
    out_ref[...] = (keep_ref[...] + came_ref[...].astype(F32)).astype(B16)


HALF = 88


def pack_small_kernel(side_ref, wide_ref, col_ref, up_ref, one_ref, two_ref, out_ref):
    filt, width = side_ref.shape
    out_ref[:filt] = side_ref[...]
    at = filt
    for ref, count in ((one_ref, 2), (two_ref, 4)):
        for r in range(count):
            for k in range(4):
                out_ref[at : at + 1] = ref[r : r + 1, k * width : (k + 1) * width]
                at += 1
    out_ref[HALF : HALF + 16] = col_ref[...]
    for k in range(4):
        out_ref[HALF + 16 + k : HALF + 17 + k] = up_ref[:, k * width : (k + 1) * width]
    out_ref[HALF + 20 : HALF + 24] = jnp.zeros((4, width), F32)
    out_ref[HALF + 24 :] = wide_ref[...]


def add_small_kernel(mine_ref, came_ref, out_ref):
    out_ref[...] = mine_ref[...] + came_ref[...]


def list_small_kernel(meta_ref, mine_ref, came_ref, out_ref):
    y = meta_ref[REP] >> 1
    out_ref[:HALF] = mine_ref[:HALF] + came_ref[:HALF]
    out_ref[pl.ds(pl.multiple_of((1 + y) * HALF, 8), HALF)] = mine_ref[HALF:]
    out_ref[pl.ds(pl.multiple_of((2 - y) * HALF, 8), HALF)] = came_ref[HALF:]


def unpack_small_kernel(
    meta_ref, mine_ref, came_ref,
    in_bias, taps, short_bias, fw, fb, iw, ib, dw, db, sf, kern_w, skip, out_b, n1g, n1s, n2g, n2s, up_b, down_b
):
    core = meta_ref[REP] & 1
    filt, width = fw.shape[2], mine_ref.shape[1]
    total = mine_ref[:HALF] + came_ref[:HALF]
    iw[0] = total[:filt, :filt]
    dw[0] = total[:filt, filt : 2 * filt]
    fw[0] = total[: fw.shape[1], 2 * filt : 3 * filt]
    for k, ref in enumerate((fb, ib, db, sf)):
        ref[...] = total[k : k + 1, 3 * filt :]
    at = filt
    for ref in (n1g, n1s, n2g, n2s, out_b, down_b):
        for k in range(4):
            ref[:, k * width : (k + 1) * width] = total[at : at + 1]
            at += 1
    for y in range(2):
        lo = (1 + y) * HALF
        mine, came = mine_ref[lo : lo + HALF], came_ref[lo : lo + HALF]
        for c in range(2):
            block = jnp.where(core == c, mine, came)
            lanes = slice((2 * y + c) * width, (2 * y + c + 1) * width)
            skip[:, lanes] = block[0:1]
            for p in range(3):
                row = 1 + 5 * p
                short_bias[0, p : p + 1, lanes] = block[row : row + 1]
                for j in range(3):
                    taps[0, j, p : p + 1, lanes] = block[row + 3 - j : row + 4 - j]
                in_bias[0, p : p + 1, lanes] = block[row + 4 : row + 5]
            for k in range(4):
                lo_up = (2 * y + c) * 4 * width + k * width
                up_b[:, lo_up : lo_up + width] = block[16 + k : 17 + k]
            kern_w[0, :, lanes] = block[24 : 24 + filt]


def tie(values, *others):
    return lax.optimization_barrier((values, others))[0]


class RingGather:
    def __init__(self, name, meta, shard):
        self.name, self.meta = name, meta
        self.pieces = [shard]
        self.send(shard, shard)

    def send(self, left, right):
        self.came = (lax.ppermute(left, "seq", AHEAD), lax.ppermute(right, "seq", BACK))

    def step(self, *others):
        left, right = tie(self.came, *others)
        self.pieces += [left, right]
        count = len(self.pieces)
        if count == 7:
            half = shape((left.shape[0] // 2,) + left.shape[1:], B16)
            left, right = call(halves_kernel, self.name + "_halves", [left, right], [half, half])
        if count < 9:
            self.send(left, right)
        return self.came

    def full(self, *others):
        left, right = tie(self.came, *others)
        pieces = self.pieces + [left, right]
        return call(
            assemble_kernel,
            self.name + "_assemble",
            [self.meta, *pieces],
            [shape((8,) + self.pieces[0].shape, B16)],
        )[0]


def gather_four(rows):
    far = swap(rows, "rep", 2)
    near = swap(rows, "rep", 1)
    diag = swap(far, "rep", 1)
    return [rows, near, far, diag]


def pass_far(give3, give1, keep2):
    came = swap(give3, "rep", 1)
    near = swap(give1, "rep", 1)
    (summed,) = call(add_far_kernel, "add_far", [keep2, came], [shape(keep2.shape, B16)])
    return near, swap(summed, "rep", 2), summed


class Halving:
    def __init__(self, name, meta, term, give, out_dims):
        self.name, self.meta, self.term, self.out_dims = name, meta, term, out_dims
        self.stage = 0
        self.came = (swap(give[0], "seq", 1), swap(give[1], "seq", 2))

    def step(self, *others):
        came = tie(self.came, *others)
        self.stage += 1
        rows, cols = self.term.shape[3] // 2, self.term.shape[4]
        if self.stage == 1:
            lead = (2, rows, cols)
            ka, kb, ga, gb = call(
                halve_one_kernel, self.name + "_one", [self.meta, self.term, *came],
                [shape(lead, F32)] * 2 + [shape(lead, B16)] * 2,
            )
            self.came = (swap(ga, "seq", 2), swap(gb, "seq", 1))
        elif self.stage == 2:
            lead = (rows, cols)
            ka, kb, ga, gb = call(
                halve_two_kernel, self.name + "_two", [self.meta, *self.keep, *came],
                [shape(lead, F32)] * 2 + [shape(lead, B16)] * 2,
            )
            self.came = (swap(ga, "seq", 4), swap(gb, "seq", 4))
        else:
            return call(halve_last_kernel, self.name + "_last", [*self.keep, *came], [shape(self.out_dims, F32)])[0]
        self.keep = (ka, kb)
        return self.keep


def per_device_fast(
    tokens,
    cotangent,
    lengths,
    in_weight,
    in_bias,
    short_taps,
    short_bias,
    feat_weight,
    feat_bias,
    inner_weight,
    inner_bias,
    deep_weight,
    deep_bias,
    sine_freq,
    kernel_weight,
    skip_gain,
    out_weight,
    out_bias,
    norm1_gain,
    norm1_shift,
    norm2_gain,
    norm2_shift,
    up_weight,
    up_bias,
    down_weight,
    down_bias,
):
    tok_rows, model = tokens.shape
    group = tok_rows * 4
    blocks = 4
    seq_len = blocks * group
    chan = model // 32
    width = model // 4
    hidden = up_weight.shape[2]
    owned = model // 8
    filt = feat_weight.shape[2]
    device = lax.axis_index("seq") * 4 + lax.axis_index("rep")
    meta = lax.dynamic_index_in_dim(jnp.asarray(meta_table(group)), device, 0, keepdims=False)
    row_f32, row_b16 = shape((tok_rows, model), F32), shape((tok_rows, model), B16)
    sums_shapes = [row_b16, row_b16, row_f32, row_f32]
    flat_shape = shape((width, group), B16)

    (io_shard,) = call(pack_io_kernel, "pack_io", [in_weight, out_weight], [shape((owned, 4 * width), B16)])
    io_ring = RingGather("io", meta, io_shard)
    (normed,) = call(norm_first_kernel, "norm_first", [tokens, norm1_gain, norm1_shift], [row_b16])
    x_one = gather_four(normed)
    twist, table = transform_tables(blocks, group)
    hi, lo = split_table(table)
    grid, ramp = feature_table(seq_len, feat_weight.shape[1])
    twist, grid, ramp = jnp.asarray(twist), jnp.asarray(grid), jnp.asarray(ramp)
    rates = jnp.asarray(decay_rates(model).T)
    cols, up_block, chans, columns, small_col, small_row = call(
        setup_kernel,
        "setup",
        [
            meta, short_taps, short_bias, in_bias, up_bias, skip_gain, rates, kernel_weight,
            feat_bias, inner_bias, deep_bias, sine_freq,
        ],
        [
            shape((width, 16), F32), shape((1, hidden), F32), shape((chan, 2), F32), shape((filt, chan), F32),
            shape((filt, 4), F32), shape((4, filt), F32),
        ],
    )
    (ud_shard,) = call(pack_ud_kernel, "pack_ud", [up_weight, down_weight], [shape((2, owned, hidden), B16)])
    (top_rows,) = call(top_kernel, "top", [meta, lengths, cotangent], [row_b16])
    io_ring.step(cols, ud_shard, top_rows)
    nets = (feat_weight, inner_weight, deep_weight)
    kern_spec, sines, cosines = call(
        filter_ahead_kernel,
        "filter_ahead",
        [grid, ramp, chans, *nets, tie(small_col, io_ring.pieces[-1]), columns, twist, hi, lo],
        [
            shape((blocks * chan, 2 * group), F32),
            shape((3, filt, seq_len), F32),
            shape((3, filt, seq_len), F32),
        ],
        scratch=[pltpu.VMEM((blocks * chan, 2 * group), F32)],
    )
    io_ring.step(kern_spec)

    edge = shape((HALO, model), B16)
    last, first = call(edges_kernel, "edges", [meta, *x_one], [edge, edge])
    before = lax.ppermute(last, "seq", [(i, (i + 1) % 8) for i in range(8)])
    after = lax.ppermute(first, "seq", [(i, (i + 7) % 8) for i in range(8)])
    io_ring.step()
    full_io = io_ring.full().reshape(model, 4 * width)
    ud_ring = RingGather("ud", meta, tie(ud_shard, full_io))
    g_top = gather_four(tie(top_rows, x_one[3]))
    proj, halo, gated = call(
        project_kernel,
        "project",
        [meta, lengths, *x_one, before, after, full_io, cols],
        [shape((3, width, group), B16), shape((3, width, 2 * LANE), B16), flat_shape],
    )
    common = [proj, halo, cols]

    received = lax.all_to_all(gated.reshape(8, chan, group), "seq", 0, 0, tiled=True)
    ud_ring.step(received)
    spec_rows = 2 * blocks * chan
    mixed_chan, kept_spec = call(
        conv_ahead_kernel,
        "conv_ahead",
        [received, kern_spec, twist, hi, lo, chans],
        [shape(received.shape, B16), shape((spec_rows, 2 * group), F32)],
        scratch=[pltpu.VMEM((spec_rows, 2 * group), F32)],
    )
    mixed = lax.all_to_all(mixed_chan, "seq", 0, 0, tiled=True).reshape(width, group)
    ud_ring.step(mixed)

    y_tok, give3, give1, keep2, keep0 = call(
        out_project_kernel,
        "out_project",
        [meta, lengths, *common, mixed, full_io],
        [shape((4, tok_rows, width), B16)] + sums_shapes,
    )
    near, far, _ = pass_far(give3, give1, keep2)
    middle, normed_two = call(
        norm_second_kernel,
        "norm_second",
        [tokens, keep0, near, far, out_bias, norm2_gain, norm2_shift],
        [row_f32, row_b16],
    )
    ud_ring.step(normed_two)
    x_two = gather_four(normed_two)
    full_ud = ud_ring.full(x_two[2])

    tall = shape((group, hidden), B16)
    act, gpre, gup = call(
        mlp_kernel, "mlp", [*x_two, *g_top, full_ud, up_block], [tall, tall, shape((1, hidden), F32)]
    )
    give3, give1, keep2, keep0 = call(partial(rows_kernel, 0), "grad_two", [gpre, full_ud], sums_shapes)
    near, far, passed = pass_far(give3, give1, keep2)
    one_way = shape((owned, hidden), B16)
    mlp_terms, left, right = call(
        mlp_grad_kernel,
        "mlp_grad",
        [meta, *x_two, *g_top, act, tie(gpre, passed)],
        [shape((8, 2, owned, hidden), B16), one_way, one_way],
    )

    def ring_send(left, right):
        return lax.ppermute(left, "seq", AHEAD), lax.ppermute(right, "seq", BACK)

    def ring_add(step, came, *others):
        left, right = tie(came, *others)
        out = shape((owned, hidden), F32 if step == 8 else B16)
        return call(
            partial(ring_add_kernel, step), "ring_add_%d" % step, [meta, mlp_terms, left, right], [out, out]
        )

    ring = ring_send(left, right)
    grad_middle, gx, norm_sums = call(
        norm_second_back_kernel,
        "norm_second_back",
        [meta, lengths, keep0, near, tie(far, left), middle, cotangent, norm2_gain],
        [row_f32, row_b16, shape((8, model), F32)],
    )
    g_mid = gather_four(gx)
    m3, m1, m2, m0 = call(partial(rows_kernel, 1), "mlp_rows", [tie(act, gx), full_ud], sums_shapes)
    ring = ring_send(*ring_add(2, ring, g_mid[2], m3))
    gy, gmix, gate_first = call(
        grad_gate_kernel,
        "grad_gate",
        [meta, lengths, *tie(tuple(g_mid), m3), full_io, *common, mixed],
        [flat_shape, flat_shape, shape((width, LANE), F32)],
    )

    grads_chan = lax.all_to_all(gmix.reshape(8, chan, group), "seq", 0, 0, tiled=True)
    gate_next = lax.ppermute(gate_first, "seq", [(i, (i + 7) % 8) for i in range(8)])
    m_near, m_far, _ = pass_far(tie(m3, gmix), m1, m2)
    ring = ring_send(*ring_add(3, ring, grads_chan))
    ggated_chan, grad_kernel = call(
        conv_back_kernel,
        "conv_back",
        [grads_chan, kept_spec, kern_spec, twist, hi, lo, chans],
        [shape((8, chan, group + LANE), B16), shape((blocks, chan, group), F32)],
        scratch=[pltpu.VMEM((spec_rows, 2 * group), F32), pltpu.VMEM((3 * spec_rows // 2, 2 * group), F32)],
    )
    out_cube = (2, 2, 2, owned, width)
    give = shape((2, 2, owned // 2, width), B16)
    out_terms, ga, gb = call(
        weight_grad_kernel,
        "grad_out",
        [meta, *tie(tuple(g_mid), grads_chan), y_tok],
        [shape(out_cube, B16), give, give],
    )
    ring = ring_send(*ring_add(4, ring, ggated_chan))
    ggated = lax.all_to_all(ggated_chan, "seq", 0, 0, tiled=True).reshape(width, group + LANE)
    out_back = Halving("grad_out", meta, out_terms, (ga, gb), (1, owned, width))
    ring = ring_send(*ring_add(5, ring, ggated))
    gproj_tok, col_sums, norm_one, give3, give1, keep2, keep0 = call(
        grad_short_kernel,
        "grad_short",
        [meta, lengths, *common, mixed, gy, ggated, gate_next, full_io, *x_one, norm1_gain, norm1_shift],
        [shape((4, tok_rows, 3 * width), B16), shape((16, width), F32), shape((2, model), F32)] + sums_shapes,
    )
    near, far, passed = pass_far(give3, give1, keep2)
    give = shape((2, 2, owned // 2, 3 * width), B16)
    in_terms, ga, gb = call(
        weight_grad_kernel,
        "grad_in",
        [meta, *x_one, gproj_tok],
        [shape((2, 2, 2, owned, 3 * width), B16), give, give],
    )
    in_back = Halving("grad_in", meta, in_terms, (ga, gb), (1, owned, 3, width))
    side, wide = call(
        filter_back_kernel,
        "filter_back",
        [
            meta, tie(grad_kernel, ga), grid, ramp, chans, *nets, small_col, small_row, columns, sines, cosines
        ],
        [shape((filt, 4 * filt), F32), shape((filt, width), F32)],
    )

    (small,) = call(
        pack_small_kernel,
        "pack_small",
        [side, wide, col_sums, gup, norm_one, norm_sums],
        [shape((2 * HALF, width), F32)],
    )
    came = swap(small, "seq", 1)
    (grad_tokens,) = call(
        norm_first_back_kernel, "norm_first_back", [keep0, near, tie(far, small), tokens, grad_middle, norm1_gain], [row_f32]
    )
    (layer_out,) = call(layer_out_kernel, "layer_out", [m0, m_near, tie(m_far, small), middle, down_bias], [row_b16])
    ring = ring_send(*ring_add(6, ring, small))
    out_back.step(small)
    (small,) = call(add_small_kernel, "add_small", [small, came], [small])
    came = swap(small, "seq", 2)
    in_back.step(small)
    ring = ring_send(*ring_add(7, ring, small))
    (small,) = call(add_small_kernel, "add_small", [small, came], [small])
    came = swap(small, "seq", 4)
    out_back.step(small)
    (small,) = call(add_small_kernel, "add_small", [small, came], [small])
    came = swap(small, "rep", 2)
    in_back.step(small)
    grad_up, grad_down = ring_add(8, ring, small)
    (small,) = call(
        list_small_kernel, "list_small", [meta, small, came], [shape((3 * HALF, width), F32)]
    )
    came = swap(small, "rep", 1)
    grad_out = out_back.step(small)
    grad_in = in_back.step(small)
    vector = shape((1, model), F32)
    square, short = shape((1, filt, filt), F32), shape((1, filt), F32)
    triple = shape((1, 3, model), F32)
    outs = call(
        unpack_small_kernel,
        "unpack_small",
        [meta, small, came],
        [
            triple, shape((1, 3, 3, model), F32), triple, shape(feat_weight.shape, F32), short, square, short, square,
            short, short, shape(kernel_weight.shape, F32), vector, vector, vector, vector, vector, vector,
            shape(up_bias.shape, F32), vector,
        ],
    )
    return (
        layer_out,
        grad_tokens,
        grad_in,
        *outs[:12],
        grad_out,
        *outs[12:17],
        grad_up[None],
        outs[17],
        grad_down[None],
        outs[18],
    )


def solution(mesh):
    rows = P(("seq", "rep"), None)
    cut = P(None, "seq", "rep")
    wide = P(None, "seq", None, "rep")
    whole = P()
    ins = [rows, rows, whole, wide] + [whole] * 12 + [cut] + [whole] * 5 + [cut, whole, cut, whole]
    outs = [rows, rows, wide] + [whole] * 12 + [cut] + [whole] * 5 + [cut, whole, cut, whole]
    fast = mesh.shape["seq"] == 8 and mesh.shape["rep"] == 4
    return jax.shard_map(
        per_device_fast if fast else per_device, mesh=mesh, in_specs=tuple(ins), out_specs=tuple(outs), check_vma=False
    )
```

```python
from functools import partial
import math

import jax
import jax.numpy as jnp
import numpy as np
from jax import lax
from jax.experimental import pallas as pl
from jax.experimental.pallas import tpu as pltpu
from jax.sharding import PartitionSpec as P

EPS = 1e-05
HIGH = lax.Precision.HIGHEST
F32 = jnp.float32
B16 = jnp.bfloat16
LANE = 128
HALO = 16
VMEM_BYTES = 48 * 2**20


def swap(values, axis_name, bit):
    size = lax.axis_size(axis_name)
    return lax.ppermute(values, axis_name, [(i, i ^ bit) for i in range(size)])


def gather_rel(rows):
    far = swap(rows, "rep", 2)
    near = swap(rows, "rep", 1)
    diag = swap(far, "rep", 1)
    return jnp.concatenate([rows, near, far, diag], axis=0)


def scatter_rel(part):
    rows = part.shape[0] // 4
    blocks = part.reshape(4, rows, part.shape[1])
    far_in = swap(blocks[3].astype(B16), "rep", 1)
    far_sum = (blocks[2] + far_in.astype(F32)).astype(B16)
    near_in = swap(blocks[1].astype(B16), "rep", 1)
    far_out = swap(far_sum, "rep", 2)
    return blocks[0] + near_in.astype(F32) + far_out.astype(F32)


def ring_order(count):
    if count == 8:
        return [0, 2, 4, 6, 7, 5, 3, 1]
    return list(range(count))


def ring_maps(count):
    order = ring_order(count)
    ahead = [(order[i], order[(i + 1) % count]) for i in range(count)]
    return order, ahead, [(b, a) for a, b in ahead]


def ring_gather(shard):
    count = lax.axis_size("seq")
    if count != 8:
        return lax.all_gather(shard, "seq", axis=0)
    order, ahead, back = ring_maps(count)
    place = jnp.asarray(np.argsort(order), jnp.int32)[lax.axis_index("seq")]
    owners = jnp.asarray(order, jnp.int32)
    full = jnp.zeros((count,) + shard.shape, shard.dtype)

    def put(full, piece, step, lo=0):
        owner = owners[(place + step + count) % count]
        start = (owner, lo) + (0,) * (shard.ndim - 1)
        return lax.dynamic_update_slice(full, piece[None], start)

    full = put(full, shard, 0)
    left = right = shard
    for step in range(1, count // 2):
        left = lax.ppermute(left, "seq", ahead)
        right = lax.ppermute(right, "seq", back)
        full = put(full, left, -step)
        full = put(full, right, step)
    half = shard.shape[0] // 2
    left = lax.ppermute(left[:half], "seq", ahead)
    right = lax.ppermute(right[half:], "seq", back)
    full = put(full, left, -(count // 2))
    full = put(full, right, count // 2, half)
    return full


def ring_scatter(term):
    count = lax.axis_size("seq")
    if count != 8:
        return lax.psum_scatter(term, "seq", scatter_dimension=0, tiled=True).astype(F32)
    order, ahead, back = ring_maps(count)
    place = jnp.asarray(np.argsort(order), jnp.int32)[lax.axis_index("seq")]
    owners = jnp.asarray(order, jnp.int32)
    rows = term.shape[0] // count
    half = rows // 2

    def mine(step, lo):
        owner = owners[(place + step + 2 * count) % count]
        return lax.dynamic_slice_in_dim(term, owner * rows + lo, half, 0)

    left, right = mine(-1, 0), mine(1, half)
    for step in range(2, count + 1):
        left = lax.ppermute(left, "seq", ahead).astype(F32) + mine(-step, 0).astype(F32)
        right = lax.ppermute(right, "seq", back).astype(F32) + mine(step, half).astype(F32)
        if step < count:
            left, right = left.astype(B16), right.astype(B16)
    return jnp.concatenate([left, right], axis=0)


def halve_scatter(term):
    count = lax.axis_size("seq")
    bits = count.bit_length() - 1
    seq = lax.axis_index("seq")
    rows = term.shape[0] // count
    half = rows // 2
    split = term.reshape((2,) * bits + (2, half, term.shape[1]))
    results = []
    for part, order in enumerate(([0] + list(range(bits - 1, 0, -1)), list(range(bits - 1, -1, -1)))):
        value = lax.index_in_dim(split, part, bits, keepdims=False)
        left = list(range(bits - 1, -1, -1))
        for bit in order:
            at = left.index(bit)
            on = (seq >> bit) & 1
            keep = lax.dynamic_index_in_dim(value, on, at, keepdims=False)
            give = lax.dynamic_index_in_dim(value, 1 - on, at, keepdims=False)
            value = keep.astype(F32) + swap(give, "seq", 1 << bit).astype(F32)
            left.remove(bit)
            if left:
                value = value.astype(B16)
        results.append(value)
    return jnp.concatenate(results, axis=0)


def spread_gather(shard):
    count = lax.axis_size("seq")
    copies = jnp.broadcast_to(shard[None], (count,) + shard.shape)
    full = lax.all_to_all(copies, "seq", 0, 0, tiled=True)
    return full.reshape((count * shard.shape[0],) + shard.shape[1:])


def shift_seq(values, step):
    count = lax.axis_size("seq")
    return lax.ppermute(values, "seq", [(i, (i + step) % count) for i in range(count)])


def unmix(values, axis, index):
    size, bit = values.shape[axis], 1
    while bit < size:
        cut = values.shape[:axis] + (size // (2 * bit), 2, bit) + values.shape[axis + 1 :]
        split = values.reshape(cut)
        values = jnp.where((index // bit) % 2 == 1, jnp.flip(split, axis + 1), split).reshape(values.shape)
        bit *= 2
    return values


def sync_small(total, group, own):
    n_seq, n_rep = lax.axis_size("seq"), lax.axis_size("rep")
    group_list, own_list = [group], [own]
    for axis_name, size in (("seq", n_seq), ("rep", n_rep)):
        bit = 1
        while bit < size:
            parts = [total] + group_list + own_list
            sizes = np.cumsum([0] + [p.shape[0] for p in parts])
            came = swap(jnp.concatenate(parts, axis=0), axis_name, bit)
            came = [came[a:b] for a, b in zip(sizes[:-1], sizes[1:])]
            total = total + came[0]
            count = len(group_list)
            if axis_name == "seq":
                group_list = [group_list[0] + came[1]]
            else:
                group_list = group_list + came[1 : 1 + count]
            own_list = own_list + came[1 + count :]
            bit *= 2
    groups = unmix(jnp.stack(group_list), 0, lax.axis_index("rep"))
    owns = jnp.stack(own_list).reshape((n_rep, n_seq) + own.shape)
    owns = unmix(unmix(owns, 0, lax.axis_index("rep")), 1, lax.axis_index("seq"))
    return total, groups, owns


def layer_norm(rows, gain, shift):
    row_mean = jnp.mean(rows, axis=-1, keepdims=True)
    centred = rows - row_mean
    variance = jnp.mean(centred * centred, axis=-1, keepdims=True)
    inverse = lax.rsqrt(variance + EPS)
    normed = centred * inverse
    return (normed * gain + shift, normed, inverse)


def norm_back(grad_rows, normed, inverse, gain):
    scaled = grad_rows * gain
    mean_one = jnp.mean(scaled, axis=-1, keepdims=True)
    mean_two = jnp.mean(scaled * normed, axis=-1, keepdims=True)
    grad_in = inverse * (scaled - mean_one - normed * mean_two)
    return (grad_in, jnp.sum(grad_rows * normed, axis=0), jnp.sum(grad_rows, axis=0))


def features(length, feat_count):
    ramp_unit = jnp.linspace(0.0, 1.0, length, dtype=F32)
    angles = jnp.arange(length, dtype=F32)[:, None] * (2.0 * math.pi / length)
    band_freqs = jnp.linspace(
        0.0001, (feat_count - 1) // 2 - 1.0, (feat_count - 1) // 2, dtype=F32
    )[None, :]
    phase_grid = band_freqs * angles
    grid_out = jnp.concatenate(
        [ramp_unit[:, None], jnp.cos(phase_grid), -jnp.sin(phase_grid)], axis=1
    )
    return (grid_out, ramp_unit)


def filter_columns(
    feature_grid,
    ramp_unit,
    start_chan,
    chan_count,
    model_width,
    feat_weight,
    feat_bias,
    inner_weight,
    inner_bias,
    deep_weight,
    deep_bias,
    sine_freq,
    columns,
):
    freq = sine_freq[:, None]

    def layer(weight, bias, below):
        grown = lax.dot_general(weight, below, (((0,), (0,)), ((), ())), precision=HIGH)
        return jnp.sin(freq * (grown + bias[:, None]))

    hidden = layer(feat_weight, feat_bias, feature_grid.T)
    hidden = layer(inner_weight, inner_bias, hidden)
    hidden = layer(deep_weight, deep_bias, hidden)
    deltas = jnp.abs(
        jnp.linspace(math.log(0.01) / 0.3, math.log(0.01) / 1.5, model_width, dtype=F32)
    )
    local_rates = lax.dynamic_slice_in_dim(deltas, start_chan, chan_count)
    return lax.dot_general(
        columns, hidden, (((0,), (0,)), ((), ())), precision=HIGH
    ) * jnp.exp(-ramp_unit[None, :] * local_rates[:, None])


def sin_cos(x):
    turns = jnp.floor(x * (1.0 / math.pi) + 0.5)
    r = x - turns * 3.140625
    r = r - turns * 9.67502593994140625e-4
    r = r - turns * 1.509957990978376432e-7
    sign = 1.0 - 2.0 * (turns - 2.0 * jnp.floor(turns * 0.5))
    q = r * r
    sin = r + r * q * (
        -1.6666666666e-1
        + q * (8.3333333e-3 + q * (-1.98412698e-4 + q * (2.7557319e-6 + q * -2.505210838e-8)))
    )
    cos = 1.0 + q * (
        -0.5
        + q * (4.16666666e-2 + q * (-1.3888888e-3 + q * (2.48015873e-5 + q * (-2.75573192e-7 + q * 2.0876757e-9))))
    )
    return sin * sign, cos * sign


def dot_high(left, right, dims):
    return lax.dot_general(left, right, (dims, ((), ())), precision=HIGH, preferred_element_type=F32)


def filter_forward_kernel(
    grid_ref, ramp_ref, rate_ref, w1_ref, w2_ref, w3_ref, small_ref, columns_ref, twist_ref, hi_ref, lo_ref,
    spec_ref, sin_ref, cos_ref, z_ref
):
    blocks, length = twist_ref.shape[0], twist_ref.shape[3]
    freq = small_ref[:, 3:4]
    below = grid_ref[...]
    for i, w_ref in enumerate((w1_ref, w2_ref, w3_ref)):
        grown = dot_high(w_ref[...].T, below, ((1,), (0,)))
        sin, cos = sin_cos(freq * (grown + small_ref[:, i : i + 1]))
        sin_ref[i] = sin
        cos_ref[i] = cos
        below = sin
    kern = dot_high(columns_ref[...].T, below, ((1,), (0,))) * jnp.exp(-rate_ref[...] * ramp_ref[...])
    cut = [kern[:, b * length : (b + 1) * length] for b in range(blocks)]
    turn_rows(cut, twist_ref, z_ref, 0, blocks)
    spec_ref[...] = dot_split(z_ref[...], hi_ref[...], lo_ref[...], ((1,), (0,)))


def filter_backward_kernel(
    gk_ref, grid_ref, ramp_ref, rate_ref, w1_ref, w2_ref, w3_ref, small_ref, columns_ref, sin_ref, cos_ref,
    gc_ref, g1_ref, g2_ref, g3_ref, gsmall_ref
):
    freq = small_ref[:, 3:4]
    gk = jnp.concatenate([gk_ref[b] for b in range(gk_ref.shape[0])], axis=1)
    gk = gk * jnp.exp(-rate_ref[...] * ramp_ref[...])
    last = ((1,), (1,))
    gc_ref[...] = dot_high(sin_ref[2], gk, last)
    grad = dot_high(columns_ref[...], gk, ((1,), (0,)))
    gfreq = jnp.zeros(freq.shape, F32)
    gbias = [None] * 3
    for i, w_ref, g_ref in ((2, w3_ref, g3_ref), (1, w2_ref, g2_ref), (0, w1_ref, g1_ref)):
        turn = grad * cos_ref[i]
        below = sin_ref[i - 1] if i else grid_ref[...]
        raw = dot_high(turn, below, last)
        total = jnp.sum(turn, axis=1, keepdims=True)
        g_ref[...] = raw * freq
        gbias[i] = total * freq
        gfreq = gfreq + jnp.sum(raw * w_ref[...].T, axis=1, keepdims=True) + total * small_ref[:, i : i + 1]
        if i:
            grad = dot_high(w_ref[...], turn * freq, ((1,), (0,)))
    gsmall_ref[...] = jnp.concatenate(gbias + [gfreq], axis=1)


def feature_table(length, feat_count):
    ramp = np.linspace(0.0, 1.0, length, dtype=np.float32)
    angles = np.arange(length, dtype=np.float32)[:, None] * np.float32(2.0 * math.pi / length)
    half = (feat_count - 1) // 2
    bands = np.linspace(0.0001, half - 1.0, half, dtype=np.float32)[None, :]
    phase = (bands * angles).astype(np.float64)
    table = np.concatenate([ramp[:, None], np.cos(phase), -np.sin(phase)], axis=1)
    return np.ascontiguousarray(table.T).astype(np.float32), ramp[None, :]


def decay_rates(model):
    return np.abs(
        np.linspace(math.log(0.01) / 0.3, math.log(0.01) / 1.5, model, dtype=np.float32)
    )[:, None]


def transform_tables(blocks, length):
    time = np.arange(blocks * length).reshape(blocks, 1, length)
    cls = np.arange(blocks).reshape(1, blocks, 1)
    period = 4 * blocks * length
    turn = (time * (2 * cls + 1)) % period * (2.0 * np.pi / period)
    twist = np.stack([np.cos(turn), -np.sin(turn)], axis=2).astype(np.float32)
    step = np.arange(length)
    turn = (step[:, None] * step[None, :]) % length * (2.0 * np.pi / length)
    cos, sin = np.cos(turn), np.sin(turn)
    table = np.block([[cos, -sin], [sin, cos]]).astype(np.float32)
    return twist, table


def split_table(table):
    hi = table.astype(B16)
    return jnp.asarray(hi), jnp.asarray((table - hi.astype(np.float32)).astype(B16))


def spectrum_of(signal, twist, table):
    turned = jnp.einsum("bqzl,brl->qrzl", twist[: signal.shape[0]], signal, precision=HIGH)
    flat = turned.reshape(turned.shape[:2] + (-1,))
    return jnp.einsum("qrk,kf->qrf", flat, table, precision=HIGH)


def signal_of(spectrum, twist, table):
    blocks, length = twist.shape[0], twist.shape[3]
    turned = jnp.einsum("qrf,kf->qrk", spectrum, table, precision=HIGH)
    turned = turned.reshape(turned.shape[:2] + (2, length))
    return jnp.einsum("bqzl,qrzl->brl", twist, turned, precision=HIGH) * (1.0 / (blocks * length))


def times(left, right, conj_right):
    half = left.shape[-1] // 2
    lr, li = left[..., :half], left[..., half:]
    rr, ri = right[..., :half], right[..., half:]
    if conj_right:
        return jnp.concatenate([lr * rr + li * ri, li * rr - lr * ri], axis=-1)
    return jnp.concatenate([lr * rr - li * ri, lr * ri + li * rr], axis=-1)


def dot_split(values, hi, lo, dims):
    top = values.astype(B16)
    rest = (values - top.astype(F32)).astype(B16)
    dot = partial(lax.dot_general, dimension_numbers=(dims, ((), ())), preferred_element_type=F32)
    return dot(top, hi) + dot(rest, hi) + dot(top, lo)


def turn_rows(blocks_in, twist_ref, z_ref, base, classes):
    rows, length = blocks_in[0].shape
    for q in range(classes):
        for z in range(2):
            acc = None
            for b, block in enumerate(blocks_in):
                term = block * twist_ref[b, q, z : z + 1]
                acc = term if acc is None else acc + term
            z_ref[base + q * rows : base + (q + 1) * rows, z * length : (z + 1) * length] = acc


def back_rows(w, base, rows, block, twist_ref, classes):
    length = w.shape[1] // 2
    acc = None
    for q in range(classes):
        lo, hi = base + q * rows, base + (q + 1) * rows
        for z in range(2):
            term = w[lo:hi, z * length : (z + 1) * length] * twist_ref[block, q, z : z + 1]
            acc = term if acc is None else acc + term
    return acc * (1.0 / (classes * length))


def conv_forward_kernel(short_blocks, x_ref, kern_ref, twist_ref, hi_ref, lo_ref, skip_ref, out_ref, spec_ref, z_ref):
    blocks = twist_ref.shape[0]
    rows = x_ref.shape[1]
    span = blocks * rows
    first = [x_ref[b].astype(F32) for b in range(blocks)]
    second = [x_ref[blocks + b].astype(F32) for b in range(short_blocks)]
    turn_rows(first, twist_ref, z_ref, 0, blocks)
    turn_rows(second, twist_ref, z_ref, span, blocks)
    spec = dot_split(z_ref[...], hi_ref[...], lo_ref[...], ((1,), (0,)))
    spec_ref[...] = spec
    kern = kern_ref[...]
    prod = jnp.concatenate([times(spec[:span], kern, False), times(spec[span:], kern, False)], axis=0)
    w = dot_split(prod, hi_ref[...], lo_ref[...], ((1,), (1,)))
    skip = skip_ref[...]
    for b in range(blocks):
        out_ref[b] = (back_rows(w, 0, rows, b, twist_ref, blocks) + skip * first[b]).astype(B16)
        acc = back_rows(w, span, rows, b, twist_ref, blocks)
        if b < short_blocks:
            acc = acc + skip * second[b]
        out_ref[blocks + b] = acc.astype(B16)


def conv_backward_kernel(
    short_blocks, g_ref, spec_ref, kern_ref, twist_ref, hi_ref, lo_ref, skip_ref, out_ref, grad_kern_ref, z_ref, p_ref
):
    blocks = twist_ref.shape[0]
    rows = g_ref.shape[1]
    span = blocks * rows
    first = [g_ref[b].astype(F32) for b in range(blocks)]
    second = [g_ref[blocks + b].astype(F32) for b in range(short_blocks)]
    turn_rows(first, twist_ref, z_ref, 0, blocks)
    turn_rows(second, twist_ref, z_ref, span, blocks)
    grad = dot_split(z_ref[...], hi_ref[...], lo_ref[...], ((1,), (0,)))
    kern = kern_ref[...]
    p_ref[0:span] = times(grad[:span], kern, True)
    p_ref[span : 2 * span] = times(grad[span:], kern, True)
    p_ref[2 * span :] = times(grad[:span], spec_ref[0:span], True) + times(
        grad[span:], spec_ref[span:], True
    )
    w = dot_split(p_ref[...], hi_ref[...], lo_ref[...], ((1,), (1,)))
    skip = skip_ref[...]
    for b in range(blocks):
        out_ref[b] = (back_rows(w, 0, rows, b, twist_ref, blocks) + skip * first[b]).astype(B16)
        if b < short_blocks:
            acc = back_rows(w, span, rows, b, twist_ref, blocks) + skip * second[b]
            out_ref[blocks + b] = acc.astype(B16)
        else:
            out_ref[blocks + b] = jnp.zeros(out_ref.shape[1:], B16)
        grad_kern_ref[b] = back_rows(w, 2 * span, rows, b, twist_ref, blocks)


def conv_forward(received, kern_spec, twist, table, skip_local):
    blocks, rows, length = received.shape[0] // 2, received.shape[1], received.shape[2]
    short_blocks = -(-blocks // 4)
    skip = skip_local[:, None]
    if blocks != 4:
        x = received.astype(F32)
        spec = jnp.concatenate(
            [
                spectrum_of(x[:blocks], twist, table),
                spectrum_of(x[blocks : blocks + short_blocks], twist, table),
            ],
            axis=0,
        )
        kern = jnp.concatenate([kern_spec, kern_spec], axis=0)
        prod = times(spec, kern, False)
        out = jnp.concatenate(
            [signal_of(prod[:blocks], twist, table), signal_of(prod[blocks:], twist, table)], axis=0
        )
        return ((out + skip * x).astype(B16), spec)
    hi, lo = split_table(table)
    height = 2 * blocks * rows
    out, spec = pl.pallas_call(
        partial(conv_forward_kernel, short_blocks),
        out_shape=(
            jax.ShapeDtypeStruct(received.shape, B16),
            jax.ShapeDtypeStruct((height, 2 * length), F32),
        ),
        scratch_shapes=[pltpu.VMEM((height, 2 * length), F32)],
        compiler_params=pltpu.CompilerParams(vmem_limit_bytes=VMEM_BYTES),
        name="conv_forward",
    )(received, kern_spec.reshape(blocks * rows, 2 * length), twist, hi, lo, skip)
    return out, spec


def conv_backward(grads, spec, kern_spec, twist, table, skip_local):
    blocks, rows, length = grads.shape[0] // 2, grads.shape[1], grads.shape[2]
    short_blocks = -(-blocks // 4)
    skip = skip_local[:, None]
    if blocks != 4:
        g = grads.astype(F32)
        first = spectrum_of(g[:blocks], twist, table)
        second = spectrum_of(g[blocks : blocks + short_blocks], twist, table)
        one = signal_of(times(first, kern_spec, True), twist, table)
        two = signal_of(times(second, kern_spec, True), twist, table)
        cross = times(first, spec[:blocks], True) + times(second, spec[blocks:], True)
        out = jnp.concatenate([one, two], axis=0) + skip * g
        return (out.astype(B16), signal_of(cross, twist, table))
    hi, lo = split_table(table)
    span = blocks * rows
    out, grad_kern = pl.pallas_call(
        partial(conv_backward_kernel, short_blocks),
        out_shape=(
            jax.ShapeDtypeStruct(grads.shape, B16),
            jax.ShapeDtypeStruct((blocks, rows, length), F32),
        ),
        scratch_shapes=[
            pltpu.VMEM((2 * span, 2 * length), F32),
            pltpu.VMEM((3 * span, 2 * length), F32),
        ],
        compiler_params=pltpu.CompilerParams(vmem_limit_bytes=VMEM_BYTES),
        name="conv_backward",
    )(grads, spec, kern_spec.reshape(span, 2 * length), twist, hi, lo, skip)
    return out, grad_kern


def in_order(ref, rep, lead=()):
    count = ref.shape[-1] // LANE
    return [
        ref[lead + (slice(None), pl.ds(pl.multiple_of((rep ^ j) * LANE, LANE), LANE))]
        for j in range(count)
    ]


def put_rel(ref, rep, values, lead=()):
    for j in range(ref.shape[-1] // LANE):
        ref[lead + (slice(None), pl.ds(pl.multiple_of((rep ^ j) * LANE, LANE), LANE))] = values[
            :, j * LANE : (j + 1) * LANE
        ]


def extended(proj_ref, halo_ref, exists, rep, p):
    blocks = [halo_ref[p, :, :LANE]] + in_order(proj_ref, rep, (p,)) + [halo_ref[p, :, LANE:]]
    return jnp.concatenate(blocks, axis=1).astype(F32) * exists


def short_of(ext, col_ref, p):
    return (
        col_ref[:, p : p + 1] * pltpu.roll(ext, 2, 1)
        + col_ref[:, 3 + p : 4 + p] * pltpu.roll(ext, 1, 1)
        + col_ref[:, 6 + p : 7 + p] * ext
        + col_ref[:, 9 + p : 10 + p]
    )


def gate_kernel(rep_ref, proj_ref, halo_ref, col_ref, mask_ref, out_ref):
    rep = rep_ref[0]
    mask, exists = mask_ref[0:1], mask_ref[1:2]
    gate_in = short_of(extended(proj_ref, halo_ref, exists, rep, 1), col_ref, 1)
    values = short_of(extended(proj_ref, halo_ref, exists, rep, 2), col_ref, 2)
    gated = values * gate_in * mask
    out_ref[...] = gated[:, LANE:-LANE].astype(B16)


def output_kernel(rep_ref, proj_ref, halo_ref, col_ref, mask_ref, mixed_ref, out_ref):
    rep = rep_ref[0]
    gate_out = short_of(extended(proj_ref, halo_ref, mask_ref[1:2], rep, 0), col_ref, 0)
    put_rel(out_ref, rep, (gate_out[:, LANE:-LANE] * mixed_ref[...].astype(F32)).astype(B16))


def grad_mix_kernel(rep_ref, proj_ref, halo_ref, col_ref, mask_ref, mixed_ref, gy_ref, out_ref, first_ref):
    rep = rep_ref[0]
    gate_out = short_of(extended(proj_ref, halo_ref, mask_ref[1:2], rep, 0), col_ref, 0)
    gy = jnp.concatenate(in_order(gy_ref, rep), axis=1).astype(F32)
    out_ref[...] = (gy * gate_out[:, LANE:-LANE]).astype(B16)
    first_ref[...] = gy[:, :LANE] * mixed_ref[:, :LANE].astype(F32)


def grad_proj_kernel(
    rep_ref, proj_ref, halo_ref, col_ref, mask_ref, mixed_ref, gy_ref, ggated_ref, gnext_ref, onext_ref, out_ref, sum_ref
):
    rep = rep_ref[0]
    mask, exists = mask_ref[0:1], mask_ref[1:2]
    size = mask_ref.shape[1]
    mid = slice(LANE, size - LANE)
    gy = jnp.concatenate(in_order(gy_ref, rep), axis=1).astype(F32)
    zero = jnp.zeros((gy.shape[0], LANE), F32)
    next_on = exists[:, size - LANE :]
    ext = [extended(proj_ref, halo_ref, exists, rep, p) for p in range(3)]
    short = [short_of(ext[p], col_ref, p) for p in range(3)]
    ggated = jnp.concatenate(
        [zero, ggated_ref[...].astype(F32), gnext_ref[...].astype(F32) * next_on], axis=1
    )
    ggated = ggated * mask
    gout = gy * mixed_ref[...].astype(F32)
    gshort = [
        jnp.concatenate([zero, gout, onext_ref[...] * next_on], axis=1),
        ggated * short[2],
        ggated * short[1],
    ]
    gated = short[2][:, mid] * short[1][:, mid] * mask[:, mid]
    sums = [jnp.sum(gy * short[0][:, mid] * gated, axis=1, keepdims=True)]
    for p in range(3):
        mine = gshort[p][:, mid]
        sums.append(jnp.sum(mine, axis=1, keepdims=True))
        sums.append(jnp.sum(mine * ext[p][:, mid], axis=1, keepdims=True))
        sums.append(jnp.sum(mine * pltpu.roll(ext[p], 1, 1)[:, mid], axis=1, keepdims=True))
        sums.append(jnp.sum(mine * pltpu.roll(ext[p], 2, 1)[:, mid], axis=1, keepdims=True))
        gproj = (
            col_ref[:, 6 + p : 7 + p] * gshort[p]
            + col_ref[:, 3 + p : 4 + p] * pltpu.roll(gshort[p], size - 1, 1)
            + col_ref[:, p : p + 1] * pltpu.roll(gshort[p], size - 2, 1)
        )[:, mid].astype(B16)
        sums.append(jnp.sum(gproj.astype(F32), axis=1, keepdims=True))
        put_rel(out_ref, rep, gproj, (p,))
    sum_ref[...] = jnp.concatenate(sums, axis=1)


def token_call(kernel, name, arrays, outs):
    step = 64

    def spec(shape, cut):
        if not cut:
            return pl.BlockSpec(shape, lambda i: (0,) * len(shape))
        if len(shape) == 3:
            return pl.BlockSpec((shape[0], step, shape[2]), lambda i: (0, i, 0))
        return pl.BlockSpec((step, shape[1]), lambda i: (i, 0))

    width = outs[0].shape[-2]
    return pl.pallas_call(
        kernel,
        grid=(width // step,),
        in_specs=[pl.BlockSpec(memory_space=pltpu.SMEM)] + [spec(a.shape, cut) for a, cut in arrays[1:]],
        out_specs=[spec(o.shape, True) for o in outs],
        out_shape=outs,
        compiler_params=pltpu.CompilerParams(vmem_limit_bytes=VMEM_BYTES),
        name=name,
    )(*[a for a, _ in arrays])


def rows128(values):
    flat = values.reshape(-1)
    return jnp.pad(flat, (0, -flat.shape[0] % 1024)).reshape(-1, 128)


def per_device(
    tokens,
    cotangent,
    lengths,
    in_weight,
    in_bias,
    short_taps,
    short_bias,
    feat_weight,
    feat_bias,
    inner_weight,
    inner_bias,
    deep_weight,
    deep_bias,
    sine_freq,
    kernel_weight,
    skip_gain,
    out_weight,
    out_bias,
    norm1_gain,
    norm1_shift,
    norm2_gain,
    norm2_shift,
    up_weight,
    up_bias,
    down_weight,
    down_bias,
):
    n_seq, n_rep = lax.axis_size("seq"), lax.axis_size("rep")
    seq, rep = lax.axis_index("seq"), lax.axis_index("rep")
    tok_rows, model = tokens.shape
    group = tok_rows * n_rep
    blocks = n_seq // 2
    seq_len = blocks * group
    chan = model // (n_seq * n_rep)
    width = model // n_rep
    hidden = up_weight.shape[2]
    block_start = rep * width
    chan_start = block_start + seq * chan
    rep_scalar = jnp.reshape(rep, (1,)).astype(jnp.int32)

    item_len = jnp.where(seq // blocks == 0, lengths[0], lengths[1])
    at = (seq % blocks) * group
    row_mask = (at + rep * tok_rows + jnp.arange(tok_rows, dtype=jnp.int32) < item_len).astype(F32)[:, None]
    position = at - LANE + jnp.arange(group + 2 * LANE, dtype=jnp.int32)
    mask_ext = jnp.stack([position < item_len, (position >= 0) & (position < seq_len)]).astype(F32)
    mask_ext = jnp.pad(mask_ext, ((0, 6), (0, 0)))

    full_in = ring_gather(in_weight[0]).reshape(model, 3, width)
    full_out = spread_gather(out_weight[0])
    full_up = lax.all_gather(up_weight[0], "seq", axis=0, tiled=True)
    full_down = lax.all_gather(down_weight[0], "seq", axis=0, tiled=True)

    residual = tokens.astype(F32)
    normed_one, unit_one, scale_one = layer_norm(residual, norm1_gain[0], norm1_shift[0])
    normed_one = normed_one.astype(B16)
    rows_one = gather_rel(normed_one)
    rel = rows_one.reshape(n_rep, tok_rows, model)
    last_rows = lax.dynamic_index_in_dim(rel, rep ^ (n_rep - 1), 0, False)[-HALO:]
    first_rows = lax.dynamic_index_in_dim(rel, rep, 0, False)[:HALO]
    before = shift_seq(last_rows, 1)
    after = shift_seq(first_rows, -1)
    gap = jnp.zeros((LANE - HALO, model), B16)
    halo_rows = jnp.concatenate([gap, before, after, gap], axis=0)
    proj_bias = lax.dynamic_slice_in_dim(in_bias[0], block_start, width, 1)[:, :, None]

    def project(rows):
        return (
            jnp.einsum("td,dpc->pct", rows, full_in, preferred_element_type=F32) + proj_bias
        ).astype(B16)

    proj = project(rows_one)
    halo = project(halo_rows)

    tap_cols = lax.dynamic_slice_in_dim(short_taps[0], block_start, width, 2).reshape(9, width)
    bias_cols = lax.dynamic_slice_in_dim(short_bias[0], block_start, width, 1)
    cols = jnp.pad(jnp.concatenate([tap_cols, bias_cols], axis=0), ((0, 4), (0, 0))).T
    common = [(rep_scalar, True), (proj, True), (halo, True), (cols, True), (mask_ext, False)]
    flat_shape = jax.ShapeDtypeStruct((width, group), B16)
    (gated,) = token_call(gate_kernel, "gate", common, [flat_shape])
    received = lax.all_to_all(gated.reshape(n_seq, chan, group), "seq", 0, 0, tiled=True)

    skip_local = lax.dynamic_slice_in_dim(skip_gain[0], chan_start, chan, 0)
    columns = lax.dynamic_slice_in_dim(kernel_weight[0], chan_start, chan, 1)
    twist, table = transform_tables(blocks, group)
    nets = (feat_weight[0], inner_weight[0], deep_weight[0])
    if blocks == 4:
        grid, ramp = feature_table(seq_len, feat_weight.shape[1])
        rates = lax.dynamic_slice_in_dim(jnp.asarray(decay_rates(model)), chan_start, chan, 0)
        smalls = jnp.concatenate([feat_bias, inner_bias, deep_bias, sine_freq], axis=0).T
        filt = smalls.shape[0]
        hi, lo = split_table(table)
        kern_spec, sines, cosines = pl.pallas_call(
            filter_forward_kernel,
            out_shape=(
                jax.ShapeDtypeStruct((blocks * chan, 2 * group), F32),
                jax.ShapeDtypeStruct((3, filt, seq_len), F32),
                jax.ShapeDtypeStruct((3, filt, seq_len), F32),
            ),
            scratch_shapes=[pltpu.VMEM((blocks * chan, 2 * group), F32)],
            compiler_params=pltpu.CompilerParams(vmem_limit_bytes=VMEM_BYTES),
            cost_estimate=pl.CostEstimate(flops=10**6, bytes_accessed=10**6, transcendentals=0),
            name="filter_forward",
        )(grid, ramp, rates, *nets, smalls, columns, twist, hi, lo)
        kern_spec = kern_spec.reshape(blocks, chan, 2 * group)

        def kernel_pull(grad_kernel):
            shapes = [columns.shape] + [w.shape[::-1] for w in nets] + [smalls.shape]
            gcols, g1, g2, g3, gsmalls = pl.pallas_call(
                filter_backward_kernel,
                out_shape=tuple(jax.ShapeDtypeStruct(shape, F32) for shape in shapes),
                compiler_params=pltpu.CompilerParams(vmem_limit_bytes=VMEM_BYTES),
                cost_estimate=pl.CostEstimate(flops=10**6, bytes_accessed=10**6, transcendentals=0),
                name="filter_backward",
            )(grad_kernel, grid, ramp, rates, *nets, smalls, columns, sines, cosines)
            gs = gsmalls.T
            return (g1.T, gs[0], g2.T, gs[1], g3.T, gs[2], gs[3], gcols)

    else:
        feature_grid, ramp_unit = features(seq_len, feat_weight.shape[1])
        kernel, pull = jax.vjp(
            partial(filter_columns, feature_grid, ramp_unit, chan_start, chan, model),
            feat_weight[0],
            feat_bias[0],
            inner_weight[0],
            inner_bias[0],
            deep_weight[0],
            deep_bias[0],
            sine_freq[0],
            columns,
        )
        kern_spec = spectrum_of(kernel.reshape(chan, blocks, group).transpose(1, 0, 2), twist, table)

        def kernel_pull(grad_kernel):
            return pull(grad_kernel.transpose(1, 0, 2).reshape(chan, seq_len))

    mixed_chan, kept_spec = conv_forward(received, kern_spec, twist, table, skip_local)
    mixed = lax.all_to_all(mixed_chan, "seq", 0, 0, tiled=True).reshape(width, group)
    (y_cols,) = token_call(output_kernel, "output", common + [(mixed, True)], [flat_shape])

    middle_part = jnp.einsum("ct,oc->to", y_cols, full_out, preferred_element_type=F32)
    middle = residual + (scatter_rel(middle_part) + out_bias[0])
    normed_two, unit_two, scale_two = layer_norm(middle, norm2_gain[0], norm2_shift[0])
    rows_two = gather_rel(normed_two.astype(B16))

    grad_top = cotangent.astype(F32) * row_mask
    grad_mlp = grad_top.astype(B16)
    mlp_rows = gather_rel(grad_mlp)
    grad_act = jnp.dot(mlp_rows, full_down, preferred_element_type=F32)
    up_block = lax.dynamic_slice_in_dim(up_bias[0], rep * hidden, hidden, 0)
    pre_act = jnp.dot(rows_two, full_up, preferred_element_type=F32) + up_block
    phi = 0.5 * (1.0 + lax.erf(pre_act * math.sqrt(0.5)))
    act_rows = (pre_act * phi).astype(B16)
    slope = phi + pre_act * (jnp.exp(-0.5 * pre_act * pre_act) * (1.0 / math.sqrt(2.0 * math.pi)))
    grad_pre = (grad_act * slope).astype(B16)
    grad_two = scatter_rel(jnp.einsum("tf,df->td", grad_pre, full_up, preferred_element_type=F32))
    mlp_part = jnp.einsum("tf,of->to", act_rows, full_down, preferred_element_type=F32)
    layer_out = (middle + (scatter_rel(mlp_part) + down_bias[0])).astype(B16)
    term_down = jnp.einsum("to,tf->of", mlp_rows, act_rows, preferred_element_type=F32)
    term_up = jnp.einsum("td,tf->df", rows_two, grad_pre, preferred_element_type=F32)
    grad_two, term_down = lax.optimization_barrier((grad_two, term_down.astype(B16)))
    grad_down_bias = jnp.sum(grad_mlp.astype(F32), axis=0)
    grad_up_block = jnp.sum(grad_pre.astype(F32), axis=0)

    grad_down = lax.psum_scatter(
        term_down, "seq", scatter_dimension=0, tiled=True
    ).astype(F32)
    grad_up = ring_scatter(term_up.astype(B16))

    grad_unit_two, grad_gain_two, grad_shift_two = norm_back(
        grad_two, unit_two, scale_two, norm2_gain[0]
    )
    grad_middle = grad_top + grad_unit_two
    grad_mix = grad_middle.astype(B16)
    grad_out_bias = jnp.sum(grad_mix.astype(F32), axis=0)
    mix_rows = gather_rel(grad_mix)
    gy_cols = jnp.einsum("to,oc->ct", mix_rows, full_out, preferred_element_type=F32).astype(B16)
    term_out = jnp.einsum("to,ct->oc", mix_rows, y_cols, preferred_element_type=F32)
    grad_out = halve_scatter(term_out.astype(B16))

    grad_mixed, gate_first = token_call(
        grad_mix_kernel,
        "grad_mix",
        common + [(mixed, True), (gy_cols, True)],
        [flat_shape, jax.ShapeDtypeStruct((width, LANE), F32)],
    )
    gate_next = shift_seq(gate_first, -1)
    grads_chan = lax.all_to_all(grad_mixed.reshape(n_seq, chan, group), "seq", 0, 0, tiled=True)
    ggated_chan, grad_kernel = conv_backward(grads_chan, kept_spec, kern_spec, twist, table, skip_local)
    ggated = lax.all_to_all(ggated_chan, "seq", 0, 0, tiled=True).reshape(width, group)
    ggated_next = shift_seq(ggated[:, :LANE], -1)
    kernel_grads = kernel_pull(grad_kernel)
    grad_proj, col_sums = token_call(
        grad_proj_kernel,
        "grad_proj",
        common
        + [(mixed, True), (gy_cols, True), (ggated, True), (ggated_next, True), (gate_next, True)],
        [jax.ShapeDtypeStruct((3, width, group), B16), jax.ShapeDtypeStruct((width, 16), F32)],
    )

    one_part = jnp.einsum("pct,dpc->td", grad_proj, full_in, preferred_element_type=F32)
    grad_one = scatter_rel(one_part)
    term_in = jnp.einsum("td,pct->dpc", rows_one, grad_proj, preferred_element_type=F32)
    grad_in = halve_scatter(term_in.reshape(model, 3 * width).astype(B16))
    grad_in = grad_in.reshape(-1, 3, width)
    grad_unit_one, grad_gain_one, grad_shift_one = norm_back(
        grad_one, unit_one, scale_one, norm1_gain[0]
    )
    grad_tokens = grad_middle + grad_unit_one

    totals = [
        *kernel_grads[:7],
        grad_gain_one,
        grad_shift_one,
        grad_gain_two,
        grad_shift_two,
        grad_out_bias,
        grad_down_bias,
    ]
    packed = [rows128(t) for t in totals]
    group_part = jnp.concatenate([rows128(col_sums.T), rows128(grad_up_block)], axis=0)
    total, groups, owns = sync_small(jnp.concatenate(packed, axis=0), group_part, rows128(kernel_grads[7]))
    outs = []
    start = 0
    for t, p in zip(totals, packed):
        outs.append(total[start : start + p.shape[0]].reshape(-1)[: t.size].reshape((1,) + t.shape))
        start += p.shape[0]
    flat = groups.reshape(n_rep, -1)
    sums = flat[:, : 16 * width].reshape(n_rep, 16, width).transpose(1, 0, 2).reshape(16, model)
    grad_up_bias = flat[:, 16 * width : 16 * width + hidden].reshape(1, -1)
    filt = columns.shape[0]
    grad_kernel_weight = (
        owns.reshape(n_rep, n_seq, -1)[:, :, : filt * chan]
        .reshape(n_rep, n_seq, filt, chan)
        .transpose(2, 0, 1, 3)
        .reshape(1, filt, model)
    )
    pick = lambda offset: jnp.stack([sums[1 + 5 * p + offset] for p in range(3)])
    grad_skip = sums[0][None]
    grad_short_bias = pick(0)[None]
    grad_short_taps = jnp.stack([pick(3), pick(2), pick(1)])[None]
    grad_in_bias = pick(4)[None]
    return (
        layer_out,
        grad_tokens,
        grad_in[None],
        grad_in_bias,
        grad_short_taps,
        grad_short_bias,
        outs[0],
        outs[1],
        outs[2],
        outs[3],
        outs[4],
        outs[5],
        outs[6],
        grad_kernel_weight,
        grad_skip,
        grad_out[None],
        outs[11],
        outs[7],
        outs[8],
        outs[9],
        outs[10],
        grad_up[None],
        grad_up_bias,
        grad_down[None],
        outs[12],
    )


NN = ((1,), (0,))
NT = ((1,), (1,))
TN = ((0,), (0,))
PART = 64
REP, SEQ, AT, ITEM, OLDER, YOUNGER, OWNER, LEFT, RIGHT = 0, 1, 2, 3, 4, 5, 8, 16, 25
RING = [0, 2, 4, 6, 7, 5, 3, 1]
AHEAD = [(RING[i], RING[(i + 1) % 8]) for i in range(8)]
BACK = [(b, a) for a, b in AHEAD]


def meta_table(group):
    rows = []
    for seq in range(8):
        p = RING.index(seq)
        for rep in range(4):
            row = [rep, seq, (seq % 4) * group, seq // 4, int(seq % 4 != 0), int(seq % 4 != 3), 0, 0]
            row += [RING[(p + k) % 8] for k in (0, -1, 1, -2, 2, -3, 3, 4)]
            row += [RING[(p - k) % 8] for k in range(9)]
            row += [RING[(p + k) % 8] for k in range(9)]
            rows.append(row)
    return np.asarray(rows, np.int32)


COST = {"start": 4000, "setup": 4000, "filter_ahead": 6000}


def call(kernel, name, args, outs, scratch=(), limit=24, away=(), out_away=(), raw=()):
    away, out_away, raw = list(away), list(out_away), list(raw)
    hbm = pl.BlockSpec(memory_space=pltpu.HBM)

    def space(i, a):
        if i in away or i in raw:
            return hbm
        small = a.dtype == jnp.int32
        return pl.BlockSpec(memory_space=pltpu.SMEM if small else pltpu.VMEM)

    n_in, n_out, n_own = len(args), len(outs), len(scratch)
    bufs = [pltpu.VMEM(args[i].shape, args[i].dtype) for i in away]
    bufs += [pltpu.VMEM(outs[i].shape, outs[i].dtype) for i in out_away]
    sems = [pltpu.SemaphoreType.DMA((len(bufs),))] if bufs else []

    def body(*refs):
        ins, results = list(refs[:n_in]), list(refs[n_in : n_in + n_out])
        own, mine = refs[n_in + n_out : n_in + n_out + n_own], refs[n_in + n_out + n_own :]
        copies = []
        for k, i in enumerate(away):
            copies.append(pltpu.make_async_copy(ins[i], mine[k], mine[-1].at[k]))
            ins[i] = mine[k]
        for copy in copies:
            copy.start()
        for copy in copies:
            copy.wait()
        copies = []
        for k, i in enumerate(out_away, len(away)):
            copies.append(pltpu.make_async_copy(mine[k], results[i], mine[-1].at[k]))
            results[i] = mine[k]
        kernel(*ins, *results, *own)
        for copy in copies:
            copy.start()
        for copy in copies:
            copy.wait()

    return pl.pallas_call(
        body,
        out_shape=outs,
        in_specs=[space(i, a) for i, a in enumerate(args)],
        out_specs=[hbm if i in out_away or (-1 - i) in raw else pl.BlockSpec(memory_space=pltpu.VMEM) for i in range(n_out)],
        scratch_shapes=list(scratch) + bufs + sems,
        compiler_params=pltpu.CompilerParams(vmem_limit_bytes=limit * 2**20),
        cost_estimate=pl.CostEstimate(flops=COST.get(name, 1) * 10**6, bytes_accessed=10**5, transcendentals=0),
        name=name,
    )(*args)


def shape(dims, kind):
    return jax.ShapeDtypeStruct(tuple(dims), kind)


def dot(left, right, dims):
    return lax.dot_general(left, right, (dims, ((), ())), preferred_element_type=F32)


def place(index):
    return pl.ds(pl.multiple_of(index * LANE, LANE), LANE)


def normed_of(rows):
    centred = rows - jnp.mean(rows, axis=1, keepdims=True)
    inverse = lax.rsqrt(jnp.mean(centred * centred, axis=1, keepdims=True) + EPS)
    return centred * inverse, inverse


def item_length(meta_ref, len_ref):
    return jnp.where(meta_ref[ITEM] == 0, len_ref[0], len_ref[1])


def lane_masks(meta_ref, len_ref, size):
    lane = lax.broadcasted_iota(jnp.int32, (1, size), 1)
    real = (meta_ref[AT] - LANE + lane < item_length(meta_ref, len_ref)).astype(F32)
    older, younger = meta_ref[OLDER].astype(F32), meta_ref[YOUNGER].astype(F32)
    exists = jnp.where(lane < LANE, older, jnp.where(lane >= size - LANE, younger, 1.0))
    return real, exists


def start_kernel(x_ref, gain_ref, shift_ref, in_ref, out_w_ref, out_ref, io_ref):
    width = out_w_ref.shape[2]
    for p in range(3):
        io_ref[:, p * width : (p + 1) * width] = in_ref[p]
    io_ref[:, 3 * width :] = out_w_ref[0]
    unit, _ = normed_of(x_ref[...].astype(F32))
    out_ref[...] = (unit * gain_ref[...] + shift_ref[...]).astype(B16)


def halves_kernel(left_ref, right_ref, a_ref, b_ref):
    half = a_ref.shape[0]
    a_ref[...] = left_ref[:half]
    b_ref[...] = right_ref[half:]


def assemble_kernel(meta_ref, p0, p1, p2, p3, p4, p5, p6, a_ref, b_ref, out_ref):
    for k, ref in enumerate((p0, p1, p2, p3, p4, p5, p6)):
        out_ref[meta_ref[OWNER + k]] = ref[...]
    half = a_ref.shape[0]
    out_ref[meta_ref[OWNER + 7], :half] = a_ref[...]
    out_ref[meta_ref[OWNER + 7], half:] = b_ref[...]


def own_mask(meta_ref, len_ref, rows):
    row = lax.broadcasted_iota(jnp.int32, (rows, 1), 0)
    return (meta_ref[AT] + meta_ref[REP] * rows + row < item_length(meta_ref, len_ref)).astype(F32)


def setup_kernel(
    meta_ref, len_ref, top_ref, up_ref, down_ref, taps_ref, short_bias_ref, in_bias_ref, up_bias_ref, skip_ref, rate_ref,
    kern_w_ref, feat_ref, fb_ref, ib_ref, db_ref, sf_ref,
    rows_ref, ud_ref, cols_ref, upb_ref, chan_ref, columns_ref, small_col_ref, small_row_ref, w1_ref, *rest
):
    sems = rest[-1]
    copies = [
        pltpu.make_async_copy(up_ref, ud_ref.at[pl.ds(0, 1)], sems.at[0]),
        pltpu.make_async_copy(down_ref, ud_ref.at[pl.ds(1, 1)], sems.at[1]),
    ]
    for copy in copies:
        copy.start()
    top, taps, short_bias, in_bias, up_bias, skip, rate, kern_w, feat, fb, ib, db, sf = (
        top_ref, taps_ref, short_bias_ref, in_bias_ref, up_bias_ref, skip_ref, rate_ref, kern_w_ref, feat_ref,
        fb_ref, ib_ref, db_ref, sf_ref,
    )
    mask = own_mask(meta_ref, len_ref, top.shape[0])
    rows_ref[...] = (top[...].astype(F32) * mask).astype(B16)
    width = cols_ref.shape[0]
    chan = chan_ref.shape[0]
    rep, seq = meta_ref[REP], meta_ref[SEQ]
    lanes = pl.ds(pl.multiple_of(rep * width, width), width)
    rows = [taps[j, p, :, lanes] for j in range(3) for p in range(3)]
    rows += [short_bias[p, :, lanes] for p in range(3)] + [in_bias[p, :, lanes] for p in range(3)]
    stack = jnp.concatenate(rows + [jnp.zeros((LANE - 15, width), F32)], axis=0)
    cols_ref[...] = stack.T[:, :16]
    upb_ref[...] = up_bias[:, pl.ds(pl.multiple_of(rep * upb_ref.shape[1], LANE), upb_ref.shape[1])]
    turn = width - seq * chan
    stack = jnp.concatenate([skip[:, lanes], rate[:, lanes], jnp.zeros((LANE - 2, width), F32)], axis=0)
    chan_ref[...] = pltpu.roll(stack, turn, 1)[:, :LANE].T[:chan, :2]
    columns_ref[...] = pltpu.roll(kern_w[0, :, lanes], turn, 1)[:, :chan]
    filt = small_row_ref.shape[1]
    small = jnp.concatenate([fb[...], ib[...], db[...], sf[...]], axis=0)
    small_row_ref[...] = small
    wide = jnp.concatenate([small, jnp.zeros((4, LANE - filt), F32)], axis=1)
    wide = jnp.concatenate([wide, jnp.zeros((LANE - 4, LANE), F32)], axis=0)
    small_col_ref[...] = wide.T[:filt, :4]
    w1_ref[...] = jnp.concatenate([feat[i] for i in range(feat.shape[0])], axis=0)
    for copy in copies:
        copy.wait()


def edges_kernel(meta_ref, x0, x1, x2, x3, last_ref, first_ref):
    rep = meta_ref[REP]
    refs = (x0, x1, x2, x3)

    def chosen(index, lo):
        value = refs[0][lo : lo + HALO]
        for i in range(1, 4):
            value = jnp.where(index == i, refs[i][lo : lo + HALO].astype(F32), value.astype(F32))
        return value.astype(B16)

    last_ref[...] = chosen(rep ^ 3, x0.shape[0] - HALO)
    first_ref[...] = chosen(rep, 0)


def ext_of(proj_ref, halo_ref, exists, p, rows):
    return (
        jnp.concatenate(
            [halo_ref[p, rows, :LANE], proj_ref[p, rows, :], halo_ref[p, rows, LANE:]], axis=1
        ).astype(F32)
        * exists
    )


def short_from(ext, cols, p):
    return (
        cols[:, p : p + 1] * pltpu.roll(ext, 2, 1)
        + cols[:, 3 + p : 4 + p] * pltpu.roll(ext, 1, 1)
        + cols[:, 6 + p : 7 + p] * ext
        + cols[:, 9 + p : 10 + p]
    )


def project_kernel(
    meta_ref, len_ref, x0, x1, x2, x3, before_ref, after_ref, cols_ref,
    p0, p1, p2, p3, p4, p5, p6, a_ref, b_ref, io_full_ref, proj_ref, halo_ref, gated_ref
):
    assemble_kernel(meta_ref, p0, p1, p2, p3, p4, p5, p6, a_ref, b_ref, io_full_ref)
    io_ref = io_full_ref.reshape(-1, io_full_ref.shape[2])
    rep = meta_ref[REP]
    width, group = gated_ref.shape
    weight = io_ref[:, : 3 * width]
    for i, x_ref in enumerate((x0, x1, x2, x3)):
        cut = dot(x_ref[...], weight, NN).T
        for p in range(3):
            proj_ref[p, :, place(rep ^ i)] = (
                cut[p * width : (p + 1) * width] + cols_ref[:, 12 + p : 13 + p]
            ).astype(B16)
    edge = dot(jnp.concatenate([before_ref[...], after_ref[...]], axis=0), weight, NN)
    gap = jnp.zeros((LANE - HALO, 3 * width), F32)
    edge = jnp.concatenate([gap, edge, gap], axis=0).T
    for p in range(3):
        halo_ref[p] = (edge[p * width : (p + 1) * width] + cols_ref[:, 12 + p : 13 + p]).astype(B16)
    mask, exists = lane_masks(meta_ref, len_ref, group + 2 * LANE)
    for lo in range(0, width, PART):
        rows = slice(lo, lo + PART)
        cols = cols_ref[rows, :]
        gate_in = short_from(ext_of(proj_ref, halo_ref, exists, 1, rows), cols, 1)
        values = short_from(ext_of(proj_ref, halo_ref, exists, 2, rows), cols, 2)
        gated_ref[rows, :] = (values * gate_in * mask)[:, LANE:-LANE].astype(B16)


def out_project_kernel(
    meta_ref, len_ref, proj_ref, halo_ref, cols_ref, io_ref, mixed_ref, y_ref, give3_ref, give1_ref, keep2_ref, keep0_ref
):
    rep = meta_ref[REP]
    width, group = mixed_ref.shape
    _, exists = lane_masks(meta_ref, len_ref, group + 2 * LANE)
    for lo in range(0, width, LANE):
        rows = slice(lo, lo + LANE)
        gate_out = short_from(ext_of(proj_ref, halo_ref, exists, 0, rows), cols_ref[rows, :], 0)
        y = gate_out[:, LANE:-LANE] * mixed_ref[rows, :].astype(F32)
        for j in range(4):
            y_ref[rep ^ j, :, rows] = y[:, j * LANE : (j + 1) * LANE].T.astype(B16)
    outs = (keep0_ref, give1_ref, keep2_ref, give3_ref)
    left = y_ref[...].reshape(-1, width)
    rows = y_ref.shape[1]
    for lo in range(0, io_ref.shape[0], 256):
        part = dot(left, io_ref[lo : lo + 256, 3 * width :], NT)
        for i, ref in enumerate(outs):
            ref[:, lo : lo + 256] = part[i * rows : (i + 1) * rows].astype(ref.dtype)


def halves_far_kernel(left_ref, right_ref, a_ref, b_ref, sems):
    half = a_ref.shape[0]
    copies = [
        pltpu.make_async_copy(left_ref.at[pl.ds(0, half)], a_ref, sems.at[0]),
        pltpu.make_async_copy(right_ref.at[pl.ds(half, half)], b_ref, sems.at[1]),
    ]
    for copy in copies:
        copy.start()
    for copy in copies:
        copy.wait()


def assemble_far_kernel(meta_ref, p0, p1, p2, p3, p4, p5, p6, a_ref, b_ref, out_ref, sems):
    half = a_ref.shape[0]
    last = out_ref.at[meta_ref[OWNER + 7]]
    copies = [
        pltpu.make_async_copy(ref, out_ref.at[meta_ref[OWNER + k]], sems.at[k])
        for k, ref in enumerate((p0, p1, p2, p3, p4, p5, p6))
    ]
    copies.append(pltpu.make_async_copy(a_ref, last.at[pl.ds(0, half)], sems.at[7]))
    copies.append(pltpu.make_async_copy(b_ref, last.at[pl.ds(half, half)], sems.at[8]))
    for copy in copies:
        copy.start()
    for copy in copies:
        copy.wait()


def norm_second_kernel(x_ref, keep_ref, near_ref, far_ref, bias_ref, gain_ref, shift_ref, middle_ref, out_ref):
    middle = x_ref[...].astype(F32) + (
        keep_ref[...] + near_ref[...].astype(F32) + far_ref[...].astype(F32) + bias_ref[...]
    )
    middle_ref[...] = middle
    unit, _ = normed_of(middle)
    out_ref[...] = (unit * gain_ref[...] + shift_ref[...]).astype(B16)


def mlp_kernel(x0, x1, x2, x3, g0, g1, g2, g3, ud_ref, bias_ref, act_ref, gpre_ref, sum_ref):
    step = 256
    rows, model = x0.shape
    pieces = ((x0, g0), (x1, g1), (x2, g2), (x3, g3))
    for lo in range(0, act_ref.shape[1], step):
        cut = slice(lo, lo + step)
        up = ud_ref[:, 0, :, cut].reshape(model, step)
        down = ud_ref[:, 1, :, cut].reshape(model, step)
        total = None
        for i, (x_ref, g_ref) in enumerate(pieces):
            at = slice(i * rows, (i + 1) * rows)
            pre = dot(x_ref[...], up, NN) + bias_ref[:, cut]
            gact = dot(g_ref[...], down, NN)
            phi = 0.5 * (1.0 + lax.erf(pre * math.sqrt(0.5)))
            slope = phi + pre * (jnp.exp(-0.5 * pre * pre) * (1.0 / math.sqrt(2.0 * math.pi)))
            act_ref[at, cut] = (pre * phi).astype(B16)
            gpre = (gact * slope).astype(B16)
            gpre_ref[at, cut] = gpre
            part = jnp.sum(gpre.astype(F32), axis=0, keepdims=True)
            total = part if total is None else total + part
        sum_ref[:, cut] = total


def rows_kernel(which, left_ref, ud_ref, give3_ref, give1_ref, keep2_ref, keep0_ref):
    rows, model = give3_ref.shape
    owned = ud_ref.shape[2]
    outs = (keep0_ref, give1_ref, keep2_ref, give3_ref)
    for k in range(0, ud_ref.shape[0], 2):
        weight = ud_ref[k : k + 2, which].reshape(2 * owned, -1)
        part = dot(left_ref[...], weight, NT)
        for i, ref in enumerate(outs):
            ref[:, k * owned : (k + 2) * owned] = part[i * rows : (i + 1) * rows].astype(ref.dtype)


def mlp_grad_kernel(meta_ref, x0, x1, x2, x3, g0, g1, g2, g3, act_ref, gpre_ref, out_ref, a_ref, b_ref):
    grad_pair((x0, x1, x2, x3), gpre_ref[...], out_ref, slice(None), 0)
    grad_pair((g0, g1, g2, g3), act_ref[...], out_ref, slice(None), out_ref.shape[3] // 2)
    give_first(meta_ref, out_ref, a_ref, b_ref)


def norm_second_back_kernel(
    meta_ref, len_ref, keep_ref, near_ref, far_ref, middle_ref, top_ref, gain_ref, out_ref, gx_ref, sum_ref
):
    grad = keep_ref[...] + near_ref[...].astype(F32) + far_ref[...].astype(F32)
    unit, inverse = normed_of(middle_ref[...])
    scaled = grad * gain_ref[...]
    one = jnp.mean(scaled, axis=1, keepdims=True)
    two = jnp.mean(scaled * unit, axis=1, keepdims=True)
    top = top_ref[...].astype(F32) * own_mask(meta_ref, len_ref, top_ref.shape[0])
    out = top + inverse * (scaled - one - unit * two)
    out_ref[...] = out
    gx = out.astype(B16)
    gx_ref[...] = gx
    rows = [grad * unit, grad, gx.astype(F32), top]
    sums = [jnp.sum(r, axis=0, keepdims=True) for r in rows]
    sum_ref[...] = jnp.concatenate(sums + [jnp.zeros((4, sums[0].shape[1]), F32)], axis=0)


def grad_gate_kernel(
    meta_ref, len_ref, x0, x1, x2, x3, io_ref, proj_ref, halo_ref, cols_ref, mixed_ref, gy_ref, first_ref, gmix_ref
):
    rep = meta_ref[REP]
    width, group = mixed_ref.shape
    _, exists = lane_masks(meta_ref, len_ref, group + 2 * LANE)
    weight = io_ref[:, 3 * width :]
    for i, x_ref in enumerate((x0, x1, x2, x3)):
        gy_ref[:, place(rep ^ i)] = dot(x_ref[...], weight, NN).T.astype(B16)
    for lo in range(0, width, PART):
        rows = slice(lo, lo + PART)
        gate_out = short_from(ext_of(proj_ref, halo_ref, exists, 0, rows), cols_ref[rows, :], 0)
        gy = gy_ref[rows, :].astype(F32)
        gmix_ref[rows, :] = (gy * gate_out[:, LANE:-LANE]).astype(B16)
        first_ref[rows, :] = gy[:, :LANE] * mixed_ref[rows, :LANE].astype(F32)


def conv_back_kernel(
    spec_ref, kern_ref, twist_ref, hi_ref, lo_ref, chan_ref, g_ref, out_ref, grad_kern_ref, z_ref, p_ref
):
    blocks, rows, length = twist_ref.shape[0], g_ref.shape[1], g_ref.shape[2]
    short_blocks = blocks // 4
    span = blocks * rows
    first = [g_ref[b].astype(F32) for b in range(blocks)]
    second = [g_ref[blocks + b].astype(F32) for b in range(short_blocks)]
    turn_rows(first, twist_ref, z_ref, 0, blocks)
    turn_rows(second, twist_ref, z_ref, span, blocks)
    grad = dot_split(z_ref[...], hi_ref[...], lo_ref[...], ((1,), (0,)))
    kern = kern_ref[...]
    p_ref[0:span] = times(grad[:span], kern, True)
    p_ref[span : 2 * span] = times(grad[span:], kern, True)
    p_ref[2 * span :] = times(grad[:span], spec_ref[0:span], True) + times(grad[span:], spec_ref[span:], True)
    w = dot_split(p_ref[...], hi_ref[...], lo_ref[...], ((1,), (1,)))
    skip = chan_ref[:, 0:1]
    for b in range(blocks):
        acc = (back_rows(w, 0, rows, b, twist_ref, blocks) + skip * first[b]).astype(B16)
        out_ref[b] = acc
        if b < short_blocks:
            acc = (back_rows(w, span, rows, b, twist_ref, blocks) + skip * second[b]).astype(B16)
        else:
            acc = jnp.zeros((rows, length), B16)
        out_ref[blocks + b] = acc
        grad_kern_ref[b] = back_rows(w, 2 * span, rows, b, twist_ref, blocks)


def conv_ahead_kernel(kern_ref, twist_ref, hi_ref, lo_ref, chan_ref, x_ref, out_ref, spec_ref, z_ref):
    conv_forward_kernel(
        twist_ref.shape[0] // 4, x_ref, kern_ref, twist_ref, hi_ref, lo_ref, chan_ref.at[:, 0:1], out_ref, spec_ref, z_ref
    )


def filter_ahead_kernel(
    chan_ref, w1_ref, small_ref, columns_ref, grid_ref, ramp_ref, w2_ref, w3_ref, twist_ref, hi_ref, lo_ref,
    spec_ref, sin_ref, cos_ref, z_ref
):
    filter_forward_kernel(
        grid_ref, ramp_ref, chan_ref.at[:, 1:2], w1_ref, w2_ref.at[0], w3_ref.at[0], small_ref, columns_ref,
        twist_ref, hi_ref, lo_ref, spec_ref, sin_ref, cos_ref, z_ref
    )


def filter_back_kernel(
    meta_ref, gk_ref, grid_ref, ramp_ref, chan_ref, w1_ref, w2_ref, w3_ref, col_ref, row_ref, columns_ref, sin_ref, cos_ref,
    side_ref, wide_ref
):
    freq, freq_row = col_ref[:, 3:4], row_ref[3:4, :]
    filt = freq.shape[0]
    gk = jnp.concatenate([gk_ref[b] for b in range(gk_ref.shape[0])], axis=1)
    gk = gk * jnp.exp(-chan_ref[:, 1:2] * ramp_ref[...])
    gcols = dot_high(sin_ref[2], gk, NT)
    chan, width = gcols.shape[1], wide_ref.shape[1]
    row = lax.broadcasted_iota(jnp.int32, (chan, width), 0)
    lane = lax.broadcasted_iota(jnp.int32, (chan, width), 1)
    pick = (lane == row + meta_ref[SEQ] * chan).astype(F32)
    wide_ref[...] = dot_high(gcols, pick, NN)
    grad = dot_high(columns_ref[...], gk, NN)
    ones = jnp.ones((8, gk.shape[1]), F32)
    gfreq = jnp.zeros((1, filt), F32)
    grads, biases = [None] * 3, [None] * 3
    for i, weight in ((2, w3_ref[0]), (1, w2_ref[0]), (0, w1_ref[...])):
        turn = grad * cos_ref[i]
        below = sin_ref[i - 1] if i else grid_ref[...]
        raw = dot_high(below, turn, NT)
        total = dot_high(ones, turn, NT)[0:1]
        grads[i] = raw * freq_row
        biases[i] = total * freq_row
        gfreq = gfreq + jnp.sum(raw * weight, axis=0, keepdims=True) + total * row_ref[i : i + 1, :]
        if i:
            grad = dot_high(weight, turn * freq, NN)
    gap = jnp.zeros((filt - grads[0].shape[0], filt), F32)
    small = jnp.concatenate(biases + [gfreq, jnp.zeros((filt - 4, filt), F32)], axis=0)
    side_ref[...] = jnp.concatenate(
        [grads[1], grads[2], jnp.concatenate([grads[0], gap], axis=0), small], axis=1
    )


def summed(value):
    total = value[:, :LANE]
    for k in range(LANE, value.shape[1], LANE):
        total = total + value[:, k : k + LANE]
    return jnp.sum(total, axis=1, keepdims=True)


def short_back(ext, cols, gshort, p, mid):
    size = ext.shape[1]
    mine = gshort[:, mid]
    gproj = (
        cols[:, 6 + p : 7 + p] * gshort
        + cols[:, 3 + p : 4 + p] * pltpu.roll(gshort, size - 1, 1)
        + cols[:, p : p + 1] * pltpu.roll(gshort, size - 2, 1)
    )[:, mid].astype(B16).astype(F32)
    sums = [
        summed(mine),
        summed(mine * ext[:, mid]),
        summed(mine * pltpu.roll(ext, 1, 1)[:, mid]),
        summed(mine * pltpu.roll(ext, 2, 1)[:, mid]),
        summed(gproj),
    ]
    return gproj, sums


def grad_first_kernel(
    meta_ref, len_ref, proj_ref, halo_ref, cols_ref, mixed_ref, gy_ref, onext_ref, io_ref, tok_ref, sum_ref, part_ref
):
    rep = meta_ref[REP]
    width, group = mixed_ref.shape
    size = group + 2 * LANE
    mask, exists = lane_masks(meta_ref, len_ref, size)
    mid = slice(LANE, size - LANE)
    next_on = exists[:, size - LANE :]
    columns = []
    for lo in range(0, width, PART):
        rows = slice(lo, lo + PART)
        cols = cols_ref[rows, :]
        gy = gy_ref[rows, :].astype(F32)
        gout = gy * mixed_ref[rows, :].astype(F32)
        gshort = jnp.concatenate([jnp.zeros((PART, LANE), F32), gout, onext_ref[rows, :] * next_on], axis=1)
        gproj, sums = short_back(ext_of(proj_ref, halo_ref, exists, 0, rows), cols, gshort, 0, mid)
        for j in range(4):
            tok_ref[rep ^ j, :, rows] = gproj[:, j * LANE : (j + 1) * LANE].T.astype(B16)
        columns.append(jnp.concatenate(sums + [jnp.zeros((PART, LANE - 5), F32)], axis=1))
    sum_ref[...] = jnp.concatenate(columns, axis=0).T[:8]
    part_ref[...] = dot(tok_ref[...].reshape(-1, width), io_ref[:, :width], NT)


def grad_short_kernel(
    meta_ref, len_ref, proj_ref, halo_ref, cols_ref, gy_ref, io_ref, before_ref,
    x0, x1, x2, x3, gain_ref, shift_ref, ggated_ref, gnext_ref,
    tok_ref, sum_ref, norm_ref, give3_ref, give1_ref, keep2_ref, keep0_ref
):
    rep = meta_ref[REP]
    width, group = gy_ref.shape
    size = group + 2 * LANE
    mask, exists = lane_masks(meta_ref, len_ref, size)
    mid = slice(LANE, size - LANE)
    columns = []
    for lo in range(0, width, PART):
        rows = slice(lo, lo + PART)
        cols = cols_ref[rows, :]
        ext = [ext_of(proj_ref, halo_ref, exists, p, rows) for p in (1, 2)]
        short = [short_from(ext[p - 1], cols, p) for p in (1, 2)]
        ggated = (
            jnp.concatenate(
                [jnp.zeros((PART, LANE), F32), ggated_ref[rows, :].astype(F32), gnext_ref[rows, :].astype(F32)], axis=1
            )
            * mask
            * exists
        )
        gate_out = short_from(ext_of(proj_ref, halo_ref, exists, 0, rows), cols, 0)[:, mid]
        gated = short[1][:, mid] * short[0][:, mid] * mask[:, mid]
        sums = [summed(gy_ref[rows, :].astype(F32) * gate_out * gated)]
        for p in (1, 2):
            gproj, more = short_back(ext[p - 1], cols, ggated * short[2 - p], p, mid)
            sums += more
            at = slice((p - 1) * width + lo, (p - 1) * width + lo + PART)
            for j in range(4):
                tok_ref[rep ^ j, :, at] = gproj[:, j * LANE : (j + 1) * LANE].T.astype(B16)
        columns.append(jnp.concatenate(sums + [jnp.zeros((PART, LANE - 11), F32)], axis=1))
    sum_ref[...] = jnp.concatenate(columns, axis=0).T[:16]
    outs = (keep0_ref, give1_ref, keep2_ref, give3_ref)
    left = tok_ref[...].reshape(-1, 2 * width)
    tall = tok_ref.shape[1]
    for lo in range(0, io_ref.shape[0], 256):
        cut = slice(lo, lo + 256)
        part = dot(left, io_ref[cut, width : 3 * width], NT) + before_ref[:, cut]
        plain = jnp.sum(part, axis=0, keepdims=True)
        cross = None
        for i, (ref, x_ref) in enumerate(zip(outs, (x0, x1, x2, x3))):
            mine = part[i * tall : (i + 1) * tall]
            ref[:, cut] = mine.astype(ref.dtype)
            two = jnp.sum(mine * x_ref[:, cut].astype(F32), axis=0, keepdims=True)
            cross = two if cross is None else cross + two
        norm_ref[0:1, cut] = (cross - shift_ref[:, cut] * plain) / gain_ref[:, cut]
        norm_ref[1:2, cut] = plain


def give_first(meta_ref, term_ref, a_ref, b_ref):
    half = a_ref.shape[2]
    seq = meta_ref[SEQ]
    s0, s1 = seq & 1, (seq >> 1) & 1
    for i in range(2):
        for j in range(2):
            a_ref[i, j] = term_ref[i, j, 1 - s0, :half]
            b_ref[i, j] = term_ref[i, 1 - s1, j, half:]


def grad_pair(refs, right, out_ref, lanes, base=0):
    owned = refs[0].shape[1] // 8
    for k in range(0, 8, 2):
        left = jnp.concatenate([r[:, k * owned : (k + 2) * owned] for r in refs], axis=0)
        part = dot(left, right, TN).astype(B16)
        out_ref[k // 4, (k // 2) % 2, 0, base : base + owned, lanes] = part[:owned]
        out_ref[k // 4, (k // 2) % 2, 1, base : base + owned, lanes] = part[owned:]


def grad_early_kernel(meta_ref, g0, g1, g2, g3, y_ref, x0, x1, x2, x3, tok_ref, out_ref, a_ref, b_ref):
    width = y_ref.shape[2]
    grad_pair((g0, g1, g2, g3), y_ref[...].reshape(-1, width), out_ref, slice(0, width))
    grad_pair((x0, x1, x2, x3), tok_ref[...].reshape(-1, width), out_ref, slice(width, 2 * width))
    give_first(meta_ref, out_ref, a_ref, b_ref)


def grad_late_kernel(meta_ref, x0, x1, x2, x3, tok_ref, out_ref, a_ref, b_ref):
    width = tok_ref.shape[2]
    grad_pair((x0, x1, x2, x3), tok_ref[...].reshape(-1, width), out_ref, slice(0, width))
    give_first(meta_ref, out_ref, a_ref, b_ref)


def halve_one_kernel(meta_ref, term_ref, a_in, b_in, keep_a, keep_b, give_a, give_b):
    half = a_in.shape[2]
    seq = meta_ref[SEQ]
    s0, s1 = seq & 1, (seq >> 1) & 1
    for i in range(2):
        keep_a[i] = term_ref[i, s1, s0, :half].astype(F32) + a_in[i, s1].astype(F32)
        give_a[i] = (term_ref[i, 1 - s1, s0, :half].astype(F32) + a_in[i, 1 - s1].astype(F32)).astype(B16)
        keep_b[i] = term_ref[i, s1, s0, half:].astype(F32) + b_in[i, s0].astype(F32)
        give_b[i] = (term_ref[i, s1, 1 - s0, half:].astype(F32) + b_in[i, 1 - s0].astype(F32)).astype(B16)


def halve_two_kernel(meta_ref, keep_a_in, keep_b_in, a_in, b_in, keep_a, keep_b, give_a, give_b):
    s2 = meta_ref[SEQ] >> 2
    keep_a[...] = keep_a_in[s2] + a_in[s2].astype(F32)
    give_a[...] = (keep_a_in[1 - s2] + a_in[1 - s2].astype(F32)).astype(B16)
    keep_b[...] = keep_b_in[s2] + b_in[s2].astype(F32)
    give_b[...] = (keep_b_in[1 - s2] + b_in[1 - s2].astype(F32)).astype(B16)


def far_last_kernel(keep_a, keep_b, a_in, b_in, up_ref, down_ref):
    up_ref[0] = keep_a[...] + a_in[...].astype(F32)
    down_ref[0] = keep_b[...] + b_in[...].astype(F32)


def early_last_kernel(keep_a, keep_b, a_in, b_in, out_ref, in_ref):
    half, width = keep_a.shape[0], out_ref.shape[2]
    for keep, came, rows in ((keep_a, a_in, slice(0, half)), (keep_b, b_in, slice(half, 2 * half))):
        out_ref[0, rows] = keep[:, :width] + came[:, :width].astype(F32)
        in_ref[rows] = keep[:, width:] + came[:, width:].astype(F32)


def late_last_kernel(keep_a, keep_b, a_in, b_in, first_ref, out_ref):
    half, width = keep_a.shape[0], out_ref.shape[3]
    out_ref[0, 0] = first_ref[...]
    for keep, came, rows in ((keep_a, a_in, slice(0, half)), (keep_b, b_in, slice(half, 2 * half))):
        for p in range(2):
            lanes = slice(p * width, (p + 1) * width)
            out_ref[0, 1 + p, rows] = keep[:, lanes] + came[:, lanes].astype(F32)


def norm_first_back_kernel(keep_ref, near_ref, far_ref, x_ref, middle_ref, gain_ref, out_ref):
    grad = keep_ref[...] + near_ref[...].astype(F32) + far_ref[...].astype(F32)
    unit, inverse = normed_of(x_ref[...].astype(F32))
    scaled = grad * gain_ref[...]
    one = jnp.mean(scaled, axis=1, keepdims=True)
    two = jnp.mean(scaled * unit, axis=1, keepdims=True)
    out_ref[...] = middle_ref[...] + inverse * (scaled - one - unit * two)


def layer_out_kernel(keep_ref, near_ref, far_ref, middle_ref, bias_ref, out_ref):
    part = keep_ref[...] + near_ref[...].astype(F32) + far_ref[...].astype(F32)
    out_ref[...] = (middle_ref[...] + (part + bias_ref[...])).astype(B16)


def heads_kernel(in_ref, out_ref):
    out_ref[...] = in_ref[:, :LANE]


def add_far_kernel(keep_ref, came_ref, out_ref):
    out_ref[...] = (keep_ref[...] + came_ref[...].astype(F32)).astype(B16)


HALF = 88


def pack_small_kernel(side_ref, wide_ref, col0_ref, col_ref, up_ref, one_ref, two_ref, out_ref):
    filt, width = side_ref.shape
    out_ref[:filt] = side_ref[...]
    at = filt
    for ref, count in ((one_ref, 2), (two_ref, 4)):
        for r in range(count):
            for k in range(4):
                out_ref[at : at + 1] = ref[r : r + 1, k * width : (k + 1) * width]
                at += 1
    out_ref[HALF : HALF + 1] = col_ref[0:1]
    out_ref[HALF + 1 : HALF + 6] = col0_ref[0:5]
    out_ref[HALF + 6 : HALF + 16] = col_ref[1:11]
    for k in range(4):
        out_ref[HALF + 16 + k : HALF + 17 + k] = up_ref[:, k * width : (k + 1) * width]
    out_ref[HALF + 20 : HALF + 24] = jnp.zeros((4, width), F32)
    out_ref[HALF + 24 :] = wide_ref[...]


def add_small_kernel(mine_ref, came_ref, out_ref):
    out_ref[...] = mine_ref[...] + came_ref[...]


def list_small_kernel(meta_ref, mine_ref, came_ref, out_ref):
    y = meta_ref[REP] >> 1
    out_ref[:HALF] = mine_ref[:HALF] + came_ref[:HALF]
    out_ref[pl.ds(pl.multiple_of((1 + y) * HALF, 8), HALF)] = mine_ref[HALF:]
    out_ref[pl.ds(pl.multiple_of((2 - y) * HALF, 8), HALF)] = came_ref[HALF:]


def unpack_small_kernel(
    meta_ref, mine_ref, came_ref,
    in_bias, taps, short_bias, fw, fb, iw, ib, dw, db, sf, kern_w, skip, out_b, n1g, n1s, n2g, n2s, up_b, down_b
):
    core = meta_ref[REP] & 1
    filt, width = iw.shape[2], mine_ref.shape[1]
    total = mine_ref[:HALF] + came_ref[:HALF]
    iw[0] = total[:filt, :filt]
    dw[0] = total[:filt, filt : 2 * filt]
    for k in range(fw.shape[0]):
        fw[k] = total[k : k + 1, 2 * filt : 3 * filt]
    for k, ref in enumerate((fb, ib, db, sf)):
        ref[...] = total[k : k + 1, 3 * filt :]
    at = filt
    for ref in (n1g, n1s, n2g, n2s, out_b, down_b):
        for k in range(4):
            ref[:, k * width : (k + 1) * width] = total[at : at + 1]
            at += 1
    for y in range(2):
        lo = (1 + y) * HALF
        mine, came = mine_ref[lo : lo + HALF], came_ref[lo : lo + HALF]
        for c in range(2):
            block = jnp.where(core == c, mine, came)
            lanes = slice((2 * y + c) * width, (2 * y + c + 1) * width)
            skip[:, lanes] = block[0:1]
            for p in range(3):
                row = 1 + 5 * p
                short_bias[p, :, lanes] = block[row : row + 1]
                for j in range(3):
                    taps[j, p, :, lanes] = block[row + 3 - j : row + 4 - j]
                in_bias[p, :, lanes] = block[row + 4 : row + 5]
            for k in range(4):
                lo_up = (2 * y + c) * 4 * width + k * width
                up_b[:, lo_up : lo_up + width] = block[16 + k : 17 + k]
            kern_w[0, :, lanes] = block[24 : 24 + filt]


def tie(values, *others):
    return lax.optimization_barrier((values, others))[0]


class RingGather:
    def __init__(self, name, meta, shard, far=False):
        self.name, self.meta, self.far = name, meta, far
        self.pieces = [shard]
        self.send(shard, shard)

    def send(self, left, right):
        self.came = (lax.ppermute(left, "seq", AHEAD), lax.ppermute(right, "seq", BACK))

    def step(self, *others):
        left, right = tie(self.came, *others)
        self.pieces += [left, right]
        count = len(self.pieces)
        if count == 7:
            half = shape((left.shape[0] // 2,) + left.shape[1:], B16)
            if self.far:
                left, right = call(
                    halves_far_kernel, self.name + "_halves", [left, right], [half, half],
                    scratch=[pltpu.SemaphoreType.DMA((2,))], raw=[0, 1, -1, -2],
                )
            else:
                left, right = call(halves_kernel, self.name + "_halves", [left, right], [half, half])
        if count < 9:
            self.send(left, right)
        return self.came

    def full(self, *others):
        left, right = tie(self.came, *others)
        pieces = self.pieces + [left, right]
        whole = [shape((8,) + self.pieces[0].shape, B16)]
        if self.far:
            return call(
                assemble_far_kernel, self.name + "_assemble", [self.meta, *pieces], whole,
                scratch=[pltpu.SemaphoreType.DMA((9,))], raw=range(1, 10),
            )[0]
        return call(assemble_kernel, self.name + "_assemble", [self.meta, *pieces], whole)[0]


def gather_four(rows):
    far = swap(rows, "rep", 2)
    near = swap(rows, "rep", 1)
    diag = swap(far, "rep", 1)
    return [rows, near, far, diag]


def pass_far(give3, give1, keep2):
    came = swap(give3, "rep", 1)
    near = swap(give1, "rep", 1)
    (summed,) = call(add_far_kernel, "add_far", [keep2, came], [shape(keep2.shape, B16)])
    return near, swap(summed, "rep", 2), summed


class Halving:
    def __init__(self, name, meta, term, give):
        self.name, self.meta, self.term = name, meta, term
        self.came = (swap(give[0], "seq", 1), swap(give[1], "seq", 2))

    def one(self, *others):
        rows, cols = self.term.shape[3] // 2, self.term.shape[4]
        outs = [shape((2, rows, cols), F32)] * 2 + [shape((2, rows, cols), B16)] * 2
        args = [self.meta, self.term, *tie(self.came, *others)]
        *self.keep, ga, gb = call(halve_one_kernel, self.name + "_one", args, outs)
        self.came = (swap(ga, "seq", 2), swap(gb, "seq", 1))
        return ga

    def two(self, *others):
        rows, cols = self.term.shape[3] // 2, self.term.shape[4]
        outs = [shape((rows, cols), F32)] * 2 + [shape((rows, cols), B16)] * 2
        args = [self.meta, *self.keep, *tie(self.came, *others)]
        *self.keep, ga, gb = call(halve_two_kernel, self.name + "_two", args, outs)
        self.came = (swap(ga, "seq", 4), swap(gb, "seq", 4))
        return ga

    def last(self, *others):
        return [*self.keep, *tie(self.came, *others)]


def exchange(blocks):
    return lax.all_to_all(blocks, "seq", 0, 0, tiled=True)


def per_device_fast(
    tokens,
    cotangent,
    lengths,
    in_weight,
    in_bias,
    short_taps,
    short_bias,
    feat_weight,
    feat_bias,
    inner_weight,
    inner_bias,
    deep_weight,
    deep_bias,
    sine_freq,
    kernel_weight,
    skip_gain,
    out_weight,
    out_bias,
    norm1_gain,
    norm1_shift,
    norm2_gain,
    norm2_shift,
    up_weight,
    up_bias,
    down_weight,
    down_bias,
):
    tok_rows, model = tokens.shape
    group = tok_rows * 4
    blocks = 4
    seq_len = blocks * group
    chan = model // 32
    width = model // 4
    hidden = up_weight.shape[2]
    owned = model // 8
    filt = feat_weight.shape[2]
    device = lax.axis_index("seq") * 4 + lax.axis_index("rep")
    meta = lax.dynamic_index_in_dim(jnp.asarray(meta_table(group)), device, 0, keepdims=False)
    row_f32, row_b16 = shape((tok_rows, model), F32), shape((tok_rows, model), B16)
    sums_shapes = [row_b16, row_b16, row_f32, row_f32]
    flat_shape = shape((width, group), B16)

    normed, io_shard = call(
        start_kernel,
        "start",
        [tokens, norm1_gain, norm1_shift, in_weight[0].transpose(1, 0, 2), out_weight],
        [row_b16, shape((owned, 4 * width), B16)],
        away=range(5),
    )
    io_ring = RingGather("io", meta, io_shard)
    x_one = gather_four(normed)
    twist, table = transform_tables(blocks, group)
    hi, lo = split_table(table)
    grid, ramp = feature_table(seq_len, feat_weight.shape[1])
    twist, grid, ramp = jnp.asarray(twist), jnp.asarray(grid), jnp.asarray(ramp)
    params = [
        cotangent, up_weight, down_weight,
        short_taps.transpose(1, 2, 0, 3), short_bias.transpose(1, 0, 2), in_bias.transpose(1, 0, 2), up_bias, skip_gain,
        jnp.asarray(decay_rates(model).T), kernel_weight, feat_weight.transpose(1, 0, 2),
        feat_bias, inner_bias, deep_bias, sine_freq,
    ]
    top_rows, ud_shard, cols, up_block, chans, columns, small_col, small_row, feat = call(
        setup_kernel,
        "setup",
        [meta, lengths, *params],
        [
            row_b16, shape((2, owned, hidden), B16),
            shape((width, 16), F32), shape((1, hidden), F32), shape((chan, 2), F32), shape((filt, chan), F32),
            shape((filt, 4), F32), shape((4, filt), F32), shape(feat_weight.shape[1:], F32),
        ],
        scratch=[pltpu.SemaphoreType.DMA((2,))],
        away=[2] + list(range(5, 2 + len(params))),
        raw=[3, 4, -2],
    )
    io_ring.step(x_one[1])
    tables = [grid, ramp, inner_weight, deep_weight, twist, hi, lo]
    kern_spec, sines, cosines = call(
        filter_ahead_kernel,
        "filter_ahead",
        [chans, feat, tie(small_col, io_ring.pieces[-1]), columns, *tables],
        [
            shape((blocks * chan, 2 * group), F32),
            shape((3, filt, seq_len), F32),
            shape((3, filt, seq_len), F32),
        ],
        scratch=[pltpu.VMEM((blocks * chan, 2 * group), F32)],
        away=range(4, 4 + len(tables)),
    )
    io_ring.step(kern_spec, x_one[2])

    edge = shape((HALO, model), B16)
    last, first = call(edges_kernel, "edges", [meta, *x_one], [edge, edge])
    before = lax.ppermute(last, "seq", [(i, (i + 1) % 8) for i in range(8)])
    after = lax.ppermute(first, "seq", [(i, (i + 7) % 8) for i in range(8)])
    io_ring.step()
    io_pieces = io_ring.pieces + list(tie(io_ring.came, before, after))
    ud_ring = RingGather("ud", meta, tie(ud_shard, io_pieces[-1]))
    g_top = gather_four(tie(top_rows, x_one[3]))
    full_io, proj, halo, gated = call(
        project_kernel,
        "project",
        [meta, lengths, *x_one, before, after, cols, *io_pieces],
        [
            shape((8, owned, 4 * width), B16), shape((3, width, group), B16), shape((3, width, 2 * LANE), B16), flat_shape
        ],
    )
    full_io = full_io.reshape(model, 4 * width)
    common = [proj, halo, cols]

    spread = (8, chan, group)
    received = exchange(gated.reshape(spread))
    ud_ring.step(received)
    spec_rows = 2 * blocks * chan
    mixed, kept_spec = call(
        conv_ahead_kernel,
        "conv_ahead",
        [kern_spec, twist, hi, lo, chans, received],
        [shape(spread, B16), shape((spec_rows, 2 * group), F32)],
        scratch=[pltpu.VMEM((spec_rows, 2 * group), F32)],
    )
    mixed = exchange(mixed).reshape(width, group)
    ud_ring.step(mixed)

    y_tok, give3, give1, keep2, keep0 = call(
        out_project_kernel,
        "out_project",
        [meta, lengths, *common, full_io, mixed],
        [shape((4, tok_rows, width), B16)] + sums_shapes,
    )
    near, far, _ = pass_far(give3, give1, keep2)
    middle, normed_two = call(
        norm_second_kernel,
        "norm_second",
        [tokens, keep0, near, far, out_bias, norm2_gain, norm2_shift],
        [row_f32, row_b16],
    )
    ud_ring.step(normed_two)
    x_two = gather_four(normed_two)
    full_ud = ud_ring.full(x_two[2])

    tall = shape((group, hidden), B16)
    act, gpre, gup = call(
        mlp_kernel, "mlp", [*x_two, *g_top, full_ud, up_block], [tall, tall, shape((1, hidden), F32)],
    )
    give3, give1, keep2, keep0 = call(partial(rows_kernel, 0), "grad_two", [gpre, full_ud], sums_shapes)
    near, far, passed = pass_far(give3, give1, keep2)
    give = shape((2, 2, owned, hidden), B16)
    mlp_terms, ga, gb = call(
        mlp_grad_kernel,
        "mlp_grad",
        [meta, *x_two, *g_top, act, tie(gpre, passed)],
        [shape((2, 2, 2, 2 * owned, hidden), B16), give, give],
    )
    wide_back = Halving("far", meta, mlp_terms, (ga, gb))
    grad_middle, gx, norm_sums = call(
        norm_second_back_kernel,
        "norm_second_back",
        [meta, lengths, keep0, near, tie(far, ga), middle, cotangent, norm2_gain],
        [row_f32, row_b16, shape((8, model), F32)],
    )
    g_mid = gather_four(gx)
    m3, m1, m2, m0 = call(partial(rows_kernel, 1), "mlp_rows", [tie(act, gx), full_ud], sums_shapes)
    gy, gate_first, gmix = call(
        grad_gate_kernel,
        "grad_gate",
        [meta, lengths, *tie(tuple(g_mid), m3), full_io, *common, mixed],
        [flat_shape, shape((width, LANE), F32), flat_shape],
    )

    received = exchange(gmix.reshape(spread))
    given = wide_back.one(received)
    gate_next = lax.ppermute(tie(gate_first, received), "seq", [(i, (i + 7) % 8) for i in range(8)])
    ggated, grad_kernel = call(
        conv_back_kernel,
        "conv_back",
        [kept_spec, kern_spec, twist, hi, lo, chans, tie(received, given)],
        [shape(spread, B16), shape((blocks, chan, group), F32)],
        scratch=[pltpu.VMEM((spec_rows, 2 * group), F32), pltpu.VMEM((3 * spec_rows // 2, 2 * group), F32)],
    )
    ggated = exchange(tie(ggated, gate_next)).reshape(width, group)
    given = wide_back.two(ggated)
    (heads,) = call(heads_kernel, "heads", [tie(ggated, given)], [shape((width, LANE), B16)])
    ggated_next = lax.ppermute(heads, "seq", [(i, (i + 7) % 8) for i in range(8)])
    tok_first, sum_first, part_first = call(
        grad_first_kernel,
        "grad_first",
        [meta, lengths, *common, mixed, gy, tie(gate_next, heads), full_io],
        [shape((4, tok_rows, width), B16), shape((8, width), F32), shape((group, model), F32)],
    )
    cube = shape((2, 2, 2, owned, 2 * width), B16)
    give = shape((2, 2, owned // 2, 2 * width), B16)
    early_terms, ga, gb = call(
        grad_early_kernel,
        "grad_early",
        [meta, *g_mid, y_tok, *x_one, tok_first],
        [cube, give, give],
    )
    early = Halving("early", meta, early_terms, (ga, gb))
    tok_rest, col_sums, norm_one, give3, give1, keep2, keep0 = call(
        grad_short_kernel,
        "grad_short",
        [meta, lengths, *common, gy, full_io, part_first, *x_one, norm1_gain, norm1_shift, tie(ggated, ga), ggated_next],
        [shape((4, tok_rows, 2 * width), B16), shape((16, width), F32), shape((2, model), F32)] + sums_shapes,
    )
    near, far, passed = pass_far(give3, give1, keep2)
    late_terms, ga, gb = call(
        grad_late_kernel, "grad_late", [meta, *tie(tuple(x_one), passed), tok_rest], [cube, give, give]
    )
    late = Halving("late", meta, late_terms, (ga, gb))
    given = early.one(ga)
    side, wide = call(
        filter_back_kernel,
        "filter_back",
        [
            meta, tie(grad_kernel, given), grid, ramp, chans, feat, inner_weight, deep_weight, small_col, small_row, columns,
            sines, cosines
        ],
        [shape((filt, 4 * filt), F32), shape((filt, width), F32)],
    )

    (small,) = call(
        pack_small_kernel,
        "pack_small",
        [side, wide, sum_first, col_sums, gup, norm_one, norm_sums],
        [shape((2 * HALF, width), F32)],
    )
    came = swap(small, "seq", 1)
    m_near, m_far, m_passed = pass_far(tie(m3, small), m1, m2)
    (grad_tokens,) = call(
        norm_first_back_kernel,
        "norm_first_back",
        [keep0, near, tie(far, small), tokens, grad_middle, norm1_gain],
        [row_f32],
    )
    given = late.one(grad_tokens, m_passed)
    (small,) = call(add_small_kernel, "add_small", [small, tie(came, given)], [small])
    came = swap(small, "seq", 2)
    given = early.two(small)
    result = shape((1, owned, hidden), F32)
    grad_up, grad_down = call(far_last_kernel, "far_last", wide_back.last(given), [result, result])
    given = late.two(grad_up)
    (small,) = call(add_small_kernel, "add_small", [small, tie(came, given)], [small])
    came = swap(small, "seq", 4)
    (layer_out,) = call(layer_out_kernel, "layer_out", [m0, m_near, tie(m_far, small), middle, down_bias], [row_b16])
    grad_out, first_in = call(
        early_last_kernel, "early_last", early.last(layer_out), [shape((1, owned, width), F32), shape((owned, width), F32)]
    )
    (small,) = call(add_small_kernel, "add_small", [small, tie(came, grad_out)], [small])
    came = swap(small, "rep", 2)
    (small,) = call(
        list_small_kernel, "list_small", [meta, small, came], [shape((3 * HALF, width), F32)]
    )
    came = swap(small, "rep", 1)
    (grad_in,) = call(
        late_last_kernel, "late_last", [*late.last(small), first_in], [shape((1, 3, owned, width), F32)]
    )
    vector = shape((1, model), F32)
    square, short = shape((1, filt, filt), F32), shape((1, filt), F32)
    triple = shape((3, 1, model), F32)
    outs = call(
        unpack_small_kernel,
        "unpack_small",
        [meta, small, came],
        [
            triple, shape((3, 3, 1, model), F32), triple, shape(params[10].shape, F32), short, square, short, square,
            short, short, shape(kernel_weight.shape, F32), vector, vector, vector, vector, vector, vector,
            shape(up_bias.shape, F32), vector,
        ],
    )
    return (
        layer_out,
        grad_tokens,
        grad_in.transpose(0, 2, 1, 3),
        outs[0].transpose(1, 0, 2),
        outs[1].transpose(2, 0, 1, 3),
        outs[2].transpose(1, 0, 2),
        outs[3].transpose(1, 0, 2),
        *outs[4:12],
        grad_out,
        *outs[12:17],
        grad_up,
        outs[17],
        grad_down,
        outs[18],
    )


def solution(mesh):
    rows = P(("seq", "rep"), None)
    cut = P(None, "seq", "rep")
    wide = P(None, "seq", None, "rep")
    whole = P()
    ins = [rows, rows, whole, wide] + [whole] * 12 + [cut] + [whole] * 5 + [cut, whole, cut, whole]
    outs = [rows, rows, wide] + [whole] * 12 + [cut] + [whole] * 5 + [cut, whole, cut, whole]
    fast = mesh.shape["seq"] == 8 and mesh.shape["rep"] == 4
    return jax.shard_map(
        per_device_fast if fast else per_device, mesh=mesh, in_specs=tuple(ins), out_specs=tuple(outs), check_vma=False
    )
```

```python
from functools import partial
import math

import jax
import jax.numpy as jnp
import numpy as np
from jax import lax
from jax.experimental import pallas as pl
from jax.experimental.pallas import tpu as pltpu
from jax.sharding import PartitionSpec as P

EPS = 1e-05
HIGH = lax.Precision.HIGHEST
F32 = jnp.float32
B16 = jnp.bfloat16
LANE = 128
HALO = 16
VMEM_BYTES = 48 * 2**20


def swap(values, axis_name, bit):
    size = lax.axis_size(axis_name)
    return lax.ppermute(values, axis_name, [(i, i ^ bit) for i in range(size)])


def gather_rel(rows):
    far = swap(rows, "rep", 2)
    near = swap(rows, "rep", 1)
    diag = swap(far, "rep", 1)
    return jnp.concatenate([rows, near, far, diag], axis=0)


def scatter_rel(part):
    rows = part.shape[0] // 4
    blocks = part.reshape(4, rows, part.shape[1])
    far_in = swap(blocks[3].astype(B16), "rep", 1)
    far_sum = (blocks[2] + far_in.astype(F32)).astype(B16)
    near_in = swap(blocks[1].astype(B16), "rep", 1)
    far_out = swap(far_sum, "rep", 2)
    return blocks[0] + near_in.astype(F32) + far_out.astype(F32)


def ring_order(count):
    if count == 8:
        return [0, 2, 4, 6, 7, 5, 3, 1]
    return list(range(count))


def ring_maps(count):
    order = ring_order(count)
    ahead = [(order[i], order[(i + 1) % count]) for i in range(count)]
    return order, ahead, [(b, a) for a, b in ahead]


def ring_gather(shard):
    count = lax.axis_size("seq")
    if count != 8:
        return lax.all_gather(shard, "seq", axis=0)
    order, ahead, back = ring_maps(count)
    place = jnp.asarray(np.argsort(order), jnp.int32)[lax.axis_index("seq")]
    owners = jnp.asarray(order, jnp.int32)
    full = jnp.zeros((count,) + shard.shape, shard.dtype)

    def put(full, piece, step, lo=0):
        owner = owners[(place + step + count) % count]
        start = (owner, lo) + (0,) * (shard.ndim - 1)
        return lax.dynamic_update_slice(full, piece[None], start)

    full = put(full, shard, 0)
    left = right = shard
    for step in range(1, count // 2):
        left = lax.ppermute(left, "seq", ahead)
        right = lax.ppermute(right, "seq", back)
        full = put(full, left, -step)
        full = put(full, right, step)
    half = shard.shape[0] // 2
    left = lax.ppermute(left[:half], "seq", ahead)
    right = lax.ppermute(right[half:], "seq", back)
    full = put(full, left, -(count // 2))
    full = put(full, right, count // 2, half)
    return full


def ring_scatter(term):
    count = lax.axis_size("seq")
    if count != 8:
        return lax.psum_scatter(term, "seq", scatter_dimension=0, tiled=True).astype(F32)
    order, ahead, back = ring_maps(count)
    place = jnp.asarray(np.argsort(order), jnp.int32)[lax.axis_index("seq")]
    owners = jnp.asarray(order, jnp.int32)
    rows = term.shape[0] // count
    half = rows // 2

    def mine(step, lo):
        owner = owners[(place + step + 2 * count) % count]
        return lax.dynamic_slice_in_dim(term, owner * rows + lo, half, 0)

    left, right = mine(-1, 0), mine(1, half)
    for step in range(2, count + 1):
        left = lax.ppermute(left, "seq", ahead).astype(F32) + mine(-step, 0).astype(F32)
        right = lax.ppermute(right, "seq", back).astype(F32) + mine(step, half).astype(F32)
        if step < count:
            left, right = left.astype(B16), right.astype(B16)
    return jnp.concatenate([left, right], axis=0)


def halve_scatter(term):
    count = lax.axis_size("seq")
    bits = count.bit_length() - 1
    seq = lax.axis_index("seq")
    rows = term.shape[0] // count
    half = rows // 2
    split = term.reshape((2,) * bits + (2, half, term.shape[1]))
    results = []
    for part, order in enumerate(([0] + list(range(bits - 1, 0, -1)), list(range(bits - 1, -1, -1)))):
        value = lax.index_in_dim(split, part, bits, keepdims=False)
        left = list(range(bits - 1, -1, -1))
        for bit in order:
            at = left.index(bit)
            on = (seq >> bit) & 1
            keep = lax.dynamic_index_in_dim(value, on, at, keepdims=False)
            give = lax.dynamic_index_in_dim(value, 1 - on, at, keepdims=False)
            value = keep.astype(F32) + swap(give, "seq", 1 << bit).astype(F32)
            left.remove(bit)
            if left:
                value = value.astype(B16)
        results.append(value)
    return jnp.concatenate(results, axis=0)


def spread_gather(shard):
    count = lax.axis_size("seq")
    copies = jnp.broadcast_to(shard[None], (count,) + shard.shape)
    full = lax.all_to_all(copies, "seq", 0, 0, tiled=True)
    return full.reshape((count * shard.shape[0],) + shard.shape[1:])


def shift_seq(values, step):
    count = lax.axis_size("seq")
    return lax.ppermute(values, "seq", [(i, (i + step) % count) for i in range(count)])


def unmix(values, axis, index):
    size, bit = values.shape[axis], 1
    while bit < size:
        cut = values.shape[:axis] + (size // (2 * bit), 2, bit) + values.shape[axis + 1 :]
        split = values.reshape(cut)
        values = jnp.where((index // bit) % 2 == 1, jnp.flip(split, axis + 1), split).reshape(values.shape)
        bit *= 2
    return values


def sync_small(total, group, own):
    n_seq, n_rep = lax.axis_size("seq"), lax.axis_size("rep")
    group_list, own_list = [group], [own]
    for axis_name, size in (("seq", n_seq), ("rep", n_rep)):
        bit = 1
        while bit < size:
            parts = [total] + group_list + own_list
            sizes = np.cumsum([0] + [p.shape[0] for p in parts])
            came = swap(jnp.concatenate(parts, axis=0), axis_name, bit)
            came = [came[a:b] for a, b in zip(sizes[:-1], sizes[1:])]
            total = total + came[0]
            count = len(group_list)
            if axis_name == "seq":
                group_list = [group_list[0] + came[1]]
            else:
                group_list = group_list + came[1 : 1 + count]
            own_list = own_list + came[1 + count :]
            bit *= 2
    groups = unmix(jnp.stack(group_list), 0, lax.axis_index("rep"))
    owns = jnp.stack(own_list).reshape((n_rep, n_seq) + own.shape)
    owns = unmix(unmix(owns, 0, lax.axis_index("rep")), 1, lax.axis_index("seq"))
    return total, groups, owns


def layer_norm(rows, gain, shift):
    row_mean = jnp.mean(rows, axis=-1, keepdims=True)
    centred = rows - row_mean
    variance = jnp.mean(centred * centred, axis=-1, keepdims=True)
    inverse = lax.rsqrt(variance + EPS)
    normed = centred * inverse
    return (normed * gain + shift, normed, inverse)


def norm_back(grad_rows, normed, inverse, gain):
    scaled = grad_rows * gain
    mean_one = jnp.mean(scaled, axis=-1, keepdims=True)
    mean_two = jnp.mean(scaled * normed, axis=-1, keepdims=True)
    grad_in = inverse * (scaled - mean_one - normed * mean_two)
    return (grad_in, jnp.sum(grad_rows * normed, axis=0), jnp.sum(grad_rows, axis=0))


def features(length, feat_count):
    ramp_unit = jnp.linspace(0.0, 1.0, length, dtype=F32)
    angles = jnp.arange(length, dtype=F32)[:, None] * (2.0 * math.pi / length)
    band_freqs = jnp.linspace(
        0.0001, (feat_count - 1) // 2 - 1.0, (feat_count - 1) // 2, dtype=F32
    )[None, :]
    phase_grid = band_freqs * angles
    grid_out = jnp.concatenate(
        [ramp_unit[:, None], jnp.cos(phase_grid), -jnp.sin(phase_grid)], axis=1
    )
    return (grid_out, ramp_unit)


def filter_columns(
    feature_grid,
    ramp_unit,
    start_chan,
    chan_count,
    model_width,
    feat_weight,
    feat_bias,
    inner_weight,
    inner_bias,
    deep_weight,
    deep_bias,
    sine_freq,
    columns,
):
    freq = sine_freq[:, None]

    def layer(weight, bias, below):
        grown = lax.dot_general(weight, below, (((0,), (0,)), ((), ())), precision=HIGH)
        return jnp.sin(freq * (grown + bias[:, None]))

    hidden = layer(feat_weight, feat_bias, feature_grid.T)
    hidden = layer(inner_weight, inner_bias, hidden)
    hidden = layer(deep_weight, deep_bias, hidden)
    deltas = jnp.abs(
        jnp.linspace(math.log(0.01) / 0.3, math.log(0.01) / 1.5, model_width, dtype=F32)
    )
    local_rates = lax.dynamic_slice_in_dim(deltas, start_chan, chan_count)
    return lax.dot_general(
        columns, hidden, (((0,), (0,)), ((), ())), precision=HIGH
    ) * jnp.exp(-ramp_unit[None, :] * local_rates[:, None])


def sin_cos(x):
    turns = jnp.floor(x * (1.0 / math.pi) + 0.5)
    r = x - turns * 3.140625
    r = r - turns * 9.67502593994140625e-4
    r = r - turns * 1.509957990978376432e-7
    sign = 1.0 - 2.0 * (turns - 2.0 * jnp.floor(turns * 0.5))
    q = r * r
    sin = r + r * q * (
        -1.6666666666e-1
        + q * (8.3333333e-3 + q * (-1.98412698e-4 + q * (2.7557319e-6 + q * -2.505210838e-8)))
    )
    cos = 1.0 + q * (
        -0.5
        + q * (4.16666666e-2 + q * (-1.3888888e-3 + q * (2.48015873e-5 + q * (-2.75573192e-7 + q * 2.0876757e-9))))
    )
    return sin * sign, cos * sign


def dot_high(left, right, dims):
    return lax.dot_general(left, right, (dims, ((), ())), precision=HIGH, preferred_element_type=F32)


def filter_forward_kernel(
    grid_ref, ramp_ref, rate_ref, w1_ref, w2_ref, w3_ref, small_ref, columns_ref, twist_ref, hi_ref, lo_ref,
    spec_ref, sin_ref, cos_ref, z_ref
):
    blocks, length = twist_ref.shape[0], twist_ref.shape[3]
    freq = small_ref[:, 3:4]
    below = grid_ref[...]
    for i, w_ref in enumerate((w1_ref, w2_ref, w3_ref)):
        grown = dot_high(w_ref[...].T, below, ((1,), (0,)))
        sin, cos = sin_cos(freq * (grown + small_ref[:, i : i + 1]))
        sin_ref[i] = sin
        cos_ref[i] = cos
        below = sin
    kern = dot_high(columns_ref[...].T, below, ((1,), (0,))) * jnp.exp(-rate_ref[...] * ramp_ref[...])
    cut = [kern[:, b * length : (b + 1) * length] for b in range(blocks)]
    turn_rows(cut, twist_ref, z_ref, 0, blocks)
    spec_ref[...] = dot_split(z_ref[...], hi_ref[...], lo_ref[...], ((1,), (0,)))


def filter_backward_kernel(
    gk_ref, grid_ref, ramp_ref, rate_ref, w1_ref, w2_ref, w3_ref, small_ref, columns_ref, sin_ref, cos_ref,
    gc_ref, g1_ref, g2_ref, g3_ref, gsmall_ref
):
    freq = small_ref[:, 3:4]
    gk = jnp.concatenate([gk_ref[b] for b in range(gk_ref.shape[0])], axis=1)
    gk = gk * jnp.exp(-rate_ref[...] * ramp_ref[...])
    last = ((1,), (1,))
    gc_ref[...] = dot_high(sin_ref[2], gk, last)
    grad = dot_high(columns_ref[...], gk, ((1,), (0,)))
    gfreq = jnp.zeros(freq.shape, F32)
    gbias = [None] * 3
    for i, w_ref, g_ref in ((2, w3_ref, g3_ref), (1, w2_ref, g2_ref), (0, w1_ref, g1_ref)):
        turn = grad * cos_ref[i]
        below = sin_ref[i - 1] if i else grid_ref[...]
        raw = dot_high(turn, below, last)
        total = jnp.sum(turn, axis=1, keepdims=True)
        g_ref[...] = raw * freq
        gbias[i] = total * freq
        gfreq = gfreq + jnp.sum(raw * w_ref[...].T, axis=1, keepdims=True) + total * small_ref[:, i : i + 1]
        if i:
            grad = dot_high(w_ref[...], turn * freq, ((1,), (0,)))
    gsmall_ref[...] = jnp.concatenate(gbias + [gfreq], axis=1)


def feature_table(length, feat_count):
    ramp = np.linspace(0.0, 1.0, length, dtype=np.float32)
    angles = np.arange(length, dtype=np.float32)[:, None] * np.float32(2.0 * math.pi / length)
    half = (feat_count - 1) // 2
    bands = np.linspace(0.0001, half - 1.0, half, dtype=np.float32)[None, :]
    phase = (bands * angles).astype(np.float64)
    table = np.concatenate([ramp[:, None], np.cos(phase), -np.sin(phase)], axis=1)
    return np.ascontiguousarray(table.T).astype(np.float32), ramp[None, :]


def decay_rates(model):
    return np.abs(
        np.linspace(math.log(0.01) / 0.3, math.log(0.01) / 1.5, model, dtype=np.float32)
    )[:, None]


def transform_tables(blocks, length):
    time = np.arange(blocks * length).reshape(blocks, 1, length)
    cls = np.arange(blocks).reshape(1, blocks, 1)
    period = 4 * blocks * length
    turn = (time * (2 * cls + 1)) % period * (2.0 * np.pi / period)
    twist = np.stack([np.cos(turn), -np.sin(turn)], axis=2).astype(np.float32)
    step = np.arange(length)
    turn = (step[:, None] * step[None, :]) % length * (2.0 * np.pi / length)
    cos, sin = np.cos(turn), np.sin(turn)
    table = np.block([[cos, -sin], [sin, cos]]).astype(np.float32)
    return twist, table


def split_table(table):
    hi = table.astype(B16)
    return jnp.asarray(hi), jnp.asarray((table - hi.astype(np.float32)).astype(B16))


def spectrum_of(signal, twist, table):
    turned = jnp.einsum("bqzl,brl->qrzl", twist[: signal.shape[0]], signal, precision=HIGH)
    flat = turned.reshape(turned.shape[:2] + (-1,))
    return jnp.einsum("qrk,kf->qrf", flat, table, precision=HIGH)


def signal_of(spectrum, twist, table):
    blocks, length = twist.shape[0], twist.shape[3]
    turned = jnp.einsum("qrf,kf->qrk", spectrum, table, precision=HIGH)
    turned = turned.reshape(turned.shape[:2] + (2, length))
    return jnp.einsum("bqzl,qrzl->brl", twist, turned, precision=HIGH) * (1.0 / (blocks * length))


def times(left, right, conj_right):
    half = left.shape[-1] // 2
    lr, li = left[..., :half], left[..., half:]
    rr, ri = right[..., :half], right[..., half:]
    if conj_right:
        return jnp.concatenate([lr * rr + li * ri, li * rr - lr * ri], axis=-1)
    return jnp.concatenate([lr * rr - li * ri, lr * ri + li * rr], axis=-1)


def dot_split(values, hi, lo, dims):
    top = values.astype(B16)
    rest = (values - top.astype(F32)).astype(B16)
    dot = partial(lax.dot_general, dimension_numbers=(dims, ((), ())), preferred_element_type=F32)
    return dot(top, hi) + dot(rest, hi) + dot(top, lo)


def turn_rows(blocks_in, twist_ref, z_ref, base, classes):
    rows, length = blocks_in[0].shape
    for q in range(classes):
        for z in range(2):
            acc = None
            for b, block in enumerate(blocks_in):
                term = block * twist_ref[b, q, z : z + 1]
                acc = term if acc is None else acc + term
            z_ref[base + q * rows : base + (q + 1) * rows, z * length : (z + 1) * length] = acc


def back_rows(w, base, rows, block, twist_ref, classes):
    length = w.shape[1] // 2
    acc = None
    for q in range(classes):
        lo, hi = base + q * rows, base + (q + 1) * rows
        for z in range(2):
            term = w[lo:hi, z * length : (z + 1) * length] * twist_ref[block, q, z : z + 1]
            acc = term if acc is None else acc + term
    return acc * (1.0 / (classes * length))


def conv_forward_kernel(short_blocks, x_ref, kern_ref, twist_ref, hi_ref, lo_ref, skip_ref, out_ref, spec_ref, z_ref):
    blocks = twist_ref.shape[0]
    rows = x_ref.shape[1]
    span = blocks * rows
    first = [x_ref[b].astype(F32) for b in range(blocks)]
    second = [x_ref[blocks + b].astype(F32) for b in range(short_blocks)]
    turn_rows(first, twist_ref, z_ref, 0, blocks)
    turn_rows(second, twist_ref, z_ref, span, blocks)
    spec = dot_split(z_ref[...], hi_ref[...], lo_ref[...], ((1,), (0,)))
    spec_ref[...] = spec
    kern = kern_ref[...]
    prod = jnp.concatenate([times(spec[:span], kern, False), times(spec[span:], kern, False)], axis=0)
    w = dot_split(prod, hi_ref[...], lo_ref[...], ((1,), (1,)))
    skip = skip_ref[...]
    for b in range(blocks):
        out_ref[b] = (back_rows(w, 0, rows, b, twist_ref, blocks) + skip * first[b]).astype(B16)
        acc = back_rows(w, span, rows, b, twist_ref, blocks)
        if b < short_blocks:
            acc = acc + skip * second[b]
        out_ref[blocks + b] = acc.astype(B16)


def conv_backward_kernel(
    short_blocks, g_ref, spec_ref, kern_ref, twist_ref, hi_ref, lo_ref, skip_ref, out_ref, grad_kern_ref, z_ref, p_ref
):
    blocks = twist_ref.shape[0]
    rows = g_ref.shape[1]
    span = blocks * rows
    first = [g_ref[b].astype(F32) for b in range(blocks)]
    second = [g_ref[blocks + b].astype(F32) for b in range(short_blocks)]
    turn_rows(first, twist_ref, z_ref, 0, blocks)
    turn_rows(second, twist_ref, z_ref, span, blocks)
    grad = dot_split(z_ref[...], hi_ref[...], lo_ref[...], ((1,), (0,)))
    kern = kern_ref[...]
    p_ref[0:span] = times(grad[:span], kern, True)
    p_ref[span : 2 * span] = times(grad[span:], kern, True)
    p_ref[2 * span :] = times(grad[:span], spec_ref[0:span], True) + times(
        grad[span:], spec_ref[span:], True
    )
    w = dot_split(p_ref[...], hi_ref[...], lo_ref[...], ((1,), (1,)))
    skip = skip_ref[...]
    for b in range(blocks):
        out_ref[b] = (back_rows(w, 0, rows, b, twist_ref, blocks) + skip * first[b]).astype(B16)
        if b < short_blocks:
            acc = back_rows(w, span, rows, b, twist_ref, blocks) + skip * second[b]
            out_ref[blocks + b] = acc.astype(B16)
        else:
            out_ref[blocks + b] = jnp.zeros(out_ref.shape[1:], B16)
        grad_kern_ref[b] = back_rows(w, 2 * span, rows, b, twist_ref, blocks)


def conv_forward(received, kern_spec, twist, table, skip_local):
    blocks, rows, length = received.shape[0] // 2, received.shape[1], received.shape[2]
    short_blocks = -(-blocks // 4)
    skip = skip_local[:, None]
    if blocks != 4:
        x = received.astype(F32)
        spec = jnp.concatenate(
            [
                spectrum_of(x[:blocks], twist, table),
                spectrum_of(x[blocks : blocks + short_blocks], twist, table),
            ],
            axis=0,
        )
        kern = jnp.concatenate([kern_spec, kern_spec], axis=0)
        prod = times(spec, kern, False)
        out = jnp.concatenate(
            [signal_of(prod[:blocks], twist, table), signal_of(prod[blocks:], twist, table)], axis=0
        )
        return ((out + skip * x).astype(B16), spec)
    hi, lo = split_table(table)
    height = 2 * blocks * rows
    out, spec = pl.pallas_call(
        partial(conv_forward_kernel, short_blocks),
        out_shape=(
            jax.ShapeDtypeStruct(received.shape, B16),
            jax.ShapeDtypeStruct((height, 2 * length), F32),
        ),
        scratch_shapes=[pltpu.VMEM((height, 2 * length), F32)],
        compiler_params=pltpu.CompilerParams(vmem_limit_bytes=VMEM_BYTES),
        name="conv_forward",
    )(received, kern_spec.reshape(blocks * rows, 2 * length), twist, hi, lo, skip)
    return out, spec


def conv_backward(grads, spec, kern_spec, twist, table, skip_local):
    blocks, rows, length = grads.shape[0] // 2, grads.shape[1], grads.shape[2]
    short_blocks = -(-blocks // 4)
    skip = skip_local[:, None]
    if blocks != 4:
        g = grads.astype(F32)
        first = spectrum_of(g[:blocks], twist, table)
        second = spectrum_of(g[blocks : blocks + short_blocks], twist, table)
        one = signal_of(times(first, kern_spec, True), twist, table)
        two = signal_of(times(second, kern_spec, True), twist, table)
        cross = times(first, spec[:blocks], True) + times(second, spec[blocks:], True)
        out = jnp.concatenate([one, two], axis=0) + skip * g
        return (out.astype(B16), signal_of(cross, twist, table))
    hi, lo = split_table(table)
    span = blocks * rows
    out, grad_kern = pl.pallas_call(
        partial(conv_backward_kernel, short_blocks),
        out_shape=(
            jax.ShapeDtypeStruct(grads.shape, B16),
            jax.ShapeDtypeStruct((blocks, rows, length), F32),
        ),
        scratch_shapes=[
            pltpu.VMEM((2 * span, 2 * length), F32),
            pltpu.VMEM((3 * span, 2 * length), F32),
        ],
        compiler_params=pltpu.CompilerParams(vmem_limit_bytes=VMEM_BYTES),
        name="conv_backward",
    )(grads, spec, kern_spec.reshape(span, 2 * length), twist, hi, lo, skip)
    return out, grad_kern


def in_order(ref, rep, lead=()):
    count = ref.shape[-1] // LANE
    return [
        ref[lead + (slice(None), pl.ds(pl.multiple_of((rep ^ j) * LANE, LANE), LANE))]
        for j in range(count)
    ]


def put_rel(ref, rep, values, lead=()):
    for j in range(ref.shape[-1] // LANE):
        ref[lead + (slice(None), pl.ds(pl.multiple_of((rep ^ j) * LANE, LANE), LANE))] = values[
            :, j * LANE : (j + 1) * LANE
        ]


def extended(proj_ref, halo_ref, exists, rep, p):
    blocks = [halo_ref[p, :, :LANE]] + in_order(proj_ref, rep, (p,)) + [halo_ref[p, :, LANE:]]
    return jnp.concatenate(blocks, axis=1).astype(F32) * exists


def short_of(ext, col_ref, p):
    return (
        col_ref[:, p : p + 1] * pltpu.roll(ext, 2, 1)
        + col_ref[:, 3 + p : 4 + p] * pltpu.roll(ext, 1, 1)
        + col_ref[:, 6 + p : 7 + p] * ext
        + col_ref[:, 9 + p : 10 + p]
    )


def gate_kernel(rep_ref, proj_ref, halo_ref, col_ref, mask_ref, out_ref):
    rep = rep_ref[0]
    mask, exists = mask_ref[0:1], mask_ref[1:2]
    gate_in = short_of(extended(proj_ref, halo_ref, exists, rep, 1), col_ref, 1)
    values = short_of(extended(proj_ref, halo_ref, exists, rep, 2), col_ref, 2)
    gated = values * gate_in * mask
    out_ref[...] = gated[:, LANE:-LANE].astype(B16)


def output_kernel(rep_ref, proj_ref, halo_ref, col_ref, mask_ref, mixed_ref, out_ref):
    rep = rep_ref[0]
    gate_out = short_of(extended(proj_ref, halo_ref, mask_ref[1:2], rep, 0), col_ref, 0)
    put_rel(out_ref, rep, (gate_out[:, LANE:-LANE] * mixed_ref[...].astype(F32)).astype(B16))


def grad_mix_kernel(rep_ref, proj_ref, halo_ref, col_ref, mask_ref, mixed_ref, gy_ref, out_ref, first_ref):
    rep = rep_ref[0]
    gate_out = short_of(extended(proj_ref, halo_ref, mask_ref[1:2], rep, 0), col_ref, 0)
    gy = jnp.concatenate(in_order(gy_ref, rep), axis=1).astype(F32)
    out_ref[...] = (gy * gate_out[:, LANE:-LANE]).astype(B16)
    first_ref[...] = gy[:, :LANE] * mixed_ref[:, :LANE].astype(F32)


def grad_proj_kernel(
    rep_ref, proj_ref, halo_ref, col_ref, mask_ref, mixed_ref, gy_ref, ggated_ref, gnext_ref, onext_ref, out_ref, sum_ref
):
    rep = rep_ref[0]
    mask, exists = mask_ref[0:1], mask_ref[1:2]
    size = mask_ref.shape[1]
    mid = slice(LANE, size - LANE)
    gy = jnp.concatenate(in_order(gy_ref, rep), axis=1).astype(F32)
    zero = jnp.zeros((gy.shape[0], LANE), F32)
    next_on = exists[:, size - LANE :]
    ext = [extended(proj_ref, halo_ref, exists, rep, p) for p in range(3)]
    short = [short_of(ext[p], col_ref, p) for p in range(3)]
    ggated = jnp.concatenate(
        [zero, ggated_ref[...].astype(F32), gnext_ref[...].astype(F32) * next_on], axis=1
    )
    ggated = ggated * mask
    gout = gy * mixed_ref[...].astype(F32)
    gshort = [
        jnp.concatenate([zero, gout, onext_ref[...] * next_on], axis=1),
        ggated * short[2],
        ggated * short[1],
    ]
    gated = short[2][:, mid] * short[1][:, mid] * mask[:, mid]
    sums = [jnp.sum(gy * short[0][:, mid] * gated, axis=1, keepdims=True)]
    for p in range(3):
        mine = gshort[p][:, mid]
        sums.append(jnp.sum(mine, axis=1, keepdims=True))
        sums.append(jnp.sum(mine * ext[p][:, mid], axis=1, keepdims=True))
        sums.append(jnp.sum(mine * pltpu.roll(ext[p], 1, 1)[:, mid], axis=1, keepdims=True))
        sums.append(jnp.sum(mine * pltpu.roll(ext[p], 2, 1)[:, mid], axis=1, keepdims=True))
        gproj = (
            col_ref[:, 6 + p : 7 + p] * gshort[p]
            + col_ref[:, 3 + p : 4 + p] * pltpu.roll(gshort[p], size - 1, 1)
            + col_ref[:, p : p + 1] * pltpu.roll(gshort[p], size - 2, 1)
        )[:, mid].astype(B16)
        sums.append(jnp.sum(gproj.astype(F32), axis=1, keepdims=True))
        put_rel(out_ref, rep, gproj, (p,))
    sum_ref[...] = jnp.concatenate(sums, axis=1)


def token_call(kernel, name, arrays, outs):
    step = 64

    def spec(shape, cut):
        if not cut:
            return pl.BlockSpec(shape, lambda i: (0,) * len(shape))
        if len(shape) == 3:
            return pl.BlockSpec((shape[0], step, shape[2]), lambda i: (0, i, 0))
        return pl.BlockSpec((step, shape[1]), lambda i: (i, 0))

    width = outs[0].shape[-2]
    return pl.pallas_call(
        kernel,
        grid=(width // step,),
        in_specs=[pl.BlockSpec(memory_space=pltpu.SMEM)] + [spec(a.shape, cut) for a, cut in arrays[1:]],
        out_specs=[spec(o.shape, True) for o in outs],
        out_shape=outs,
        compiler_params=pltpu.CompilerParams(vmem_limit_bytes=VMEM_BYTES),
        name=name,
    )(*[a for a, _ in arrays])


def rows128(values):
    flat = values.reshape(-1)
    return jnp.pad(flat, (0, -flat.shape[0] % 1024)).reshape(-1, 128)


def per_device(
    tokens,
    cotangent,
    lengths,
    in_weight,
    in_bias,
    short_taps,
    short_bias,
    feat_weight,
    feat_bias,
    inner_weight,
    inner_bias,
    deep_weight,
    deep_bias,
    sine_freq,
    kernel_weight,
    skip_gain,
    out_weight,
    out_bias,
    norm1_gain,
    norm1_shift,
    norm2_gain,
    norm2_shift,
    up_weight,
    up_bias,
    down_weight,
    down_bias,
):
    n_seq, n_rep = lax.axis_size("seq"), lax.axis_size("rep")
    seq, rep = lax.axis_index("seq"), lax.axis_index("rep")
    tok_rows, model = tokens.shape
    group = tok_rows * n_rep
    blocks = n_seq // 2
    seq_len = blocks * group
    chan = model // (n_seq * n_rep)
    width = model // n_rep
    hidden = up_weight.shape[2]
    block_start = rep * width
    chan_start = block_start + seq * chan
    rep_scalar = jnp.reshape(rep, (1,)).astype(jnp.int32)

    item_len = jnp.where(seq // blocks == 0, lengths[0], lengths[1])
    at = (seq % blocks) * group
    row_mask = (at + rep * tok_rows + jnp.arange(tok_rows, dtype=jnp.int32) < item_len).astype(F32)[:, None]
    position = at - LANE + jnp.arange(group + 2 * LANE, dtype=jnp.int32)
    mask_ext = jnp.stack([position < item_len, (position >= 0) & (position < seq_len)]).astype(F32)
    mask_ext = jnp.pad(mask_ext, ((0, 6), (0, 0)))

    full_in = ring_gather(in_weight[0]).reshape(model, 3, width)
    full_out = spread_gather(out_weight[0])
    full_up = lax.all_gather(up_weight[0], "seq", axis=0, tiled=True)
    full_down = lax.all_gather(down_weight[0], "seq", axis=0, tiled=True)

    residual = tokens.astype(F32)
    normed_one, unit_one, scale_one = layer_norm(residual, norm1_gain[0], norm1_shift[0])
    normed_one = normed_one.astype(B16)
    rows_one = gather_rel(normed_one)
    rel = rows_one.reshape(n_rep, tok_rows, model)
    last_rows = lax.dynamic_index_in_dim(rel, rep ^ (n_rep - 1), 0, False)[-HALO:]
    first_rows = lax.dynamic_index_in_dim(rel, rep, 0, False)[:HALO]
    before = shift_seq(last_rows, 1)
    after = shift_seq(first_rows, -1)
    gap = jnp.zeros((LANE - HALO, model), B16)
    halo_rows = jnp.concatenate([gap, before, after, gap], axis=0)
    proj_bias = lax.dynamic_slice_in_dim(in_bias[0], block_start, width, 1)[:, :, None]

    def project(rows):
        return (
            jnp.einsum("td,dpc->pct", rows, full_in, preferred_element_type=F32) + proj_bias
        ).astype(B16)

    proj = project(rows_one)
    halo = project(halo_rows)

    tap_cols = lax.dynamic_slice_in_dim(short_taps[0], block_start, width, 2).reshape(9, width)
    bias_cols = lax.dynamic_slice_in_dim(short_bias[0], block_start, width, 1)
    cols = jnp.pad(jnp.concatenate([tap_cols, bias_cols], axis=0), ((0, 4), (0, 0))).T
    common = [(rep_scalar, True), (proj, True), (halo, True), (cols, True), (mask_ext, False)]
    flat_shape = jax.ShapeDtypeStruct((width, group), B16)
    (gated,) = token_call(gate_kernel, "gate", common, [flat_shape])
    received = lax.all_to_all(gated.reshape(n_seq, chan, group), "seq", 0, 0, tiled=True)

    skip_local = lax.dynamic_slice_in_dim(skip_gain[0], chan_start, chan, 0)
    columns = lax.dynamic_slice_in_dim(kernel_weight[0], chan_start, chan, 1)
    twist, table = transform_tables(blocks, group)
    nets = (feat_weight[0], inner_weight[0], deep_weight[0])
    if blocks == 4:
        grid, ramp = feature_table(seq_len, feat_weight.shape[1])
        rates = lax.dynamic_slice_in_dim(jnp.asarray(decay_rates(model)), chan_start, chan, 0)
        smalls = jnp.concatenate([feat_bias, inner_bias, deep_bias, sine_freq], axis=0).T
        filt = smalls.shape[0]
        hi, lo = split_table(table)
        kern_spec, sines, cosines = pl.pallas_call(
            filter_forward_kernel,
            out_shape=(
                jax.ShapeDtypeStruct((blocks * chan, 2 * group), F32),
                jax.ShapeDtypeStruct((3, filt, seq_len), F32),
                jax.ShapeDtypeStruct((3, filt, seq_len), F32),
            ),
            scratch_shapes=[pltpu.VMEM((blocks * chan, 2 * group), F32)],
            compiler_params=pltpu.CompilerParams(vmem_limit_bytes=VMEM_BYTES),
            cost_estimate=pl.CostEstimate(flops=10**6, bytes_accessed=10**6, transcendentals=0),
            name="filter_forward",
        )(grid, ramp, rates, *nets, smalls, columns, twist, hi, lo)
        kern_spec = kern_spec.reshape(blocks, chan, 2 * group)

        def kernel_pull(grad_kernel):
            shapes = [columns.shape] + [w.shape[::-1] for w in nets] + [smalls.shape]
            gcols, g1, g2, g3, gsmalls = pl.pallas_call(
                filter_backward_kernel,
                out_shape=tuple(jax.ShapeDtypeStruct(shape, F32) for shape in shapes),
                compiler_params=pltpu.CompilerParams(vmem_limit_bytes=VMEM_BYTES),
                cost_estimate=pl.CostEstimate(flops=10**6, bytes_accessed=10**6, transcendentals=0),
                name="filter_backward",
            )(grad_kernel, grid, ramp, rates, *nets, smalls, columns, sines, cosines)
            gs = gsmalls.T
            return (g1.T, gs[0], g2.T, gs[1], g3.T, gs[2], gs[3], gcols)

    else:
        feature_grid, ramp_unit = features(seq_len, feat_weight.shape[1])
        kernel, pull = jax.vjp(
            partial(filter_columns, feature_grid, ramp_unit, chan_start, chan, model),
            feat_weight[0],
            feat_bias[0],
            inner_weight[0],
            inner_bias[0],
            deep_weight[0],
            deep_bias[0],
            sine_freq[0],
            columns,
        )
        kern_spec = spectrum_of(kernel.reshape(chan, blocks, group).transpose(1, 0, 2), twist, table)

        def kernel_pull(grad_kernel):
            return pull(grad_kernel.transpose(1, 0, 2).reshape(chan, seq_len))

    mixed_chan, kept_spec = conv_forward(received, kern_spec, twist, table, skip_local)
    mixed = lax.all_to_all(mixed_chan, "seq", 0, 0, tiled=True).reshape(width, group)
    (y_cols,) = token_call(output_kernel, "output", common + [(mixed, True)], [flat_shape])

    middle_part = jnp.einsum("ct,oc->to", y_cols, full_out, preferred_element_type=F32)
    middle = residual + (scatter_rel(middle_part) + out_bias[0])
    normed_two, unit_two, scale_two = layer_norm(middle, norm2_gain[0], norm2_shift[0])
    rows_two = gather_rel(normed_two.astype(B16))

    grad_top = cotangent.astype(F32) * row_mask
    grad_mlp = grad_top.astype(B16)
    mlp_rows = gather_rel(grad_mlp)
    grad_act = jnp.dot(mlp_rows, full_down, preferred_element_type=F32)
    up_block = lax.dynamic_slice_in_dim(up_bias[0], rep * hidden, hidden, 0)
    pre_act = jnp.dot(rows_two, full_up, preferred_element_type=F32) + up_block
    phi = 0.5 * (1.0 + lax.erf(pre_act * math.sqrt(0.5)))
    act_rows = (pre_act * phi).astype(B16)
    slope = phi + pre_act * (jnp.exp(-0.5 * pre_act * pre_act) * (1.0 / math.sqrt(2.0 * math.pi)))
    grad_pre = (grad_act * slope).astype(B16)
    grad_two = scatter_rel(jnp.einsum("tf,df->td", grad_pre, full_up, preferred_element_type=F32))
    mlp_part = jnp.einsum("tf,of->to", act_rows, full_down, preferred_element_type=F32)
    layer_out = (middle + (scatter_rel(mlp_part) + down_bias[0])).astype(B16)
    term_down = jnp.einsum("to,tf->of", mlp_rows, act_rows, preferred_element_type=F32)
    term_up = jnp.einsum("td,tf->df", rows_two, grad_pre, preferred_element_type=F32)
    grad_two, term_down = lax.optimization_barrier((grad_two, term_down.astype(B16)))
    grad_down_bias = jnp.sum(grad_mlp.astype(F32), axis=0)
    grad_up_block = jnp.sum(grad_pre.astype(F32), axis=0)

    grad_down = lax.psum_scatter(
        term_down, "seq", scatter_dimension=0, tiled=True
    ).astype(F32)
    grad_up = ring_scatter(term_up.astype(B16))

    grad_unit_two, grad_gain_two, grad_shift_two = norm_back(
        grad_two, unit_two, scale_two, norm2_gain[0]
    )
    grad_middle = grad_top + grad_unit_two
    grad_mix = grad_middle.astype(B16)
    grad_out_bias = jnp.sum(grad_mix.astype(F32), axis=0)
    mix_rows = gather_rel(grad_mix)
    gy_cols = jnp.einsum("to,oc->ct", mix_rows, full_out, preferred_element_type=F32).astype(B16)
    term_out = jnp.einsum("to,ct->oc", mix_rows, y_cols, preferred_element_type=F32)
    grad_out = halve_scatter(term_out.astype(B16))

    grad_mixed, gate_first = token_call(
        grad_mix_kernel,
        "grad_mix",
        common + [(mixed, True), (gy_cols, True)],
        [flat_shape, jax.ShapeDtypeStruct((width, LANE), F32)],
    )
    gate_next = shift_seq(gate_first, -1)
    grads_chan = lax.all_to_all(grad_mixed.reshape(n_seq, chan, group), "seq", 0, 0, tiled=True)
    ggated_chan, grad_kernel = conv_backward(grads_chan, kept_spec, kern_spec, twist, table, skip_local)
    ggated = lax.all_to_all(ggated_chan, "seq", 0, 0, tiled=True).reshape(width, group)
    ggated_next = shift_seq(ggated[:, :LANE], -1)
    kernel_grads = kernel_pull(grad_kernel)
    grad_proj, col_sums = token_call(
        grad_proj_kernel,
        "grad_proj",
        common
        + [(mixed, True), (gy_cols, True), (ggated, True), (ggated_next, True), (gate_next, True)],
        [jax.ShapeDtypeStruct((3, width, group), B16), jax.ShapeDtypeStruct((width, 16), F32)],
    )

    one_part = jnp.einsum("pct,dpc->td", grad_proj, full_in, preferred_element_type=F32)
    grad_one = scatter_rel(one_part)
    term_in = jnp.einsum("td,pct->dpc", rows_one, grad_proj, preferred_element_type=F32)
    grad_in = halve_scatter(term_in.reshape(model, 3 * width).astype(B16))
    grad_in = grad_in.reshape(-1, 3, width)
    grad_unit_one, grad_gain_one, grad_shift_one = norm_back(
        grad_one, unit_one, scale_one, norm1_gain[0]
    )
    grad_tokens = grad_middle + grad_unit_one

    totals = [
        *kernel_grads[:7],
        grad_gain_one,
        grad_shift_one,
        grad_gain_two,
        grad_shift_two,
        grad_out_bias,
        grad_down_bias,
    ]
    packed = [rows128(t) for t in totals]
    group_part = jnp.concatenate([rows128(col_sums.T), rows128(grad_up_block)], axis=0)
    total, groups, owns = sync_small(jnp.concatenate(packed, axis=0), group_part, rows128(kernel_grads[7]))
    outs = []
    start = 0
    for t, p in zip(totals, packed):
        outs.append(total[start : start + p.shape[0]].reshape(-1)[: t.size].reshape((1,) + t.shape))
        start += p.shape[0]
    flat = groups.reshape(n_rep, -1)
    sums = flat[:, : 16 * width].reshape(n_rep, 16, width).transpose(1, 0, 2).reshape(16, model)
    grad_up_bias = flat[:, 16 * width : 16 * width + hidden].reshape(1, -1)
    filt = columns.shape[0]
    grad_kernel_weight = (
        owns.reshape(n_rep, n_seq, -1)[:, :, : filt * chan]
        .reshape(n_rep, n_seq, filt, chan)
        .transpose(2, 0, 1, 3)
        .reshape(1, filt, model)
    )
    pick = lambda offset: jnp.stack([sums[1 + 5 * p + offset] for p in range(3)])
    grad_skip = sums[0][None]
    grad_short_bias = pick(0)[None]
    grad_short_taps = jnp.stack([pick(3), pick(2), pick(1)])[None]
    grad_in_bias = pick(4)[None]
    return (
        layer_out,
        grad_tokens,
        grad_in[None],
        grad_in_bias,
        grad_short_taps,
        grad_short_bias,
        outs[0],
        outs[1],
        outs[2],
        outs[3],
        outs[4],
        outs[5],
        outs[6],
        grad_kernel_weight,
        grad_skip,
        grad_out[None],
        outs[11],
        outs[7],
        outs[8],
        outs[9],
        outs[10],
        grad_up[None],
        grad_up_bias,
        grad_down[None],
        outs[12],
    )


NN = ((1,), (0,))
NT = ((1,), (1,))
TN = ((0,), (0,))
PART = 64
REP, SEQ, AT, ITEM, OLDER, YOUNGER, OWNER, LEFT, RIGHT = 0, 1, 2, 3, 4, 5, 8, 16, 25
RING = [0, 2, 4, 6, 7, 5, 3, 1]
AHEAD = [(RING[i], RING[(i + 1) % 8]) for i in range(8)]
BACK = [(b, a) for a, b in AHEAD]


def meta_table(group):
    rows = []
    for seq in range(8):
        p = RING.index(seq)
        for rep in range(4):
            row = [rep, seq, (seq % 4) * group, seq // 4, int(seq % 4 != 0), int(seq % 4 != 3), 0, 0]
            row += [RING[(p + k) % 8] for k in (0, -1, 1, -2, 2, -3, 3, 4)]
            row += [RING[(p - k) % 8] for k in range(9)]
            row += [RING[(p + k) % 8] for k in range(9)]
            rows.append(row)
    return np.asarray(rows, np.int32)


COST = {"start": 4000, "setup": 4000, "filter_ahead": 6000}


def call(kernel, name, args, outs, scratch=(), limit=24, away=(), out_away=(), raw=()):
    away, out_away, raw = list(away), list(out_away), list(raw)
    hbm = pl.BlockSpec(memory_space=pltpu.HBM)

    def space(i, a):
        if i in away or i in raw:
            return hbm
        small = a.dtype == jnp.int32
        return pl.BlockSpec(memory_space=pltpu.SMEM if small else pltpu.VMEM)

    n_in, n_out, n_own = len(args), len(outs), len(scratch)
    bufs = [pltpu.VMEM(args[i].shape, args[i].dtype) for i in away]
    bufs += [pltpu.VMEM(outs[i].shape, outs[i].dtype) for i in out_away]
    sems = [pltpu.SemaphoreType.DMA((len(bufs),))] if bufs else []

    def body(*refs):
        ins, results = list(refs[:n_in]), list(refs[n_in : n_in + n_out])
        own, mine = refs[n_in + n_out : n_in + n_out + n_own], refs[n_in + n_out + n_own :]
        copies = []
        for k, i in enumerate(away):
            copies.append(pltpu.make_async_copy(ins[i], mine[k], mine[-1].at[k]))
            ins[i] = mine[k]
        for copy in copies:
            copy.start()
        for copy in copies:
            copy.wait()
        copies = []
        for k, i in enumerate(out_away, len(away)):
            copies.append(pltpu.make_async_copy(mine[k], results[i], mine[-1].at[k]))
            results[i] = mine[k]
        kernel(*ins, *results, *own)
        for copy in copies:
            copy.start()
        for copy in copies:
            copy.wait()

    return pl.pallas_call(
        body,
        out_shape=outs,
        in_specs=[space(i, a) for i, a in enumerate(args)],
        out_specs=[hbm if i in out_away or (-1 - i) in raw else pl.BlockSpec(memory_space=pltpu.VMEM) for i in range(n_out)],
        scratch_shapes=list(scratch) + bufs + sems,
        compiler_params=pltpu.CompilerParams(vmem_limit_bytes=limit * 2**20),
        cost_estimate=pl.CostEstimate(flops=COST.get(name, 1) * 10**6, bytes_accessed=10**5, transcendentals=0),
        name=name,
    )(*args)


def shape(dims, kind):
    return jax.ShapeDtypeStruct(tuple(dims), kind)


def dot(left, right, dims):
    return lax.dot_general(left, right, (dims, ((), ())), preferred_element_type=F32)


def place(index):
    return pl.ds(pl.multiple_of(index * LANE, LANE), LANE)


def normed_of(rows):
    centred = rows - jnp.mean(rows, axis=1, keepdims=True)
    inverse = lax.rsqrt(jnp.mean(centred * centred, axis=1, keepdims=True) + EPS)
    return centred * inverse, inverse


def item_length(meta_ref, len_ref):
    return jnp.where(meta_ref[ITEM] == 0, len_ref[0], len_ref[1])


def lane_masks(meta_ref, len_ref, size):
    lane = lax.broadcasted_iota(jnp.int32, (1, size), 1)
    real = (meta_ref[AT] - LANE + lane < item_length(meta_ref, len_ref)).astype(F32)
    older, younger = meta_ref[OLDER].astype(F32), meta_ref[YOUNGER].astype(F32)
    exists = jnp.where(lane < LANE, older, jnp.where(lane >= size - LANE, younger, 1.0))
    return real, exists


def start_kernel(x_ref, gain_ref, shift_ref, in_ref, out_w_ref, out_ref, io_ref):
    width = out_w_ref.shape[2]
    for p in range(3):
        io_ref[:, p * width : (p + 1) * width] = in_ref[p]
    io_ref[:, 3 * width :] = out_w_ref[0]
    unit, _ = normed_of(x_ref[...].astype(F32))
    out_ref[...] = (unit * gain_ref[...] + shift_ref[...]).astype(B16)


def halves_kernel(left_ref, right_ref, a_ref, b_ref):
    half = a_ref.shape[0]
    a_ref[...] = left_ref[:half]
    b_ref[...] = right_ref[half:]


def assemble_kernel(meta_ref, p0, p1, p2, p3, p4, p5, p6, a_ref, b_ref, out_ref):
    for k, ref in enumerate((p0, p1, p2, p3, p4, p5, p6)):
        out_ref[meta_ref[OWNER + k]] = ref[...]
    half = a_ref.shape[0]
    out_ref[meta_ref[OWNER + 7], :half] = a_ref[...]
    out_ref[meta_ref[OWNER + 7], half:] = b_ref[...]


def own_mask(meta_ref, len_ref, rows):
    row = lax.broadcasted_iota(jnp.int32, (rows, 1), 0)
    return (meta_ref[AT] + meta_ref[REP] * rows + row < item_length(meta_ref, len_ref)).astype(F32)


def setup_kernel(
    meta_ref, len_ref, top_ref, up_ref, down_ref, taps_ref, short_bias_ref, in_bias_ref, up_bias_ref, skip_ref, rate_ref,
    kern_w_ref, feat_ref, fb_ref, ib_ref, db_ref, sf_ref,
    rows_ref, ud_ref, cols_ref, upb_ref, chan_ref, columns_ref, small_col_ref, small_row_ref, w1_ref, *rest
):
    sems = rest[-1]
    copies = [
        pltpu.make_async_copy(up_ref, ud_ref.at[pl.ds(0, 1)], sems.at[0]),
        pltpu.make_async_copy(down_ref, ud_ref.at[pl.ds(1, 1)], sems.at[1]),
    ]
    for copy in copies:
        copy.start()
    top, taps, short_bias, in_bias, up_bias, skip, rate, kern_w, feat, fb, ib, db, sf = (
        top_ref, taps_ref, short_bias_ref, in_bias_ref, up_bias_ref, skip_ref, rate_ref, kern_w_ref, feat_ref,
        fb_ref, ib_ref, db_ref, sf_ref,
    )
    mask = own_mask(meta_ref, len_ref, top.shape[0])
    rows_ref[...] = (top[...].astype(F32) * mask).astype(B16)
    width = cols_ref.shape[0]
    chan = chan_ref.shape[0]
    rep, seq = meta_ref[REP], meta_ref[SEQ]
    lanes = pl.ds(pl.multiple_of(rep * width, width), width)
    rows = [taps[j, p, :, lanes] for j in range(3) for p in range(3)]
    rows += [short_bias[p, :, lanes] for p in range(3)] + [in_bias[p, :, lanes] for p in range(3)]
    stack = jnp.concatenate(rows + [jnp.zeros((LANE - 15, width), F32)], axis=0)
    cols_ref[...] = stack.T[:, :16]
    upb_ref[...] = up_bias[:, pl.ds(pl.multiple_of(rep * upb_ref.shape[1], LANE), upb_ref.shape[1])]
    turn = width - seq * chan
    stack = jnp.concatenate([skip[:, lanes], rate[:, lanes], jnp.zeros((LANE - 2, width), F32)], axis=0)
    chan_ref[...] = pltpu.roll(stack, turn, 1)[:, :LANE].T[:chan, :2]
    columns_ref[...] = pltpu.roll(kern_w[0, :, lanes], turn, 1)[:, :chan]
    filt = small_row_ref.shape[1]
    small = jnp.concatenate([fb[...], ib[...], db[...], sf[...]], axis=0)
    small_row_ref[...] = small
    wide = jnp.concatenate([small, jnp.zeros((4, LANE - filt), F32)], axis=1)
    wide = jnp.concatenate([wide, jnp.zeros((LANE - 4, LANE), F32)], axis=0)
    small_col_ref[...] = wide.T[:filt, :4]
    w1_ref[...] = jnp.concatenate([feat[i] for i in range(feat.shape[0])], axis=0)
    for copy in copies:
        copy.wait()


def edges_kernel(meta_ref, x0, x1, x2, x3, last_ref, first_ref):
    rep = meta_ref[REP]
    refs = (x0, x1, x2, x3)

    def chosen(index, lo):
        value = refs[0][lo : lo + HALO]
        for i in range(1, 4):
            value = jnp.where(index == i, refs[i][lo : lo + HALO].astype(F32), value.astype(F32))
        return value.astype(B16)

    last_ref[...] = chosen(rep ^ 3, x0.shape[0] - HALO)
    first_ref[...] = chosen(rep, 0)


def ext_of(proj_ref, halo_ref, exists, p, rows):
    return (
        jnp.concatenate(
            [halo_ref[p, rows, :LANE], proj_ref[p, rows, :], halo_ref[p, rows, LANE:]], axis=1
        ).astype(F32)
        * exists
    )


def short_from(ext, cols, p):
    return (
        cols[:, p : p + 1] * pltpu.roll(ext, 2, 1)
        + cols[:, 3 + p : 4 + p] * pltpu.roll(ext, 1, 1)
        + cols[:, 6 + p : 7 + p] * ext
        + cols[:, 9 + p : 10 + p]
    )


def project_kernel(
    meta_ref, len_ref, x0, x1, x2, x3, before_ref, after_ref, cols_ref,
    p0, p1, p2, p3, p4, p5, p6, a_ref, b_ref, io_full_ref, proj_ref, halo_ref, gated_ref
):
    assemble_kernel(meta_ref, p0, p1, p2, p3, p4, p5, p6, a_ref, b_ref, io_full_ref)
    io_ref = io_full_ref.reshape(-1, io_full_ref.shape[2])
    rep = meta_ref[REP]
    width, group = gated_ref.shape
    weight = io_ref[:, : 3 * width]
    for i, x_ref in enumerate((x0, x1, x2, x3)):
        cut = dot(x_ref[...], weight, NN).T
        for p in range(3):
            proj_ref[p, :, place(rep ^ i)] = (
                cut[p * width : (p + 1) * width] + cols_ref[:, 12 + p : 13 + p]
            ).astype(B16)
    edge = dot(jnp.concatenate([before_ref[...], after_ref[...]], axis=0), weight, NN)
    gap = jnp.zeros((LANE - HALO, 3 * width), F32)
    edge = jnp.concatenate([gap, edge, gap], axis=0).T
    for p in range(3):
        halo_ref[p] = (edge[p * width : (p + 1) * width] + cols_ref[:, 12 + p : 13 + p]).astype(B16)
    mask, exists = lane_masks(meta_ref, len_ref, group + 2 * LANE)
    for lo in range(0, width, PART):
        rows = slice(lo, lo + PART)
        cols = cols_ref[rows, :]
        gate_in = short_from(ext_of(proj_ref, halo_ref, exists, 1, rows), cols, 1)
        values = short_from(ext_of(proj_ref, halo_ref, exists, 2, rows), cols, 2)
        gated_ref[rows, :] = (values * gate_in * mask)[:, LANE:-LANE].astype(B16)


def out_project_kernel(
    meta_ref, len_ref, proj_ref, halo_ref, cols_ref, io_ref, mixed_ref, y_ref, give3_ref, give1_ref, keep2_ref, keep0_ref
):
    rep = meta_ref[REP]
    width, group = mixed_ref.shape
    _, exists = lane_masks(meta_ref, len_ref, group + 2 * LANE)
    for lo in range(0, width, LANE):
        rows = slice(lo, lo + LANE)
        gate_out = short_from(ext_of(proj_ref, halo_ref, exists, 0, rows), cols_ref[rows, :], 0)
        y = gate_out[:, LANE:-LANE] * mixed_ref[rows, :].astype(F32)
        for j in range(4):
            y_ref[rep ^ j, :, rows] = y[:, j * LANE : (j + 1) * LANE].T.astype(B16)
    outs = (keep0_ref, give1_ref, keep2_ref, give3_ref)
    left = y_ref[...].reshape(-1, width)
    rows = y_ref.shape[1]
    for lo in range(0, io_ref.shape[0], 256):
        part = dot(left, io_ref[lo : lo + 256, 3 * width :], NT)
        for i, ref in enumerate(outs):
            ref[:, lo : lo + 256] = part[i * rows : (i + 1) * rows].astype(ref.dtype)


def halves_far_kernel(left_ref, right_ref, a_ref, b_ref, sems):
    half = a_ref.shape[0]
    copies = [
        pltpu.make_async_copy(left_ref.at[pl.ds(0, half)], a_ref, sems.at[0]),
        pltpu.make_async_copy(right_ref.at[pl.ds(half, half)], b_ref, sems.at[1]),
    ]
    for copy in copies:
        copy.start()
    for copy in copies:
        copy.wait()


def assemble_far_kernel(meta_ref, p0, p1, p2, p3, p4, p5, p6, a_ref, b_ref, out_ref, sems):
    half = a_ref.shape[0]
    last = out_ref.at[meta_ref[OWNER + 7]]
    copies = [
        pltpu.make_async_copy(ref, out_ref.at[meta_ref[OWNER + k]], sems.at[k])
        for k, ref in enumerate((p0, p1, p2, p3, p4, p5, p6))
    ]
    copies.append(pltpu.make_async_copy(a_ref, last.at[pl.ds(0, half)], sems.at[7]))
    copies.append(pltpu.make_async_copy(b_ref, last.at[pl.ds(half, half)], sems.at[8]))
    for copy in copies:
        copy.start()
    for copy in copies:
        copy.wait()


def norm_second_kernel(x_ref, keep_ref, near_ref, far_ref, bias_ref, gain_ref, shift_ref, middle_ref, out_ref):
    middle = x_ref[...].astype(F32) + (
        keep_ref[...] + near_ref[...].astype(F32) + far_ref[...].astype(F32) + bias_ref[...]
    )
    middle_ref[...] = middle
    unit, _ = normed_of(middle)
    out_ref[...] = (unit * gain_ref[...] + shift_ref[...]).astype(B16)


def mlp_kernel(x0, x1, x2, x3, g0, g1, g2, g3, ud_ref, bias_ref, act_ref, gpre_ref, sum_ref):
    step = 256
    rows, model = x0.shape
    pieces = ((x0, g0), (x1, g1), (x2, g2), (x3, g3))
    for lo in range(0, act_ref.shape[1], step):
        cut = slice(lo, lo + step)
        up = ud_ref[:, 0, :, cut].reshape(model, step)
        down = ud_ref[:, 1, :, cut].reshape(model, step)
        total = None
        for i, (x_ref, g_ref) in enumerate(pieces):
            at = slice(i * rows, (i + 1) * rows)
            pre = dot(x_ref[...], up, NN) + bias_ref[:, cut]
            gact = dot(g_ref[...], down, NN)
            phi = 0.5 * (1.0 + lax.erf(pre * math.sqrt(0.5)))
            slope = phi + pre * (jnp.exp(-0.5 * pre * pre) * (1.0 / math.sqrt(2.0 * math.pi)))
            act_ref[at, cut] = (pre * phi).astype(B16)
            gpre = (gact * slope).astype(B16)
            gpre_ref[at, cut] = gpre
            part = jnp.sum(gpre.astype(F32), axis=0, keepdims=True)
            total = part if total is None else total + part
        sum_ref[:, cut] = total


def rows_kernel(which, left_ref, ud_ref, give3_ref, give1_ref, keep2_ref, keep0_ref):
    rows, model = give3_ref.shape
    owned = ud_ref.shape[2]
    outs = (keep0_ref, give1_ref, keep2_ref, give3_ref)
    for k in range(0, ud_ref.shape[0], 2):
        weight = ud_ref[k : k + 2, which].reshape(2 * owned, -1)
        part = dot(left_ref[...], weight, NT)
        for i, ref in enumerate(outs):
            ref[:, k * owned : (k + 2) * owned] = part[i * rows : (i + 1) * rows].astype(ref.dtype)


def mlp_grad_kernel(meta_ref, x0, x1, x2, x3, g0, g1, g2, g3, act_ref, gpre_ref, out_ref, a_ref, b_ref):
    grad_pair((x0, x1, x2, x3), gpre_ref[...], out_ref, slice(None), 0)
    grad_pair((g0, g1, g2, g3), act_ref[...], out_ref, slice(None), out_ref.shape[3] // 2)
    give_first(meta_ref, out_ref, a_ref, b_ref)


def norm_second_back_kernel(
    meta_ref, len_ref, keep_ref, near_ref, far_ref, middle_ref, top_ref, gain_ref, out_ref, gx_ref, sum_ref
):
    grad = keep_ref[...] + near_ref[...].astype(F32) + far_ref[...].astype(F32)
    unit, inverse = normed_of(middle_ref[...])
    scaled = grad * gain_ref[...]
    one = jnp.mean(scaled, axis=1, keepdims=True)
    two = jnp.mean(scaled * unit, axis=1, keepdims=True)
    top = top_ref[...].astype(F32) * own_mask(meta_ref, len_ref, top_ref.shape[0])
    out = top + inverse * (scaled - one - unit * two)
    out_ref[...] = out
    gx = out.astype(B16)
    gx_ref[...] = gx
    rows = [grad * unit, grad, gx.astype(F32), top]
    sums = [jnp.sum(r, axis=0, keepdims=True) for r in rows]
    sum_ref[...] = jnp.concatenate(sums + [jnp.zeros((4, sums[0].shape[1]), F32)], axis=0)


def grad_gate_kernel(
    meta_ref, len_ref, x0, x1, x2, x3, io_ref, proj_ref, halo_ref, cols_ref, mixed_ref, gy_ref, first_ref, gmix_ref
):
    rep = meta_ref[REP]
    width, group = mixed_ref.shape
    _, exists = lane_masks(meta_ref, len_ref, group + 2 * LANE)
    weight = io_ref[:, 3 * width :]
    for i, x_ref in enumerate((x0, x1, x2, x3)):
        gy_ref[:, place(rep ^ i)] = dot(x_ref[...], weight, NN).T.astype(B16)
    for lo in range(0, width, PART):
        rows = slice(lo, lo + PART)
        gate_out = short_from(ext_of(proj_ref, halo_ref, exists, 0, rows), cols_ref[rows, :], 0)
        gy = gy_ref[rows, :].astype(F32)
        gmix_ref[rows, :] = (gy * gate_out[:, LANE:-LANE]).astype(B16)
        first_ref[rows, :] = gy[:, :LANE] * mixed_ref[rows, :LANE].astype(F32)


def conv_back_kernel(
    spec_ref, kern_ref, twist_ref, hi_ref, lo_ref, chan_ref, g_ref, out_ref, grad_kern_ref, z_ref, p_ref
):
    blocks, rows, length = twist_ref.shape[0], g_ref.shape[1], g_ref.shape[2]
    short_blocks = blocks // 4
    span = blocks * rows
    first = [g_ref[b].astype(F32) for b in range(blocks)]
    second = [g_ref[blocks + b].astype(F32) for b in range(short_blocks)]
    turn_rows(first, twist_ref, z_ref, 0, blocks)
    turn_rows(second, twist_ref, z_ref, span, blocks)
    grad = dot_split(z_ref[...], hi_ref[...], lo_ref[...], ((1,), (0,)))
    kern = kern_ref[...]
    p_ref[0:span] = times(grad[:span], kern, True)
    p_ref[span : 2 * span] = times(grad[span:], kern, True)
    p_ref[2 * span :] = times(grad[:span], spec_ref[0:span], True) + times(grad[span:], spec_ref[span:], True)
    w = dot_split(p_ref[...], hi_ref[...], lo_ref[...], ((1,), (1,)))
    skip = chan_ref[:, 0:1]
    for b in range(blocks):
        acc = (back_rows(w, 0, rows, b, twist_ref, blocks) + skip * first[b]).astype(B16)
        out_ref[b] = acc
        if b < short_blocks:
            acc = (back_rows(w, span, rows, b, twist_ref, blocks) + skip * second[b]).astype(B16)
        else:
            acc = jnp.zeros((rows, length), B16)
        out_ref[blocks + b] = acc
        grad_kern_ref[b] = back_rows(w, 2 * span, rows, b, twist_ref, blocks)


def conv_ahead_kernel(kern_ref, twist_ref, hi_ref, lo_ref, chan_ref, x_ref, out_ref, spec_ref, z_ref):
    conv_forward_kernel(
        twist_ref.shape[0] // 4, x_ref, kern_ref, twist_ref, hi_ref, lo_ref, chan_ref.at[:, 0:1], out_ref, spec_ref, z_ref
    )


def filter_ahead_kernel(
    chan_ref, w1_ref, small_ref, columns_ref, grid_ref, ramp_ref, w2_ref, w3_ref, twist_ref, hi_ref, lo_ref,
    spec_ref, sin_ref, cos_ref, z_ref
):
    filter_forward_kernel(
        grid_ref, ramp_ref, chan_ref.at[:, 1:2], w1_ref, w2_ref.at[0], w3_ref.at[0], small_ref, columns_ref,
        twist_ref, hi_ref, lo_ref, spec_ref, sin_ref, cos_ref, z_ref
    )


def halves_of(values):
    top = values.astype(B16)
    return top, (values - top.astype(F32)).astype(B16)


def dot_halves(left, right, dims):
    return dot(left[0], right[0], dims) + dot(left[1], right[0], dims) + dot(left[0], right[1], dims)


def filter_back_kernel(
    meta_ref, gk_ref, grid_ref, ramp_ref, chan_ref, w1_ref, w2_ref, w3_ref, col_ref, row_ref, columns_ref, sin_ref, cos_ref,
    side_ref, wide_ref
):
    freq, freq_row = col_ref[:, 3:4], row_ref[3:4, :]
    filt = freq.shape[0]
    gk = jnp.concatenate([gk_ref[b] for b in range(gk_ref.shape[0])], axis=1)
    gk = halves_of(gk * jnp.exp(-chan_ref[:, 1:2] * ramp_ref[...]))
    gcols = dot_halves(halves_of(sin_ref[2]), gk, NT)
    chan, width = gcols.shape[1], wide_ref.shape[1]
    row = lax.broadcasted_iota(jnp.int32, (chan, width), 0)
    lane = lax.broadcasted_iota(jnp.int32, (chan, width), 1)
    pick = (lane == row + meta_ref[SEQ] * chan).astype(F32)
    wide_ref[...] = dot_high(gcols, pick, NN)
    grad = dot_halves(halves_of(columns_ref[...]), gk, NN)
    ones = jnp.ones((16, grad.shape[1]), B16)
    gfreq = jnp.zeros((1, filt), F32)
    grads, biases = [None] * 3, [None] * 3
    for i, weight in ((2, w3_ref[0]), (1, w2_ref[0]), (0, w1_ref[...])):
        turn = grad * cos_ref[i]
        pair = halves_of(turn)
        below = halves_of(sin_ref[i - 1] if i else grid_ref[...])
        raw = dot_halves(below, pair, NT)
        total = (dot(ones, pair[0], NT) + dot(ones, pair[1], NT))[0:1]
        grads[i] = raw * freq_row
        biases[i] = total * freq_row
        gfreq = gfreq + jnp.sum(raw * weight, axis=0, keepdims=True) + total * row_ref[i : i + 1, :]
        if i:
            grad = dot_halves(halves_of(weight * freq_row), pair, NN)
    gap = jnp.zeros((filt - grads[0].shape[0], filt), F32)
    small = jnp.concatenate(biases + [gfreq, jnp.zeros((filt - 4, filt), F32)], axis=0)
    side_ref[...] = jnp.concatenate(
        [grads[1], grads[2], jnp.concatenate([grads[0], gap], axis=0), small], axis=1
    )


def summed(value):
    total = value[:, :LANE]
    for k in range(LANE, value.shape[1], LANE):
        total = total + value[:, k : k + LANE]
    return jnp.sum(total, axis=1, keepdims=True)


def short_back(ext, cols, gshort, p, mid):
    size = ext.shape[1]
    mine = gshort[:, mid]
    gproj = (
        cols[:, 6 + p : 7 + p] * gshort
        + cols[:, 3 + p : 4 + p] * pltpu.roll(gshort, size - 1, 1)
        + cols[:, p : p + 1] * pltpu.roll(gshort, size - 2, 1)
    )[:, mid].astype(B16).astype(F32)
    sums = [
        summed(mine),
        summed(mine * ext[:, mid]),
        summed(mine * pltpu.roll(ext, 1, 1)[:, mid]),
        summed(mine * pltpu.roll(ext, 2, 1)[:, mid]),
        summed(gproj),
    ]
    return gproj, sums


def grad_first_kernel(
    meta_ref, len_ref, proj_ref, halo_ref, cols_ref, mixed_ref, gy_ref, onext_ref, io_ref, tok_ref, sum_ref, part_ref
):
    rep = meta_ref[REP]
    width, group = mixed_ref.shape
    size = group + 2 * LANE
    mask, exists = lane_masks(meta_ref, len_ref, size)
    mid = slice(LANE, size - LANE)
    next_on = exists[:, size - LANE :]
    columns = []
    for lo in range(0, width, PART):
        rows = slice(lo, lo + PART)
        cols = cols_ref[rows, :]
        gy = gy_ref[rows, :].astype(F32)
        gout = gy * mixed_ref[rows, :].astype(F32)
        gshort = jnp.concatenate([jnp.zeros((PART, LANE), F32), gout, onext_ref[rows, :] * next_on], axis=1)
        gproj, sums = short_back(ext_of(proj_ref, halo_ref, exists, 0, rows), cols, gshort, 0, mid)
        for j in range(4):
            tok_ref[rep ^ j, :, rows] = gproj[:, j * LANE : (j + 1) * LANE].T.astype(B16)
        columns.append(jnp.concatenate(sums + [jnp.zeros((PART, LANE - 5), F32)], axis=1))
    sum_ref[...] = jnp.concatenate(columns, axis=0).T[:8]
    part_ref[...] = dot(tok_ref[...].reshape(-1, width), io_ref[:, :width], NT)


def grad_short_kernel(
    meta_ref, len_ref, proj_ref, halo_ref, cols_ref, gy_ref, io_ref, before_ref,
    x0, x1, x2, x3, gain_ref, shift_ref, ggated_ref, gnext_ref,
    tok_ref, sum_ref, norm_ref, give3_ref, give1_ref, keep2_ref, keep0_ref
):
    rep = meta_ref[REP]
    width, group = gy_ref.shape
    size = group + 2 * LANE
    mask, exists = lane_masks(meta_ref, len_ref, size)
    mid = slice(LANE, size - LANE)
    columns = []
    for lo in range(0, width, PART):
        rows = slice(lo, lo + PART)
        cols = cols_ref[rows, :]
        ext = [ext_of(proj_ref, halo_ref, exists, p, rows) for p in (1, 2)]
        short = [short_from(ext[p - 1], cols, p) for p in (1, 2)]
        ggated = (
            jnp.concatenate(
                [jnp.zeros((PART, LANE), F32), ggated_ref[rows, :].astype(F32), gnext_ref[rows, :].astype(F32)], axis=1
            )
            * mask
            * exists
        )
        gate_out = short_from(ext_of(proj_ref, halo_ref, exists, 0, rows), cols, 0)[:, mid]
        gated = short[1][:, mid] * short[0][:, mid] * mask[:, mid]
        sums = [summed(gy_ref[rows, :].astype(F32) * gate_out * gated)]
        for p in (1, 2):
            gproj, more = short_back(ext[p - 1], cols, ggated * short[2 - p], p, mid)
            sums += more
            at = slice((p - 1) * width + lo, (p - 1) * width + lo + PART)
            for j in range(4):
                tok_ref[rep ^ j, :, at] = gproj[:, j * LANE : (j + 1) * LANE].T.astype(B16)
        columns.append(jnp.concatenate(sums + [jnp.zeros((PART, LANE - 11), F32)], axis=1))
    sum_ref[...] = jnp.concatenate(columns, axis=0).T[:16]
    outs = (keep0_ref, give1_ref, keep2_ref, give3_ref)
    left = tok_ref[...].reshape(-1, 2 * width)
    tall = tok_ref.shape[1]
    for lo in range(0, io_ref.shape[0], 256):
        cut = slice(lo, lo + 256)
        part = dot(left, io_ref[cut, width : 3 * width], NT) + before_ref[:, cut]
        plain = jnp.sum(part, axis=0, keepdims=True)
        cross = None
        for i, (ref, x_ref) in enumerate(zip(outs, (x0, x1, x2, x3))):
            mine = part[i * tall : (i + 1) * tall]
            ref[:, cut] = mine.astype(ref.dtype)
            two = jnp.sum(mine * x_ref[:, cut].astype(F32), axis=0, keepdims=True)
            cross = two if cross is None else cross + two
        norm_ref[0:1, cut] = (cross - shift_ref[:, cut] * plain) / gain_ref[:, cut]
        norm_ref[1:2, cut] = plain


def give_first(meta_ref, term_ref, a_ref, b_ref):
    half = a_ref.shape[2]
    seq = meta_ref[SEQ]
    s0, s1 = seq & 1, (seq >> 1) & 1
    for i in range(2):
        for j in range(2):
            a_ref[i, j] = term_ref[i, j, 1 - s0, :half]
            b_ref[i, j] = term_ref[i, 1 - s1, j, half:]


def grad_pair(refs, right, out_ref, lanes, base=0):
    owned = refs[0].shape[1] // 8
    for k in range(0, 8, 2):
        left = jnp.concatenate([r[:, k * owned : (k + 2) * owned] for r in refs], axis=0)
        part = dot(left, right, TN).astype(B16)
        out_ref[k // 4, (k // 2) % 2, 0, base : base + owned, lanes] = part[:owned]
        out_ref[k // 4, (k // 2) % 2, 1, base : base + owned, lanes] = part[owned:]


def grad_early_kernel(meta_ref, g0, g1, g2, g3, y_ref, x0, x1, x2, x3, tok_ref, out_ref, a_ref, b_ref):
    width = y_ref.shape[2]
    grad_pair((g0, g1, g2, g3), y_ref[...].reshape(-1, width), out_ref, slice(0, width))
    grad_pair((x0, x1, x2, x3), tok_ref[...].reshape(-1, width), out_ref, slice(width, 2 * width))
    give_first(meta_ref, out_ref, a_ref, b_ref)


def grad_late_kernel(meta_ref, x0, x1, x2, x3, tok_ref, out_ref, a_ref, b_ref):
    width = tok_ref.shape[2]
    grad_pair((x0, x1, x2, x3), tok_ref[...].reshape(-1, width), out_ref, slice(0, width))
    give_first(meta_ref, out_ref, a_ref, b_ref)


def halve_one_kernel(meta_ref, term_ref, a_in, b_in, keep_a, keep_b, give_a, give_b):
    half = a_in.shape[2]
    seq = meta_ref[SEQ]
    s0, s1 = seq & 1, (seq >> 1) & 1
    for i in range(2):
        keep_a[i] = term_ref[i, s1, s0, :half].astype(F32) + a_in[i, s1].astype(F32)
        give_a[i] = (term_ref[i, 1 - s1, s0, :half].astype(F32) + a_in[i, 1 - s1].astype(F32)).astype(B16)
        keep_b[i] = term_ref[i, s1, s0, half:].astype(F32) + b_in[i, s0].astype(F32)
        give_b[i] = (term_ref[i, s1, 1 - s0, half:].astype(F32) + b_in[i, 1 - s0].astype(F32)).astype(B16)


def halve_two_kernel(meta_ref, keep_a_in, keep_b_in, a_in, b_in, keep_a, keep_b, give_a, give_b):
    s2 = meta_ref[SEQ] >> 2
    keep_a[...] = keep_a_in[s2] + a_in[s2].astype(F32)
    give_a[...] = (keep_a_in[1 - s2] + a_in[1 - s2].astype(F32)).astype(B16)
    keep_b[...] = keep_b_in[s2] + b_in[s2].astype(F32)
    give_b[...] = (keep_b_in[1 - s2] + b_in[1 - s2].astype(F32)).astype(B16)


def add_last_kernel(keep_ref, came_ref, out_ref):
    out_ref[0] = keep_ref[...] + came_ref[...].astype(F32)


def early_last_kernel(keep_a, keep_b, a_in, b_in, out_ref, in_ref):
    half, width = keep_a.shape[0], out_ref.shape[2]
    for keep, came, rows in ((keep_a, a_in, slice(0, half)), (keep_b, b_in, slice(half, 2 * half))):
        out_ref[0, rows] = keep[:, :width] + came[:, :width].astype(F32)
        in_ref[rows] = keep[:, width:] + came[:, width:].astype(F32)


def late_last_kernel(keep_a, keep_b, a_in, b_in, first_ref, out_ref):
    half, width = keep_a.shape[0], out_ref.shape[3]
    out_ref[0, 0] = first_ref[...]
    for keep, came, rows in ((keep_a, a_in, slice(0, half)), (keep_b, b_in, slice(half, 2 * half))):
        for p in range(2):
            lanes = slice(p * width, (p + 1) * width)
            out_ref[0, 1 + p, rows] = keep[:, lanes] + came[:, lanes].astype(F32)


def norm_first_back_kernel(keep_ref, near_ref, far_ref, x_ref, middle_ref, gain_ref, out_ref):
    grad = keep_ref[...] + near_ref[...].astype(F32) + far_ref[...].astype(F32)
    unit, inverse = normed_of(x_ref[...].astype(F32))
    scaled = grad * gain_ref[...]
    one = jnp.mean(scaled, axis=1, keepdims=True)
    two = jnp.mean(scaled * unit, axis=1, keepdims=True)
    out_ref[...] = middle_ref[...] + inverse * (scaled - one - unit * two)


def layer_out_kernel(keep_ref, near_ref, far_ref, middle_ref, bias_ref, out_ref):
    part = keep_ref[...] + near_ref[...].astype(F32) + far_ref[...].astype(F32)
    out_ref[...] = (middle_ref[...] + (part + bias_ref[...])).astype(B16)


def heads_kernel(in_ref, out_ref):
    out_ref[...] = in_ref[:, :LANE]


def add_far_kernel(keep_ref, came_ref, out_ref):
    out_ref[...] = (keep_ref[...] + came_ref[...].astype(F32)).astype(B16)


HALF = 88


def pack_small_kernel(side_ref, wide_ref, col0_ref, col_ref, up_ref, one_ref, two_ref, out_ref):
    filt, width = side_ref.shape
    out_ref[:filt] = side_ref[...]
    at = filt
    for ref, count in ((one_ref, 2), (two_ref, 4)):
        for r in range(count):
            for k in range(4):
                out_ref[at : at + 1] = ref[r : r + 1, k * width : (k + 1) * width]
                at += 1
    out_ref[HALF : HALF + 1] = col_ref[0:1]
    out_ref[HALF + 1 : HALF + 6] = col0_ref[0:5]
    out_ref[HALF + 6 : HALF + 16] = col_ref[1:11]
    for k in range(4):
        out_ref[HALF + 16 + k : HALF + 17 + k] = up_ref[:, k * width : (k + 1) * width]
    out_ref[HALF + 20 : HALF + 24] = jnp.zeros((4, width), F32)
    out_ref[HALF + 24 :] = wide_ref[...]


def add_small_kernel(mine_ref, came_ref, out_ref):
    out_ref[...] = mine_ref[...] + came_ref[...]


def list_small_kernel(meta_ref, mine_ref, came_ref, out_ref):
    y = meta_ref[REP] >> 1
    out_ref[:HALF] = mine_ref[:HALF] + came_ref[:HALF]
    out_ref[pl.ds(pl.multiple_of((1 + y) * HALF, 8), HALF)] = mine_ref[HALF:]
    out_ref[pl.ds(pl.multiple_of((2 - y) * HALF, 8), HALF)] = came_ref[HALF:]


def unpack_small_kernel(
    meta_ref, mine_ref, came_ref,
    in_bias, taps, short_bias, fw, fb, iw, ib, dw, db, sf, kern_w, skip, out_b, n1g, n1s, n2g, n2s, up_b, down_b
):
    core = meta_ref[REP] & 1
    filt, width = iw.shape[2], mine_ref.shape[1]
    total = mine_ref[:HALF] + came_ref[:HALF]
    iw[0] = total[:filt, :filt]
    dw[0] = total[:filt, filt : 2 * filt]
    for k in range(fw.shape[0]):
        fw[k] = total[k : k + 1, 2 * filt : 3 * filt]
    for k, ref in enumerate((fb, ib, db, sf)):
        ref[...] = total[k : k + 1, 3 * filt :]
    at = filt
    for ref in (n1g, n1s, n2g, n2s, out_b, down_b):
        for k in range(4):
            ref[:, k * width : (k + 1) * width] = total[at : at + 1]
            at += 1
    for y in range(2):
        lo = (1 + y) * HALF
        mine, came = mine_ref[lo : lo + HALF], came_ref[lo : lo + HALF]
        for c in range(2):
            block = jnp.where(core == c, mine, came)
            lanes = slice((2 * y + c) * width, (2 * y + c + 1) * width)
            skip[:, lanes] = block[0:1]
            for p in range(3):
                row = 1 + 5 * p
                short_bias[p, :, lanes] = block[row : row + 1]
                for j in range(3):
                    taps[j, p, :, lanes] = block[row + 3 - j : row + 4 - j]
                in_bias[p, :, lanes] = block[row + 4 : row + 5]
            for k in range(4):
                lo_up = (2 * y + c) * 4 * width + k * width
                up_b[:, lo_up : lo_up + width] = block[16 + k : 17 + k]
            kern_w[0, :, lanes] = block[24 : 24 + filt]


def tie(values, *others):
    return lax.optimization_barrier((values, others))[0]


class RingGather:
    def __init__(self, name, meta, shard, far=False):
        self.name, self.meta, self.far = name, meta, far
        self.pieces = [shard]
        self.send(shard, shard)

    def send(self, left, right):
        self.came = (lax.ppermute(left, "seq", AHEAD), lax.ppermute(right, "seq", BACK))

    def step(self, *others):
        left, right = tie(self.came, *others)
        self.pieces += [left, right]
        count = len(self.pieces)
        if count == 7:
            half = shape((left.shape[0] // 2,) + left.shape[1:], B16)
            if self.far:
                left, right = call(
                    halves_far_kernel, self.name + "_halves", [left, right], [half, half],
                    scratch=[pltpu.SemaphoreType.DMA((2,))], raw=[0, 1, -1, -2],
                )
            else:
                left, right = call(halves_kernel, self.name + "_halves", [left, right], [half, half])
        if count < 9:
            self.send(left, right)
        return self.came

    def full(self, *others):
        left, right = tie(self.came, *others)
        pieces = self.pieces + [left, right]
        whole = [shape((8,) + self.pieces[0].shape, B16)]
        if self.far:
            return call(
                assemble_far_kernel, self.name + "_assemble", [self.meta, *pieces], whole,
                scratch=[pltpu.SemaphoreType.DMA((9,))], raw=range(1, 10),
            )[0]
        return call(assemble_kernel, self.name + "_assemble", [self.meta, *pieces], whole)[0]


def gather_four(rows):
    far = swap(rows, "rep", 2)
    near = swap(rows, "rep", 1)
    diag = swap(far, "rep", 1)
    return [rows, near, far, diag]


def pass_far(give3, give1, keep2):
    came = swap(give3, "rep", 1)
    near = swap(give1, "rep", 1)
    (summed,) = call(add_far_kernel, "add_far", [keep2, came], [shape(keep2.shape, B16)])
    return near, swap(summed, "rep", 2), summed


class Halving:
    def __init__(self, name, meta, term, give):
        self.name, self.meta, self.term = name, meta, term
        self.came = (swap(give[0], "seq", 1), swap(give[1], "seq", 2))

    def one(self, *others):
        rows, cols = self.term.shape[3] // 2, self.term.shape[4]
        outs = [shape((2, rows, cols), F32)] * 2 + [shape((2, rows, cols), B16)] * 2
        args = [self.meta, self.term, *tie(self.came, *others)]
        *self.keep, ga, gb = call(halve_one_kernel, self.name + "_one", args, outs)
        self.came = (swap(ga, "seq", 2), swap(gb, "seq", 1))
        return ga

    def two_kept(self, *others):
        rows, cols = self.term.shape[3] // 2, self.term.shape[4]
        outs = [shape((rows, cols), F32)] * 2 + [shape((rows, cols), B16)] * 2
        args = [self.meta, *self.keep, *tie(self.came, *others)]
        return call(halve_two_kernel, self.name + "_two", args, outs)

    def two(self, *others):
        *self.keep, ga, gb = self.two_kept(*others)
        self.came = (swap(ga, "seq", 4), swap(gb, "seq", 4))
        return ga

    def last(self, *others):
        return [*self.keep, *tie(self.came, *others)]


def exchange(blocks):
    return lax.all_to_all(blocks, "seq", 0, 0, tiled=True)


def per_device_fast(
    tokens,
    cotangent,
    lengths,
    in_weight,
    in_bias,
    short_taps,
    short_bias,
    feat_weight,
    feat_bias,
    inner_weight,
    inner_bias,
    deep_weight,
    deep_bias,
    sine_freq,
    kernel_weight,
    skip_gain,
    out_weight,
    out_bias,
    norm1_gain,
    norm1_shift,
    norm2_gain,
    norm2_shift,
    up_weight,
    up_bias,
    down_weight,
    down_bias,
):
    tok_rows, model = tokens.shape
    group = tok_rows * 4
    blocks = 4
    seq_len = blocks * group
    chan = model // 32
    width = model // 4
    hidden = up_weight.shape[2]
    owned = model // 8
    filt = feat_weight.shape[2]
    device = lax.axis_index("seq") * 4 + lax.axis_index("rep")
    meta = lax.dynamic_index_in_dim(jnp.asarray(meta_table(group)), device, 0, keepdims=False)
    row_f32, row_b16 = shape((tok_rows, model), F32), shape((tok_rows, model), B16)
    sums_shapes = [row_b16, row_b16, row_f32, row_f32]
    flat_shape = shape((width, group), B16)

    normed, io_shard = call(
        start_kernel,
        "start",
        [tokens, norm1_gain, norm1_shift, in_weight[0].transpose(1, 0, 2), out_weight],
        [row_b16, shape((owned, 4 * width), B16)],
        away=range(5),
    )
    io_ring = RingGather("io", meta, io_shard)
    x_one = gather_four(normed)
    twist, table = transform_tables(blocks, group)
    hi, lo = split_table(table)
    grid, ramp = feature_table(seq_len, feat_weight.shape[1])
    twist, grid, ramp = jnp.asarray(twist), jnp.asarray(grid), jnp.asarray(ramp)
    params = [
        cotangent, up_weight, down_weight,
        short_taps.transpose(1, 2, 0, 3), short_bias.transpose(1, 0, 2), in_bias.transpose(1, 0, 2), up_bias, skip_gain,
        jnp.asarray(decay_rates(model).T), kernel_weight, feat_weight.transpose(1, 0, 2),
        feat_bias, inner_bias, deep_bias, sine_freq,
    ]
    top_rows, ud_shard, cols, up_block, chans, columns, small_col, small_row, feat = call(
        setup_kernel,
        "setup",
        [meta, lengths, *params],
        [
            row_b16, shape((2, owned, hidden), B16),
            shape((width, 16), F32), shape((1, hidden), F32), shape((chan, 2), F32), shape((filt, chan), F32),
            shape((filt, 4), F32), shape((4, filt), F32), shape(feat_weight.shape[1:], F32),
        ],
        scratch=[pltpu.SemaphoreType.DMA((2,))],
        away=[2] + list(range(5, 2 + len(params))),
        raw=[3, 4, -2],
    )
    io_ring.step(x_one[1])
    tables = [grid, ramp, inner_weight, deep_weight, twist, hi, lo]
    kern_spec, sines, cosines = call(
        filter_ahead_kernel,
        "filter_ahead",
        [chans, feat, tie(small_col, io_ring.pieces[-1]), columns, *tables],
        [
            shape((blocks * chan, 2 * group), F32),
            shape((3, filt, seq_len), F32),
            shape((3, filt, seq_len), F32),
        ],
        scratch=[pltpu.VMEM((blocks * chan, 2 * group), F32)],
        away=range(4, 4 + len(tables)),
    )
    io_ring.step(kern_spec, x_one[2])

    edge = shape((HALO, model), B16)
    last, first = call(edges_kernel, "edges", [meta, *x_one], [edge, edge])
    before = lax.ppermute(last, "seq", [(i, (i + 1) % 8) for i in range(8)])
    after = lax.ppermute(first, "seq", [(i, (i + 7) % 8) for i in range(8)])
    io_ring.step()
    io_pieces = io_ring.pieces + list(tie(io_ring.came, before, after))
    ud_ring = RingGather("ud", meta, tie(ud_shard, io_pieces[-1]))
    g_top = gather_four(tie(top_rows, x_one[3]))
    full_io, proj, halo, gated = call(
        project_kernel,
        "project",
        [meta, lengths, *x_one, before, after, cols, *io_pieces],
        [
            shape((8, owned, 4 * width), B16), shape((3, width, group), B16), shape((3, width, 2 * LANE), B16), flat_shape
        ],
    )
    full_io = full_io.reshape(model, 4 * width)
    common = [proj, halo, cols]

    spread = (8, chan, group)
    received = exchange(gated.reshape(spread))
    ud_ring.step(received)
    spec_rows = 2 * blocks * chan
    mixed, kept_spec = call(
        conv_ahead_kernel,
        "conv_ahead",
        [kern_spec, twist, hi, lo, chans, received],
        [shape(spread, B16), shape((spec_rows, 2 * group), F32)],
        scratch=[pltpu.VMEM((spec_rows, 2 * group), F32)],
    )
    mixed = exchange(mixed).reshape(width, group)
    ud_ring.step(mixed)

    y_tok, give3, give1, keep2, keep0 = call(
        out_project_kernel,
        "out_project",
        [meta, lengths, *common, full_io, mixed],
        [shape((4, tok_rows, width), B16)] + sums_shapes,
    )
    near, far, _ = pass_far(give3, give1, keep2)
    middle, normed_two = call(
        norm_second_kernel,
        "norm_second",
        [tokens, keep0, near, far, out_bias, norm2_gain, norm2_shift],
        [row_f32, row_b16],
    )
    ud_ring.step(normed_two)
    x_two = gather_four(normed_two)
    full_ud = ud_ring.full(x_two[2])

    tall = shape((group, hidden), B16)
    act, gpre, gup = call(
        mlp_kernel, "mlp", [*x_two, *g_top, full_ud, up_block], [tall, tall, shape((1, hidden), F32)],
    )
    give3, give1, keep2, keep0 = call(partial(rows_kernel, 0), "grad_two", [gpre, full_ud], sums_shapes)
    near, far, passed = pass_far(give3, give1, keep2)
    give = shape((2, 2, owned, hidden), B16)
    mlp_terms, ga, gb = call(
        mlp_grad_kernel,
        "mlp_grad",
        [meta, *x_two, *g_top, act, tie(gpre, passed)],
        [shape((2, 2, 2, 2 * owned, hidden), B16), give, give],
    )
    wide_back = Halving("far", meta, mlp_terms, (ga, gb))
    grad_middle, gx, norm_sums = call(
        norm_second_back_kernel,
        "norm_second_back",
        [meta, lengths, keep0, near, tie(far, ga), middle, cotangent, norm2_gain],
        [row_f32, row_b16, shape((8, model), F32)],
    )
    g_mid = gather_four(gx)
    m3, m1, m2, m0 = call(partial(rows_kernel, 1), "mlp_rows", [tie(act, gx), full_ud], sums_shapes)
    gy, gate_first, gmix = call(
        grad_gate_kernel,
        "grad_gate",
        [meta, lengths, *tie(tuple(g_mid), m3), full_io, *common, mixed],
        [flat_shape, shape((width, LANE), F32), flat_shape],
    )

    received = exchange(gmix.reshape(spread))
    given = wide_back.one(received)
    gate_next = lax.ppermute(tie(gate_first, received), "seq", [(i, (i + 7) % 8) for i in range(8)])
    ggated, grad_kernel = call(
        conv_back_kernel,
        "conv_back",
        [kept_spec, kern_spec, twist, hi, lo, chans, tie(received, given)],
        [shape(spread, B16), shape((blocks, chan, group), F32)],
        scratch=[pltpu.VMEM((spec_rows, 2 * group), F32), pltpu.VMEM((3 * spec_rows // 2, 2 * group), F32)],
    )
    ggated = exchange(tie(ggated, gate_next)).reshape(width, group)
    up_keep, down_keep, up_give, down_give = wide_back.two_kept(ggated)
    up_came = swap(up_give, "seq", 4)
    (heads,) = call(heads_kernel, "heads", [tie(ggated, up_give)], [shape((width, LANE), B16)])
    ggated_next = lax.ppermute(heads, "seq", [(i, (i + 7) % 8) for i in range(8)])
    tok_first, sum_first, part_first = call(
        grad_first_kernel,
        "grad_first",
        [meta, lengths, *common, mixed, gy, tie(gate_next, heads), full_io],
        [shape((4, tok_rows, width), B16), shape((8, width), F32), shape((group, model), F32)],
    )
    cube = shape((2, 2, 2, owned, 2 * width), B16)
    give = shape((2, 2, owned // 2, 2 * width), B16)
    early_terms, ga, gb = call(
        grad_early_kernel,
        "grad_early",
        [meta, *g_mid, y_tok, *x_one, tok_first],
        [cube, give, give],
    )
    early = Halving("early", meta, early_terms, (ga, gb))
    tok_rest, col_sums, norm_one, give3, give1, keep2, keep0 = call(
        grad_short_kernel,
        "grad_short",
        [
            meta, lengths, *common, gy, full_io, part_first, *x_one, norm1_gain, norm1_shift, tie(ggated, ga),
            ggated_next
        ],
        [shape((4, tok_rows, 2 * width), B16), shape((16, width), F32), shape((2, model), F32)] + sums_shapes,
    )
    result = shape((1, owned, hidden), F32)
    down_came = swap(tie(down_give, give3), "seq", 4)
    (grad_up,) = call(add_last_kernel, "up_last", [up_keep, tie(up_came, give3)], [result])
    given = early.one(grad_up)
    near, far, passed = pass_far(give3, give1, tie(keep2, given))
    late_terms, ga, gb = call(
        grad_late_kernel, "grad_late", [meta, *tie(tuple(x_one), passed), tok_rest], [cube, give, give]
    )
    late = Halving("late", meta, late_terms, (ga, gb))
    side, wide = call(
        filter_back_kernel,
        "filter_back",
        [
            meta, tie(grad_kernel, ga), grid, ramp, chans, feat, inner_weight, deep_weight, small_col, small_row, columns,
            sines, cosines
        ],
        [shape((filt, 4 * filt), F32), shape((filt, width), F32)],
    )

    (small,) = call(
        pack_small_kernel,
        "pack_small",
        [side, wide, sum_first, col_sums, gup, norm_one, norm_sums],
        [shape((2 * HALF, width), F32)],
    )
    came = swap(small, "seq", 1)
    (grad_down,) = call(add_last_kernel, "down_last", [down_keep, tie(down_came, small)], [result])
    given = early.two(grad_down)
    (grad_tokens,) = call(
        norm_first_back_kernel,
        "norm_first_back",
        [keep0, near, tie(far, given), tokens, grad_middle, norm1_gain],
        [row_f32],
    )
    given = late.one(grad_tokens)
    (small,) = call(add_small_kernel, "add_small", [small, tie(came, given)], [small])
    came = swap(small, "seq", 2)
    m_near, m_far, m_passed = pass_far(tie(m3, small), m1, m2)
    grad_out, first_in = call(
        early_last_kernel, "early_last", early.last(small), [shape((1, owned, width), F32), shape((owned, width), F32)]
    )
    (small,) = call(add_small_kernel, "add_small", [small, tie(came, grad_out, m_passed)], [small])
    came = swap(small, "seq", 4)
    given = late.two(small)
    (small,) = call(add_small_kernel, "add_small", [small, tie(came, given)], [small])
    came = swap(small, "rep", 2)
    (layer_out,) = call(layer_out_kernel, "layer_out", [m0, m_near, tie(m_far, small), middle, down_bias], [row_b16])
    (small,) = call(
        list_small_kernel, "list_small", [meta, small, tie(came, layer_out)], [shape((3 * HALF, width), F32)]
    )
    came = swap(small, "rep", 1)
    (grad_in,) = call(
        late_last_kernel, "late_last", [*late.last(small), first_in], [shape((1, 3, owned, width), F32)]
    )
    vector = shape((1, model), F32)
    square, short = shape((1, filt, filt), F32), shape((1, filt), F32)
    triple = shape((3, 1, model), F32)
    outs = call(
        unpack_small_kernel,
        "unpack_small",
        [meta, small, came],
        [
            triple, shape((3, 3, 1, model), F32), triple, shape(params[10].shape, F32), short, square, short, square,
            short, short, shape(kernel_weight.shape, F32), vector, vector, vector, vector, vector, vector,
            shape(up_bias.shape, F32), vector,
        ],
    )
    return (
        layer_out,
        grad_tokens,
        grad_in.transpose(0, 2, 1, 3),
        outs[0].transpose(1, 0, 2),
        outs[1].transpose(2, 0, 1, 3),
        outs[2].transpose(1, 0, 2),
        outs[3].transpose(1, 0, 2),
        *outs[4:12],
        grad_out,
        *outs[12:17],
        grad_up,
        outs[17],
        grad_down,
        outs[18],
    )


def solution(mesh):
    rows = P(("seq", "rep"), None)
    cut = P(None, "seq", "rep")
    wide = P(None, "seq", None, "rep")
    whole = P()
    ins = [rows, rows, whole, wide] + [whole] * 12 + [cut] + [whole] * 5 + [cut, whole, cut, whole]
    outs = [rows, rows, wide] + [whole] * 12 + [cut] + [whole] * 5 + [cut, whole, cut, whole]
    fast = mesh.shape["seq"] == 8 and mesh.shape["rep"] == 4
    return jax.shard_map(
        per_device_fast if fast else per_device, mesh=mesh, in_specs=tuple(ins), out_specs=tuple(outs), check_vma=False
    )
```

```python
from functools import partial
import math

import jax
import jax.numpy as jnp
import numpy as np
from jax import lax
from jax.experimental import pallas as pl
from jax.experimental.pallas import tpu as pltpu
from jax.sharding import PartitionSpec as P

EPS = 1e-05
HIGH = lax.Precision.HIGHEST
F32 = jnp.float32
B16 = jnp.bfloat16
LANE = 128
HALO = 16
VMEM_BYTES = 48 * 2**20


def swap(values, axis_name, bit):
    size = lax.axis_size(axis_name)
    return lax.ppermute(values, axis_name, [(i, i ^ bit) for i in range(size)])


def gather_rel(rows):
    far = swap(rows, "rep", 2)
    near = swap(rows, "rep", 1)
    diag = swap(far, "rep", 1)
    return jnp.concatenate([rows, near, far, diag], axis=0)


def scatter_rel(part):
    rows = part.shape[0] // 4
    blocks = part.reshape(4, rows, part.shape[1])
    far_in = swap(blocks[3].astype(B16), "rep", 1)
    far_sum = (blocks[2] + far_in.astype(F32)).astype(B16)
    near_in = swap(blocks[1].astype(B16), "rep", 1)
    far_out = swap(far_sum, "rep", 2)
    return blocks[0] + near_in.astype(F32) + far_out.astype(F32)


def ring_order(count):
    if count == 8:
        return [0, 2, 4, 6, 7, 5, 3, 1]
    return list(range(count))


def ring_maps(count):
    order = ring_order(count)
    ahead = [(order[i], order[(i + 1) % count]) for i in range(count)]
    return order, ahead, [(b, a) for a, b in ahead]


def ring_gather(shard):
    count = lax.axis_size("seq")
    if count != 8:
        return lax.all_gather(shard, "seq", axis=0)
    order, ahead, back = ring_maps(count)
    place = jnp.asarray(np.argsort(order), jnp.int32)[lax.axis_index("seq")]
    owners = jnp.asarray(order, jnp.int32)
    full = jnp.zeros((count,) + shard.shape, shard.dtype)

    def put(full, piece, step, lo=0):
        owner = owners[(place + step + count) % count]
        start = (owner, lo) + (0,) * (shard.ndim - 1)
        return lax.dynamic_update_slice(full, piece[None], start)

    full = put(full, shard, 0)
    left = right = shard
    for step in range(1, count // 2):
        left = lax.ppermute(left, "seq", ahead)
        right = lax.ppermute(right, "seq", back)
        full = put(full, left, -step)
        full = put(full, right, step)
    half = shard.shape[0] // 2
    left = lax.ppermute(left[:half], "seq", ahead)
    right = lax.ppermute(right[half:], "seq", back)
    full = put(full, left, -(count // 2))
    full = put(full, right, count // 2, half)
    return full


def ring_scatter(term):
    count = lax.axis_size("seq")
    if count != 8:
        return lax.psum_scatter(term, "seq", scatter_dimension=0, tiled=True).astype(F32)
    order, ahead, back = ring_maps(count)
    place = jnp.asarray(np.argsort(order), jnp.int32)[lax.axis_index("seq")]
    owners = jnp.asarray(order, jnp.int32)
    rows = term.shape[0] // count
    half = rows // 2

    def mine(step, lo):
        owner = owners[(place + step + 2 * count) % count]
        return lax.dynamic_slice_in_dim(term, owner * rows + lo, half, 0)

    left, right = mine(-1, 0), mine(1, half)
    for step in range(2, count + 1):
        left = lax.ppermute(left, "seq", ahead).astype(F32) + mine(-step, 0).astype(F32)
        right = lax.ppermute(right, "seq", back).astype(F32) + mine(step, half).astype(F32)
        if step < count:
            left, right = left.astype(B16), right.astype(B16)
    return jnp.concatenate([left, right], axis=0)


def halve_scatter(term):
    count = lax.axis_size("seq")
    bits = count.bit_length() - 1
    seq = lax.axis_index("seq")
    rows = term.shape[0] // count
    half = rows // 2
    split = term.reshape((2,) * bits + (2, half, term.shape[1]))
    results = []
    for part, order in enumerate(([0] + list(range(bits - 1, 0, -1)), list(range(bits - 1, -1, -1)))):
        value = lax.index_in_dim(split, part, bits, keepdims=False)
        left = list(range(bits - 1, -1, -1))
        for bit in order:
            at = left.index(bit)
            on = (seq >> bit) & 1
            keep = lax.dynamic_index_in_dim(value, on, at, keepdims=False)
            give = lax.dynamic_index_in_dim(value, 1 - on, at, keepdims=False)
            value = keep.astype(F32) + swap(give, "seq", 1 << bit).astype(F32)
            left.remove(bit)
            if left:
                value = value.astype(B16)
        results.append(value)
    return jnp.concatenate(results, axis=0)


def spread_gather(shard):
    count = lax.axis_size("seq")
    copies = jnp.broadcast_to(shard[None], (count,) + shard.shape)
    full = lax.all_to_all(copies, "seq", 0, 0, tiled=True)
    return full.reshape((count * shard.shape[0],) + shard.shape[1:])


def shift_seq(values, step):
    count = lax.axis_size("seq")
    return lax.ppermute(values, "seq", [(i, (i + step) % count) for i in range(count)])


def unmix(values, axis, index):
    size, bit = values.shape[axis], 1
    while bit < size:
        cut = values.shape[:axis] + (size // (2 * bit), 2, bit) + values.shape[axis + 1 :]
        split = values.reshape(cut)
        values = jnp.where((index // bit) % 2 == 1, jnp.flip(split, axis + 1), split).reshape(values.shape)
        bit *= 2
    return values


def sync_small(total, group, own):
    n_seq, n_rep = lax.axis_size("seq"), lax.axis_size("rep")
    group_list, own_list = [group], [own]
    for axis_name, size in (("seq", n_seq), ("rep", n_rep)):
        bit = 1
        while bit < size:
            parts = [total] + group_list + own_list
            sizes = np.cumsum([0] + [p.shape[0] for p in parts])
            came = swap(jnp.concatenate(parts, axis=0), axis_name, bit)
            came = [came[a:b] for a, b in zip(sizes[:-1], sizes[1:])]
            total = total + came[0]
            count = len(group_list)
            if axis_name == "seq":
                group_list = [group_list[0] + came[1]]
            else:
                group_list = group_list + came[1 : 1 + count]
            own_list = own_list + came[1 + count :]
            bit *= 2
    groups = unmix(jnp.stack(group_list), 0, lax.axis_index("rep"))
    owns = jnp.stack(own_list).reshape((n_rep, n_seq) + own.shape)
    owns = unmix(unmix(owns, 0, lax.axis_index("rep")), 1, lax.axis_index("seq"))
    return total, groups, owns


def layer_norm(rows, gain, shift):
    row_mean = jnp.mean(rows, axis=-1, keepdims=True)
    centred = rows - row_mean
    variance = jnp.mean(centred * centred, axis=-1, keepdims=True)
    inverse = lax.rsqrt(variance + EPS)
    normed = centred * inverse
    return (normed * gain + shift, normed, inverse)


def norm_back(grad_rows, normed, inverse, gain):
    scaled = grad_rows * gain
    mean_one = jnp.mean(scaled, axis=-1, keepdims=True)
    mean_two = jnp.mean(scaled * normed, axis=-1, keepdims=True)
    grad_in = inverse * (scaled - mean_one - normed * mean_two)
    return (grad_in, jnp.sum(grad_rows * normed, axis=0), jnp.sum(grad_rows, axis=0))


def features(length, feat_count):
    ramp_unit = jnp.linspace(0.0, 1.0, length, dtype=F32)
    angles = jnp.arange(length, dtype=F32)[:, None] * (2.0 * math.pi / length)
    band_freqs = jnp.linspace(
        0.0001, (feat_count - 1) // 2 - 1.0, (feat_count - 1) // 2, dtype=F32
    )[None, :]
    phase_grid = band_freqs * angles
    grid_out = jnp.concatenate(
        [ramp_unit[:, None], jnp.cos(phase_grid), -jnp.sin(phase_grid)], axis=1
    )
    return (grid_out, ramp_unit)


def filter_columns(
    feature_grid,
    ramp_unit,
    start_chan,
    chan_count,
    model_width,
    feat_weight,
    feat_bias,
    inner_weight,
    inner_bias,
    deep_weight,
    deep_bias,
    sine_freq,
    columns,
):
    freq = sine_freq[:, None]

    def layer(weight, bias, below):
        grown = lax.dot_general(weight, below, (((0,), (0,)), ((), ())), precision=HIGH)
        return jnp.sin(freq * (grown + bias[:, None]))

    hidden = layer(feat_weight, feat_bias, feature_grid.T)
    hidden = layer(inner_weight, inner_bias, hidden)
    hidden = layer(deep_weight, deep_bias, hidden)
    deltas = jnp.abs(
        jnp.linspace(math.log(0.01) / 0.3, math.log(0.01) / 1.5, model_width, dtype=F32)
    )
    local_rates = lax.dynamic_slice_in_dim(deltas, start_chan, chan_count)
    return lax.dot_general(
        columns, hidden, (((0,), (0,)), ((), ())), precision=HIGH
    ) * jnp.exp(-ramp_unit[None, :] * local_rates[:, None])


def sin_cos(x):
    turns = jnp.floor(x * (1.0 / math.pi) + 0.5)
    r = x - turns * 3.140625
    r = r - turns * 9.67502593994140625e-4
    r = r - turns * 1.509957990978376432e-7
    sign = 1.0 - 2.0 * (turns - 2.0 * jnp.floor(turns * 0.5))
    q = r * r
    sin = r + r * q * (
        -1.6666666666e-1
        + q * (8.3333333e-3 + q * (-1.98412698e-4 + q * (2.7557319e-6 + q * -2.505210838e-8)))
    )
    cos = 1.0 + q * (
        -0.5
        + q * (4.16666666e-2 + q * (-1.3888888e-3 + q * (2.48015873e-5 + q * (-2.75573192e-7 + q * 2.0876757e-9))))
    )
    return sin * sign, cos * sign


def dot_high(left, right, dims):
    return lax.dot_general(left, right, (dims, ((), ())), precision=HIGH, preferred_element_type=F32)


def filter_forward_kernel(
    grid_ref, ramp_ref, rate_ref, w1_ref, w2_ref, w3_ref, small_ref, columns_ref, twist_ref, hi_ref, lo_ref,
    spec_ref, sin_ref, cos_ref, z_ref
):
    blocks, length = twist_ref.shape[0], twist_ref.shape[3]
    freq = small_ref[:, 3:4]
    below = grid_ref[...]
    for i, w_ref in enumerate((w1_ref, w2_ref, w3_ref)):
        grown = dot_high(w_ref[...].T, below, ((1,), (0,)))
        sin, cos = sin_cos(freq * (grown + small_ref[:, i : i + 1]))
        sin_ref[i] = sin
        cos_ref[i] = cos
        below = sin
    kern = dot_high(columns_ref[...].T, below, ((1,), (0,))) * jnp.exp(-rate_ref[...] * ramp_ref[...])
    cut = [kern[:, b * length : (b + 1) * length] for b in range(blocks)]
    turn_rows(cut, twist_ref, z_ref, 0, blocks)
    spec_ref[...] = dot_split(z_ref[...], hi_ref[...], lo_ref[...], ((1,), (0,)))


def filter_backward_kernel(
    gk_ref, grid_ref, ramp_ref, rate_ref, w1_ref, w2_ref, w3_ref, small_ref, columns_ref, sin_ref, cos_ref,
    gc_ref, g1_ref, g2_ref, g3_ref, gsmall_ref
):
    freq = small_ref[:, 3:4]
    gk = jnp.concatenate([gk_ref[b] for b in range(gk_ref.shape[0])], axis=1)
    gk = gk * jnp.exp(-rate_ref[...] * ramp_ref[...])
    last = ((1,), (1,))
    gc_ref[...] = dot_high(sin_ref[2], gk, last)
    grad = dot_high(columns_ref[...], gk, ((1,), (0,)))
    gfreq = jnp.zeros(freq.shape, F32)
    gbias = [None] * 3
    for i, w_ref, g_ref in ((2, w3_ref, g3_ref), (1, w2_ref, g2_ref), (0, w1_ref, g1_ref)):
        turn = grad * cos_ref[i]
        below = sin_ref[i - 1] if i else grid_ref[...]
        raw = dot_high(turn, below, last)
        total = jnp.sum(turn, axis=1, keepdims=True)
        g_ref[...] = raw * freq
        gbias[i] = total * freq
        gfreq = gfreq + jnp.sum(raw * w_ref[...].T, axis=1, keepdims=True) + total * small_ref[:, i : i + 1]
        if i:
            grad = dot_high(w_ref[...], turn * freq, ((1,), (0,)))
    gsmall_ref[...] = jnp.concatenate(gbias + [gfreq], axis=1)


def feature_table(length, feat_count):
    ramp = np.linspace(0.0, 1.0, length, dtype=np.float32)
    angles = np.arange(length, dtype=np.float32)[:, None] * np.float32(2.0 * math.pi / length)
    half = (feat_count - 1) // 2
    bands = np.linspace(0.0001, half - 1.0, half, dtype=np.float32)[None, :]
    phase = (bands * angles).astype(np.float64)
    table = np.concatenate([ramp[:, None], np.cos(phase), -np.sin(phase)], axis=1)
    return np.ascontiguousarray(table.T).astype(np.float32), ramp[None, :]


def decay_rates(model):
    return np.abs(
        np.linspace(math.log(0.01) / 0.3, math.log(0.01) / 1.5, model, dtype=np.float32)
    )[:, None]


def transform_tables(blocks, length):
    time = np.arange(blocks * length).reshape(blocks, 1, length)
    cls = np.arange(blocks).reshape(1, blocks, 1)
    period = 4 * blocks * length
    turn = (time * (2 * cls + 1)) % period * (2.0 * np.pi / period)
    twist = np.stack([np.cos(turn), -np.sin(turn)], axis=2).astype(np.float32)
    step = np.arange(length)
    turn = (step[:, None] * step[None, :]) % length * (2.0 * np.pi / length)
    cos, sin = np.cos(turn), np.sin(turn)
    table = np.block([[cos, -sin], [sin, cos]]).astype(np.float32)
    return twist, table


def split_table(table):
    hi = table.astype(B16)
    return jnp.asarray(hi), jnp.asarray((table - hi.astype(np.float32)).astype(B16))


def spectrum_of(signal, twist, table):
    turned = jnp.einsum("bqzl,brl->qrzl", twist[: signal.shape[0]], signal, precision=HIGH)
    flat = turned.reshape(turned.shape[:2] + (-1,))
    return jnp.einsum("qrk,kf->qrf", flat, table, precision=HIGH)


def signal_of(spectrum, twist, table):
    blocks, length = twist.shape[0], twist.shape[3]
    turned = jnp.einsum("qrf,kf->qrk", spectrum, table, precision=HIGH)
    turned = turned.reshape(turned.shape[:2] + (2, length))
    return jnp.einsum("bqzl,qrzl->brl", twist, turned, precision=HIGH) * (1.0 / (blocks * length))


def times(left, right, conj_right):
    half = left.shape[-1] // 2
    lr, li = left[..., :half], left[..., half:]
    rr, ri = right[..., :half], right[..., half:]
    if conj_right:
        return jnp.concatenate([lr * rr + li * ri, li * rr - lr * ri], axis=-1)
    return jnp.concatenate([lr * rr - li * ri, lr * ri + li * rr], axis=-1)


def dot_split(values, hi, lo, dims):
    top = values.astype(B16)
    rest = (values - top.astype(F32)).astype(B16)
    dot = partial(lax.dot_general, dimension_numbers=(dims, ((), ())), preferred_element_type=F32)
    return dot(top, hi) + dot(rest, hi) + dot(top, lo)


def turn_rows(blocks_in, twist_ref, z_ref, base, classes):
    rows, length = blocks_in[0].shape
    for q in range(classes):
        for z in range(2):
            acc = None
            for b, block in enumerate(blocks_in):
                term = block * twist_ref[b, q, z : z + 1]
                acc = term if acc is None else acc + term
            z_ref[base + q * rows : base + (q + 1) * rows, z * length : (z + 1) * length] = acc


def back_rows(w, base, rows, block, twist_ref, classes):
    length = w.shape[1] // 2
    acc = None
    for q in range(classes):
        lo, hi = base + q * rows, base + (q + 1) * rows
        for z in range(2):
            term = w[lo:hi, z * length : (z + 1) * length] * twist_ref[block, q, z : z + 1]
            acc = term if acc is None else acc + term
    return acc * (1.0 / (classes * length))


def conv_forward_kernel(short_blocks, x_ref, kern_ref, twist_ref, hi_ref, lo_ref, skip_ref, out_ref, spec_ref, z_ref):
    blocks = twist_ref.shape[0]
    rows = x_ref.shape[1]
    span = blocks * rows
    first = [x_ref[b].astype(F32) for b in range(blocks)]
    second = [x_ref[blocks + b].astype(F32) for b in range(short_blocks)]
    turn_rows(first, twist_ref, z_ref, 0, blocks)
    turn_rows(second, twist_ref, z_ref, span, blocks)
    spec = dot_split(z_ref[...], hi_ref[...], lo_ref[...], ((1,), (0,)))
    spec_ref[...] = spec
    kern = kern_ref[...]
    prod = jnp.concatenate([times(spec[:span], kern, False), times(spec[span:], kern, False)], axis=0)
    w = dot_split(prod, hi_ref[...], lo_ref[...], ((1,), (1,)))
    skip = skip_ref[...]
    for b in range(blocks):
        out_ref[b] = (back_rows(w, 0, rows, b, twist_ref, blocks) + skip * first[b]).astype(B16)
        acc = back_rows(w, span, rows, b, twist_ref, blocks)
        if b < short_blocks:
            acc = acc + skip * second[b]
        out_ref[blocks + b] = acc.astype(B16)


def conv_backward_kernel(
    short_blocks, g_ref, spec_ref, kern_ref, twist_ref, hi_ref, lo_ref, skip_ref, out_ref, grad_kern_ref, z_ref, p_ref
):
    blocks = twist_ref.shape[0]
    rows = g_ref.shape[1]
    span = blocks * rows
    first = [g_ref[b].astype(F32) for b in range(blocks)]
    second = [g_ref[blocks + b].astype(F32) for b in range(short_blocks)]
    turn_rows(first, twist_ref, z_ref, 0, blocks)
    turn_rows(second, twist_ref, z_ref, span, blocks)
    grad = dot_split(z_ref[...], hi_ref[...], lo_ref[...], ((1,), (0,)))
    kern = kern_ref[...]
    p_ref[0:span] = times(grad[:span], kern, True)
    p_ref[span : 2 * span] = times(grad[span:], kern, True)
    p_ref[2 * span :] = times(grad[:span], spec_ref[0:span], True) + times(
        grad[span:], spec_ref[span:], True
    )
    w = dot_split(p_ref[...], hi_ref[...], lo_ref[...], ((1,), (1,)))
    skip = skip_ref[...]
    for b in range(blocks):
        out_ref[b] = (back_rows(w, 0, rows, b, twist_ref, blocks) + skip * first[b]).astype(B16)
        if b < short_blocks:
            acc = back_rows(w, span, rows, b, twist_ref, blocks) + skip * second[b]
            out_ref[blocks + b] = acc.astype(B16)
        else:
            out_ref[blocks + b] = jnp.zeros(out_ref.shape[1:], B16)
        grad_kern_ref[b] = back_rows(w, 2 * span, rows, b, twist_ref, blocks)


def conv_forward(received, kern_spec, twist, table, skip_local):
    blocks, rows, length = received.shape[0] // 2, received.shape[1], received.shape[2]
    short_blocks = -(-blocks // 4)
    skip = skip_local[:, None]
    if blocks != 4:
        x = received.astype(F32)
        spec = jnp.concatenate(
            [
                spectrum_of(x[:blocks], twist, table),
                spectrum_of(x[blocks : blocks + short_blocks], twist, table),
            ],
            axis=0,
        )
        kern = jnp.concatenate([kern_spec, kern_spec], axis=0)
        prod = times(spec, kern, False)
        out = jnp.concatenate(
            [signal_of(prod[:blocks], twist, table), signal_of(prod[blocks:], twist, table)], axis=0
        )
        return ((out + skip * x).astype(B16), spec)
    hi, lo = split_table(table)
    height = 2 * blocks * rows
    out, spec = pl.pallas_call(
        partial(conv_forward_kernel, short_blocks),
        out_shape=(
            jax.ShapeDtypeStruct(received.shape, B16),
            jax.ShapeDtypeStruct((height, 2 * length), F32),
        ),
        scratch_shapes=[pltpu.VMEM((height, 2 * length), F32)],
        compiler_params=pltpu.CompilerParams(vmem_limit_bytes=VMEM_BYTES),
        name="conv_forward",
    )(received, kern_spec.reshape(blocks * rows, 2 * length), twist, hi, lo, skip)
    return out, spec


def conv_backward(grads, spec, kern_spec, twist, table, skip_local):
    blocks, rows, length = grads.shape[0] // 2, grads.shape[1], grads.shape[2]
    short_blocks = -(-blocks // 4)
    skip = skip_local[:, None]
    if blocks != 4:
        g = grads.astype(F32)
        first = spectrum_of(g[:blocks], twist, table)
        second = spectrum_of(g[blocks : blocks + short_blocks], twist, table)
        one = signal_of(times(first, kern_spec, True), twist, table)
        two = signal_of(times(second, kern_spec, True), twist, table)
        cross = times(first, spec[:blocks], True) + times(second, spec[blocks:], True)
        out = jnp.concatenate([one, two], axis=0) + skip * g
        return (out.astype(B16), signal_of(cross, twist, table))
    hi, lo = split_table(table)
    span = blocks * rows
    out, grad_kern = pl.pallas_call(
        partial(conv_backward_kernel, short_blocks),
        out_shape=(
            jax.ShapeDtypeStruct(grads.shape, B16),
            jax.ShapeDtypeStruct((blocks, rows, length), F32),
        ),
        scratch_shapes=[
            pltpu.VMEM((2 * span, 2 * length), F32),
            pltpu.VMEM((3 * span, 2 * length), F32),
        ],
        compiler_params=pltpu.CompilerParams(vmem_limit_bytes=VMEM_BYTES),
        name="conv_backward",
    )(grads, spec, kern_spec.reshape(span, 2 * length), twist, hi, lo, skip)
    return out, grad_kern


def in_order(ref, rep, lead=()):
    count = ref.shape[-1] // LANE
    return [
        ref[lead + (slice(None), pl.ds(pl.multiple_of((rep ^ j) * LANE, LANE), LANE))]
        for j in range(count)
    ]


def put_rel(ref, rep, values, lead=()):
    for j in range(ref.shape[-1] // LANE):
        ref[lead + (slice(None), pl.ds(pl.multiple_of((rep ^ j) * LANE, LANE), LANE))] = values[
            :, j * LANE : (j + 1) * LANE
        ]


def extended(proj_ref, halo_ref, exists, rep, p):
    blocks = [halo_ref[p, :, :LANE]] + in_order(proj_ref, rep, (p,)) + [halo_ref[p, :, LANE:]]
    return jnp.concatenate(blocks, axis=1).astype(F32) * exists


def short_of(ext, col_ref, p):
    return (
        col_ref[:, p : p + 1] * pltpu.roll(ext, 2, 1)
        + col_ref[:, 3 + p : 4 + p] * pltpu.roll(ext, 1, 1)
        + col_ref[:, 6 + p : 7 + p] * ext
        + col_ref[:, 9 + p : 10 + p]
    )


def gate_kernel(rep_ref, proj_ref, halo_ref, col_ref, mask_ref, out_ref):
    rep = rep_ref[0]
    mask, exists = mask_ref[0:1], mask_ref[1:2]
    gate_in = short_of(extended(proj_ref, halo_ref, exists, rep, 1), col_ref, 1)
    values = short_of(extended(proj_ref, halo_ref, exists, rep, 2), col_ref, 2)
    gated = values * gate_in * mask
    out_ref[...] = gated[:, LANE:-LANE].astype(B16)


def output_kernel(rep_ref, proj_ref, halo_ref, col_ref, mask_ref, mixed_ref, out_ref):
    rep = rep_ref[0]
    gate_out = short_of(extended(proj_ref, halo_ref, mask_ref[1:2], rep, 0), col_ref, 0)
    put_rel(out_ref, rep, (gate_out[:, LANE:-LANE] * mixed_ref[...].astype(F32)).astype(B16))


def grad_mix_kernel(rep_ref, proj_ref, halo_ref, col_ref, mask_ref, mixed_ref, gy_ref, out_ref, first_ref):
    rep = rep_ref[0]
    gate_out = short_of(extended(proj_ref, halo_ref, mask_ref[1:2], rep, 0), col_ref, 0)
    gy = jnp.concatenate(in_order(gy_ref, rep), axis=1).astype(F32)
    out_ref[...] = (gy * gate_out[:, LANE:-LANE]).astype(B16)
    first_ref[...] = gy[:, :LANE] * mixed_ref[:, :LANE].astype(F32)


def grad_proj_kernel(
    rep_ref, proj_ref, halo_ref, col_ref, mask_ref, mixed_ref, gy_ref, ggated_ref, gnext_ref, onext_ref, out_ref, sum_ref
):
    rep = rep_ref[0]
    mask, exists = mask_ref[0:1], mask_ref[1:2]
    size = mask_ref.shape[1]
    mid = slice(LANE, size - LANE)
    gy = jnp.concatenate(in_order(gy_ref, rep), axis=1).astype(F32)
    zero = jnp.zeros((gy.shape[0], LANE), F32)
    next_on = exists[:, size - LANE :]
    ext = [extended(proj_ref, halo_ref, exists, rep, p) for p in range(3)]
    short = [short_of(ext[p], col_ref, p) for p in range(3)]
    ggated = jnp.concatenate(
        [zero, ggated_ref[...].astype(F32), gnext_ref[...].astype(F32) * next_on], axis=1
    )
    ggated = ggated * mask
    gout = gy * mixed_ref[...].astype(F32)
    gshort = [
        jnp.concatenate([zero, gout, onext_ref[...] * next_on], axis=1),
        ggated * short[2],
        ggated * short[1],
    ]
    gated = short[2][:, mid] * short[1][:, mid] * mask[:, mid]
    sums = [jnp.sum(gy * short[0][:, mid] * gated, axis=1, keepdims=True)]
    for p in range(3):
        mine = gshort[p][:, mid]
        sums.append(jnp.sum(mine, axis=1, keepdims=True))
        sums.append(jnp.sum(mine * ext[p][:, mid], axis=1, keepdims=True))
        sums.append(jnp.sum(mine * pltpu.roll(ext[p], 1, 1)[:, mid], axis=1, keepdims=True))
        sums.append(jnp.sum(mine * pltpu.roll(ext[p], 2, 1)[:, mid], axis=1, keepdims=True))
        gproj = (
            col_ref[:, 6 + p : 7 + p] * gshort[p]
            + col_ref[:, 3 + p : 4 + p] * pltpu.roll(gshort[p], size - 1, 1)
            + col_ref[:, p : p + 1] * pltpu.roll(gshort[p], size - 2, 1)
        )[:, mid].astype(B16)
        sums.append(jnp.sum(gproj.astype(F32), axis=1, keepdims=True))
        put_rel(out_ref, rep, gproj, (p,))
    sum_ref[...] = jnp.concatenate(sums, axis=1)


def token_call(kernel, name, arrays, outs):
    step = 64

    def spec(shape, cut):
        if not cut:
            return pl.BlockSpec(shape, lambda i: (0,) * len(shape))
        if len(shape) == 3:
            return pl.BlockSpec((shape[0], step, shape[2]), lambda i: (0, i, 0))
        return pl.BlockSpec((step, shape[1]), lambda i: (i, 0))

    width = outs[0].shape[-2]
    return pl.pallas_call(
        kernel,
        grid=(width // step,),
        in_specs=[pl.BlockSpec(memory_space=pltpu.SMEM)] + [spec(a.shape, cut) for a, cut in arrays[1:]],
        out_specs=[spec(o.shape, True) for o in outs],
        out_shape=outs,
        compiler_params=pltpu.CompilerParams(vmem_limit_bytes=VMEM_BYTES),
        name=name,
    )(*[a for a, _ in arrays])


def rows128(values):
    flat = values.reshape(-1)
    return jnp.pad(flat, (0, -flat.shape[0] % 1024)).reshape(-1, 128)


def per_device(
    tokens,
    cotangent,
    lengths,
    in_weight,
    in_bias,
    short_taps,
    short_bias,
    feat_weight,
    feat_bias,
    inner_weight,
    inner_bias,
    deep_weight,
    deep_bias,
    sine_freq,
    kernel_weight,
    skip_gain,
    out_weight,
    out_bias,
    norm1_gain,
    norm1_shift,
    norm2_gain,
    norm2_shift,
    up_weight,
    up_bias,
    down_weight,
    down_bias,
):
    n_seq, n_rep = lax.axis_size("seq"), lax.axis_size("rep")
    seq, rep = lax.axis_index("seq"), lax.axis_index("rep")
    tok_rows, model = tokens.shape
    group = tok_rows * n_rep
    blocks = n_seq // 2
    seq_len = blocks * group
    chan = model // (n_seq * n_rep)
    width = model // n_rep
    hidden = up_weight.shape[2]
    block_start = rep * width
    chan_start = block_start + seq * chan
    rep_scalar = jnp.reshape(rep, (1,)).astype(jnp.int32)

    item_len = jnp.where(seq // blocks == 0, lengths[0], lengths[1])
    at = (seq % blocks) * group
    row_mask = (at + rep * tok_rows + jnp.arange(tok_rows, dtype=jnp.int32) < item_len).astype(F32)[:, None]
    position = at - LANE + jnp.arange(group + 2 * LANE, dtype=jnp.int32)
    mask_ext = jnp.stack([position < item_len, (position >= 0) & (position < seq_len)]).astype(F32)
    mask_ext = jnp.pad(mask_ext, ((0, 6), (0, 0)))

    full_in = ring_gather(in_weight[0]).reshape(model, 3, width)
    full_out = spread_gather(out_weight[0])
    full_up = lax.all_gather(up_weight[0], "seq", axis=0, tiled=True)
    full_down = lax.all_gather(down_weight[0], "seq", axis=0, tiled=True)

    residual = tokens.astype(F32)
    normed_one, unit_one, scale_one = layer_norm(residual, norm1_gain[0], norm1_shift[0])
    normed_one = normed_one.astype(B16)
    rows_one = gather_rel(normed_one)
    rel = rows_one.reshape(n_rep, tok_rows, model)
    last_rows = lax.dynamic_index_in_dim(rel, rep ^ (n_rep - 1), 0, False)[-HALO:]
    first_rows = lax.dynamic_index_in_dim(rel, rep, 0, False)[:HALO]
    before = shift_seq(last_rows, 1)
    after = shift_seq(first_rows, -1)
    gap = jnp.zeros((LANE - HALO, model), B16)
    halo_rows = jnp.concatenate([gap, before, after, gap], axis=0)
    proj_bias = lax.dynamic_slice_in_dim(in_bias[0], block_start, width, 1)[:, :, None]

    def project(rows):
        return (
            jnp.einsum("td,dpc->pct", rows, full_in, preferred_element_type=F32) + proj_bias
        ).astype(B16)

    proj = project(rows_one)
    halo = project(halo_rows)

    tap_cols = lax.dynamic_slice_in_dim(short_taps[0], block_start, width, 2).reshape(9, width)
    bias_cols = lax.dynamic_slice_in_dim(short_bias[0], block_start, width, 1)
    cols = jnp.pad(jnp.concatenate([tap_cols, bias_cols], axis=0), ((0, 4), (0, 0))).T
    common = [(rep_scalar, True), (proj, True), (halo, True), (cols, True), (mask_ext, False)]
    flat_shape = jax.ShapeDtypeStruct((width, group), B16)
    (gated,) = token_call(gate_kernel, "gate", common, [flat_shape])
    received = lax.all_to_all(gated.reshape(n_seq, chan, group), "seq", 0, 0, tiled=True)

    skip_local = lax.dynamic_slice_in_dim(skip_gain[0], chan_start, chan, 0)
    columns = lax.dynamic_slice_in_dim(kernel_weight[0], chan_start, chan, 1)
    twist, table = transform_tables(blocks, group)
    nets = (feat_weight[0], inner_weight[0], deep_weight[0])
    if blocks == 4:
        grid, ramp = feature_table(seq_len, feat_weight.shape[1])
        rates = lax.dynamic_slice_in_dim(jnp.asarray(decay_rates(model)), chan_start, chan, 0)
        smalls = jnp.concatenate([feat_bias, inner_bias, deep_bias, sine_freq], axis=0).T
        filt = smalls.shape[0]
        hi, lo = split_table(table)
        kern_spec, sines, cosines = pl.pallas_call(
            filter_forward_kernel,
            out_shape=(
                jax.ShapeDtypeStruct((blocks * chan, 2 * group), F32),
                jax.ShapeDtypeStruct((3, filt, seq_len), F32),
                jax.ShapeDtypeStruct((3, filt, seq_len), F32),
            ),
            scratch_shapes=[pltpu.VMEM((blocks * chan, 2 * group), F32)],
            compiler_params=pltpu.CompilerParams(vmem_limit_bytes=VMEM_BYTES),
            cost_estimate=pl.CostEstimate(flops=10**6, bytes_accessed=10**6, transcendentals=0),
            name="filter_forward",
        )(grid, ramp, rates, *nets, smalls, columns, twist, hi, lo)
        kern_spec = kern_spec.reshape(blocks, chan, 2 * group)

        def kernel_pull(grad_kernel):
            shapes = [columns.shape] + [w.shape[::-1] for w in nets] + [smalls.shape]
            gcols, g1, g2, g3, gsmalls = pl.pallas_call(
                filter_backward_kernel,
                out_shape=tuple(jax.ShapeDtypeStruct(shape, F32) for shape in shapes),
                compiler_params=pltpu.CompilerParams(vmem_limit_bytes=VMEM_BYTES),
                cost_estimate=pl.CostEstimate(flops=10**6, bytes_accessed=10**6, transcendentals=0),
                name="filter_backward",
            )(grad_kernel, grid, ramp, rates, *nets, smalls, columns, sines, cosines)
            gs = gsmalls.T
            return (g1.T, gs[0], g2.T, gs[1], g3.T, gs[2], gs[3], gcols)

    else:
        feature_grid, ramp_unit = features(seq_len, feat_weight.shape[1])
        kernel, pull = jax.vjp(
            partial(filter_columns, feature_grid, ramp_unit, chan_start, chan, model),
            feat_weight[0],
            feat_bias[0],
            inner_weight[0],
            inner_bias[0],
            deep_weight[0],
            deep_bias[0],
            sine_freq[0],
            columns,
        )
        kern_spec = spectrum_of(kernel.reshape(chan, blocks, group).transpose(1, 0, 2), twist, table)

        def kernel_pull(grad_kernel):
            return pull(grad_kernel.transpose(1, 0, 2).reshape(chan, seq_len))

    mixed_chan, kept_spec = conv_forward(received, kern_spec, twist, table, skip_local)
    mixed = lax.all_to_all(mixed_chan, "seq", 0, 0, tiled=True).reshape(width, group)
    (y_cols,) = token_call(output_kernel, "output", common + [(mixed, True)], [flat_shape])

    middle_part = jnp.einsum("ct,oc->to", y_cols, full_out, preferred_element_type=F32)
    middle = residual + (scatter_rel(middle_part) + out_bias[0])
    normed_two, unit_two, scale_two = layer_norm(middle, norm2_gain[0], norm2_shift[0])
    rows_two = gather_rel(normed_two.astype(B16))

    grad_top = cotangent.astype(F32) * row_mask
    grad_mlp = grad_top.astype(B16)
    mlp_rows = gather_rel(grad_mlp)
    grad_act = jnp.dot(mlp_rows, full_down, preferred_element_type=F32)
    up_block = lax.dynamic_slice_in_dim(up_bias[0], rep * hidden, hidden, 0)
    pre_act = jnp.dot(rows_two, full_up, preferred_element_type=F32) + up_block
    phi = 0.5 * (1.0 + lax.erf(pre_act * math.sqrt(0.5)))
    act_rows = (pre_act * phi).astype(B16)
    slope = phi + pre_act * (jnp.exp(-0.5 * pre_act * pre_act) * (1.0 / math.sqrt(2.0 * math.pi)))
    grad_pre = (grad_act * slope).astype(B16)
    grad_two = scatter_rel(jnp.einsum("tf,df->td", grad_pre, full_up, preferred_element_type=F32))
    mlp_part = jnp.einsum("tf,of->to", act_rows, full_down, preferred_element_type=F32)
    layer_out = (middle + (scatter_rel(mlp_part) + down_bias[0])).astype(B16)
    term_down = jnp.einsum("to,tf->of", mlp_rows, act_rows, preferred_element_type=F32)
    term_up = jnp.einsum("td,tf->df", rows_two, grad_pre, preferred_element_type=F32)
    grad_two, term_down = lax.optimization_barrier((grad_two, term_down.astype(B16)))
    grad_down_bias = jnp.sum(grad_mlp.astype(F32), axis=0)
    grad_up_block = jnp.sum(grad_pre.astype(F32), axis=0)

    grad_down = lax.psum_scatter(
        term_down, "seq", scatter_dimension=0, tiled=True
    ).astype(F32)
    grad_up = ring_scatter(term_up.astype(B16))

    grad_unit_two, grad_gain_two, grad_shift_two = norm_back(
        grad_two, unit_two, scale_two, norm2_gain[0]
    )
    grad_middle = grad_top + grad_unit_two
    grad_mix = grad_middle.astype(B16)
    grad_out_bias = jnp.sum(grad_mix.astype(F32), axis=0)
    mix_rows = gather_rel(grad_mix)
    gy_cols = jnp.einsum("to,oc->ct", mix_rows, full_out, preferred_element_type=F32).astype(B16)
    term_out = jnp.einsum("to,ct->oc", mix_rows, y_cols, preferred_element_type=F32)
    grad_out = halve_scatter(term_out.astype(B16))

    grad_mixed, gate_first = token_call(
        grad_mix_kernel,
        "grad_mix",
        common + [(mixed, True), (gy_cols, True)],
        [flat_shape, jax.ShapeDtypeStruct((width, LANE), F32)],
    )
    gate_next = shift_seq(gate_first, -1)
    grads_chan = lax.all_to_all(grad_mixed.reshape(n_seq, chan, group), "seq", 0, 0, tiled=True)
    ggated_chan, grad_kernel = conv_backward(grads_chan, kept_spec, kern_spec, twist, table, skip_local)
    ggated = lax.all_to_all(ggated_chan, "seq", 0, 0, tiled=True).reshape(width, group)
    ggated_next = shift_seq(ggated[:, :LANE], -1)
    kernel_grads = kernel_pull(grad_kernel)
    grad_proj, col_sums = token_call(
        grad_proj_kernel,
        "grad_proj",
        common
        + [(mixed, True), (gy_cols, True), (ggated, True), (ggated_next, True), (gate_next, True)],
        [jax.ShapeDtypeStruct((3, width, group), B16), jax.ShapeDtypeStruct((width, 16), F32)],
    )

    one_part = jnp.einsum("pct,dpc->td", grad_proj, full_in, preferred_element_type=F32)
    grad_one = scatter_rel(one_part)
    term_in = jnp.einsum("td,pct->dpc", rows_one, grad_proj, preferred_element_type=F32)
    grad_in = halve_scatter(term_in.reshape(model, 3 * width).astype(B16))
    grad_in = grad_in.reshape(-1, 3, width)
    grad_unit_one, grad_gain_one, grad_shift_one = norm_back(
        grad_one, unit_one, scale_one, norm1_gain[0]
    )
    grad_tokens = grad_middle + grad_unit_one

    totals = [
        *kernel_grads[:7],
        grad_gain_one,
        grad_shift_one,
        grad_gain_two,
        grad_shift_two,
        grad_out_bias,
        grad_down_bias,
    ]
    packed = [rows128(t) for t in totals]
    group_part = jnp.concatenate([rows128(col_sums.T), rows128(grad_up_block)], axis=0)
    total, groups, owns = sync_small(jnp.concatenate(packed, axis=0), group_part, rows128(kernel_grads[7]))
    outs = []
    start = 0
    for t, p in zip(totals, packed):
        outs.append(total[start : start + p.shape[0]].reshape(-1)[: t.size].reshape((1,) + t.shape))
        start += p.shape[0]
    flat = groups.reshape(n_rep, -1)
    sums = flat[:, : 16 * width].reshape(n_rep, 16, width).transpose(1, 0, 2).reshape(16, model)
    grad_up_bias = flat[:, 16 * width : 16 * width + hidden].reshape(1, -1)
    filt = columns.shape[0]
    grad_kernel_weight = (
        owns.reshape(n_rep, n_seq, -1)[:, :, : filt * chan]
        .reshape(n_rep, n_seq, filt, chan)
        .transpose(2, 0, 1, 3)
        .reshape(1, filt, model)
    )
    pick = lambda offset: jnp.stack([sums[1 + 5 * p + offset] for p in range(3)])
    grad_skip = sums[0][None]
    grad_short_bias = pick(0)[None]
    grad_short_taps = jnp.stack([pick(3), pick(2), pick(1)])[None]
    grad_in_bias = pick(4)[None]
    return (
        layer_out,
        grad_tokens,
        grad_in[None],
        grad_in_bias,
        grad_short_taps,
        grad_short_bias,
        outs[0],
        outs[1],
        outs[2],
        outs[3],
        outs[4],
        outs[5],
        outs[6],
        grad_kernel_weight,
        grad_skip,
        grad_out[None],
        outs[11],
        outs[7],
        outs[8],
        outs[9],
        outs[10],
        grad_up[None],
        grad_up_bias,
        grad_down[None],
        outs[12],
    )


NN = ((1,), (0,))
NT = ((1,), (1,))
TN = ((0,), (0,))
PART = 64
REP, SEQ, AT, ITEM, OLDER, YOUNGER, OWNER, LEFT, RIGHT = 0, 1, 2, 3, 4, 5, 8, 16, 25
RING = [0, 2, 4, 6, 7, 5, 3, 1]
AHEAD = [(RING[i], RING[(i + 1) % 8]) for i in range(8)]
BACK = [(b, a) for a, b in AHEAD]


def meta_table(group):
    rows = []
    for seq in range(8):
        p = RING.index(seq)
        for rep in range(4):
            row = [rep, seq, (seq % 4) * group, seq // 4, int(seq % 4 != 0), int(seq % 4 != 3), 0, 0]
            row += [RING[(p + k) % 8] for k in (0, -1, 1, -2, 2, -3, 3, 4)]
            row += [RING[(p - k) % 8] for k in range(9)]
            row += [RING[(p + k) % 8] for k in range(9)]
            rows.append(row)
    return np.asarray(rows, np.int32)


COST = {"start": 4000, "setup": 4000, "filter_ahead": 6000}


def call(kernel, name, args, outs, scratch=(), limit=24, away=(), out_away=(), raw=()):
    away, out_away, raw = list(away), list(out_away), list(raw)
    hbm = pl.BlockSpec(memory_space=pltpu.HBM)

    def space(i, a):
        if i in away or i in raw:
            return hbm
        small = a.dtype == jnp.int32
        return pl.BlockSpec(memory_space=pltpu.SMEM if small else pltpu.VMEM)

    n_in, n_out, n_own = len(args), len(outs), len(scratch)
    bufs = [pltpu.VMEM(args[i].shape, args[i].dtype) for i in away]
    bufs += [pltpu.VMEM(outs[i].shape, outs[i].dtype) for i in out_away]
    sems = [pltpu.SemaphoreType.DMA((len(bufs),))] if bufs else []

    def body(*refs):
        ins, results = list(refs[:n_in]), list(refs[n_in : n_in + n_out])
        own, mine = refs[n_in + n_out : n_in + n_out + n_own], refs[n_in + n_out + n_own :]
        copies = []
        for k, i in enumerate(away):
            copies.append(pltpu.make_async_copy(ins[i], mine[k], mine[-1].at[k]))
            ins[i] = mine[k]
        for copy in copies:
            copy.start()
        for copy in copies:
            copy.wait()
        copies = []
        for k, i in enumerate(out_away, len(away)):
            copies.append(pltpu.make_async_copy(mine[k], results[i], mine[-1].at[k]))
            results[i] = mine[k]
        kernel(*ins, *results, *own)
        for copy in copies:
            copy.start()
        for copy in copies:
            copy.wait()

    return pl.pallas_call(
        body,
        out_shape=outs,
        in_specs=[space(i, a) for i, a in enumerate(args)],
        out_specs=[hbm if i in out_away or (-1 - i) in raw else pl.BlockSpec(memory_space=pltpu.VMEM) for i in range(n_out)],
        scratch_shapes=list(scratch) + bufs + sems,
        compiler_params=pltpu.CompilerParams(vmem_limit_bytes=limit * 2**20),
        cost_estimate=pl.CostEstimate(flops=COST.get(name, 1) * 10**6, bytes_accessed=10**5, transcendentals=0),
        name=name,
    )(*args)


def shape(dims, kind):
    return jax.ShapeDtypeStruct(tuple(dims), kind)


def dot(left, right, dims):
    return lax.dot_general(left, right, (dims, ((), ())), preferred_element_type=F32)


def place(index):
    return pl.ds(pl.multiple_of(index * LANE, LANE), LANE)


def normed_of(rows):
    centred = rows - jnp.mean(rows, axis=1, keepdims=True)
    inverse = lax.rsqrt(jnp.mean(centred * centred, axis=1, keepdims=True) + EPS)
    return centred * inverse, inverse


def item_length(meta_ref, len_ref):
    return jnp.where(meta_ref[ITEM] == 0, len_ref[0], len_ref[1])


def lane_masks(meta_ref, len_ref, size):
    lane = lax.broadcasted_iota(jnp.int32, (1, size), 1)
    real = (meta_ref[AT] - LANE + lane < item_length(meta_ref, len_ref)).astype(F32)
    older, younger = meta_ref[OLDER].astype(F32), meta_ref[YOUNGER].astype(F32)
    exists = jnp.where(lane < LANE, older, jnp.where(lane >= size - LANE, younger, 1.0))
    return real, exists


def start_kernel(x_ref, gain_ref, shift_ref, in_ref, out_w_ref, out_ref, io_ref):
    width = out_w_ref.shape[2]
    for p in range(3):
        io_ref[:, p * width : (p + 1) * width] = in_ref[p]
    io_ref[:, 3 * width :] = out_w_ref[0]
    unit, _ = normed_of(x_ref[...].astype(F32))
    out_ref[...] = (unit * gain_ref[...] + shift_ref[...]).astype(B16)


def halves_kernel(left_ref, right_ref, a_ref, b_ref):
    half = a_ref.shape[0]
    a_ref[...] = left_ref[:half]
    b_ref[...] = right_ref[half:]


def assemble_kernel(meta_ref, p0, p1, p2, p3, p4, p5, p6, a_ref, b_ref, out_ref):
    for k, ref in enumerate((p0, p1, p2, p3, p4, p5, p6)):
        out_ref[meta_ref[OWNER + k]] = ref[...]
    half = a_ref.shape[0]
    out_ref[meta_ref[OWNER + 7], :half] = a_ref[...]
    out_ref[meta_ref[OWNER + 7], half:] = b_ref[...]


def own_mask(meta_ref, len_ref, rows):
    row = lax.broadcasted_iota(jnp.int32, (rows, 1), 0)
    return (meta_ref[AT] + meta_ref[REP] * rows + row < item_length(meta_ref, len_ref)).astype(F32)


def setup_kernel(
    meta_ref, len_ref, top_ref, up_ref, down_ref, taps_ref, short_bias_ref, in_bias_ref, up_bias_ref, skip_ref, rate_ref,
    kern_w_ref, feat_ref, fb_ref, ib_ref, db_ref, sf_ref,
    rows_ref, ud_ref, cols_ref, upb_ref, chan_ref, columns_ref, small_col_ref, small_row_ref, w1_ref, *rest
):
    sems = rest[-1]
    copies = [
        pltpu.make_async_copy(up_ref, ud_ref.at[pl.ds(0, 1)], sems.at[0]),
        pltpu.make_async_copy(down_ref, ud_ref.at[pl.ds(1, 1)], sems.at[1]),
    ]
    for copy in copies:
        copy.start()
    top, taps, short_bias, in_bias, up_bias, skip, rate, kern_w, feat, fb, ib, db, sf = (
        top_ref, taps_ref, short_bias_ref, in_bias_ref, up_bias_ref, skip_ref, rate_ref, kern_w_ref, feat_ref,
        fb_ref, ib_ref, db_ref, sf_ref,
    )
    mask = own_mask(meta_ref, len_ref, top.shape[0])
    rows_ref[...] = (top[...].astype(F32) * mask).astype(B16)
    width = cols_ref.shape[0]
    chan = chan_ref.shape[0]
    rep, seq = meta_ref[REP], meta_ref[SEQ]
    lanes = pl.ds(pl.multiple_of(rep * width, width), width)
    rows = [taps[j, p, :, lanes] for j in range(3) for p in range(3)]
    rows += [short_bias[p, :, lanes] for p in range(3)] + [in_bias[p, :, lanes] for p in range(3)]
    stack = jnp.concatenate(rows + [jnp.zeros((LANE - 15, width), F32)], axis=0)
    cols_ref[...] = stack.T[:, :16]
    upb_ref[...] = up_bias[:, pl.ds(pl.multiple_of(rep * upb_ref.shape[1], LANE), upb_ref.shape[1])]
    turn = width - seq * chan
    stack = jnp.concatenate([skip[:, lanes], rate[:, lanes], jnp.zeros((LANE - 2, width), F32)], axis=0)
    chan_ref[...] = pltpu.roll(stack, turn, 1)[:, :LANE].T[:chan, :2]
    columns_ref[...] = pltpu.roll(kern_w[0, :, lanes], turn, 1)[:, :chan]
    filt = small_row_ref.shape[1]
    small = jnp.concatenate([fb[...], ib[...], db[...], sf[...]], axis=0)
    small_row_ref[...] = small
    wide = jnp.concatenate([small, jnp.zeros((4, LANE - filt), F32)], axis=1)
    wide = jnp.concatenate([wide, jnp.zeros((LANE - 4, LANE), F32)], axis=0)
    small_col_ref[...] = wide.T[:filt, :4]
    w1_ref[...] = jnp.concatenate([feat[i] for i in range(feat.shape[0])], axis=0)
    for copy in copies:
        copy.wait()


def edges_kernel(meta_ref, x0, x1, x2, x3, last_ref, first_ref):
    rep = meta_ref[REP]
    refs = (x0, x1, x2, x3)

    def chosen(index, lo):
        value = refs[0][lo : lo + HALO]
        for i in range(1, 4):
            value = jnp.where(index == i, refs[i][lo : lo + HALO].astype(F32), value.astype(F32))
        return value.astype(B16)

    last_ref[...] = chosen(rep ^ 3, x0.shape[0] - HALO)
    first_ref[...] = chosen(rep, 0)


def ext_of(proj_ref, halo_ref, exists, p, rows):
    return (
        jnp.concatenate(
            [halo_ref[p, rows, :LANE], proj_ref[p, rows, :], halo_ref[p, rows, LANE:]], axis=1
        ).astype(F32)
        * exists
    )


def short_from(ext, cols, p):
    return (
        cols[:, p : p + 1] * pltpu.roll(ext, 2, 1)
        + cols[:, 3 + p : 4 + p] * pltpu.roll(ext, 1, 1)
        + cols[:, 6 + p : 7 + p] * ext
        + cols[:, 9 + p : 10 + p]
    )


def project_kernel(
    meta_ref, len_ref, x0, x1, x2, x3, before_ref, after_ref, cols_ref,
    p0, p1, p2, p3, p4, p5, p6, a_ref, b_ref, io_full_ref, proj_ref, halo_ref, gated_ref
):
    assemble_kernel(meta_ref, p0, p1, p2, p3, p4, p5, p6, a_ref, b_ref, io_full_ref)
    io_ref = io_full_ref.reshape(-1, io_full_ref.shape[2])
    rep = meta_ref[REP]
    width, group = gated_ref.shape
    weight = io_ref[:, : 3 * width]
    for i, x_ref in enumerate((x0, x1, x2, x3)):
        cut = dot(x_ref[...], weight, NN).T
        for p in range(3):
            proj_ref[p, :, place(rep ^ i)] = (
                cut[p * width : (p + 1) * width] + cols_ref[:, 12 + p : 13 + p]
            ).astype(B16)
    edge = dot(jnp.concatenate([before_ref[...], after_ref[...]], axis=0), weight, NN)
    gap = jnp.zeros((LANE - HALO, 3 * width), F32)
    edge = jnp.concatenate([gap, edge, gap], axis=0).T
    for p in range(3):
        halo_ref[p] = (edge[p * width : (p + 1) * width] + cols_ref[:, 12 + p : 13 + p]).astype(B16)
    mask, exists = lane_masks(meta_ref, len_ref, group + 2 * LANE)
    for lo in range(0, width, PART):
        rows = slice(lo, lo + PART)
        cols = cols_ref[rows, :]
        gate_in = short_from(ext_of(proj_ref, halo_ref, exists, 1, rows), cols, 1)
        values = short_from(ext_of(proj_ref, halo_ref, exists, 2, rows), cols, 2)
        gated_ref[rows, :] = (values * gate_in * mask)[:, LANE:-LANE].astype(B16)


def out_project_kernel(
    meta_ref, len_ref, proj_ref, halo_ref, cols_ref, io_ref, mixed_ref, y_ref, give3_ref, give1_ref, keep2_ref, keep0_ref
):
    rep = meta_ref[REP]
    width, group = mixed_ref.shape
    _, exists = lane_masks(meta_ref, len_ref, group + 2 * LANE)
    for lo in range(0, width, LANE):
        rows = slice(lo, lo + LANE)
        gate_out = short_from(ext_of(proj_ref, halo_ref, exists, 0, rows), cols_ref[rows, :], 0)
        y = gate_out[:, LANE:-LANE] * mixed_ref[rows, :].astype(F32)
        for j in range(4):
            y_ref[rep ^ j, :, rows] = y[:, j * LANE : (j + 1) * LANE].T.astype(B16)
    outs = (keep0_ref, give1_ref, keep2_ref, give3_ref)
    left = y_ref[...].reshape(-1, width)
    rows = y_ref.shape[1]
    for lo in range(0, io_ref.shape[0], 256):
        part = dot(left, io_ref[lo : lo + 256, 3 * width :], NT)
        for i, ref in enumerate(outs):
            ref[:, lo : lo + 256] = part[i * rows : (i + 1) * rows].astype(ref.dtype)


def halves_far_kernel(left_ref, right_ref, a_ref, b_ref, sems):
    half = a_ref.shape[0]
    copies = [
        pltpu.make_async_copy(left_ref.at[pl.ds(0, half)], a_ref, sems.at[0]),
        pltpu.make_async_copy(right_ref.at[pl.ds(half, half)], b_ref, sems.at[1]),
    ]
    for copy in copies:
        copy.start()
    for copy in copies:
        copy.wait()


def assemble_far_kernel(meta_ref, p0, p1, p2, p3, p4, p5, p6, a_ref, b_ref, out_ref, sems):
    half = a_ref.shape[0]
    last = out_ref.at[meta_ref[OWNER + 7]]
    copies = [
        pltpu.make_async_copy(ref, out_ref.at[meta_ref[OWNER + k]], sems.at[k])
        for k, ref in enumerate((p0, p1, p2, p3, p4, p5, p6))
    ]
    copies.append(pltpu.make_async_copy(a_ref, last.at[pl.ds(0, half)], sems.at[7]))
    copies.append(pltpu.make_async_copy(b_ref, last.at[pl.ds(half, half)], sems.at[8]))
    for copy in copies:
        copy.start()
    for copy in copies:
        copy.wait()


def norm_second_kernel(x_ref, keep_ref, near_ref, far_ref, bias_ref, gain_ref, shift_ref, middle_ref, out_ref):
    middle = x_ref[...].astype(F32) + (
        keep_ref[...] + near_ref[...].astype(F32) + far_ref[...].astype(F32) + bias_ref[...]
    )
    middle_ref[...] = middle
    unit, _ = normed_of(middle)
    out_ref[...] = (unit * gain_ref[...] + shift_ref[...]).astype(B16)


def mlp_kernel(x0, x1, x2, x3, g0, g1, g2, g3, ud_ref, bias_ref, act_ref, gpre_ref, sum_ref):
    step = 256
    rows, model = x0.shape
    pieces = ((x0, g0), (x1, g1), (x2, g2), (x3, g3))
    for lo in range(0, act_ref.shape[1], step):
        cut = slice(lo, lo + step)
        up = ud_ref[:, 0, :, cut].reshape(model, step)
        down = ud_ref[:, 1, :, cut].reshape(model, step)
        total = None
        for i, (x_ref, g_ref) in enumerate(pieces):
            at = slice(i * rows, (i + 1) * rows)
            pre = dot(x_ref[...], up, NN) + bias_ref[:, cut]
            gact = dot(g_ref[...], down, NN)
            phi = 0.5 * (1.0 + lax.erf(pre * math.sqrt(0.5)))
            slope = phi + pre * (jnp.exp(-0.5 * pre * pre) * (1.0 / math.sqrt(2.0 * math.pi)))
            act_ref[at, cut] = (pre * phi).astype(B16)
            gpre = (gact * slope).astype(B16)
            gpre_ref[at, cut] = gpre
            part = jnp.sum(gpre.astype(F32), axis=0, keepdims=True)
            total = part if total is None else total + part
        sum_ref[:, cut] = total


def rows_kernel(which, left_ref, ud_ref, give3_ref, give1_ref, keep2_ref, keep0_ref):
    rows, model = give3_ref.shape
    owned = ud_ref.shape[2]
    outs = (keep0_ref, give1_ref, keep2_ref, give3_ref)
    for k in range(0, ud_ref.shape[0], 2):
        weight = ud_ref[k : k + 2, which].reshape(2 * owned, -1)
        part = dot(left_ref[...], weight, NT)
        for i, ref in enumerate(outs):
            ref[:, k * owned : (k + 2) * owned] = part[i * rows : (i + 1) * rows].astype(ref.dtype)


def mlp_grad_kernel(meta_ref, x0, x1, x2, x3, g0, g1, g2, g3, act_ref, gpre_ref, out_ref, a_ref, b_ref):
    grad_pair((x0, x1, x2, x3), gpre_ref[...], out_ref, slice(None), 0)
    grad_pair((g0, g1, g2, g3), act_ref[...], out_ref, slice(None), out_ref.shape[3] // 2)
    give_first(meta_ref, out_ref, a_ref, b_ref)


def norm_second_back_kernel(
    meta_ref, len_ref, keep_ref, near_ref, far_ref, middle_ref, top_ref, gain_ref, out_ref, gx_ref, sum_ref
):
    grad = keep_ref[...] + near_ref[...].astype(F32) + far_ref[...].astype(F32)
    unit, inverse = normed_of(middle_ref[...])
    scaled = grad * gain_ref[...]
    one = jnp.mean(scaled, axis=1, keepdims=True)
    two = jnp.mean(scaled * unit, axis=1, keepdims=True)
    top = top_ref[...].astype(F32) * own_mask(meta_ref, len_ref, top_ref.shape[0])
    out = top + inverse * (scaled - one - unit * two)
    out_ref[...] = out
    gx = out.astype(B16)
    gx_ref[...] = gx
    rows = [grad * unit, grad, gx.astype(F32), top]
    sums = [jnp.sum(r, axis=0, keepdims=True) for r in rows]
    sum_ref[...] = jnp.concatenate(sums + [jnp.zeros((4, sums[0].shape[1]), F32)], axis=0)


def grad_gate_kernel(
    meta_ref, len_ref, x0, x1, x2, x3, io_ref, proj_ref, halo_ref, cols_ref, mixed_ref, gy_ref, first_ref, gmix_ref
):
    rep = meta_ref[REP]
    width, group = mixed_ref.shape
    _, exists = lane_masks(meta_ref, len_ref, group + 2 * LANE)
    weight = io_ref[:, 3 * width :]
    for i, x_ref in enumerate((x0, x1, x2, x3)):
        gy_ref[:, place(rep ^ i)] = dot(x_ref[...], weight, NN).T.astype(B16)
    for lo in range(0, width, PART):
        rows = slice(lo, lo + PART)
        gate_out = short_from(ext_of(proj_ref, halo_ref, exists, 0, rows), cols_ref[rows, :], 0)
        gy = gy_ref[rows, :].astype(F32)
        gmix_ref[rows, :] = (gy * gate_out[:, LANE:-LANE]).astype(B16)
        first_ref[rows, :] = gy[:, :LANE] * mixed_ref[rows, :LANE].astype(F32)


def conv_back_kernel(
    spec_ref, kern_ref, twist_ref, hi_ref, lo_ref, chan_ref, g_ref, out_ref, grad_kern_ref, z_ref, p_ref
):
    blocks, rows, length = twist_ref.shape[0], g_ref.shape[1], g_ref.shape[2]
    short_blocks = blocks // 4
    span = blocks * rows
    first = [g_ref[b].astype(F32) for b in range(blocks)]
    second = [g_ref[blocks + b].astype(F32) for b in range(short_blocks)]
    turn_rows(first, twist_ref, z_ref, 0, blocks)
    turn_rows(second, twist_ref, z_ref, span, blocks)
    grad = dot_split(z_ref[...], hi_ref[...], lo_ref[...], ((1,), (0,)))
    kern = kern_ref[...]
    p_ref[0:span] = times(grad[:span], kern, True)
    p_ref[span : 2 * span] = times(grad[span:], kern, True)
    p_ref[2 * span :] = times(grad[:span], spec_ref[0:span], True) + times(grad[span:], spec_ref[span:], True)
    w = dot_split(p_ref[...], hi_ref[...], lo_ref[...], ((1,), (1,)))
    skip = chan_ref[:, 0:1]
    for b in range(blocks):
        acc = (back_rows(w, 0, rows, b, twist_ref, blocks) + skip * first[b]).astype(B16)
        out_ref[b] = acc
        if b < short_blocks:
            acc = (back_rows(w, span, rows, b, twist_ref, blocks) + skip * second[b]).astype(B16)
        else:
            acc = jnp.zeros((rows, length), B16)
        out_ref[blocks + b] = acc
        grad_kern_ref[b] = back_rows(w, 2 * span, rows, b, twist_ref, blocks)


def conv_ahead_kernel(kern_ref, twist_ref, hi_ref, lo_ref, chan_ref, x_ref, out_ref, spec_ref, z_ref):
    conv_forward_kernel(
        twist_ref.shape[0] // 4, x_ref, kern_ref, twist_ref, hi_ref, lo_ref, chan_ref.at[:, 0:1], out_ref, spec_ref, z_ref
    )


def filter_ahead_kernel(
    chan_ref, w1_ref, small_ref, columns_ref, grid_ref, ramp_ref, w2_ref, w3_ref, twist_ref, hi_ref, lo_ref,
    spec_ref, sin_ref, cos_ref, z_ref
):
    filter_forward_kernel(
        grid_ref, ramp_ref, chan_ref.at[:, 1:2], w1_ref, w2_ref.at[0], w3_ref.at[0], small_ref, columns_ref,
        twist_ref, hi_ref, lo_ref, spec_ref, sin_ref, cos_ref, z_ref
    )


def halves_of(values):
    top = values.astype(B16)
    return top, (values - top.astype(F32)).astype(B16)


def dot_halves(left, right, dims):
    return dot(left[0], right[0], dims) + dot(left[1], right[0], dims) + dot(left[0], right[1], dims)


def filter_back_kernel(
    meta_ref, gk_ref, grid_ref, ramp_ref, chan_ref, w1_ref, w2_ref, w3_ref, col_ref, row_ref, columns_ref, sin_ref, cos_ref,
    side_ref, wide_ref
):
    freq, freq_row = col_ref[:, 3:4], row_ref[3:4, :]
    filt = freq.shape[0]
    gk = jnp.concatenate([gk_ref[b] for b in range(gk_ref.shape[0])], axis=1)
    gk = halves_of(gk * jnp.exp(-chan_ref[:, 1:2] * ramp_ref[...]))
    gcols = dot_halves(halves_of(sin_ref[2]), gk, NT)
    chan, width = gcols.shape[1], wide_ref.shape[1]
    row = lax.broadcasted_iota(jnp.int32, (chan, width), 0)
    lane = lax.broadcasted_iota(jnp.int32, (chan, width), 1)
    pick = (lane == row + meta_ref[SEQ] * chan).astype(F32)
    wide_ref[...] = dot_high(gcols, pick, NN)
    grad = dot_halves(halves_of(columns_ref[...]), gk, NN)
    ones = jnp.ones((16, grad.shape[1]), B16)
    gfreq = jnp.zeros((1, filt), F32)
    grads, biases = [None] * 3, [None] * 3
    for i, weight in ((2, w3_ref[0]), (1, w2_ref[0]), (0, w1_ref[...])):
        turn = grad * cos_ref[i]
        pair = halves_of(turn)
        below = halves_of(sin_ref[i - 1] if i else grid_ref[...])
        raw = dot_halves(below, pair, NT)
        total = (dot(ones, pair[0], NT) + dot(ones, pair[1], NT))[0:1]
        grads[i] = raw * freq_row
        biases[i] = total * freq_row
        gfreq = gfreq + jnp.sum(raw * weight, axis=0, keepdims=True) + total * row_ref[i : i + 1, :]
        if i:
            grad = dot_halves(halves_of(weight * freq_row), pair, NN)
    gap = jnp.zeros((filt - grads[0].shape[0], filt), F32)
    small = jnp.concatenate(biases + [gfreq, jnp.zeros((filt - 4, filt), F32)], axis=0)
    side_ref[...] = jnp.concatenate(
        [grads[1], grads[2], jnp.concatenate([grads[0], gap], axis=0), small], axis=1
    )


def summed(value):
    total = value[:, :LANE]
    for k in range(LANE, value.shape[1], LANE):
        total = total + value[:, k : k + LANE]
    return jnp.sum(total, axis=1, keepdims=True)


def short_back(ext, cols, gshort, p, mid):
    size = ext.shape[1]
    mine = gshort[:, mid]
    gproj = (
        cols[:, 6 + p : 7 + p] * gshort
        + cols[:, 3 + p : 4 + p] * pltpu.roll(gshort, size - 1, 1)
        + cols[:, p : p + 1] * pltpu.roll(gshort, size - 2, 1)
    )[:, mid].astype(B16).astype(F32)
    sums = [
        summed(mine),
        summed(mine * ext[:, mid]),
        summed(mine * pltpu.roll(ext, 1, 1)[:, mid]),
        summed(mine * pltpu.roll(ext, 2, 1)[:, mid]),
        summed(gproj),
    ]
    return gproj, sums


def grad_first_kernel(
    meta_ref, len_ref, proj_ref, halo_ref, cols_ref, mixed_ref, gy_ref, onext_ref, io_ref, tok_ref, sum_ref, part_ref
):
    rep = meta_ref[REP]
    width, group = mixed_ref.shape
    size = group + 2 * LANE
    mask, exists = lane_masks(meta_ref, len_ref, size)
    mid = slice(LANE, size - LANE)
    next_on = exists[:, size - LANE :]
    columns = []
    for lo in range(0, width, PART):
        rows = slice(lo, lo + PART)
        cols = cols_ref[rows, :]
        gy = gy_ref[rows, :].astype(F32)
        gout = gy * mixed_ref[rows, :].astype(F32)
        gshort = jnp.concatenate([jnp.zeros((PART, LANE), F32), gout, onext_ref[rows, :] * next_on], axis=1)
        gproj, sums = short_back(ext_of(proj_ref, halo_ref, exists, 0, rows), cols, gshort, 0, mid)
        for j in range(4):
            tok_ref[rep ^ j, :, rows] = gproj[:, j * LANE : (j + 1) * LANE].T.astype(B16)
        columns.append(jnp.concatenate(sums + [jnp.zeros((PART, LANE - 5), F32)], axis=1))
    sum_ref[...] = jnp.concatenate(columns, axis=0).T[:8]
    part_ref[...] = dot(tok_ref[...].reshape(-1, width), io_ref[:, :width], NT)


def grad_short_kernel(
    meta_ref, len_ref, proj_ref, halo_ref, cols_ref, gy_ref, io_ref, before_ref,
    x0, x1, x2, x3, gain_ref, shift_ref, ggated_ref, gnext_ref,
    tok_ref, sum_ref, norm_ref, give3_ref, give1_ref, keep2_ref, keep0_ref
):
    rep = meta_ref[REP]
    width, group = gy_ref.shape
    size = group + 2 * LANE
    mask, exists = lane_masks(meta_ref, len_ref, size)
    mid = slice(LANE, size - LANE)
    columns = []
    for lo in range(0, width, PART):
        rows = slice(lo, lo + PART)
        cols = cols_ref[rows, :]
        ext = [ext_of(proj_ref, halo_ref, exists, p, rows) for p in (1, 2)]
        short = [short_from(ext[p - 1], cols, p) for p in (1, 2)]
        ggated = (
            jnp.concatenate(
                [jnp.zeros((PART, LANE), F32), ggated_ref[rows, :].astype(F32), gnext_ref[rows, :].astype(F32)], axis=1
            )
            * mask
            * exists
        )
        gate_out = short_from(ext_of(proj_ref, halo_ref, exists, 0, rows), cols, 0)[:, mid]
        gated = short[1][:, mid] * short[0][:, mid] * mask[:, mid]
        sums = [summed(gy_ref[rows, :].astype(F32) * gate_out * gated)]
        for p in (1, 2):
            gproj, more = short_back(ext[p - 1], cols, ggated * short[2 - p], p, mid)
            sums += more
            at = slice((p - 1) * width + lo, (p - 1) * width + lo + PART)
            for j in range(4):
                tok_ref[rep ^ j, :, at] = gproj[:, j * LANE : (j + 1) * LANE].T.astype(B16)
        columns.append(jnp.concatenate(sums + [jnp.zeros((PART, LANE - 11), F32)], axis=1))
    sum_ref[...] = jnp.concatenate(columns, axis=0).T[:16]
    outs = (keep0_ref, give1_ref, keep2_ref, give3_ref)
    left = tok_ref[...].reshape(-1, 2 * width)
    tall = tok_ref.shape[1]
    for lo in range(0, io_ref.shape[0], 256):
        cut = slice(lo, lo + 256)
        part = dot(left, io_ref[cut, width : 3 * width], NT) + before_ref[:, cut]
        plain = jnp.sum(part, axis=0, keepdims=True)
        cross = None
        for i, (ref, x_ref) in enumerate(zip(outs, (x0, x1, x2, x3))):
            mine = part[i * tall : (i + 1) * tall]
            ref[:, cut] = mine.astype(ref.dtype)
            two = jnp.sum(mine * x_ref[:, cut].astype(F32), axis=0, keepdims=True)
            cross = two if cross is None else cross + two
        norm_ref[0:1, cut] = (cross - shift_ref[:, cut] * plain) / gain_ref[:, cut]
        norm_ref[1:2, cut] = plain


def give_first(meta_ref, term_ref, a_ref, b_ref):
    half = a_ref.shape[2]
    seq = meta_ref[SEQ]
    s0, s1 = seq & 1, (seq >> 1) & 1
    for i in range(2):
        for j in range(2):
            a_ref[i, j] = term_ref[i, j, 1 - s0, :half]
            b_ref[i, j] = term_ref[i, 1 - s1, j, half:]


def grad_pair(refs, right, out_ref, lanes, base=0):
    owned = refs[0].shape[1] // 8
    for k in range(0, 8, 2):
        left = jnp.concatenate([r[:, k * owned : (k + 2) * owned] for r in refs], axis=0)
        part = dot(left, right, TN).astype(B16)
        out_ref[k // 4, (k // 2) % 2, 0, base : base + owned, lanes] = part[:owned]
        out_ref[k // 4, (k // 2) % 2, 1, base : base + owned, lanes] = part[owned:]


def grad_early_kernel(meta_ref, g0, g1, g2, g3, y_ref, x0, x1, x2, x3, tok_ref, out_ref, a_ref, b_ref):
    width = y_ref.shape[2]
    grad_pair((g0, g1, g2, g3), y_ref[...].reshape(-1, width), out_ref, slice(0, width))
    grad_pair((x0, x1, x2, x3), tok_ref[...].reshape(-1, width), out_ref, slice(width, 2 * width))
    give_first(meta_ref, out_ref, a_ref, b_ref)


def grad_late_kernel(meta_ref, x0, x1, x2, x3, tok_ref, out_ref, a_ref, b_ref):
    width = tok_ref.shape[2]
    grad_pair((x0, x1, x2, x3), tok_ref[...].reshape(-1, width), out_ref, slice(0, width))
    give_first(meta_ref, out_ref, a_ref, b_ref)


def halve_one_kernel(meta_ref, term_ref, a_in, b_in, keep_a, keep_b, give_a, give_b):
    half = a_in.shape[2]
    seq = meta_ref[SEQ]
    s0, s1 = seq & 1, (seq >> 1) & 1
    for i in range(2):
        keep_a[i] = term_ref[i, s1, s0, :half].astype(F32) + a_in[i, s1].astype(F32)
        give_a[i] = (term_ref[i, 1 - s1, s0, :half].astype(F32) + a_in[i, 1 - s1].astype(F32)).astype(B16)
        keep_b[i] = term_ref[i, s1, s0, half:].astype(F32) + b_in[i, s0].astype(F32)
        give_b[i] = (term_ref[i, s1, 1 - s0, half:].astype(F32) + b_in[i, 1 - s0].astype(F32)).astype(B16)


def halve_two_kernel(meta_ref, keep_a_in, keep_b_in, a_in, b_in, keep_a, keep_b, give_a, give_b):
    s2 = meta_ref[SEQ] >> 2
    keep_a[...] = keep_a_in[s2] + a_in[s2].astype(F32)
    give_a[...] = (keep_a_in[1 - s2] + a_in[1 - s2].astype(F32)).astype(B16)
    keep_b[...] = keep_b_in[s2] + b_in[s2].astype(F32)
    give_b[...] = (keep_b_in[1 - s2] + b_in[1 - s2].astype(F32)).astype(B16)


def add_last_kernel(keep_ref, came_ref, out_ref):
    out_ref[0] = keep_ref[...] + came_ref[...].astype(F32)


def early_last_kernel(keep_a, keep_b, a_in, b_in, out_ref, in_ref):
    half, width = keep_a.shape[0], out_ref.shape[2]
    for keep, came, rows in ((keep_a, a_in, slice(0, half)), (keep_b, b_in, slice(half, 2 * half))):
        out_ref[0, rows] = keep[:, :width] + came[:, :width].astype(F32)
        in_ref[rows] = keep[:, width:] + came[:, width:].astype(F32)


def late_last_kernel(keep_a, keep_b, a_in, b_in, first_ref, out_ref):
    half, width = keep_a.shape[0], out_ref.shape[3]
    out_ref[0, 0] = first_ref[...]
    for keep, came, rows in ((keep_a, a_in, slice(0, half)), (keep_b, b_in, slice(half, 2 * half))):
        for p in range(2):
            lanes = slice(p * width, (p + 1) * width)
            out_ref[0, 1 + p, rows] = keep[:, lanes] + came[:, lanes].astype(F32)


def norm_first_back_kernel(keep_ref, near_ref, far_ref, x_ref, middle_ref, gain_ref, out_ref):
    grad = keep_ref[...] + near_ref[...].astype(F32) + far_ref[...].astype(F32)
    unit, inverse = normed_of(x_ref[...].astype(F32))
    scaled = grad * gain_ref[...]
    one = jnp.mean(scaled, axis=1, keepdims=True)
    two = jnp.mean(scaled * unit, axis=1, keepdims=True)
    out_ref[...] = middle_ref[...] + inverse * (scaled - one - unit * two)


def layer_out_kernel(keep_ref, near_ref, far_ref, middle_ref, bias_ref, out_ref):
    part = keep_ref[...] + near_ref[...].astype(F32) + far_ref[...].astype(F32)
    out_ref[...] = (middle_ref[...] + (part + bias_ref[...])).astype(B16)


def heads_kernel(in_ref, out_ref):
    out_ref[...] = in_ref[:, :LANE]


def add_far_kernel(keep_ref, came_ref, out_ref):
    out_ref[...] = (keep_ref[...] + came_ref[...].astype(F32)).astype(B16)


HALF = 88


def pack_small_kernel(side_ref, wide_ref, col0_ref, col_ref, up_ref, one_ref, two_ref, out_ref):
    filt, width = side_ref.shape
    out_ref[:filt] = side_ref[...]
    at = filt
    for ref, count in ((one_ref, 2), (two_ref, 4)):
        for r in range(count):
            for k in range(4):
                out_ref[at : at + 1] = ref[r : r + 1, k * width : (k + 1) * width]
                at += 1
    out_ref[HALF : HALF + 1] = col_ref[0:1]
    out_ref[HALF + 1 : HALF + 6] = col0_ref[0:5]
    out_ref[HALF + 6 : HALF + 16] = col_ref[1:11]
    for k in range(4):
        out_ref[HALF + 16 + k : HALF + 17 + k] = up_ref[:, k * width : (k + 1) * width]
    out_ref[HALF + 20 : HALF + 24] = jnp.zeros((4, width), F32)
    out_ref[HALF + 24 :] = wide_ref[...]


def add_small_kernel(mine_ref, came_ref, out_ref):
    out_ref[...] = mine_ref[...] + came_ref[...]


def list_small_kernel(meta_ref, mine_ref, came_ref, out_ref):
    y = meta_ref[REP] >> 1
    out_ref[:HALF] = mine_ref[:HALF] + came_ref[:HALF]
    out_ref[pl.ds(pl.multiple_of((1 + y) * HALF, 8), HALF)] = mine_ref[HALF:]
    out_ref[pl.ds(pl.multiple_of((2 - y) * HALF, 8), HALF)] = came_ref[HALF:]


def unpack_small_kernel(
    meta_ref, mine_ref, came_ref,
    in_bias, taps, short_bias, fw, fb, iw, ib, dw, db, sf, kern_w, skip, out_b, n1g, n1s, n2g, n2s, up_b, down_b
):
    core = meta_ref[REP] & 1
    filt, width = iw.shape[2], mine_ref.shape[1]
    total = mine_ref[:HALF] + came_ref[:HALF]
    iw[0] = total[:filt, :filt]
    dw[0] = total[:filt, filt : 2 * filt]
    for k in range(fw.shape[0]):
        fw[k] = total[k : k + 1, 2 * filt : 3 * filt]
    for k, ref in enumerate((fb, ib, db, sf)):
        ref[...] = total[k : k + 1, 3 * filt :]
    at = filt
    for ref in (n1g, n1s, n2g, n2s, out_b, down_b):
        for k in range(4):
            ref[:, k * width : (k + 1) * width] = total[at : at + 1]
            at += 1
    for y in range(2):
        lo = (1 + y) * HALF
        mine, came = mine_ref[lo : lo + HALF], came_ref[lo : lo + HALF]
        for c in range(2):
            block = jnp.where(core == c, mine, came)
            lanes = slice((2 * y + c) * width, (2 * y + c + 1) * width)
            skip[:, lanes] = block[0:1]
            for p in range(3):
                row = 1 + 5 * p
                short_bias[p, :, lanes] = block[row : row + 1]
                for j in range(3):
                    taps[j, p, :, lanes] = block[row + 3 - j : row + 4 - j]
                in_bias[p, :, lanes] = block[row + 4 : row + 5]
            for k in range(4):
                lo_up = (2 * y + c) * 4 * width + k * width
                up_b[:, lo_up : lo_up + width] = block[16 + k : 17 + k]
            kern_w[0, :, lanes] = block[24 : 24 + filt]


def tie(values, *others):
    return lax.optimization_barrier((values, others))[0]


class RingGather:
    def __init__(self, name, meta, shard, far=False):
        self.name, self.meta, self.far = name, meta, far
        self.pieces = [shard]
        self.send(shard, shard)

    def send(self, left, right):
        self.came = (lax.ppermute(left, "seq", AHEAD), lax.ppermute(right, "seq", BACK))

    def step(self, *others):
        left, right = tie(self.came, *others)
        self.pieces += [left, right]
        count = len(self.pieces)
        if count == 7:
            half = shape((left.shape[0] // 2,) + left.shape[1:], B16)
            if self.far:
                left, right = call(
                    halves_far_kernel, self.name + "_halves", [left, right], [half, half],
                    scratch=[pltpu.SemaphoreType.DMA((2,))], raw=[0, 1, -1, -2],
                )
            else:
                left, right = call(halves_kernel, self.name + "_halves", [left, right], [half, half])
        if count < 9:
            self.send(left, right)
        return self.came

    def full(self, *others):
        left, right = tie(self.came, *others)
        pieces = self.pieces + [left, right]
        whole = [shape((8,) + self.pieces[0].shape, B16)]
        if self.far:
            return call(
                assemble_far_kernel, self.name + "_assemble", [self.meta, *pieces], whole,
                scratch=[pltpu.SemaphoreType.DMA((9,))], raw=range(1, 10),
            )[0]
        return call(assemble_kernel, self.name + "_assemble", [self.meta, *pieces], whole)[0]


def gather_four(rows):
    far = swap(rows, "rep", 2)
    near = swap(rows, "rep", 1)
    diag = swap(far, "rep", 1)
    return [rows, near, far, diag]


def pass_far(give3, give1, keep2):
    came = swap(give3, "rep", 1)
    near = swap(give1, "rep", 1)
    (summed,) = call(add_far_kernel, "add_far", [keep2, came], [shape(keep2.shape, B16)])
    return near, swap(summed, "rep", 2), summed


class Halving:
    def __init__(self, name, meta, term, give):
        self.name, self.meta, self.term = name, meta, term
        self.came = (swap(give[0], "seq", 1), swap(give[1], "seq", 2))

    def one(self, *others):
        rows, cols = self.term.shape[3] // 2, self.term.shape[4]
        outs = [shape((2, rows, cols), F32)] * 2 + [shape((2, rows, cols), B16)] * 2
        args = [self.meta, self.term, *tie(self.came, *others)]
        *self.keep, ga, gb = call(halve_one_kernel, self.name + "_one", args, outs)
        self.came = (swap(ga, "seq", 2), swap(gb, "seq", 1))
        return ga

    def two_kept(self, *others):
        rows, cols = self.term.shape[3] // 2, self.term.shape[4]
        outs = [shape((rows, cols), F32)] * 2 + [shape((rows, cols), B16)] * 2
        args = [self.meta, *self.keep, *tie(self.came, *others)]
        return call(halve_two_kernel, self.name + "_two", args, outs)

    def two(self, *others):
        *self.keep, ga, gb = self.two_kept(*others)
        self.came = (swap(ga, "seq", 4), swap(gb, "seq", 4))
        return ga

    def last(self, *others):
        return [*self.keep, *tie(self.came, *others)]


def exchange(blocks):
    return lax.all_to_all(blocks, "seq", 0, 0, tiled=True)


def per_device_fast(
    tokens,
    cotangent,
    lengths,
    in_weight,
    in_bias,
    short_taps,
    short_bias,
    feat_weight,
    feat_bias,
    inner_weight,
    inner_bias,
    deep_weight,
    deep_bias,
    sine_freq,
    kernel_weight,
    skip_gain,
    out_weight,
    out_bias,
    norm1_gain,
    norm1_shift,
    norm2_gain,
    norm2_shift,
    up_weight,
    up_bias,
    down_weight,
    down_bias,
):
    tok_rows, model = tokens.shape
    group = tok_rows * 4
    blocks = 4
    seq_len = blocks * group
    chan = model // 32
    width = model // 4
    hidden = up_weight.shape[2]
    owned = model // 8
    filt = feat_weight.shape[2]
    device = lax.axis_index("seq") * 4 + lax.axis_index("rep")
    meta = lax.dynamic_index_in_dim(jnp.asarray(meta_table(group)), device, 0, keepdims=False)
    row_f32, row_b16 = shape((tok_rows, model), F32), shape((tok_rows, model), B16)
    sums_shapes = [row_b16, row_b16, row_f32, row_f32]
    flat_shape = shape((width, group), B16)

    normed, io_shard = call(
        start_kernel,
        "start",
        [tokens, norm1_gain, norm1_shift, in_weight[0].transpose(1, 0, 2), out_weight],
        [row_b16, shape((owned, 4 * width), B16)],
        away=range(5),
        limit=62,
    )
    io_ring = RingGather("io", meta, io_shard)
    x_one = gather_four(normed)
    twist, table = transform_tables(blocks, group)
    hi, lo = split_table(table)
    grid, ramp = feature_table(seq_len, feat_weight.shape[1])
    twist, grid, ramp = jnp.asarray(twist), jnp.asarray(grid), jnp.asarray(ramp)
    params = [
        cotangent, up_weight, down_weight,
        short_taps.transpose(1, 2, 0, 3), short_bias.transpose(1, 0, 2), in_bias.transpose(1, 0, 2), up_bias, skip_gain,
        jnp.asarray(decay_rates(model).T), kernel_weight, feat_weight.transpose(1, 0, 2),
        feat_bias, inner_bias, deep_bias, sine_freq,
    ]
    top_rows, ud_shard, cols, up_block, chans, columns, small_col, small_row, feat = call(
        setup_kernel,
        "setup",
        [meta, lengths, *params],
        [
            row_b16, shape((2, owned, hidden), B16),
            shape((width, 16), F32), shape((1, hidden), F32), shape((chan, 2), F32), shape((filt, chan), F32),
            shape((filt, 4), F32), shape((4, filt), F32), shape(feat_weight.shape[1:], F32),
        ],
        scratch=[pltpu.SemaphoreType.DMA((2,))],
        away=[2] + list(range(5, 2 + len(params))),
        raw=[3, 4, -2],
    )
    io_ring.step(x_one[1])
    tables = [grid, ramp, inner_weight, deep_weight, twist, hi, lo]
    kern_spec, sines, cosines = call(
        filter_ahead_kernel,
        "filter_ahead",
        [chans, feat, tie(small_col, io_ring.pieces[-1]), columns, *tables],
        [
            shape((blocks * chan, 2 * group), F32),
            shape((3, filt, seq_len), F32),
            shape((3, filt, seq_len), F32),
        ],
        scratch=[pltpu.VMEM((blocks * chan, 2 * group), F32)],
        away=range(4, 4 + len(tables)),
    )
    io_ring.step(kern_spec, x_one[2])

    edge = shape((HALO, model), B16)
    last, first = call(edges_kernel, "edges", [meta, *x_one], [edge, edge])
    before = lax.ppermute(last, "seq", [(i, (i + 1) % 8) for i in range(8)])
    after = lax.ppermute(first, "seq", [(i, (i + 7) % 8) for i in range(8)])
    io_ring.step()
    io_pieces = io_ring.pieces + list(tie(io_ring.came, before, after))
    ud_ring = RingGather("ud", meta, tie(ud_shard, io_pieces[-1]))
    g_top = gather_four(tie(top_rows, x_one[3]))
    full_io, proj, halo, gated = call(
        project_kernel,
        "project",
        [meta, lengths, *x_one, before, after, cols, *io_pieces],
        [
            shape((8, owned, 4 * width), B16), shape((3, width, group), B16), shape((3, width, 2 * LANE), B16), flat_shape
        ],
    )
    full_io = full_io.reshape(model, 4 * width)
    common = [proj, halo, cols]

    spread = (8, chan, group)
    received = exchange(gated.reshape(spread))
    spec_rows = 2 * blocks * chan
    mixed, kept_spec = call(
        conv_ahead_kernel,
        "conv_ahead",
        [kern_spec, twist, hi, lo, chans, received],
        [shape(spread, B16), shape((spec_rows, 2 * group), F32)],
        scratch=[pltpu.VMEM((spec_rows, 2 * group), F32)],
    )
    ud_ring.step(mixed)
    mixed = exchange(mixed).reshape(width, group)
    ud_ring.step(mixed)

    y_tok, give3, give1, keep2, keep0 = call(
        out_project_kernel,
        "out_project",
        [meta, lengths, *common, full_io, mixed],
        [shape((4, tok_rows, width), B16)] + sums_shapes,
    )
    near, far, _ = pass_far(give3, give1, keep2)
    middle, normed_two = call(
        norm_second_kernel,
        "norm_second",
        [tokens, keep0, near, far, out_bias, norm2_gain, norm2_shift],
        [row_f32, row_b16],
    )
    ud_ring.step(normed_two)
    x_two = gather_four(normed_two)
    full_ud = ud_ring.full(x_two[2])

    tall = shape((group, hidden), B16)
    act, gpre, gup = call(
        mlp_kernel, "mlp", [*x_two, *g_top, full_ud, up_block], [tall, tall, shape((1, hidden), F32)],
    )
    give3, give1, keep2, keep0 = call(partial(rows_kernel, 0), "grad_two", [gpre, full_ud], sums_shapes)
    near, far, passed = pass_far(give3, give1, keep2)
    give = shape((2, 2, owned, hidden), B16)
    mlp_terms, ga, gb = call(
        mlp_grad_kernel,
        "mlp_grad",
        [meta, *x_two, *g_top, act, tie(gpre, passed)],
        [shape((2, 2, 2, 2 * owned, hidden), B16), give, give],
    )
    wide_back = Halving("far", meta, mlp_terms, (ga, gb))
    grad_middle, gx, norm_sums = call(
        norm_second_back_kernel,
        "norm_second_back",
        [meta, lengths, keep0, near, tie(far, ga), middle, cotangent, norm2_gain],
        [row_f32, row_b16, shape((8, model), F32)],
    )
    g_mid = gather_four(gx)
    m3, m1, m2, m0 = call(partial(rows_kernel, 1), "mlp_rows", [tie(act, gx), full_ud], sums_shapes)
    gy, gate_first, gmix = call(
        grad_gate_kernel,
        "grad_gate",
        [meta, lengths, *tie(tuple(g_mid), m3), full_io, *common, mixed],
        [flat_shape, shape((width, LANE), F32), flat_shape],
    )

    received = exchange(gmix.reshape(spread))
    given = wide_back.one(received)
    gate_next = lax.ppermute(tie(gate_first, received), "seq", [(i, (i + 7) % 8) for i in range(8)])
    ggated, grad_kernel = call(
        conv_back_kernel,
        "conv_back",
        [kept_spec, kern_spec, twist, hi, lo, chans, tie(received, given)],
        [shape(spread, B16), shape((blocks, chan, group), F32)],
        scratch=[pltpu.VMEM((spec_rows, 2 * group), F32), pltpu.VMEM((3 * spec_rows // 2, 2 * group), F32)],
    )
    ggated = exchange(tie(ggated, gate_next)).reshape(width, group)
    up_keep, down_keep, up_give, down_give = wide_back.two_kept(ggated)
    up_came = swap(up_give, "seq", 4)
    (heads,) = call(heads_kernel, "heads", [tie(ggated, up_give)], [shape((width, LANE), B16)])
    ggated_next = lax.ppermute(heads, "seq", [(i, (i + 7) % 8) for i in range(8)])
    tok_first, sum_first, part_first = call(
        grad_first_kernel,
        "grad_first",
        [meta, lengths, *common, mixed, gy, tie(gate_next, heads), full_io],
        [shape((4, tok_rows, width), B16), shape((8, width), F32), shape((group, model), F32)],
    )
    cube = shape((2, 2, 2, owned, 2 * width), B16)
    give = shape((2, 2, owned // 2, 2 * width), B16)
    early_terms, ga, gb = call(
        grad_early_kernel,
        "grad_early",
        [meta, *g_mid, y_tok, *x_one, tok_first],
        [cube, give, give],
    )
    early = Halving("early", meta, early_terms, (ga, gb))
    tok_rest, col_sums, norm_one, give3, give1, keep2, keep0 = call(
        grad_short_kernel,
        "grad_short",
        [
            meta, lengths, *common, gy, full_io, part_first, *x_one, norm1_gain, norm1_shift, tie(ggated, ga),
            ggated_next
        ],
        [shape((4, tok_rows, 2 * width), B16), shape((16, width), F32), shape((2, model), F32)] + sums_shapes,
    )
    result = shape((1, owned, hidden), F32)
    down_came = swap(tie(down_give, give3), "seq", 4)
    (grad_up,) = call(add_last_kernel, "up_last", [up_keep, tie(up_came, give3)], [result])
    given = early.one(grad_up)
    near, far, passed = pass_far(give3, give1, tie(keep2, given))
    late_terms, ga, gb = call(
        grad_late_kernel, "grad_late", [meta, *tie(tuple(x_one), passed), tok_rest], [cube, give, give]
    )
    late = Halving("late", meta, late_terms, (ga, gb))
    side, wide = call(
        filter_back_kernel,
        "filter_back",
        [
            meta, tie(grad_kernel, ga), grid, ramp, chans, feat, inner_weight, deep_weight, small_col, small_row, columns,
            sines, cosines
        ],
        [shape((filt, 4 * filt), F32), shape((filt, width), F32)],
    )

    (small,) = call(
        pack_small_kernel,
        "pack_small",
        [side, wide, sum_first, col_sums, gup, norm_one, norm_sums],
        [shape((2 * HALF, width), F32)],
    )
    came = swap(small, "seq", 1)
    (grad_down,) = call(add_last_kernel, "down_last", [down_keep, tie(down_came, small)], [result])
    given = early.two(grad_down)
    (grad_tokens,) = call(
        norm_first_back_kernel,
        "norm_first_back",
        [keep0, near, tie(far, given), tokens, grad_middle, norm1_gain],
        [row_f32],
    )
    given = late.one(grad_tokens)
    (small,) = call(add_small_kernel, "add_small", [small, tie(came, given)], [small])
    came = swap(small, "seq", 2)
    given = late.two(small)
    m_near, m_far, m_passed = pass_far(tie(m3, given), m1, m2)
    grad_out, first_in = call(
        early_last_kernel, "early_last", early.last(given), [shape((1, owned, width), F32), shape((owned, width), F32)]
    )
    (small,) = call(add_small_kernel, "add_small", [small, tie(came, grad_out, m_passed)], [small])
    came = swap(small, "seq", 4)
    (grad_in,) = call(
        late_last_kernel, "late_last", [*late.last(small), first_in], [shape((1, 3, owned, width), F32)]
    )
    (small,) = call(add_small_kernel, "add_small", [small, tie(came, grad_in)], [small])
    came = swap(small, "rep", 2)
    (layer_out,) = call(layer_out_kernel, "layer_out", [m0, m_near, tie(m_far, small), middle, down_bias], [row_b16])
    (small,) = call(
        list_small_kernel, "list_small", [meta, small, tie(came, layer_out)], [shape((3 * HALF, width), F32)]
    )
    came = swap(small, "rep", 1)
    vector = shape((1, model), F32)
    square, short = shape((1, filt, filt), F32), shape((1, filt), F32)
    triple = shape((3, 1, model), F32)
    outs = call(
        unpack_small_kernel,
        "unpack_small",
        [meta, small, came],
        [
            triple, shape((3, 3, 1, model), F32), triple, shape(params[10].shape, F32), short, square, short, square,
            short, short, shape(kernel_weight.shape, F32), vector, vector, vector, vector, vector, vector,
            shape(up_bias.shape, F32), vector,
        ],
    )
    return (
        layer_out,
        grad_tokens,
        grad_in.transpose(0, 2, 1, 3),
        outs[0].transpose(1, 0, 2),
        outs[1].transpose(2, 0, 1, 3),
        outs[2].transpose(1, 0, 2),
        outs[3].transpose(1, 0, 2),
        *outs[4:12],
        grad_out,
        *outs[12:17],
        grad_up,
        outs[17],
        grad_down,
        outs[18],
    )


def solution(mesh):
    rows = P(("seq", "rep"), None)
    cut = P(None, "seq", "rep")
    wide = P(None, "seq", None, "rep")
    whole = P()
    ins = [rows, rows, whole, wide] + [whole] * 12 + [cut] + [whole] * 5 + [cut, whole, cut, whole]
    outs = [rows, rows, wide] + [whole] * 12 + [cut] + [whole] * 5 + [cut, whole, cut, whole]
    fast = mesh.shape["seq"] == 8 and mesh.shape["rep"] == 4
    return jax.shard_map(
        per_device_fast if fast else per_device, mesh=mesh, in_specs=tuple(ins), out_specs=tuple(outs), check_vma=False
    )
```

```python
from functools import partial
import math

import jax
import jax.numpy as jnp
import numpy as np
from jax import lax
from jax.experimental import pallas as pl
from jax.experimental.pallas import tpu as pltpu
from jax.sharding import PartitionSpec as P

EPS = 1e-05
HIGH = lax.Precision.HIGHEST
F32 = jnp.float32
B16 = jnp.bfloat16
LANE = 128
HALO = 16
VMEM_BYTES = 48 * 2**20


def swap(values, axis_name, bit):
    size = lax.axis_size(axis_name)
    return lax.ppermute(values, axis_name, [(i, i ^ bit) for i in range(size)])


def gather_rel(rows):
    far = swap(rows, "rep", 2)
    near = swap(rows, "rep", 1)
    diag = swap(far, "rep", 1)
    return jnp.concatenate([rows, near, far, diag], axis=0)


def scatter_rel(part):
    rows = part.shape[0] // 4
    blocks = part.reshape(4, rows, part.shape[1])
    far_in = swap(blocks[3].astype(B16), "rep", 1)
    far_sum = (blocks[2] + far_in.astype(F32)).astype(B16)
    near_in = swap(blocks[1].astype(B16), "rep", 1)
    far_out = swap(far_sum, "rep", 2)
    return blocks[0] + near_in.astype(F32) + far_out.astype(F32)


def ring_order(count):
    if count == 8:
        return [0, 2, 4, 6, 7, 5, 3, 1]
    return list(range(count))


def ring_maps(count):
    order = ring_order(count)
    ahead = [(order[i], order[(i + 1) % count]) for i in range(count)]
    return order, ahead, [(b, a) for a, b in ahead]


def ring_gather(shard):
    count = lax.axis_size("seq")
    if count != 8:
        return lax.all_gather(shard, "seq", axis=0)
    order, ahead, back = ring_maps(count)
    place = jnp.asarray(np.argsort(order), jnp.int32)[lax.axis_index("seq")]
    owners = jnp.asarray(order, jnp.int32)
    full = jnp.zeros((count,) + shard.shape, shard.dtype)

    def put(full, piece, step, lo=0):
        owner = owners[(place + step + count) % count]
        start = (owner, lo) + (0,) * (shard.ndim - 1)
        return lax.dynamic_update_slice(full, piece[None], start)

    full = put(full, shard, 0)
    left = right = shard
    for step in range(1, count // 2):
        left = lax.ppermute(left, "seq", ahead)
        right = lax.ppermute(right, "seq", back)
        full = put(full, left, -step)
        full = put(full, right, step)
    half = shard.shape[0] // 2
    left = lax.ppermute(left[:half], "seq", ahead)
    right = lax.ppermute(right[half:], "seq", back)
    full = put(full, left, -(count // 2))
    full = put(full, right, count // 2, half)
    return full


def ring_scatter(term):
    count = lax.axis_size("seq")
    if count != 8:
        return lax.psum_scatter(term, "seq", scatter_dimension=0, tiled=True).astype(F32)
    order, ahead, back = ring_maps(count)
    place = jnp.asarray(np.argsort(order), jnp.int32)[lax.axis_index("seq")]
    owners = jnp.asarray(order, jnp.int32)
    rows = term.shape[0] // count
    half = rows // 2

    def mine(step, lo):
        owner = owners[(place + step + 2 * count) % count]
        return lax.dynamic_slice_in_dim(term, owner * rows + lo, half, 0)

    left, right = mine(-1, 0), mine(1, half)
    for step in range(2, count + 1):
        left = lax.ppermute(left, "seq", ahead).astype(F32) + mine(-step, 0).astype(F32)
        right = lax.ppermute(right, "seq", back).astype(F32) + mine(step, half).astype(F32)
        if step < count:
            left, right = left.astype(B16), right.astype(B16)
    return jnp.concatenate([left, right], axis=0)


def halve_scatter(term):
    count = lax.axis_size("seq")
    bits = count.bit_length() - 1
    seq = lax.axis_index("seq")
    rows = term.shape[0] // count
    half = rows // 2
    split = term.reshape((2,) * bits + (2, half, term.shape[1]))
    results = []
    for part, order in enumerate(([0] + list(range(bits - 1, 0, -1)), list(range(bits - 1, -1, -1)))):
        value = lax.index_in_dim(split, part, bits, keepdims=False)
        left = list(range(bits - 1, -1, -1))
        for bit in order:
            at = left.index(bit)
            on = (seq >> bit) & 1
            keep = lax.dynamic_index_in_dim(value, on, at, keepdims=False)
            give = lax.dynamic_index_in_dim(value, 1 - on, at, keepdims=False)
            value = keep.astype(F32) + swap(give, "seq", 1 << bit).astype(F32)
            left.remove(bit)
            if left:
                value = value.astype(B16)
        results.append(value)
    return jnp.concatenate(results, axis=0)


def spread_gather(shard):
    count = lax.axis_size("seq")
    copies = jnp.broadcast_to(shard[None], (count,) + shard.shape)
    full = lax.all_to_all(copies, "seq", 0, 0, tiled=True)
    return full.reshape((count * shard.shape[0],) + shard.shape[1:])


def shift_seq(values, step):
    count = lax.axis_size("seq")
    return lax.ppermute(values, "seq", [(i, (i + step) % count) for i in range(count)])


def unmix(values, axis, index):
    size, bit = values.shape[axis], 1
    while bit < size:
        cut = values.shape[:axis] + (size // (2 * bit), 2, bit) + values.shape[axis + 1 :]
        split = values.reshape(cut)
        values = jnp.where((index // bit) % 2 == 1, jnp.flip(split, axis + 1), split).reshape(values.shape)
        bit *= 2
    return values


def sync_small(total, group, own):
    n_seq, n_rep = lax.axis_size("seq"), lax.axis_size("rep")
    group_list, own_list = [group], [own]
    for axis_name, size in (("seq", n_seq), ("rep", n_rep)):
        bit = 1
        while bit < size:
            parts = [total] + group_list + own_list
            sizes = np.cumsum([0] + [p.shape[0] for p in parts])
            came = swap(jnp.concatenate(parts, axis=0), axis_name, bit)
            came = [came[a:b] for a, b in zip(sizes[:-1], sizes[1:])]
            total = total + came[0]
            count = len(group_list)
            if axis_name == "seq":
                group_list = [group_list[0] + came[1]]
            else:
                group_list = group_list + came[1 : 1 + count]
            own_list = own_list + came[1 + count :]
            bit *= 2
    groups = unmix(jnp.stack(group_list), 0, lax.axis_index("rep"))
    owns = jnp.stack(own_list).reshape((n_rep, n_seq) + own.shape)
    owns = unmix(unmix(owns, 0, lax.axis_index("rep")), 1, lax.axis_index("seq"))
    return total, groups, owns


def layer_norm(rows, gain, shift):
    row_mean = jnp.mean(rows, axis=-1, keepdims=True)
    centred = rows - row_mean
    variance = jnp.mean(centred * centred, axis=-1, keepdims=True)
    inverse = lax.rsqrt(variance + EPS)
    normed = centred * inverse
    return (normed * gain + shift, normed, inverse)


def norm_back(grad_rows, normed, inverse, gain):
    scaled = grad_rows * gain
    mean_one = jnp.mean(scaled, axis=-1, keepdims=True)
    mean_two = jnp.mean(scaled * normed, axis=-1, keepdims=True)
    grad_in = inverse * (scaled - mean_one - normed * mean_two)
    return (grad_in, jnp.sum(grad_rows * normed, axis=0), jnp.sum(grad_rows, axis=0))


def features(length, feat_count):
    ramp_unit = jnp.linspace(0.0, 1.0, length, dtype=F32)
    angles = jnp.arange(length, dtype=F32)[:, None] * (2.0 * math.pi / length)
    band_freqs = jnp.linspace(
        0.0001, (feat_count - 1) // 2 - 1.0, (feat_count - 1) // 2, dtype=F32
    )[None, :]
    phase_grid = band_freqs * angles
    grid_out = jnp.concatenate(
        [ramp_unit[:, None], jnp.cos(phase_grid), -jnp.sin(phase_grid)], axis=1
    )
    return (grid_out, ramp_unit)


def filter_columns(
    feature_grid,
    ramp_unit,
    start_chan,
    chan_count,
    model_width,
    feat_weight,
    feat_bias,
    inner_weight,
    inner_bias,
    deep_weight,
    deep_bias,
    sine_freq,
    columns,
):
    freq = sine_freq[:, None]

    def layer(weight, bias, below):
        grown = lax.dot_general(weight, below, (((0,), (0,)), ((), ())), precision=HIGH)
        return jnp.sin(freq * (grown + bias[:, None]))

    hidden = layer(feat_weight, feat_bias, feature_grid.T)
    hidden = layer(inner_weight, inner_bias, hidden)
    hidden = layer(deep_weight, deep_bias, hidden)
    deltas = jnp.abs(
        jnp.linspace(math.log(0.01) / 0.3, math.log(0.01) / 1.5, model_width, dtype=F32)
    )
    local_rates = lax.dynamic_slice_in_dim(deltas, start_chan, chan_count)
    return lax.dot_general(
        columns, hidden, (((0,), (0,)), ((), ())), precision=HIGH
    ) * jnp.exp(-ramp_unit[None, :] * local_rates[:, None])


def sin_cos(x):
    turns = jnp.floor(x * (1.0 / math.pi) + 0.5)
    r = x - turns * 3.140625
    r = r - turns * 9.67502593994140625e-4
    r = r - turns * 1.509957990978376432e-7
    sign = 1.0 - 2.0 * (turns - 2.0 * jnp.floor(turns * 0.5))
    q = r * r
    sin = r + r * q * (
        -1.6666666666e-1
        + q * (8.3333333e-3 + q * (-1.98412698e-4 + q * (2.7557319e-6 + q * -2.505210838e-8)))
    )
    cos = 1.0 + q * (
        -0.5
        + q * (4.16666666e-2 + q * (-1.3888888e-3 + q * (2.48015873e-5 + q * (-2.75573192e-7 + q * 2.0876757e-9))))
    )
    return sin * sign, cos * sign


def dot_high(left, right, dims):
    return lax.dot_general(left, right, (dims, ((), ())), precision=HIGH, preferred_element_type=F32)


def filter_forward_kernel(
    grid_ref, ramp_ref, rate_ref, w1_ref, w2_ref, w3_ref, small_ref, columns_ref, twist_ref, hi_ref, lo_ref,
    spec_ref, sin_ref, cos_ref, z_ref
):
    blocks, length = twist_ref.shape[0], twist_ref.shape[3]
    freq = small_ref[:, 3:4]
    below = grid_ref[...]
    for i, w_ref in enumerate((w1_ref, w2_ref, w3_ref)):
        grown = dot_high(w_ref[...].T, below, ((1,), (0,)))
        sin, cos = sin_cos(freq * (grown + small_ref[:, i : i + 1]))
        sin_ref[i] = sin
        cos_ref[i] = cos
        below = sin
    kern = dot_high(columns_ref[...].T, below, ((1,), (0,))) * jnp.exp(-rate_ref[...] * ramp_ref[...])
    cut = [kern[:, b * length : (b + 1) * length] for b in range(blocks)]
    turn_rows(cut, twist_ref, z_ref, 0, blocks)
    spec_ref[...] = dot_split(z_ref[...], hi_ref[...], lo_ref[...], ((1,), (0,)))


def filter_backward_kernel(
    gk_ref, grid_ref, ramp_ref, rate_ref, w1_ref, w2_ref, w3_ref, small_ref, columns_ref, sin_ref, cos_ref,
    gc_ref, g1_ref, g2_ref, g3_ref, gsmall_ref
):
    freq = small_ref[:, 3:4]
    gk = jnp.concatenate([gk_ref[b] for b in range(gk_ref.shape[0])], axis=1)
    gk = gk * jnp.exp(-rate_ref[...] * ramp_ref[...])
    last = ((1,), (1,))
    gc_ref[...] = dot_high(sin_ref[2], gk, last)
    grad = dot_high(columns_ref[...], gk, ((1,), (0,)))
    gfreq = jnp.zeros(freq.shape, F32)
    gbias = [None] * 3
    for i, w_ref, g_ref in ((2, w3_ref, g3_ref), (1, w2_ref, g2_ref), (0, w1_ref, g1_ref)):
        turn = grad * cos_ref[i]
        below = sin_ref[i - 1] if i else grid_ref[...]
        raw = dot_high(turn, below, last)
        total = jnp.sum(turn, axis=1, keepdims=True)
        g_ref[...] = raw * freq
        gbias[i] = total * freq
        gfreq = gfreq + jnp.sum(raw * w_ref[...].T, axis=1, keepdims=True) + total * small_ref[:, i : i + 1]
        if i:
            grad = dot_high(w_ref[...], turn * freq, ((1,), (0,)))
    gsmall_ref[...] = jnp.concatenate(gbias + [gfreq], axis=1)


def feature_table(length, feat_count):
    ramp = np.linspace(0.0, 1.0, length, dtype=np.float32)
    angles = np.arange(length, dtype=np.float32)[:, None] * np.float32(2.0 * math.pi / length)
    half = (feat_count - 1) // 2
    bands = np.linspace(0.0001, half - 1.0, half, dtype=np.float32)[None, :]
    phase = (bands * angles).astype(np.float64)
    table = np.concatenate([ramp[:, None], np.cos(phase), -np.sin(phase)], axis=1)
    return np.ascontiguousarray(table.T).astype(np.float32), ramp[None, :]


def decay_rates(model):
    return np.abs(
        np.linspace(math.log(0.01) / 0.3, math.log(0.01) / 1.5, model, dtype=np.float32)
    )[:, None]


def transform_tables(blocks, length):
    time = np.arange(blocks * length).reshape(blocks, 1, length)
    cls = np.arange(blocks).reshape(1, blocks, 1)
    period = 4 * blocks * length
    turn = (time * (2 * cls + 1)) % period * (2.0 * np.pi / period)
    twist = np.stack([np.cos(turn), -np.sin(turn)], axis=2).astype(np.float32)
    step = np.arange(length)
    turn = (step[:, None] * step[None, :]) % length * (2.0 * np.pi / length)
    cos, sin = np.cos(turn), np.sin(turn)
    table = np.block([[cos, -sin], [sin, cos]]).astype(np.float32)
    return twist, table


def split_table(table):
    hi = table.astype(B16)
    return jnp.asarray(hi), jnp.asarray((table - hi.astype(np.float32)).astype(B16))


def spectrum_of(signal, twist, table):
    turned = jnp.einsum("bqzl,brl->qrzl", twist[: signal.shape[0]], signal, precision=HIGH)
    flat = turned.reshape(turned.shape[:2] + (-1,))
    return jnp.einsum("qrk,kf->qrf", flat, table, precision=HIGH)


def signal_of(spectrum, twist, table):
    blocks, length = twist.shape[0], twist.shape[3]
    turned = jnp.einsum("qrf,kf->qrk", spectrum, table, precision=HIGH)
    turned = turned.reshape(turned.shape[:2] + (2, length))
    return jnp.einsum("bqzl,qrzl->brl", twist, turned, precision=HIGH) * (1.0 / (blocks * length))


def times(left, right, conj_right):
    half = left.shape[-1] // 2
    lr, li = left[..., :half], left[..., half:]
    rr, ri = right[..., :half], right[..., half:]
    if conj_right:
        return jnp.concatenate([lr * rr + li * ri, li * rr - lr * ri], axis=-1)
    return jnp.concatenate([lr * rr - li * ri, lr * ri + li * rr], axis=-1)


def dot_split(values, hi, lo, dims):
    top = values.astype(B16)
    rest = (values - top.astype(F32)).astype(B16)
    dot = partial(lax.dot_general, dimension_numbers=(dims, ((), ())), preferred_element_type=F32)
    return dot(top, hi) + dot(rest, hi) + dot(top, lo)


def dot_twice(values, hi, dims):
    top = values.astype(B16)
    rest = (values - top.astype(F32)).astype(B16)
    dot = partial(lax.dot_general, dimension_numbers=(dims, ((), ())), preferred_element_type=F32)
    return dot(top, hi) + dot(rest, hi)


def turn_rows(blocks_in, twist_ref, z_ref, base, classes):
    rows, length = blocks_in[0].shape
    for q in range(classes):
        for z in range(2):
            acc = None
            for b, block in enumerate(blocks_in):
                term = block * twist_ref[b, q, z : z + 1]
                acc = term if acc is None else acc + term
            z_ref[base + q * rows : base + (q + 1) * rows, z * length : (z + 1) * length] = acc


def back_rows(w, base, rows, block, twist_ref, classes):
    length = w.shape[1] // 2
    acc = None
    for q in range(classes):
        lo, hi = base + q * rows, base + (q + 1) * rows
        for z in range(2):
            term = w[lo:hi, z * length : (z + 1) * length] * twist_ref[block, q, z : z + 1]
            acc = term if acc is None else acc + term
    return acc * (1.0 / (classes * length))


def conv_forward_kernel(short_blocks, x_ref, kern_ref, twist_ref, hi_ref, lo_ref, skip_ref, out_ref, spec_ref, z_ref):
    blocks = twist_ref.shape[0]
    rows = x_ref.shape[1]
    span = blocks * rows
    first = [x_ref[b].astype(F32) for b in range(blocks)]
    second = [x_ref[blocks + b].astype(F32) for b in range(short_blocks)]
    turn_rows(first, twist_ref, z_ref, 0, blocks)
    turn_rows(second, twist_ref, z_ref, span, blocks)
    spec = dot_twice(z_ref[...], hi_ref[...], ((1,), (0,)))
    spec_ref[...] = spec
    kern = kern_ref[...]
    prod = jnp.concatenate([times(spec[:span], kern, False), times(spec[span:], kern, False)], axis=0)
    w = dot_twice(prod, hi_ref[...], ((1,), (1,)))
    skip = skip_ref[...]
    for b in range(blocks):
        out_ref[b] = (back_rows(w, 0, rows, b, twist_ref, blocks) + skip * first[b]).astype(B16)
        acc = back_rows(w, span, rows, b, twist_ref, blocks)
        if b < short_blocks:
            acc = acc + skip * second[b]
        out_ref[blocks + b] = acc.astype(B16)


def conv_backward_kernel(
    short_blocks, g_ref, spec_ref, kern_ref, twist_ref, hi_ref, lo_ref, skip_ref, out_ref, grad_kern_ref, z_ref, p_ref
):
    blocks = twist_ref.shape[0]
    rows = g_ref.shape[1]
    span = blocks * rows
    first = [g_ref[b].astype(F32) for b in range(blocks)]
    second = [g_ref[blocks + b].astype(F32) for b in range(short_blocks)]
    turn_rows(first, twist_ref, z_ref, 0, blocks)
    turn_rows(second, twist_ref, z_ref, span, blocks)
    grad = dot_split(z_ref[...], hi_ref[...], lo_ref[...], ((1,), (0,)))
    kern = kern_ref[...]
    p_ref[0:span] = times(grad[:span], kern, True)
    p_ref[span : 2 * span] = times(grad[span:], kern, True)
    p_ref[2 * span :] = times(grad[:span], spec_ref[0:span], True) + times(
        grad[span:], spec_ref[span:], True
    )
    w = dot_split(p_ref[...], hi_ref[...], lo_ref[...], ((1,), (1,)))
    skip = skip_ref[...]
    for b in range(blocks):
        out_ref[b] = (back_rows(w, 0, rows, b, twist_ref, blocks) + skip * first[b]).astype(B16)
        if b < short_blocks:
            acc = back_rows(w, span, rows, b, twist_ref, blocks) + skip * second[b]
            out_ref[blocks + b] = acc.astype(B16)
        else:
            out_ref[blocks + b] = jnp.zeros(out_ref.shape[1:], B16)
        grad_kern_ref[b] = back_rows(w, 2 * span, rows, b, twist_ref, blocks)


def conv_forward(received, kern_spec, twist, table, skip_local):
    blocks, rows, length = received.shape[0] // 2, received.shape[1], received.shape[2]
    short_blocks = -(-blocks // 4)
    skip = skip_local[:, None]
    if blocks != 4:
        x = received.astype(F32)
        spec = jnp.concatenate(
            [
                spectrum_of(x[:blocks], twist, table),
                spectrum_of(x[blocks : blocks + short_blocks], twist, table),
            ],
            axis=0,
        )
        kern = jnp.concatenate([kern_spec, kern_spec], axis=0)
        prod = times(spec, kern, False)
        out = jnp.concatenate(
            [signal_of(prod[:blocks], twist, table), signal_of(prod[blocks:], twist, table)], axis=0
        )
        return ((out + skip * x).astype(B16), spec)
    hi, lo = split_table(table)
    height = 2 * blocks * rows
    out, spec = pl.pallas_call(
        partial(conv_forward_kernel, short_blocks),
        out_shape=(
            jax.ShapeDtypeStruct(received.shape, B16),
            jax.ShapeDtypeStruct((height, 2 * length), F32),
        ),
        scratch_shapes=[pltpu.VMEM((height, 2 * length), F32)],
        compiler_params=pltpu.CompilerParams(vmem_limit_bytes=VMEM_BYTES),
        name="conv_forward",
    )(received, kern_spec.reshape(blocks * rows, 2 * length), twist, hi, lo, skip)
    return out, spec


def conv_backward(grads, spec, kern_spec, twist, table, skip_local):
    blocks, rows, length = grads.shape[0] // 2, grads.shape[1], grads.shape[2]
    short_blocks = -(-blocks // 4)
    skip = skip_local[:, None]
    if blocks != 4:
        g = grads.astype(F32)
        first = spectrum_of(g[:blocks], twist, table)
        second = spectrum_of(g[blocks : blocks + short_blocks], twist, table)
        one = signal_of(times(first, kern_spec, True), twist, table)
        two = signal_of(times(second, kern_spec, True), twist, table)
        cross = times(first, spec[:blocks], True) + times(second, spec[blocks:], True)
        out = jnp.concatenate([one, two], axis=0) + skip * g
        return (out.astype(B16), signal_of(cross, twist, table))
    hi, lo = split_table(table)
    span = blocks * rows
    out, grad_kern = pl.pallas_call(
        partial(conv_backward_kernel, short_blocks),
        out_shape=(
            jax.ShapeDtypeStruct(grads.shape, B16),
            jax.ShapeDtypeStruct((blocks, rows, length), F32),
        ),
        scratch_shapes=[
            pltpu.VMEM((2 * span, 2 * length), F32),
            pltpu.VMEM((3 * span, 2 * length), F32),
        ],
        compiler_params=pltpu.CompilerParams(vmem_limit_bytes=VMEM_BYTES),
        name="conv_backward",
    )(grads, spec, kern_spec.reshape(span, 2 * length), twist, hi, lo, skip)
    return out, grad_kern


def in_order(ref, rep, lead=()):
    count = ref.shape[-1] // LANE
    return [
        ref[lead + (slice(None), pl.ds(pl.multiple_of((rep ^ j) * LANE, LANE), LANE))]
        for j in range(count)
    ]


def put_rel(ref, rep, values, lead=()):
    for j in range(ref.shape[-1] // LANE):
        ref[lead + (slice(None), pl.ds(pl.multiple_of((rep ^ j) * LANE, LANE), LANE))] = values[
            :, j * LANE : (j + 1) * LANE
        ]


def extended(proj_ref, halo_ref, exists, rep, p):
    blocks = [halo_ref[p, :, :LANE]] + in_order(proj_ref, rep, (p,)) + [halo_ref[p, :, LANE:]]
    return jnp.concatenate(blocks, axis=1).astype(F32) * exists


def short_of(ext, col_ref, p):
    return (
        col_ref[:, p : p + 1] * pltpu.roll(ext, 2, 1)
        + col_ref[:, 3 + p : 4 + p] * pltpu.roll(ext, 1, 1)
        + col_ref[:, 6 + p : 7 + p] * ext
        + col_ref[:, 9 + p : 10 + p]
    )


def gate_kernel(rep_ref, proj_ref, halo_ref, col_ref, mask_ref, out_ref):
    rep = rep_ref[0]
    mask, exists = mask_ref[0:1], mask_ref[1:2]
    gate_in = short_of(extended(proj_ref, halo_ref, exists, rep, 1), col_ref, 1)
    values = short_of(extended(proj_ref, halo_ref, exists, rep, 2), col_ref, 2)
    gated = values * gate_in * mask
    out_ref[...] = gated[:, LANE:-LANE].astype(B16)


def output_kernel(rep_ref, proj_ref, halo_ref, col_ref, mask_ref, mixed_ref, out_ref):
    rep = rep_ref[0]
    gate_out = short_of(extended(proj_ref, halo_ref, mask_ref[1:2], rep, 0), col_ref, 0)
    put_rel(out_ref, rep, (gate_out[:, LANE:-LANE] * mixed_ref[...].astype(F32)).astype(B16))


def grad_mix_kernel(rep_ref, proj_ref, halo_ref, col_ref, mask_ref, mixed_ref, gy_ref, out_ref, first_ref):
    rep = rep_ref[0]
    gate_out = short_of(extended(proj_ref, halo_ref, mask_ref[1:2], rep, 0), col_ref, 0)
    gy = jnp.concatenate(in_order(gy_ref, rep), axis=1).astype(F32)
    out_ref[...] = (gy * gate_out[:, LANE:-LANE]).astype(B16)
    first_ref[...] = gy[:, :LANE] * mixed_ref[:, :LANE].astype(F32)


def grad_proj_kernel(
    rep_ref, proj_ref, halo_ref, col_ref, mask_ref, mixed_ref, gy_ref, ggated_ref, gnext_ref, onext_ref, out_ref, sum_ref
):
    rep = rep_ref[0]
    mask, exists = mask_ref[0:1], mask_ref[1:2]
    size = mask_ref.shape[1]
    mid = slice(LANE, size - LANE)
    gy = jnp.concatenate(in_order(gy_ref, rep), axis=1).astype(F32)
    zero = jnp.zeros((gy.shape[0], LANE), F32)
    next_on = exists[:, size - LANE :]
    ext = [extended(proj_ref, halo_ref, exists, rep, p) for p in range(3)]
    short = [short_of(ext[p], col_ref, p) for p in range(3)]
    ggated = jnp.concatenate(
        [zero, ggated_ref[...].astype(F32), gnext_ref[...].astype(F32) * next_on], axis=1
    )
    ggated = ggated * mask
    gout = gy * mixed_ref[...].astype(F32)
    gshort = [
        jnp.concatenate([zero, gout, onext_ref[...] * next_on], axis=1),
        ggated * short[2],
        ggated * short[1],
    ]
    gated = short[2][:, mid] * short[1][:, mid] * mask[:, mid]
    sums = [jnp.sum(gy * short[0][:, mid] * gated, axis=1, keepdims=True)]
    for p in range(3):
        mine = gshort[p][:, mid]
        sums.append(jnp.sum(mine, axis=1, keepdims=True))
        sums.append(jnp.sum(mine * ext[p][:, mid], axis=1, keepdims=True))
        sums.append(jnp.sum(mine * pltpu.roll(ext[p], 1, 1)[:, mid], axis=1, keepdims=True))
        sums.append(jnp.sum(mine * pltpu.roll(ext[p], 2, 1)[:, mid], axis=1, keepdims=True))
        gproj = (
            col_ref[:, 6 + p : 7 + p] * gshort[p]
            + col_ref[:, 3 + p : 4 + p] * pltpu.roll(gshort[p], size - 1, 1)
            + col_ref[:, p : p + 1] * pltpu.roll(gshort[p], size - 2, 1)
        )[:, mid].astype(B16)
        sums.append(jnp.sum(gproj.astype(F32), axis=1, keepdims=True))
        put_rel(out_ref, rep, gproj, (p,))
    sum_ref[...] = jnp.concatenate(sums, axis=1)


def token_call(kernel, name, arrays, outs):
    step = 64

    def spec(shape, cut):
        if not cut:
            return pl.BlockSpec(shape, lambda i: (0,) * len(shape))
        if len(shape) == 3:
            return pl.BlockSpec((shape[0], step, shape[2]), lambda i: (0, i, 0))
        return pl.BlockSpec((step, shape[1]), lambda i: (i, 0))

    width = outs[0].shape[-2]
    return pl.pallas_call(
        kernel,
        grid=(width // step,),
        in_specs=[pl.BlockSpec(memory_space=pltpu.SMEM)] + [spec(a.shape, cut) for a, cut in arrays[1:]],
        out_specs=[spec(o.shape, True) for o in outs],
        out_shape=outs,
        compiler_params=pltpu.CompilerParams(vmem_limit_bytes=VMEM_BYTES),
        name=name,
    )(*[a for a, _ in arrays])


def rows128(values):
    flat = values.reshape(-1)
    return jnp.pad(flat, (0, -flat.shape[0] % 1024)).reshape(-1, 128)


def per_device(
    tokens,
    cotangent,
    lengths,
    in_weight,
    in_bias,
    short_taps,
    short_bias,
    feat_weight,
    feat_bias,
    inner_weight,
    inner_bias,
    deep_weight,
    deep_bias,
    sine_freq,
    kernel_weight,
    skip_gain,
    out_weight,
    out_bias,
    norm1_gain,
    norm1_shift,
    norm2_gain,
    norm2_shift,
    up_weight,
    up_bias,
    down_weight,
    down_bias,
):
    n_seq, n_rep = lax.axis_size("seq"), lax.axis_size("rep")
    seq, rep = lax.axis_index("seq"), lax.axis_index("rep")
    tok_rows, model = tokens.shape
    group = tok_rows * n_rep
    blocks = n_seq // 2
    seq_len = blocks * group
    chan = model // (n_seq * n_rep)
    width = model // n_rep
    hidden = up_weight.shape[2]
    block_start = rep * width
    chan_start = block_start + seq * chan
    rep_scalar = jnp.reshape(rep, (1,)).astype(jnp.int32)

    item_len = jnp.where(seq // blocks == 0, lengths[0], lengths[1])
    at = (seq % blocks) * group
    row_mask = (at + rep * tok_rows + jnp.arange(tok_rows, dtype=jnp.int32) < item_len).astype(F32)[:, None]
    position = at - LANE + jnp.arange(group + 2 * LANE, dtype=jnp.int32)
    mask_ext = jnp.stack([position < item_len, (position >= 0) & (position < seq_len)]).astype(F32)
    mask_ext = jnp.pad(mask_ext, ((0, 6), (0, 0)))

    full_in = ring_gather(in_weight[0]).reshape(model, 3, width)
    full_out = spread_gather(out_weight[0])
    full_up = lax.all_gather(up_weight[0], "seq", axis=0, tiled=True)
    full_down = lax.all_gather(down_weight[0], "seq", axis=0, tiled=True)

    residual = tokens.astype(F32)
    normed_one, unit_one, scale_one = layer_norm(residual, norm1_gain[0], norm1_shift[0])
    normed_one = normed_one.astype(B16)
    rows_one = gather_rel(normed_one)
    rel = rows_one.reshape(n_rep, tok_rows, model)
    last_rows = lax.dynamic_index_in_dim(rel, rep ^ (n_rep - 1), 0, False)[-HALO:]
    first_rows = lax.dynamic_index_in_dim(rel, rep, 0, False)[:HALO]
    before = shift_seq(last_rows, 1)
    after = shift_seq(first_rows, -1)
    gap = jnp.zeros((LANE - HALO, model), B16)
    halo_rows = jnp.concatenate([gap, before, after, gap], axis=0)
    proj_bias = lax.dynamic_slice_in_dim(in_bias[0], block_start, width, 1)[:, :, None]

    def project(rows):
        return (
            jnp.einsum("td,dpc->pct", rows, full_in, preferred_element_type=F32) + proj_bias
        ).astype(B16)

    proj = project(rows_one)
    halo = project(halo_rows)

    tap_cols = lax.dynamic_slice_in_dim(short_taps[0], block_start, width, 2).reshape(9, width)
    bias_cols = lax.dynamic_slice_in_dim(short_bias[0], block_start, width, 1)
    cols = jnp.pad(jnp.concatenate([tap_cols, bias_cols], axis=0), ((0, 4), (0, 0))).T
    common = [(rep_scalar, True), (proj, True), (halo, True), (cols, True), (mask_ext, False)]
    flat_shape = jax.ShapeDtypeStruct((width, group), B16)
    (gated,) = token_call(gate_kernel, "gate", common, [flat_shape])
    received = lax.all_to_all(gated.reshape(n_seq, chan, group), "seq", 0, 0, tiled=True)

    skip_local = lax.dynamic_slice_in_dim(skip_gain[0], chan_start, chan, 0)
    columns = lax.dynamic_slice_in_dim(kernel_weight[0], chan_start, chan, 1)
    twist, table = transform_tables(blocks, group)
    nets = (feat_weight[0], inner_weight[0], deep_weight[0])
    if blocks == 4:
        grid, ramp = feature_table(seq_len, feat_weight.shape[1])
        rates = lax.dynamic_slice_in_dim(jnp.asarray(decay_rates(model)), chan_start, chan, 0)
        smalls = jnp.concatenate([feat_bias, inner_bias, deep_bias, sine_freq], axis=0).T
        filt = smalls.shape[0]
        hi, lo = split_table(table)
        kern_spec, sines, cosines = pl.pallas_call(
            filter_forward_kernel,
            out_shape=(
                jax.ShapeDtypeStruct((blocks * chan, 2 * group), F32),
                jax.ShapeDtypeStruct((3, filt, seq_len), F32),
                jax.ShapeDtypeStruct((3, filt, seq_len), F32),
            ),
            scratch_shapes=[pltpu.VMEM((blocks * chan, 2 * group), F32)],
            compiler_params=pltpu.CompilerParams(vmem_limit_bytes=VMEM_BYTES),
            cost_estimate=pl.CostEstimate(flops=10**6, bytes_accessed=10**6, transcendentals=0),
            name="filter_forward",
        )(grid, ramp, rates, *nets, smalls, columns, twist, hi, lo)
        kern_spec = kern_spec.reshape(blocks, chan, 2 * group)

        def kernel_pull(grad_kernel):
            shapes = [columns.shape] + [w.shape[::-1] for w in nets] + [smalls.shape]
            gcols, g1, g2, g3, gsmalls = pl.pallas_call(
                filter_backward_kernel,
                out_shape=tuple(jax.ShapeDtypeStruct(shape, F32) for shape in shapes),
                compiler_params=pltpu.CompilerParams(vmem_limit_bytes=VMEM_BYTES),
                cost_estimate=pl.CostEstimate(flops=10**6, bytes_accessed=10**6, transcendentals=0),
                name="filter_backward",
            )(grad_kernel, grid, ramp, rates, *nets, smalls, columns, sines, cosines)
            gs = gsmalls.T
            return (g1.T, gs[0], g2.T, gs[1], g3.T, gs[2], gs[3], gcols)

    else:
        feature_grid, ramp_unit = features(seq_len, feat_weight.shape[1])
        kernel, pull = jax.vjp(
            partial(filter_columns, feature_grid, ramp_unit, chan_start, chan, model),
            feat_weight[0],
            feat_bias[0],
            inner_weight[0],
            inner_bias[0],
            deep_weight[0],
            deep_bias[0],
            sine_freq[0],
            columns,
        )
        kern_spec = spectrum_of(kernel.reshape(chan, blocks, group).transpose(1, 0, 2), twist, table)

        def kernel_pull(grad_kernel):
            return pull(grad_kernel.transpose(1, 0, 2).reshape(chan, seq_len))

    mixed_chan, kept_spec = conv_forward(received, kern_spec, twist, table, skip_local)
    mixed = lax.all_to_all(mixed_chan, "seq", 0, 0, tiled=True).reshape(width, group)
    (y_cols,) = token_call(output_kernel, "output", common + [(mixed, True)], [flat_shape])

    middle_part = jnp.einsum("ct,oc->to", y_cols, full_out, preferred_element_type=F32)
    middle = residual + (scatter_rel(middle_part) + out_bias[0])
    normed_two, unit_two, scale_two = layer_norm(middle, norm2_gain[0], norm2_shift[0])
    rows_two = gather_rel(normed_two.astype(B16))

    grad_top = cotangent.astype(F32) * row_mask
    grad_mlp = grad_top.astype(B16)
    mlp_rows = gather_rel(grad_mlp)
    grad_act = jnp.dot(mlp_rows, full_down, preferred_element_type=F32)
    up_block = lax.dynamic_slice_in_dim(up_bias[0], rep * hidden, hidden, 0)
    pre_act = jnp.dot(rows_two, full_up, preferred_element_type=F32) + up_block
    phi = 0.5 * (1.0 + lax.erf(pre_act * math.sqrt(0.5)))
    act_rows = (pre_act * phi).astype(B16)
    slope = phi + pre_act * (jnp.exp(-0.5 * pre_act * pre_act) * (1.0 / math.sqrt(2.0 * math.pi)))
    grad_pre = (grad_act * slope).astype(B16)
    grad_two = scatter_rel(jnp.einsum("tf,df->td", grad_pre, full_up, preferred_element_type=F32))
    mlp_part = jnp.einsum("tf,of->to", act_rows, full_down, preferred_element_type=F32)
    layer_out = (middle + (scatter_rel(mlp_part) + down_bias[0])).astype(B16)
    term_down = jnp.einsum("to,tf->of", mlp_rows, act_rows, preferred_element_type=F32)
    term_up = jnp.einsum("td,tf->df", rows_two, grad_pre, preferred_element_type=F32)
    grad_two, term_down = lax.optimization_barrier((grad_two, term_down.astype(B16)))
    grad_down_bias = jnp.sum(grad_mlp.astype(F32), axis=0)
    grad_up_block = jnp.sum(grad_pre.astype(F32), axis=0)

    grad_down = lax.psum_scatter(
        term_down, "seq", scatter_dimension=0, tiled=True
    ).astype(F32)
    grad_up = ring_scatter(term_up.astype(B16))

    grad_unit_two, grad_gain_two, grad_shift_two = norm_back(
        grad_two, unit_two, scale_two, norm2_gain[0]
    )
    grad_middle = grad_top + grad_unit_two
    grad_mix = grad_middle.astype(B16)
    grad_out_bias = jnp.sum(grad_mix.astype(F32), axis=0)
    mix_rows = gather_rel(grad_mix)
    gy_cols = jnp.einsum("to,oc->ct", mix_rows, full_out, preferred_element_type=F32).astype(B16)
    term_out = jnp.einsum("to,ct->oc", mix_rows, y_cols, preferred_element_type=F32)
    grad_out = halve_scatter(term_out.astype(B16))

    grad_mixed, gate_first = token_call(
        grad_mix_kernel,
        "grad_mix",
        common + [(mixed, True), (gy_cols, True)],
        [flat_shape, jax.ShapeDtypeStruct((width, LANE), F32)],
    )
    gate_next = shift_seq(gate_first, -1)
    grads_chan = lax.all_to_all(grad_mixed.reshape(n_seq, chan, group), "seq", 0, 0, tiled=True)
    ggated_chan, grad_kernel = conv_backward(grads_chan, kept_spec, kern_spec, twist, table, skip_local)
    ggated = lax.all_to_all(ggated_chan, "seq", 0, 0, tiled=True).reshape(width, group)
    ggated_next = shift_seq(ggated[:, :LANE], -1)
    kernel_grads = kernel_pull(grad_kernel)
    grad_proj, col_sums = token_call(
        grad_proj_kernel,
        "grad_proj",
        common
        + [(mixed, True), (gy_cols, True), (ggated, True), (ggated_next, True), (gate_next, True)],
        [jax.ShapeDtypeStruct((3, width, group), B16), jax.ShapeDtypeStruct((width, 16), F32)],
    )

    one_part = jnp.einsum("pct,dpc->td", grad_proj, full_in, preferred_element_type=F32)
    grad_one = scatter_rel(one_part)
    term_in = jnp.einsum("td,pct->dpc", rows_one, grad_proj, preferred_element_type=F32)
    grad_in = halve_scatter(term_in.reshape(model, 3 * width).astype(B16))
    grad_in = grad_in.reshape(-1, 3, width)
    grad_unit_one, grad_gain_one, grad_shift_one = norm_back(
        grad_one, unit_one, scale_one, norm1_gain[0]
    )
    grad_tokens = grad_middle + grad_unit_one

    totals = [
        *kernel_grads[:7],
        grad_gain_one,
        grad_shift_one,
        grad_gain_two,
        grad_shift_two,
        grad_out_bias,
        grad_down_bias,
    ]
    packed = [rows128(t) for t in totals]
    group_part = jnp.concatenate([rows128(col_sums.T), rows128(grad_up_block)], axis=0)
    total, groups, owns = sync_small(jnp.concatenate(packed, axis=0), group_part, rows128(kernel_grads[7]))
    outs = []
    start = 0
    for t, p in zip(totals, packed):
        outs.append(total[start : start + p.shape[0]].reshape(-1)[: t.size].reshape((1,) + t.shape))
        start += p.shape[0]
    flat = groups.reshape(n_rep, -1)
    sums = flat[:, : 16 * width].reshape(n_rep, 16, width).transpose(1, 0, 2).reshape(16, model)
    grad_up_bias = flat[:, 16 * width : 16 * width + hidden].reshape(1, -1)
    filt = columns.shape[0]
    grad_kernel_weight = (
        owns.reshape(n_rep, n_seq, -1)[:, :, : filt * chan]
        .reshape(n_rep, n_seq, filt, chan)
        .transpose(2, 0, 1, 3)
        .reshape(1, filt, model)
    )
    pick = lambda offset: jnp.stack([sums[1 + 5 * p + offset] for p in range(3)])
    grad_skip = sums[0][None]
    grad_short_bias = pick(0)[None]
    grad_short_taps = jnp.stack([pick(3), pick(2), pick(1)])[None]
    grad_in_bias = pick(4)[None]
    return (
        layer_out,
        grad_tokens,
        grad_in[None],
        grad_in_bias,
        grad_short_taps,
        grad_short_bias,
        outs[0],
        outs[1],
        outs[2],
        outs[3],
        outs[4],
        outs[5],
        outs[6],
        grad_kernel_weight,
        grad_skip,
        grad_out[None],
        outs[11],
        outs[7],
        outs[8],
        outs[9],
        outs[10],
        grad_up[None],
        grad_up_bias,
        grad_down[None],
        outs[12],
    )


NN = ((1,), (0,))
NT = ((1,), (1,))
TN = ((0,), (0,))
PART = 64
REP, SEQ, AT, ITEM, OLDER, YOUNGER, OWNER, LEFT, RIGHT = 0, 1, 2, 3, 4, 5, 8, 16, 25
RING = [0, 2, 4, 6, 7, 5, 3, 1]
AHEAD = [(RING[i], RING[(i + 1) % 8]) for i in range(8)]
BACK = [(b, a) for a, b in AHEAD]


def meta_table(group):
    rows = []
    for seq in range(8):
        p = RING.index(seq)
        for rep in range(4):
            row = [rep, seq, (seq % 4) * group, seq // 4, int(seq % 4 != 0), int(seq % 4 != 3), 0, 0]
            row += [RING[(p + k) % 8] for k in (0, -1, 1, -2, 2, -3, 3, 4)]
            row += [RING[(p - k) % 8] for k in range(9)]
            row += [RING[(p + k) % 8] for k in range(9)]
            rows.append(row)
    return np.asarray(rows, np.int32)


COST = {"start": 4000, "setup": 4000, "filter_ahead": 6000}


def call(kernel, name, args, outs, scratch=(), limit=24, away=(), out_away=(), raw=()):
    away, out_away, raw = list(away), list(out_away), list(raw)
    hbm = pl.BlockSpec(memory_space=pltpu.HBM)

    def space(i, a):
        if i in away or i in raw:
            return hbm
        small = a.dtype == jnp.int32
        return pl.BlockSpec(memory_space=pltpu.SMEM if small else pltpu.VMEM)

    n_in, n_out, n_own = len(args), len(outs), len(scratch)
    bufs = [pltpu.VMEM(args[i].shape, args[i].dtype) for i in away]
    bufs += [pltpu.VMEM(outs[i].shape, outs[i].dtype) for i in out_away]
    sems = [pltpu.SemaphoreType.DMA((len(bufs),))] if bufs else []

    def body(*refs):
        ins, results = list(refs[:n_in]), list(refs[n_in : n_in + n_out])
        own, mine = refs[n_in + n_out : n_in + n_out + n_own], refs[n_in + n_out + n_own :]
        copies = []
        for k, i in enumerate(away):
            copies.append(pltpu.make_async_copy(ins[i], mine[k], mine[-1].at[k]))
            ins[i] = mine[k]
        for copy in copies:
            copy.start()
        for copy in copies:
            copy.wait()
        copies = []
        for k, i in enumerate(out_away, len(away)):
            copies.append(pltpu.make_async_copy(mine[k], results[i], mine[-1].at[k]))
            results[i] = mine[k]
        kernel(*ins, *results, *own)
        for copy in copies:
            copy.start()
        for copy in copies:
            copy.wait()

    return pl.pallas_call(
        body,
        out_shape=outs,
        in_specs=[space(i, a) for i, a in enumerate(args)],
        out_specs=[hbm if i in out_away or (-1 - i) in raw else pl.BlockSpec(memory_space=pltpu.VMEM) for i in range(n_out)],
        scratch_shapes=list(scratch) + bufs + sems,
        compiler_params=pltpu.CompilerParams(vmem_limit_bytes=limit * 2**20),
        cost_estimate=pl.CostEstimate(flops=COST.get(name, 1) * 10**6, bytes_accessed=10**5, transcendentals=0),
        name=name,
    )(*args)


def shape(dims, kind):
    return jax.ShapeDtypeStruct(tuple(dims), kind)


def dot(left, right, dims):
    return lax.dot_general(left, right, (dims, ((), ())), preferred_element_type=F32)


def place(index):
    return pl.ds(pl.multiple_of(index * LANE, LANE), LANE)


def normed_of(rows):
    centred = rows - jnp.mean(rows, axis=1, keepdims=True)
    inverse = lax.rsqrt(jnp.mean(centred * centred, axis=1, keepdims=True) + EPS)
    return centred * inverse, inverse


def item_length(meta_ref, len_ref):
    return jnp.where(meta_ref[ITEM] == 0, len_ref[0], len_ref[1])


def lane_masks(meta_ref, len_ref, size):
    lane = lax.broadcasted_iota(jnp.int32, (1, size), 1)
    real = (meta_ref[AT] - LANE + lane < item_length(meta_ref, len_ref)).astype(F32)
    older, younger = meta_ref[OLDER].astype(F32), meta_ref[YOUNGER].astype(F32)
    exists = jnp.where(lane < LANE, older, jnp.where(lane >= size - LANE, younger, 1.0))
    return real, exists


def start_kernel(x_ref, gain_ref, shift_ref, in_ref, out_w_ref, out_ref, io_ref):
    width = out_w_ref.shape[2]
    for p in range(3):
        io_ref[:, p * width : (p + 1) * width] = in_ref[p]
    io_ref[:, 3 * width :] = out_w_ref[0]
    unit, _ = normed_of(x_ref[...].astype(F32))
    out_ref[...] = (unit * gain_ref[...] + shift_ref[...]).astype(B16)


def halves_kernel(left_ref, right_ref, a_ref, b_ref):
    half = a_ref.shape[0]
    a_ref[...] = left_ref[:half]
    b_ref[...] = right_ref[half:]


def assemble_kernel(meta_ref, p0, p1, p2, p3, p4, p5, p6, a_ref, b_ref, out_ref):
    for k, ref in enumerate((p0, p1, p2, p3, p4, p5, p6)):
        out_ref[meta_ref[OWNER + k]] = ref[...]
    half = a_ref.shape[0]
    out_ref[meta_ref[OWNER + 7], :half] = a_ref[...]
    out_ref[meta_ref[OWNER + 7], half:] = b_ref[...]


def own_mask(meta_ref, len_ref, rows):
    row = lax.broadcasted_iota(jnp.int32, (rows, 1), 0)
    return (meta_ref[AT] + meta_ref[REP] * rows + row < item_length(meta_ref, len_ref)).astype(F32)


def setup_kernel(
    meta_ref, len_ref, top_ref, up_ref, down_ref, taps_ref, short_bias_ref, in_bias_ref, up_bias_ref, skip_ref, rate_ref,
    kern_w_ref, feat_ref, fb_ref, ib_ref, db_ref, sf_ref,
    rows_ref, ud_ref, cols_ref, upb_ref, chan_ref, columns_ref, small_col_ref, small_row_ref, w1_ref, *rest
):
    sems = rest[-1]
    copies = [
        pltpu.make_async_copy(up_ref, ud_ref.at[pl.ds(0, 1)], sems.at[0]),
        pltpu.make_async_copy(down_ref, ud_ref.at[pl.ds(1, 1)], sems.at[1]),
    ]
    for copy in copies:
        copy.start()
    top, taps, short_bias, in_bias, up_bias, skip, rate, kern_w, feat, fb, ib, db, sf = (
        top_ref, taps_ref, short_bias_ref, in_bias_ref, up_bias_ref, skip_ref, rate_ref, kern_w_ref, feat_ref,
        fb_ref, ib_ref, db_ref, sf_ref,
    )
    mask = own_mask(meta_ref, len_ref, top.shape[0])
    rows_ref[...] = (top[...].astype(F32) * mask).astype(B16)
    width = cols_ref.shape[0]
    chan = chan_ref.shape[0]
    rep, seq = meta_ref[REP], meta_ref[SEQ]
    lanes = pl.ds(pl.multiple_of(rep * width, width), width)
    rows = [taps[j, p, :, lanes] for j in range(3) for p in range(3)]
    rows += [short_bias[p, :, lanes] for p in range(3)] + [in_bias[p, :, lanes] for p in range(3)]
    stack = jnp.concatenate(rows + [jnp.zeros((LANE - 15, width), F32)], axis=0)
    cols_ref[...] = stack.T[:, :16]
    upb_ref[...] = up_bias[:, pl.ds(pl.multiple_of(rep * upb_ref.shape[1], LANE), upb_ref.shape[1])]
    turn = width - seq * chan
    stack = jnp.concatenate([skip[:, lanes], rate[:, lanes], jnp.zeros((LANE - 2, width), F32)], axis=0)
    chan_ref[...] = pltpu.roll(stack, turn, 1)[:, :LANE].T[:chan, :2]
    columns_ref[...] = pltpu.roll(kern_w[0, :, lanes], turn, 1)[:, :chan]
    filt = small_row_ref.shape[1]
    small = jnp.concatenate([fb[...], ib[...], db[...], sf[...]], axis=0)
    small_row_ref[...] = small
    wide = jnp.concatenate([small, jnp.zeros((4, LANE - filt), F32)], axis=1)
    wide = jnp.concatenate([wide, jnp.zeros((LANE - 4, LANE), F32)], axis=0)
    small_col_ref[...] = wide.T[:filt, :4]
    w1_ref[...] = jnp.concatenate([feat[i] for i in range(feat.shape[0])], axis=0)
    for copy in copies:
        copy.wait()


def edges_kernel(meta_ref, x0, x1, x2, x3, last_ref, first_ref):
    rep = meta_ref[REP]
    refs = (x0, x1, x2, x3)

    def chosen(index, lo):
        value = refs[0][lo : lo + HALO]
        for i in range(1, 4):
            value = jnp.where(index == i, refs[i][lo : lo + HALO].astype(F32), value.astype(F32))
        return value.astype(B16)

    last_ref[...] = chosen(rep ^ 3, x0.shape[0] - HALO)
    first_ref[...] = chosen(rep, 0)


def ext_of(proj_ref, halo_ref, exists, p, rows):
    return (
        jnp.concatenate(
            [halo_ref[p, rows, :LANE], proj_ref[p, rows, :], halo_ref[p, rows, LANE:]], axis=1
        ).astype(F32)
        * exists
    )


def short_from(ext, cols, p):
    return (
        cols[:, p : p + 1] * pltpu.roll(ext, 2, 1)
        + cols[:, 3 + p : 4 + p] * pltpu.roll(ext, 1, 1)
        + cols[:, 6 + p : 7 + p] * ext
        + cols[:, 9 + p : 10 + p]
    )


def project_kernel(
    meta_ref, len_ref, x0, x1, x2, x3, before_ref, after_ref, cols_ref,
    p0, p1, p2, p3, p4, p5, p6, a_ref, b_ref, io_full_ref, proj_ref, halo_ref, gated_ref
):
    assemble_kernel(meta_ref, p0, p1, p2, p3, p4, p5, p6, a_ref, b_ref, io_full_ref)
    io_ref = io_full_ref.reshape(-1, io_full_ref.shape[2])
    rep = meta_ref[REP]
    width, group = gated_ref.shape
    weight = io_ref[:, : 3 * width]
    for i, x_ref in enumerate((x0, x1, x2, x3)):
        cut = dot(x_ref[...], weight, NN).T
        for p in range(3):
            proj_ref[p, :, place(rep ^ i)] = (
                cut[p * width : (p + 1) * width] + cols_ref[:, 12 + p : 13 + p]
            ).astype(B16)
    edge = dot(jnp.concatenate([before_ref[...], after_ref[...]], axis=0), weight, NN)
    gap = jnp.zeros((LANE - HALO, 3 * width), F32)
    edge = jnp.concatenate([gap, edge, gap], axis=0).T
    for p in range(3):
        halo_ref[p] = (edge[p * width : (p + 1) * width] + cols_ref[:, 12 + p : 13 + p]).astype(B16)
    mask, exists = lane_masks(meta_ref, len_ref, group + 2 * LANE)
    for lo in range(0, width, PART):
        rows = slice(lo, lo + PART)
        cols = cols_ref[rows, :]
        gate_in = short_from(ext_of(proj_ref, halo_ref, exists, 1, rows), cols, 1)
        values = short_from(ext_of(proj_ref, halo_ref, exists, 2, rows), cols, 2)
        gated_ref[rows, :] = (values * gate_in * mask)[:, LANE:-LANE].astype(B16)


def out_project_kernel(
    meta_ref, len_ref, proj_ref, halo_ref, cols_ref, io_ref, mixed_ref, y_ref, give3_ref, give1_ref, keep2_ref, keep0_ref
):
    rep = meta_ref[REP]
    width, group = mixed_ref.shape
    _, exists = lane_masks(meta_ref, len_ref, group + 2 * LANE)
    for lo in range(0, width, LANE):
        rows = slice(lo, lo + LANE)
        gate_out = short_from(ext_of(proj_ref, halo_ref, exists, 0, rows), cols_ref[rows, :], 0)
        y = gate_out[:, LANE:-LANE] * mixed_ref[rows, :].astype(F32)
        for j in range(4):
            y_ref[rep ^ j, :, rows] = y[:, j * LANE : (j + 1) * LANE].T.astype(B16)
    outs = (keep0_ref, give1_ref, keep2_ref, give3_ref)
    left = y_ref[...].reshape(-1, width)
    rows = y_ref.shape[1]
    for lo in range(0, io_ref.shape[0], 256):
        part = dot(left, io_ref[lo : lo + 256, 3 * width :], NT)
        for i, ref in enumerate(outs):
            ref[:, lo : lo + 256] = part[i * rows : (i + 1) * rows].astype(ref.dtype)


def halves_far_kernel(left_ref, right_ref, a_ref, b_ref, sems):
    half = a_ref.shape[0]
    copies = [
        pltpu.make_async_copy(left_ref.at[pl.ds(0, half)], a_ref, sems.at[0]),
        pltpu.make_async_copy(right_ref.at[pl.ds(half, half)], b_ref, sems.at[1]),
    ]
    for copy in copies:
        copy.start()
    for copy in copies:
        copy.wait()


def assemble_far_kernel(meta_ref, p0, p1, p2, p3, p4, p5, p6, a_ref, b_ref, out_ref, sems):
    half = a_ref.shape[0]
    last = out_ref.at[meta_ref[OWNER + 7]]
    copies = [
        pltpu.make_async_copy(ref, out_ref.at[meta_ref[OWNER + k]], sems.at[k])
        for k, ref in enumerate((p0, p1, p2, p3, p4, p5, p6))
    ]
    copies.append(pltpu.make_async_copy(a_ref, last.at[pl.ds(0, half)], sems.at[7]))
    copies.append(pltpu.make_async_copy(b_ref, last.at[pl.ds(half, half)], sems.at[8]))
    for copy in copies:
        copy.start()
    for copy in copies:
        copy.wait()


def norm_second_kernel(x_ref, keep_ref, near_ref, far_ref, bias_ref, gain_ref, shift_ref, middle_ref, out_ref):
    middle = x_ref[...].astype(F32) + (
        keep_ref[...] + near_ref[...].astype(F32) + far_ref[...].astype(F32) + bias_ref[...]
    )
    middle_ref[...] = middle
    unit, _ = normed_of(middle)
    out_ref[...] = (unit * gain_ref[...] + shift_ref[...]).astype(B16)


def mlp_kernel(x0, x1, x2, x3, g0, g1, g2, g3, ud_ref, bias_ref, act_ref, gpre_ref, sum_ref):
    step = 256
    rows, model = x0.shape
    pieces = ((x0, g0), (x1, g1), (x2, g2), (x3, g3))
    for lo in range(0, act_ref.shape[1], step):
        cut = slice(lo, lo + step)
        up = ud_ref[:, 0, :, cut].reshape(model, step)
        down = ud_ref[:, 1, :, cut].reshape(model, step)
        total = None
        for i, (x_ref, g_ref) in enumerate(pieces):
            at = slice(i * rows, (i + 1) * rows)
            pre = dot(x_ref[...], up, NN) + bias_ref[:, cut]
            gact = dot(g_ref[...], down, NN)
            phi = 0.5 * (1.0 + lax.erf(pre * math.sqrt(0.5)))
            slope = phi + pre * (jnp.exp(-0.5 * pre * pre) * (1.0 / math.sqrt(2.0 * math.pi)))
            act_ref[at, cut] = (pre * phi).astype(B16)
            gpre = (gact * slope).astype(B16)
            gpre_ref[at, cut] = gpre
            part = jnp.sum(gpre.astype(F32), axis=0, keepdims=True)
            total = part if total is None else total + part
        sum_ref[:, cut] = total


def rows_kernel(which, left_ref, ud_ref, give3_ref, give1_ref, keep2_ref, keep0_ref):
    rows, model = give3_ref.shape
    owned = ud_ref.shape[2]
    outs = (keep0_ref, give1_ref, keep2_ref, give3_ref)
    for k in range(0, ud_ref.shape[0], 2):
        weight = ud_ref[k : k + 2, which].reshape(2 * owned, -1)
        part = dot(left_ref[...], weight, NT)
        for i, ref in enumerate(outs):
            ref[:, k * owned : (k + 2) * owned] = part[i * rows : (i + 1) * rows].astype(ref.dtype)


def mlp_grad_kernel(meta_ref, x0, x1, x2, x3, g0, g1, g2, g3, act_ref, gpre_ref, out_ref, a_ref, b_ref):
    grad_pair((x0, x1, x2, x3), gpre_ref[...], out_ref, slice(None), 0)
    grad_pair((g0, g1, g2, g3), act_ref[...], out_ref, slice(None), out_ref.shape[3] // 2)
    give_first(meta_ref, out_ref, a_ref, b_ref)


def norm_second_back_kernel(
    meta_ref, len_ref, keep_ref, near_ref, far_ref, middle_ref, top_ref, gain_ref, out_ref, gx_ref, sum_ref
):
    grad = keep_ref[...] + near_ref[...].astype(F32) + far_ref[...].astype(F32)
    unit, inverse = normed_of(middle_ref[...])
    scaled = grad * gain_ref[...]
    one = jnp.mean(scaled, axis=1, keepdims=True)
    two = jnp.mean(scaled * unit, axis=1, keepdims=True)
    top = top_ref[...].astype(F32) * own_mask(meta_ref, len_ref, top_ref.shape[0])
    out = top + inverse * (scaled - one - unit * two)
    out_ref[...] = out
    gx = out.astype(B16)
    gx_ref[...] = gx
    rows = [grad * unit, grad, gx.astype(F32), top]
    sums = [jnp.sum(r, axis=0, keepdims=True) for r in rows]
    sum_ref[...] = jnp.concatenate(sums + [jnp.zeros((4, sums[0].shape[1]), F32)], axis=0)


def grad_gate_kernel(
    meta_ref, len_ref, x0, x1, x2, x3, io_ref, proj_ref, halo_ref, cols_ref, mixed_ref, gy_ref, first_ref, gmix_ref
):
    rep = meta_ref[REP]
    width, group = mixed_ref.shape
    _, exists = lane_masks(meta_ref, len_ref, group + 2 * LANE)
    weight = io_ref[:, 3 * width :]
    for i, x_ref in enumerate((x0, x1, x2, x3)):
        gy_ref[:, place(rep ^ i)] = dot(x_ref[...], weight, NN).T.astype(B16)
    for lo in range(0, width, PART):
        rows = slice(lo, lo + PART)
        gate_out = short_from(ext_of(proj_ref, halo_ref, exists, 0, rows), cols_ref[rows, :], 0)
        gy = gy_ref[rows, :].astype(F32)
        gmix_ref[rows, :] = (gy * gate_out[:, LANE:-LANE]).astype(B16)
        first_ref[rows, :] = gy[:, :LANE] * mixed_ref[rows, :LANE].astype(F32)


def conv_back_kernel(
    spec_ref, kern_ref, twist_ref, hi_ref, lo_ref, chan_ref, g_ref, out_ref, grad_kern_ref, z_ref, p_ref
):
    blocks, rows, length = twist_ref.shape[0], g_ref.shape[1], g_ref.shape[2]
    short_blocks = blocks // 4
    span = blocks * rows
    first = [g_ref[b].astype(F32) for b in range(blocks)]
    second = [g_ref[blocks + b].astype(F32) for b in range(short_blocks)]
    turn_rows(first, twist_ref, z_ref, 0, blocks)
    turn_rows(second, twist_ref, z_ref, span, blocks)
    grad = dot_twice(z_ref[...], hi_ref[...], ((1,), (0,)))
    kern = kern_ref[...]
    p_ref[0:span] = times(grad[:span], kern, True)
    p_ref[span : 2 * span] = times(grad[span:], kern, True)
    p_ref[2 * span :] = times(grad[:span], spec_ref[0:span], True) + times(grad[span:], spec_ref[span:], True)
    w = dot_twice(p_ref[...], hi_ref[...], ((1,), (1,)))
    skip = chan_ref[:, 0:1]
    for b in range(blocks):
        acc = (back_rows(w, 0, rows, b, twist_ref, blocks) + skip * first[b]).astype(B16)
        out_ref[b] = acc
        if b < short_blocks:
            acc = (back_rows(w, span, rows, b, twist_ref, blocks) + skip * second[b]).astype(B16)
        else:
            acc = jnp.zeros((rows, length), B16)
        out_ref[blocks + b] = acc
        grad_kern_ref[b] = back_rows(w, 2 * span, rows, b, twist_ref, blocks)


def conv_ahead_kernel(kern_ref, twist_ref, hi_ref, lo_ref, chan_ref, x_ref, out_ref, spec_ref, z_ref):
    conv_forward_kernel(
        twist_ref.shape[0] // 4, x_ref, kern_ref, twist_ref, hi_ref, lo_ref, chan_ref.at[:, 0:1], out_ref, spec_ref, z_ref
    )


def filter_ahead_kernel(
    chan_ref, w1_ref, small_ref, columns_ref, grid_ref, ramp_ref, w2_ref, w3_ref, twist_ref, hi_ref, lo_ref,
    spec_ref, sin_ref, cos_ref, z_ref
):
    filter_forward_kernel(
        grid_ref, ramp_ref, chan_ref.at[:, 1:2], w1_ref, w2_ref.at[0], w3_ref.at[0], small_ref, columns_ref,
        twist_ref, hi_ref, lo_ref, spec_ref, sin_ref, cos_ref, z_ref
    )


def halves_of(values):
    top = values.astype(B16)
    return top, (values - top.astype(F32)).astype(B16)


def dot_halves(left, right, dims):
    return dot(left[0], right[0], dims) + dot(left[1], right[0], dims) + dot(left[0], right[1], dims)


def filter_back_kernel(
    meta_ref, gk_ref, grid_ref, ramp_ref, chan_ref, w1_ref, w2_ref, w3_ref, col_ref, row_ref, columns_ref, sin_ref, cos_ref,
    side_ref, wide_ref
):
    freq, freq_row = col_ref[:, 3:4], row_ref[3:4, :]
    filt = freq.shape[0]
    gk = jnp.concatenate([gk_ref[b] for b in range(gk_ref.shape[0])], axis=1)
    gk = halves_of(gk * jnp.exp(-chan_ref[:, 1:2] * ramp_ref[...]))
    gcols = dot_halves(halves_of(sin_ref[2]), gk, NT)
    chan, width = gcols.shape[1], wide_ref.shape[1]
    row = lax.broadcasted_iota(jnp.int32, (chan, width), 0)
    lane = lax.broadcasted_iota(jnp.int32, (chan, width), 1)
    pick = (lane == row + meta_ref[SEQ] * chan).astype(F32)
    wide_ref[...] = dot_high(gcols, pick, NN)
    grad = dot_halves(halves_of(columns_ref[...]), gk, NN)
    ones = jnp.ones((16, grad.shape[1]), B16)
    gfreq = jnp.zeros((1, filt), F32)
    grads, biases = [None] * 3, [None] * 3
    for i, weight in ((2, w3_ref[0]), (1, w2_ref[0]), (0, w1_ref[...])):
        turn = grad * cos_ref[i]
        pair = halves_of(turn)
        below = halves_of(sin_ref[i - 1] if i else grid_ref[...])
        raw = dot_halves(below, pair, NT)
        total = (dot(ones, pair[0], NT) + dot(ones, pair[1], NT))[0:1]
        grads[i] = raw * freq_row
        biases[i] = total * freq_row
        gfreq = gfreq + jnp.sum(raw * weight, axis=0, keepdims=True) + total * row_ref[i : i + 1, :]
        if i:
            grad = dot_halves(halves_of(weight * freq_row), pair, NN)
    gap = jnp.zeros((filt - grads[0].shape[0], filt), F32)
    small = jnp.concatenate(biases + [gfreq, jnp.zeros((filt - 4, filt), F32)], axis=0)
    side_ref[...] = jnp.concatenate(
        [grads[1], grads[2], jnp.concatenate([grads[0], gap], axis=0), small], axis=1
    )


def summed(value):
    total = value[:, :LANE]
    for k in range(LANE, value.shape[1], LANE):
        total = total + value[:, k : k + LANE]
    return jnp.sum(total, axis=1, keepdims=True)


def short_back(ext, cols, gshort, p, mid):
    size = ext.shape[1]
    mine = gshort[:, mid]
    gproj = (
        cols[:, 6 + p : 7 + p] * gshort
        + cols[:, 3 + p : 4 + p] * pltpu.roll(gshort, size - 1, 1)
        + cols[:, p : p + 1] * pltpu.roll(gshort, size - 2, 1)
    )[:, mid].astype(B16).astype(F32)
    sums = [
        summed(mine),
        summed(mine * ext[:, mid]),
        summed(mine * pltpu.roll(ext, 1, 1)[:, mid]),
        summed(mine * pltpu.roll(ext, 2, 1)[:, mid]),
        summed(gproj),
    ]
    return gproj, sums


def grad_first_kernel(
    meta_ref, len_ref, proj_ref, halo_ref, cols_ref, mixed_ref, gy_ref, onext_ref, io_ref, tok_ref, sum_ref, part_ref
):
    rep = meta_ref[REP]
    width, group = mixed_ref.shape
    size = group + 2 * LANE
    mask, exists = lane_masks(meta_ref, len_ref, size)
    mid = slice(LANE, size - LANE)
    next_on = exists[:, size - LANE :]
    columns = []
    for lo in range(0, width, PART):
        rows = slice(lo, lo + PART)
        cols = cols_ref[rows, :]
        gy = gy_ref[rows, :].astype(F32)
        gout = gy * mixed_ref[rows, :].astype(F32)
        gshort = jnp.concatenate([jnp.zeros((PART, LANE), F32), gout, onext_ref[rows, :] * next_on], axis=1)
        gproj, sums = short_back(ext_of(proj_ref, halo_ref, exists, 0, rows), cols, gshort, 0, mid)
        for j in range(4):
            tok_ref[rep ^ j, :, rows] = gproj[:, j * LANE : (j + 1) * LANE].T.astype(B16)
        columns.append(jnp.concatenate(sums + [jnp.zeros((PART, LANE - 5), F32)], axis=1))
    sum_ref[...] = jnp.concatenate(columns, axis=0).T[:8]
    part_ref[...] = dot(tok_ref[...].reshape(-1, width), io_ref[:, :width], NT)


def grad_short_kernel(
    meta_ref, len_ref, proj_ref, halo_ref, cols_ref, gy_ref, io_ref, before_ref,
    x0, x1, x2, x3, gain_ref, shift_ref, ggated_ref, gnext_ref,
    tok_ref, sum_ref, norm_ref, give3_ref, give1_ref, keep2_ref, keep0_ref
):
    rep = meta_ref[REP]
    width, group = gy_ref.shape
    size = group + 2 * LANE
    mask, exists = lane_masks(meta_ref, len_ref, size)
    mid = slice(LANE, size - LANE)
    columns = []
    for lo in range(0, width, PART):
        rows = slice(lo, lo + PART)
        cols = cols_ref[rows, :]
        ext = [ext_of(proj_ref, halo_ref, exists, p, rows) for p in (1, 2)]
        short = [short_from(ext[p - 1], cols, p) for p in (1, 2)]
        ggated = (
            jnp.concatenate(
                [jnp.zeros((PART, LANE), F32), ggated_ref[rows, :].astype(F32), gnext_ref[rows, :].astype(F32)], axis=1
            )
            * mask
            * exists
        )
        gate_out = short_from(ext_of(proj_ref, halo_ref, exists, 0, rows), cols, 0)[:, mid]
        gated = short[1][:, mid] * short[0][:, mid] * mask[:, mid]
        sums = [summed(gy_ref[rows, :].astype(F32) * gate_out * gated)]
        for p in (1, 2):
            gproj, more = short_back(ext[p - 1], cols, ggated * short[2 - p], p, mid)
            sums += more
            at = slice((p - 1) * width + lo, (p - 1) * width + lo + PART)
            for j in range(4):
                tok_ref[rep ^ j, :, at] = gproj[:, j * LANE : (j + 1) * LANE].T.astype(B16)
        columns.append(jnp.concatenate(sums + [jnp.zeros((PART, LANE - 11), F32)], axis=1))
    sum_ref[...] = jnp.concatenate(columns, axis=0).T[:16]
    outs = (keep0_ref, give1_ref, keep2_ref, give3_ref)
    left = tok_ref[...].reshape(-1, 2 * width)
    tall = tok_ref.shape[1]
    for lo in range(0, io_ref.shape[0], 256):
        cut = slice(lo, lo + 256)
        part = dot(left, io_ref[cut, width : 3 * width], NT) + before_ref[:, cut]
        plain = jnp.sum(part, axis=0, keepdims=True)
        cross = None
        for i, (ref, x_ref) in enumerate(zip(outs, (x0, x1, x2, x3))):
            mine = part[i * tall : (i + 1) * tall]
            ref[:, cut] = mine.astype(ref.dtype)
            two = jnp.sum(mine * x_ref[:, cut].astype(F32), axis=0, keepdims=True)
            cross = two if cross is None else cross + two
        norm_ref[0:1, cut] = (cross - shift_ref[:, cut] * plain) / gain_ref[:, cut]
        norm_ref[1:2, cut] = plain


def give_first(meta_ref, term_ref, a_ref, b_ref):
    half = a_ref.shape[2]
    seq = meta_ref[SEQ]
    s0, s1 = seq & 1, (seq >> 1) & 1
    for i in range(2):
        for j in range(2):
            a_ref[i, j] = term_ref[i, j, 1 - s0, :half]
            b_ref[i, j] = term_ref[i, 1 - s1, j, half:]


def grad_pair(refs, right, out_ref, lanes, base=0):
    owned = refs[0].shape[1] // 8
    for k in range(0, 8, 2):
        left = jnp.concatenate([r[:, k * owned : (k + 2) * owned] for r in refs], axis=0)
        part = dot(left, right, TN).astype(B16)
        out_ref[k // 4, (k // 2) % 2, 0, base : base + owned, lanes] = part[:owned]
        out_ref[k // 4, (k // 2) % 2, 1, base : base + owned, lanes] = part[owned:]


def grad_early_kernel(meta_ref, g0, g1, g2, g3, y_ref, x0, x1, x2, x3, tok_ref, out_ref, a_ref, b_ref):
    width = y_ref.shape[2]
    grad_pair((g0, g1, g2, g3), y_ref[...].reshape(-1, width), out_ref, slice(0, width))
    grad_pair((x0, x1, x2, x3), tok_ref[...].reshape(-1, width), out_ref, slice(width, 2 * width))
    give_first(meta_ref, out_ref, a_ref, b_ref)


def grad_late_kernel(meta_ref, x0, x1, x2, x3, tok_ref, out_ref, a_ref, b_ref):
    width = tok_ref.shape[2]
    grad_pair((x0, x1, x2, x3), tok_ref[...].reshape(-1, width), out_ref, slice(0, width))
    give_first(meta_ref, out_ref, a_ref, b_ref)


def halve_one_kernel(meta_ref, term_ref, a_in, b_in, keep_a, keep_b, give_a, give_b):
    half = a_in.shape[2]
    seq = meta_ref[SEQ]
    s0, s1 = seq & 1, (seq >> 1) & 1
    for i in range(2):
        keep_a[i] = term_ref[i, s1, s0, :half].astype(F32) + a_in[i, s1].astype(F32)
        give_a[i] = (term_ref[i, 1 - s1, s0, :half].astype(F32) + a_in[i, 1 - s1].astype(F32)).astype(B16)
        keep_b[i] = term_ref[i, s1, s0, half:].astype(F32) + b_in[i, s0].astype(F32)
        give_b[i] = (term_ref[i, s1, 1 - s0, half:].astype(F32) + b_in[i, 1 - s0].astype(F32)).astype(B16)


def halve_two_kernel(meta_ref, keep_a_in, keep_b_in, a_in, b_in, keep_a, keep_b, give_a, give_b):
    s2 = meta_ref[SEQ] >> 2
    keep_a[...] = keep_a_in[s2] + a_in[s2].astype(F32)
    give_a[...] = (keep_a_in[1 - s2] + a_in[1 - s2].astype(F32)).astype(B16)
    keep_b[...] = keep_b_in[s2] + b_in[s2].astype(F32)
    give_b[...] = (keep_b_in[1 - s2] + b_in[1 - s2].astype(F32)).astype(B16)


def add_last_kernel(keep_ref, came_ref, out_ref):
    out_ref[0] = keep_ref[...] + came_ref[...].astype(F32)


def early_last_kernel(keep_a, keep_b, a_in, b_in, out_ref, in_ref):
    half, width = keep_a.shape[0], out_ref.shape[2]
    for keep, came, rows in ((keep_a, a_in, slice(0, half)), (keep_b, b_in, slice(half, 2 * half))):
        out_ref[0, rows] = keep[:, :width] + came[:, :width].astype(F32)
        in_ref[rows] = keep[:, width:] + came[:, width:].astype(F32)


def late_last_kernel(keep_a, keep_b, a_in, b_in, first_ref, out_ref):
    half, width = keep_a.shape[0], out_ref.shape[3]
    out_ref[0, 0] = first_ref[...]
    for keep, came, rows in ((keep_a, a_in, slice(0, half)), (keep_b, b_in, slice(half, 2 * half))):
        for p in range(2):
            lanes = slice(p * width, (p + 1) * width)
            out_ref[0, 1 + p, rows] = keep[:, lanes] + came[:, lanes].astype(F32)


def norm_first_back_kernel(keep_ref, near_ref, far_ref, x_ref, middle_ref, gain_ref, out_ref):
    grad = keep_ref[...] + near_ref[...].astype(F32) + far_ref[...].astype(F32)
    unit, inverse = normed_of(x_ref[...].astype(F32))
    scaled = grad * gain_ref[...]
    one = jnp.mean(scaled, axis=1, keepdims=True)
    two = jnp.mean(scaled * unit, axis=1, keepdims=True)
    out_ref[...] = middle_ref[...] + inverse * (scaled - one - unit * two)


def layer_out_kernel(keep_ref, near_ref, far_ref, middle_ref, bias_ref, out_ref):
    part = keep_ref[...] + near_ref[...].astype(F32) + far_ref[...].astype(F32)
    out_ref[...] = (middle_ref[...] + (part + bias_ref[...])).astype(B16)


def heads_kernel(in_ref, out_ref):
    out_ref[...] = in_ref[:, :LANE]


def add_far_kernel(keep_ref, came_ref, out_ref):
    out_ref[...] = (keep_ref[...] + came_ref[...].astype(F32)).astype(B16)


HALF = 88


def pack_small_kernel(side_ref, wide_ref, col0_ref, col_ref, up_ref, one_ref, two_ref, out_ref):
    filt, width = side_ref.shape
    out_ref[:filt] = side_ref[...]
    at = filt
    for ref, count in ((one_ref, 2), (two_ref, 4)):
        for r in range(count):
            for k in range(4):
                out_ref[at : at + 1] = ref[r : r + 1, k * width : (k + 1) * width]
                at += 1
    out_ref[HALF : HALF + 1] = col_ref[0:1]
    out_ref[HALF + 1 : HALF + 6] = col0_ref[0:5]
    out_ref[HALF + 6 : HALF + 16] = col_ref[1:11]
    for k in range(4):
        out_ref[HALF + 16 + k : HALF + 17 + k] = up_ref[:, k * width : (k + 1) * width]
    out_ref[HALF + 20 : HALF + 24] = jnp.zeros((4, width), F32)
    out_ref[HALF + 24 :] = wide_ref[...]


def add_small_kernel(mine_ref, came_ref, out_ref):
    out_ref[...] = mine_ref[...] + came_ref[...]


def list_small_kernel(meta_ref, mine_ref, came_ref, out_ref):
    y = meta_ref[REP] >> 1
    out_ref[:HALF] = mine_ref[:HALF] + came_ref[:HALF]
    out_ref[pl.ds(pl.multiple_of((1 + y) * HALF, 8), HALF)] = mine_ref[HALF:]
    out_ref[pl.ds(pl.multiple_of((2 - y) * HALF, 8), HALF)] = came_ref[HALF:]


def unpack_small_kernel(
    meta_ref, mine_ref, came_ref,
    in_bias, taps, short_bias, fw, fb, iw, ib, dw, db, sf, kern_w, skip, out_b, n1g, n1s, n2g, n2s, up_b, down_b
):
    core = meta_ref[REP] & 1
    filt, width = iw.shape[2], mine_ref.shape[1]
    total = mine_ref[:HALF] + came_ref[:HALF]
    iw[0] = total[:filt, :filt]
    dw[0] = total[:filt, filt : 2 * filt]
    for k in range(fw.shape[0]):
        fw[k] = total[k : k + 1, 2 * filt : 3 * filt]
    for k, ref in enumerate((fb, ib, db, sf)):
        ref[...] = total[k : k + 1, 3 * filt :]
    at = filt
    for ref in (n1g, n1s, n2g, n2s, out_b, down_b):
        for k in range(4):
            ref[:, k * width : (k + 1) * width] = total[at : at + 1]
            at += 1
    for y in range(2):
        lo = (1 + y) * HALF
        mine, came = mine_ref[lo : lo + HALF], came_ref[lo : lo + HALF]
        for c in range(2):
            block = jnp.where(core == c, mine, came)
            lanes = slice((2 * y + c) * width, (2 * y + c + 1) * width)
            skip[:, lanes] = block[0:1]
            for p in range(3):
                row = 1 + 5 * p
                short_bias[p, :, lanes] = block[row : row + 1]
                for j in range(3):
                    taps[j, p, :, lanes] = block[row + 3 - j : row + 4 - j]
                in_bias[p, :, lanes] = block[row + 4 : row + 5]
            for k in range(4):
                lo_up = (2 * y + c) * 4 * width + k * width
                up_b[:, lo_up : lo_up + width] = block[16 + k : 17 + k]
            kern_w[0, :, lanes] = block[24 : 24 + filt]


def tie(values, *others):
    return lax.optimization_barrier((values, others))[0]


class RingGather:
    def __init__(self, name, meta, shard, far=False):
        self.name, self.meta, self.far = name, meta, far
        self.pieces = [shard]
        self.send(shard, shard)

    def send(self, left, right):
        self.came = (lax.ppermute(left, "seq", AHEAD), lax.ppermute(right, "seq", BACK))

    def step(self, *others):
        left, right = tie(self.came, *others)
        self.pieces += [left, right]
        count = len(self.pieces)
        if count == 7:
            half = shape((left.shape[0] // 2,) + left.shape[1:], B16)
            if self.far:
                left, right = call(
                    halves_far_kernel, self.name + "_halves", [left, right], [half, half],
                    scratch=[pltpu.SemaphoreType.DMA((2,))], raw=[0, 1, -1, -2],
                )
            else:
                left, right = call(halves_kernel, self.name + "_halves", [left, right], [half, half])
        if count < 9:
            self.send(left, right)
        return self.came

    def full(self, *others):
        left, right = tie(self.came, *others)
        pieces = self.pieces + [left, right]
        whole = [shape((8,) + self.pieces[0].shape, B16)]
        if self.far:
            return call(
                assemble_far_kernel, self.name + "_assemble", [self.meta, *pieces], whole,
                scratch=[pltpu.SemaphoreType.DMA((9,))], raw=range(1, 10),
            )[0]
        return call(assemble_kernel, self.name + "_assemble", [self.meta, *pieces], whole)[0]


def gather_four(rows):
    far = swap(rows, "rep", 2)
    near = swap(rows, "rep", 1)
    diag = swap(far, "rep", 1)
    return [rows, near, far, diag]


def pass_far(give3, give1, keep2):
    came = swap(give3, "rep", 1)
    near = swap(give1, "rep", 1)
    (summed,) = call(add_far_kernel, "add_far", [keep2, came], [shape(keep2.shape, B16)])
    return near, swap(summed, "rep", 2), summed


class Halving:
    def __init__(self, name, meta, term, give):
        self.name, self.meta, self.term = name, meta, term
        self.came = (swap(give[0], "seq", 1), swap(give[1], "seq", 2))

    def one(self, *others):
        rows, cols = self.term.shape[3] // 2, self.term.shape[4]
        outs = [shape((2, rows, cols), F32)] * 2 + [shape((2, rows, cols), B16)] * 2
        args = [self.meta, self.term, *tie(self.came, *others)]
        *self.keep, ga, gb = call(halve_one_kernel, self.name + "_one", args, outs)
        self.came = (swap(ga, "seq", 2), swap(gb, "seq", 1))
        return ga

    def two_kept(self, *others):
        rows, cols = self.term.shape[3] // 2, self.term.shape[4]
        outs = [shape((rows, cols), F32)] * 2 + [shape((rows, cols), B16)] * 2
        args = [self.meta, *self.keep, *tie(self.came, *others)]
        return call(halve_two_kernel, self.name + "_two", args, outs)

    def two(self, *others):
        *self.keep, ga, gb = self.two_kept(*others)
        self.came = (swap(ga, "seq", 4), swap(gb, "seq", 4))
        return ga

    def last(self, *others):
        return [*self.keep, *tie(self.came, *others)]


def exchange(blocks):
    return lax.all_to_all(blocks, "seq", 0, 0, tiled=True)


def per_device_fast(
    tokens,
    cotangent,
    lengths,
    in_weight,
    in_bias,
    short_taps,
    short_bias,
    feat_weight,
    feat_bias,
    inner_weight,
    inner_bias,
    deep_weight,
    deep_bias,
    sine_freq,
    kernel_weight,
    skip_gain,
    out_weight,
    out_bias,
    norm1_gain,
    norm1_shift,
    norm2_gain,
    norm2_shift,
    up_weight,
    up_bias,
    down_weight,
    down_bias,
):
    tok_rows, model = tokens.shape
    group = tok_rows * 4
    blocks = 4
    seq_len = blocks * group
    chan = model // 32
    width = model // 4
    hidden = up_weight.shape[2]
    owned = model // 8
    filt = feat_weight.shape[2]
    device = lax.axis_index("seq") * 4 + lax.axis_index("rep")
    meta = lax.dynamic_index_in_dim(jnp.asarray(meta_table(group)), device, 0, keepdims=False)
    row_f32, row_b16 = shape((tok_rows, model), F32), shape((tok_rows, model), B16)
    sums_shapes = [row_b16, row_b16, row_f32, row_f32]
    flat_shape = shape((width, group), B16)

    normed, io_shard = call(
        start_kernel,
        "start",
        [tokens, norm1_gain, norm1_shift, in_weight[0].transpose(1, 0, 2), out_weight],
        [row_b16, shape((owned, 4 * width), B16)],
        away=range(5),
        limit=62,
    )
    io_ring = RingGather("io", meta, io_shard)
    x_one = gather_four(normed)
    twist, table = transform_tables(blocks, group)
    hi, lo = split_table(table)
    grid, ramp = feature_table(seq_len, feat_weight.shape[1])
    twist, grid, ramp = jnp.asarray(twist), jnp.asarray(grid), jnp.asarray(ramp)
    params = [
        cotangent, up_weight, down_weight,
        short_taps.transpose(1, 2, 0, 3), short_bias.transpose(1, 0, 2), in_bias.transpose(1, 0, 2), up_bias, skip_gain,
        jnp.asarray(decay_rates(model).T), kernel_weight, feat_weight.transpose(1, 0, 2),
        feat_bias, inner_bias, deep_bias, sine_freq,
    ]
    top_rows, ud_shard, cols, up_block, chans, columns, small_col, small_row, feat = call(
        setup_kernel,
        "setup",
        [meta, lengths, *params],
        [
            row_b16, shape((2, owned, hidden), B16),
            shape((width, 16), F32), shape((1, hidden), F32), shape((chan, 2), F32), shape((filt, chan), F32),
            shape((filt, 4), F32), shape((4, filt), F32), shape(feat_weight.shape[1:], F32),
        ],
        scratch=[pltpu.SemaphoreType.DMA((2,))],
        away=[2] + list(range(5, 2 + len(params))),
        raw=[3, 4, -2],
    )
    io_ring.step(x_one[1])
    tables = [grid, ramp, inner_weight, deep_weight, twist, hi, lo]
    kern_spec, sines, cosines = call(
        filter_ahead_kernel,
        "filter_ahead",
        [chans, feat, tie(small_col, io_ring.pieces[-1]), columns, *tables],
        [
            shape((blocks * chan, 2 * group), F32),
            shape((3, filt, seq_len), F32),
            shape((3, filt, seq_len), F32),
        ],
        scratch=[pltpu.VMEM((blocks * chan, 2 * group), F32)],
        away=range(4, 4 + len(tables)),
    )
    io_ring.step(kern_spec, x_one[2])

    edge = shape((HALO, model), B16)
    last, first = call(edges_kernel, "edges", [meta, *x_one], [edge, edge])
    before = lax.ppermute(last, "seq", [(i, (i + 1) % 8) for i in range(8)])
    after = lax.ppermute(first, "seq", [(i, (i + 7) % 8) for i in range(8)])
    io_ring.step()
    io_pieces = io_ring.pieces + list(tie(io_ring.came, before, after))
    ud_ring = RingGather("ud", meta, tie(ud_shard, io_pieces[-1]))
    g_top = gather_four(tie(top_rows, x_one[3]))
    full_io, proj, halo, gated = call(
        project_kernel,
        "project",
        [meta, lengths, *x_one, before, after, cols, *io_pieces],
        [
            shape((8, owned, 4 * width), B16), shape((3, width, group), B16), shape((3, width, 2 * LANE), B16), flat_shape
        ],
    )
    full_io = full_io.reshape(model, 4 * width)
    common = [proj, halo, cols]

    spread = (8, chan, group)
    received = exchange(gated.reshape(spread))
    spec_rows = 2 * blocks * chan
    mixed, kept_spec = call(
        conv_ahead_kernel,
        "conv_ahead",
        [kern_spec, twist, hi, lo, chans, received],
        [shape(spread, B16), shape((spec_rows, 2 * group), F32)],
        scratch=[pltpu.VMEM((spec_rows, 2 * group), F32)],
    )
    ud_ring.step(mixed)
    mixed = exchange(mixed).reshape(width, group)
    ud_ring.step(mixed)

    y_tok, give3, give1, keep2, keep0 = call(
        out_project_kernel,
        "out_project",
        [meta, lengths, *common, full_io, mixed],
        [shape((4, tok_rows, width), B16)] + sums_shapes,
    )
    near, far, _ = pass_far(give3, give1, keep2)
    middle, normed_two = call(
        norm_second_kernel,
        "norm_second",
        [tokens, keep0, near, far, out_bias, norm2_gain, norm2_shift],
        [row_f32, row_b16],
    )
    ud_ring.step(normed_two)
    x_two = gather_four(normed_two)
    full_ud = ud_ring.full(x_two[2])

    tall = shape((group, hidden), B16)
    act, gpre, gup = call(
        mlp_kernel, "mlp", [*x_two, *g_top, full_ud, up_block], [tall, tall, shape((1, hidden), F32)],
    )
    give3, give1, keep2, keep0 = call(partial(rows_kernel, 0), "grad_two", [gpre, full_ud], sums_shapes)
    near, far, passed = pass_far(give3, give1, keep2)
    give = shape((2, 2, owned, hidden), B16)
    mlp_terms, ga, gb = call(
        mlp_grad_kernel,
        "mlp_grad",
        [meta, *x_two, *g_top, act, tie(gpre, passed)],
        [shape((2, 2, 2, 2 * owned, hidden), B16), give, give],
    )
    wide_back = Halving("far", meta, mlp_terms, (ga, gb))
    grad_middle, gx, norm_sums = call(
        norm_second_back_kernel,
        "norm_second_back",
        [meta, lengths, keep0, near, tie(far, ga), middle, cotangent, norm2_gain],
        [row_f32, row_b16, shape((8, model), F32)],
    )
    g_far, g_near = swap(gx, "rep", 2), swap(gx, "rep", 1)
    m3, m1, m2, m0 = call(partial(rows_kernel, 1), "mlp_rows", [tie(act, gx), full_ud], sums_shapes)
    g_mid = [gx, g_near, g_far, swap(tie(g_far, m3), "rep", 1)]
    gy, gate_first, gmix = call(
        grad_gate_kernel,
        "grad_gate",
        [meta, lengths, *tie(tuple(g_mid), m3), full_io, *common, mixed],
        [flat_shape, shape((width, LANE), F32), flat_shape],
    )

    received = exchange(gmix.reshape(spread))
    given = wide_back.one(received)
    gate_next = lax.ppermute(tie(gate_first, received), "seq", [(i, (i + 7) % 8) for i in range(8)])
    ggated, grad_kernel = call(
        conv_back_kernel,
        "conv_back",
        [kept_spec, kern_spec, twist, hi, lo, chans, tie(received, given)],
        [shape(spread, B16), shape((blocks, chan, group), F32)],
        scratch=[pltpu.VMEM((spec_rows, 2 * group), F32), pltpu.VMEM((3 * spec_rows // 2, 2 * group), F32)],
    )
    ggated = exchange(tie(ggated, gate_next)).reshape(width, group)
    up_keep, down_keep, up_give, down_give = wide_back.two_kept(ggated)
    up_came = swap(up_give, "seq", 4)
    (heads,) = call(heads_kernel, "heads", [tie(ggated, up_give)], [shape((width, LANE), B16)])
    ggated_next = lax.ppermute(heads, "seq", [(i, (i + 7) % 8) for i in range(8)])
    tok_first, sum_first, part_first = call(
        grad_first_kernel,
        "grad_first",
        [meta, lengths, *common, mixed, gy, tie(gate_next, heads), full_io],
        [shape((4, tok_rows, width), B16), shape((8, width), F32), shape((group, model), F32)],
    )
    cube = shape((2, 2, 2, owned, 2 * width), B16)
    give = shape((2, 2, owned // 2, 2 * width), B16)
    early_terms, ga, gb = call(
        grad_early_kernel,
        "grad_early",
        [meta, *g_mid, y_tok, *x_one, tok_first],
        [cube, give, give],
    )
    early = Halving("early", meta, early_terms, (ga, gb))
    tok_rest, col_sums, norm_one, give3, give1, keep2, keep0 = call(
        grad_short_kernel,
        "grad_short",
        [
            meta, lengths, *common, gy, full_io, part_first, *x_one, norm1_gain, norm1_shift, tie(ggated, ga),
            ggated_next
        ],
        [shape((4, tok_rows, 2 * width), B16), shape((16, width), F32), shape((2, model), F32)] + sums_shapes,
    )
    result = shape((1, owned, hidden), F32)
    down_came = swap(tie(down_give, give3), "seq", 4)
    (grad_up,) = call(add_last_kernel, "up_last", [up_keep, tie(up_came, give3)], [result])
    given = early.one(grad_up)
    near, far, passed = pass_far(give3, give1, tie(keep2, given))
    late_terms, ga, gb = call(
        grad_late_kernel, "grad_late", [meta, *tie(tuple(x_one), passed), tok_rest], [cube, give, give]
    )
    late = Halving("late", meta, late_terms, (ga, gb))
    side, wide = call(
        filter_back_kernel,
        "filter_back",
        [
            meta, tie(grad_kernel, ga), grid, ramp, chans, feat, inner_weight, deep_weight, small_col, small_row, columns,
            sines, cosines
        ],
        [shape((filt, 4 * filt), F32), shape((filt, width), F32)],
    )

    (small,) = call(
        pack_small_kernel,
        "pack_small",
        [side, wide, sum_first, col_sums, gup, norm_one, norm_sums],
        [shape((2 * HALF, width), F32)],
    )
    came = swap(small, "seq", 1)
    (grad_down,) = call(add_last_kernel, "down_last", [down_keep, tie(down_came, small)], [result])
    given = early.two(grad_down)
    (grad_tokens,) = call(
        norm_first_back_kernel,
        "norm_first_back",
        [keep0, near, tie(far, given), tokens, grad_middle, norm1_gain],
        [row_f32],
    )
    given = late.one(grad_tokens)
    (small,) = call(add_small_kernel, "add_small", [small, tie(came, given)], [small])
    came = swap(small, "seq", 2)
    given = late.two(small)
    m_near, m_far, m_passed = pass_far(tie(m3, given), m1, m2)
    grad_out, first_in = call(
        early_last_kernel, "early_last", early.last(given), [shape((1, owned, width), F32), shape((owned, width), F32)]
    )
    (small,) = call(add_small_kernel, "add_small", [small, tie(came, grad_out, m_passed)], [small])
    came = swap(small, "seq", 4)
    (grad_in,) = call(
        late_last_kernel, "late_last", [*late.last(small), first_in], [shape((1, 3, owned, width), F32)]
    )
    (small,) = call(add_small_kernel, "add_small", [small, tie(came, grad_in)], [small])
    came = swap(small, "rep", 2)
    (layer_out,) = call(layer_out_kernel, "layer_out", [m0, m_near, tie(m_far, small), middle, down_bias], [row_b16])
    (small,) = call(
        list_small_kernel, "list_small", [meta, small, tie(came, layer_out)], [shape((3 * HALF, width), F32)]
    )
    came = swap(small, "rep", 1)
    vector = shape((1, model), F32)
    square, short = shape((1, filt, filt), F32), shape((1, filt), F32)
    triple = shape((3, 1, model), F32)
    outs = call(
        unpack_small_kernel,
        "unpack_small",
        [meta, small, came],
        [
            triple, shape((3, 3, 1, model), F32), triple, shape(params[10].shape, F32), short, square, short, square,
            short, short, shape(kernel_weight.shape, F32), vector, vector, vector, vector, vector, vector,
            shape(up_bias.shape, F32), vector,
        ],
    )
    return (
        layer_out,
        grad_tokens,
        grad_in.transpose(0, 2, 1, 3),
        outs[0].transpose(1, 0, 2),
        outs[1].transpose(2, 0, 1, 3),
        outs[2].transpose(1, 0, 2),
        outs[3].transpose(1, 0, 2),
        *outs[4:12],
        grad_out,
        *outs[12:17],
        grad_up,
        outs[17],
        grad_down,
        outs[18],
    )


def solution(mesh):
    rows = P(("seq", "rep"), None)
    cut = P(None, "seq", "rep")
    wide = P(None, "seq", None, "rep")
    whole = P()
    ins = [rows, rows, whole, wide] + [whole] * 12 + [cut] + [whole] * 5 + [cut, whole, cut, whole]
    outs = [rows, rows, wide] + [whole] * 12 + [cut] + [whole] * 5 + [cut, whole, cut, whole]
    fast = mesh.shape["seq"] == 8 and mesh.shape["rep"] == 4
    return jax.shard_map(
        per_device_fast if fast else per_device, mesh=mesh, in_specs=tuple(ins), out_specs=tuple(outs), check_vma=False
    )
```
